32 devices in a mesh: sec: 2 (over x), ty: 4 (over y, core), tx: 4 (over z).
Axes of the slice: x: 2, y: 2, z: 4, core: 2. Of those that a mesh axis runs over, the one named last changes fastest.
Arguments:
- descriptors: bfloat16 [2, 4, 4, 1024, 128], P('sec', 'ty', 'tx'), may hold values from -4 to 4, as said below
- positions: bfloat16 [2, 4, 4, 2, 1024], P('sec', 'ty', 'tx'), may hold values from -1 to 1
- vertex_ids: int32 [2, 4, 4, 1024], P('sec', 'ty', 'tx'), may hold values from 0 to 262143, as said below
- candidate_blocks: int32 [2, 4, 4, 32], P('sec', 'ty', 'tx'), may hold values from 0 to 127, as said below
- candidate_count: int32 [2, 4, 4], P('sec', 'ty', 'tx'), may hold values from 8 to 32, as said below
- displacement: float32 [2, 2, 512, 512], P('sec', None, 'ty', 'tx'), may hold values from -3 to 3
- stiffness: float32 [2, 512, 512], P('sec', 'ty', 'tx'), may hold values from 0.25 to 4
Outputs:
- relaxed: float32 [2, 2, 512, 512], P('sec', None, 'ty', 'tx')
The draws below stay inside these ranges and needn't reach their ends.
Inputs may be any that keep to these rules, and one draw needn't show every extreme that they name: `descriptors`: descriptor entries stay within the range. `candidate_blocks`: A list names distinct blocks tile * 8 + j of the next section; among its live entries at most 4 blocks come from any one tile, and some list has 4 live blocks of one tile. `candidate_count`: some tile has all 32 entries live. `vertex_ids`: ids follow the vertex numbering of the steps, anywhere in the section.
All inputs are finite; a program needn't handle non-finite values.
Results may differ from the reference program's by a relative error of at most 0.0019.
Values may be sent and summed in bfloat16 or wider, within the bound.
No kernel may reach another device: no remote copies, remote signals or barrier semaphores. Data moves between devices by JAX's collectives and lax.ppermute only.
A program may use at most 192 MiB of HBM per device.

```python
import math
import jax
import jax.numpy as jnp
from jax import lax

DESC = 128
PTS = 1024
BLK = 128
CAND = 32
MV = 128
ITERS = 4
NS = 2
TILE_ROWS = 4
TILE_COLS = 4
NTILE = 16
NB = 8
CAPB = 4
NYV = 512
NXV = 512


def first_blocks(block_key):
    return jax.random.permutation(block_key, NB)[:CAPB]


def one_list(list_key):
    order_key, block_key, mix_key = jax.random.split(list_key, 3)
    tile_order = jax.random.permutation(order_key, NTILE)
    chosen_blocks = jax.vmap(first_blocks)(jax.random.split(block_key, NTILE))
    block_pool = (tile_order[:, None] * NB + chosen_blocks[tile_order]).reshape(-1)
    picked = block_pool[:CAND]
    return picked[jax.random.permutation(mix_key, CAND)]


def candidate_lists(base_key):
    list_total = NS * NTILE
    all_lists = jax.vmap(one_list)(jax.random.split(jax.random.fold_in(base_key, 1), list_total))
    counts = jax.random.randint(jax.random.fold_in(base_key, 2), (list_total,), max(1, CAND // 4), CAND + 1)
    counts = counts.at[0].set(CAND)
    return (all_lists.reshape(NS, TILE_ROWS, TILE_COLS, CAND).astype(jnp.int32), counts.reshape(NS, TILE_ROWS, TILE_COLS).astype(jnp.int32))


def draw_candidate_blocks(key, part):
    return candidate_lists(jax.random.fold_in(key, 7))[0]


def draw_candidate_count(key, part):
    return candidate_lists(jax.random.fold_in(key, 7))[1]


def draw_vertex_ids(key, part):
    shape = (NS, TILE_ROWS, TILE_COLS, PTS)
    own_key, other_key, pick_key = jax.random.split(jax.random.fold_in(key, 5), 3)
    tile_base = (jnp.arange(NTILE, dtype=jnp.int32) * (MV * MV)).reshape(1, TILE_ROWS, TILE_COLS, 1)
    own_vertex = tile_base + jax.random.randint(own_key, shape, 0, MV * MV)
    other_vertex = jax.random.randint(other_key, shape, 0, NTILE * MV * MV)
    chosen = jax.random.randint(pick_key, shape, 0, 4) == 0
    vertex = jnp.where(chosen, other_vertex, own_vertex)
    vertex = vertex.at[0, 0, 0, 0].set(NTILE * MV * MV - 1)
    return vertex.astype(jnp.int32)


def draw_descriptors(key, part):
    shape = (NS, NTILE, PTS, DESC)
    base_key = jax.random.fold_in(key, 11)
    entries = jax.random.truncated_normal(base_key, -4.0, 4.0, shape, jnp.float32)
    return entries.reshape(NS, TILE_ROWS, TILE_COLS, PTS, DESC).astype(jnp.bfloat16)


def level_of(key, shape, pieces, least, top_value):
    def one(axis_at, parts):
        heights = jax.random.uniform(jax.random.fold_in(jax.random.fold_in(key, 6), axis_at), (parts,), jnp.float32, least / len(pieces), top_value / len(pieces))
        return jnp.repeat(jnp.exp(heights), shape[axis_at] // parts).reshape((-1,) + (1,) * (len(shape) - axis_at - 1))

    gain = one(*pieces[0])
    for cut in pieces[1:]:
        gain = gain * one(*cut)
    return gain


def noise(key, shape, deviation, most, cuts=(), held_as=jnp.bfloat16):
    values = deviation * jax.random.normal(key, shape, jnp.float32)
    if cuts:
        values = values * level_of(key, shape, cuts, -0.22, 0.18)
    return jnp.clip(values, -most, most).astype(held_as)


def setup_inputs(seed: int = 0) -> dict:
    arg_keys = jax.random.split(jax.random.key(seed), 8)
    descriptors = draw_descriptors(jax.random.fold_in(arg_keys[7], 71), 0)
    positions = jnp.clip(jax.random.uniform(arg_keys[1], (NS, TILE_ROWS, TILE_COLS, 2, PTS), jnp.float32, -1.0, 1.0) * level_of(arg_keys[1], (NS, TILE_ROWS, TILE_COLS, 2, PTS), ((0, 2), (1, 4), (2, 4)), -0.4, 0.0), -1.0, 1.0).astype(jnp.bfloat16)
    vertex_ids = draw_vertex_ids(jax.random.fold_in(arg_keys[7], 71), 0)
    candidate_blocks = draw_candidate_blocks(jax.random.fold_in(arg_keys[7], 71), 0)
    candidate_count = draw_candidate_count(jax.random.fold_in(arg_keys[7], 71), 0)
    displacement = noise(arg_keys[5], (NS, 2, NYV, NXV), 0.5, 3.0, ((0, 2), (2, 4), (3, 4)), jnp.float32)
    stiffness = jnp.clip(jnp.exp(math.log(4.0) - 2.7725887 * jax.random.uniform(arg_keys[6], (NS, NYV, NXV), jnp.float32) ** level_of(arg_keys[6], (NS, NYV, NXV), ((0, 2), (1, 4), (2, 4)), -0.2, 0.2)), 0.25, 4.0)
    return {"descriptors": descriptors, "positions": positions, "vertex_ids": vertex_ids, "candidate_blocks": candidate_blocks, "candidate_count": candidate_count, "displacement": displacement, "stiffness": stiffness}


def reference(descriptors, positions, vertex_ids, candidate_blocks, candidate_count, displacement, stiffness):
    spring_sec = 0.5
    spring_match = 1.0
    relax_rate = 0.8
    score_factor = 16.0 / DESC
    desc_all = descriptors.reshape(NS, NTILE, PTS, DESC)
    place_all = positions.reshape(NS, NTILE, 2, PTS).astype(jnp.float32)
    list_all = candidate_blocks.reshape(NS * NTILE, CAND)
    live_all = candidate_count.reshape(NS * NTILE)

    def match_tile(list_index):
        section = list_index // NTILE
        tile_index = list_index % NTILE
        following = jnp.minimum(section + 1, NS - 1)
        queries = desc_all[section, tile_index]
        next_plane = desc_all[following].reshape(NTILE * NB, BLK, DESC)
        plane_place = place_all[following].reshape(NTILE, 2, NB, BLK).transpose(0, 2, 1, 3).reshape(NTILE * NB, 2, BLK)
        block_list = list_all[list_index]
        key_rows = next_plane[block_list].reshape(CAND * BLK, DESC)
        key_place = plane_place[block_list].transpose(1, 0, 2).reshape(2, CAND * BLK)
        is_live = jnp.repeat(jnp.arange(CAND) < live_all[list_index], BLK)
        scores = jnp.dot(queries, key_rows.T, preferred_element_type=jnp.float32) * score_factor
        masked = jnp.where(is_live[None, :], scores, -1e30)
        row_top = jnp.max(masked, axis=1)
        weights = jnp.where(is_live[None, :], jnp.exp(masked - row_top[:, None]), 0.0)
        denominator = jnp.sum(weights, axis=1)
        target = jnp.einsum("ck,qk->cq", key_place, weights, precision=lax.Precision.HIGHEST) / denominator[None, :]
        has_next = (section < NS - 1).astype(jnp.float32)
        pull_vec = (target - place_all[section, tile_index]) * has_next
        return jnp.concatenate([pull_vec, jnp.broadcast_to(has_next, (1, PTS)).astype(jnp.float32)], axis=0)

    pulls = lax.map(match_tile, jnp.arange(NS * NTILE, dtype=jnp.int32))
    vertex = vertex_ids.reshape(NS * NTILE, PTS)
    tile_of = vertex // (MV * MV)
    within = vertex % (MV * MV)
    grid_row = (tile_of // TILE_COLS) * MV + within // MV
    grid_col = (tile_of % TILE_COLS) * MV + within % MV
    sec_of = jnp.broadcast_to((jnp.arange(NS * NTILE, dtype=jnp.int32) // NTILE)[:, None], vertex.shape)
    sums = jnp.zeros((NS, 3, NYV, NXV), jnp.float32)
    for channel in range(3):
        sums = sums.at[sec_of, channel, grid_row, grid_col].add(pulls[:, channel, :])
    pulled = sums[:, 0:2]
    matched = sums[:, 2][:, None]
    linked = ((jnp.arange(NS) > 0).astype(jnp.float32) + (jnp.arange(NS) < NS - 1).astype(jnp.float32))[:, None, None, None]
    gains = stiffness[:, None]
    moving = displacement
    for sweep in range(ITERS):
        padded = jnp.pad(moving, ((0, 0), (0, 0), (1, 1), (1, 1)))
        laplace = padded[:, :, 2:, 1:-1] + padded[:, :, :-2, 1:-1] + padded[:, :, 1:-1, 2:] + padded[:, :, 1:-1, :-2] - 4.0 * moving
        lower_sec = jnp.concatenate([jnp.zeros_like(moving[:1]), moving[:-1]], axis=0)
        upper_sec = jnp.concatenate([moving[1:], jnp.zeros_like(moving[:1])], axis=0)
        spring_force = gains * laplace + spring_sec * (lower_sec + upper_sec - linked * moving) + spring_match * (pulled - matched * moving)
        diagonal = 4.0 * gains + spring_sec * linked + spring_match * matched
        moving = moving + relax_rate * spring_force / diagonal
    return moving
```

```python
import functools
import math

import jax
import jax.numpy as jnp
from jax import lax
from jax.experimental import pallas as pl
from jax.experimental.pallas import tpu as pltpu
from jax.sharding import PartitionSpec as P

BLK = 128
ITERS = 4
LANES = 128
VMEM_BYTES = 48 * 1024 * 1024

spring_sec = 0.5
spring_match = 1.0
relax_rate = 0.8


def passed_along(value, axis, by):
    devices = lax.axis_size(axis)
    pairs = [(i, i + by) for i in range(devices) if 0 <= i + by < devices]
    return lax.ppermute(value, axis, pairs)


def nt_dot(a, b):
    return lax.dot_general(a, b, (((1,), (1,)), ((), ())), preferred_element_type=jnp.float32)


def match_kernel(
    point_total,
    score_scale,
    list_ref,
    query_ref,
    ids_ref,
    keys_hbm,
    out_ref,
    key_buf,
    place_buf,
    top_buf,
    sum_buf,
    key_sems,
    place_sem,
):
    cand = key_buf.shape[0] - 1
    per_tile = point_total // BLK
    count = list_ref[cand]
    pairs = (count + 1) // 2
    slots = pairs * 2

    place_copy = pltpu.make_async_copy(
        keys_hbm.at[:, pl.ds(point_total, 2 * per_tile), :], place_buf, place_sem
    )
    place_copy.start()

    def block_at(slot):
        return list_ref[jnp.where(slot < count, slot, 0)]

    def key_copy(slot):
        block = block_at(slot)
        return pltpu.make_async_copy(
            keys_hbm.at[
                block // per_tile, pl.ds(pl.multiple_of((block % per_tile) * BLK, BLK), BLK), :
            ],
            key_buf.at[slot],
            key_sems.at[slot],
        )

    @pl.loop(0, slots)
    def _(slot):
        key_copy(slot).start()

    place_copy.wait()

    @pl.loop(0, slots)
    def _(slot):
        key_copy(slot).wait()

    queries = query_ref[pl.ds(0, point_total), :]

    def pair_scores(pair):
        keys = key_buf[pl.ds(pair * 2, 2)].reshape(2 * BLK, key_buf.shape[2])
        return nt_dot(queries, keys) * score_scale

    def place_rows(slot):
        block = block_at(slot)
        rows = place_buf[block // per_tile].astype(jnp.float32)
        row_at = lax.broadcasted_iota(jnp.int32, rows.shape, 0)
        within = block % per_tile
        x = jnp.sum(jnp.where(row_at == within, rows, 0.0), axis=0, keepdims=True)
        y = jnp.sum(jnp.where(row_at == per_tile + within, rows, 0.0), axis=0, keepdims=True)
        return x, y

    def accumulate():
        sum_buf[...] = jnp.zeros_like(sum_buf)

        @pl.loop(0, pairs)
        def _(pair):
            scores = pair_scores(pair)
            top = top_buf[...]
            weights = jnp.exp2(scores - jnp.concatenate([top, top], axis=1)).astype(jnp.bfloat16)
            x0, y0 = place_rows(pair * 2)
            x1, y1 = place_rows(pair * 2 + 1)
            live = jnp.where(pair * 2 + 1 < count, 1.0, 0.0).astype(jnp.float32)
            x = jnp.concatenate([x0, x1 * live], axis=1)
            y = jnp.concatenate([y0, y1 * live], axis=1)
            ones = jnp.concatenate([jnp.ones_like(x0), jnp.full_like(x0, live)], axis=1)
            row_at = lax.broadcasted_iota(jnp.int32, (LANES, 2 * BLK), 0)
            place = jnp.where(
                row_at == 0, x, jnp.where(row_at == 1, y, jnp.where(row_at == 2, ones, 0.0))
            )
            sum_buf[...] += nt_dot(weights, place.astype(jnp.bfloat16))

    def set_top(top):
        top_buf[...] = jnp.broadcast_to(top, top_buf.shape)

    set_top(jnp.max(pair_scores(0), axis=1, keepdims=True))
    accumulate()

    total = sum_buf[:, 2:3]
    fits = jnp.min(jnp.where(total < 1e38, 1.0, 0.0))

    @pl.when((fits < 0.5) & (count > 0))
    def _():
        top_buf[...] = jnp.full_like(top_buf, -jnp.inf)

        @pl.loop(0, pairs)
        def _(pair):
            top = jnp.max(pair_scores(pair), axis=1, keepdims=True)
            top_buf[...] = jnp.maximum(top_buf[...], top)

        accumulate()

    own = query_ref[pl.ds(point_total, 2 * per_tile), :].astype(jnp.float32)
    for chunk in range(per_tile):
        summed = sum_buf[pl.ds(chunk * BLK, BLK), :].T
        target = summed[0:2, :] / summed[2:3, :]
        out_ref[pl.ds(chunk, 1), :] = target[0:1, :] - own[chunk : chunk + 1, :]
        out_ref[pl.ds(per_tile + chunk, 1), :] = (
            target[1:2, :] - own[per_tile + chunk : per_tile + chunk + 1, :]
        )
    out_ref[pl.ds(2 * per_tile, per_tile), :] = ids_ref[...].astype(jnp.float32)


def match(block_list, queries, ids, keys, score_factor):
    point_total = ids.shape[0] * LANES
    cand = block_list.shape[0] - 1
    width = queries.shape[1]
    tiles = keys.shape[0]
    per_tile = point_total // BLK
    return pl.pallas_call(
        functools.partial(match_kernel, point_total, score_factor * math.log2(math.e)),
        out_shape=jax.ShapeDtypeStruct((3 * per_tile, LANES), jnp.float32),
        in_specs=[
            pl.BlockSpec(memory_space=pltpu.SMEM),
            pl.BlockSpec(memory_space=pltpu.VMEM),
            pl.BlockSpec(memory_space=pltpu.VMEM),
            pl.BlockSpec(memory_space=pl.ANY),
        ],
        out_specs=pl.BlockSpec(memory_space=pltpu.VMEM),
        scratch_shapes=[
            pltpu.VMEM((cand + 1, BLK, width), jnp.bfloat16),
            pltpu.VMEM((tiles, 2 * per_tile, LANES), jnp.bfloat16),
            pltpu.VMEM((point_total, LANES), jnp.float32),
            pltpu.VMEM((point_total, LANES), jnp.float32),
            pltpu.SemaphoreType.DMA((cand + 1,)),
            pltpu.SemaphoreType.DMA,
        ],
        compiler_params=pltpu.CompilerParams(vmem_limit_bytes=VMEM_BYTES),
        cost_estimate=pl.CostEstimate(
            flops=4 * point_total * cand * BLK * width,
            bytes_accessed=2 * cand * BLK * width,
            transcendentals=point_total * cand * BLK,
        ),
        name="match",
    )(block_list, queries, ids, keys)


def vertex_sums(side, halo, tile_cols, row_base, col_base, tiles, points_ref, sum_ref):
    span = side + 2 * halo
    tall = -(-span // 16) * 16
    wide = sum_ref.shape[2]
    per_tile = points_ref.shape[1] // 3

    def folded(at):
        return jnp.where(
            (at >= 0) & (at < side + halo), at, jnp.where((at < 0) & (at >= -halo), at + span, -1)
        )

    sum_ref[...] = jnp.zeros_like(sum_ref)

    @pl.loop(0, tiles)
    def _(tile):
        values = points_ref[tile]
        ids = values[2 * per_tile : 3 * per_tile, :].astype(jnp.int32)
        tile_of = lax.div(ids, side * side)
        within = lax.rem(ids, side * side)
        row = folded(lax.div(tile_of, tile_cols) * side + lax.div(within, side) - row_base)
        col = folded(lax.rem(tile_of, tile_cols) * side + lax.rem(within, side) - col_base)
        along = functools.partial(jnp.concatenate, axis=1)

        def flat(v):
            return along([v[i : i + 1, :] for i in range(per_tile)])

        at = lax.broadcasted_iota(jnp.int32, (tall, per_tile * LANES), 0)
        row_hit = at == flat(row)
        col_hit = jnp.where(at == flat(col), 1.0, 0.0).astype(jnp.bfloat16)
        col_hit = jnp.concatenate(
            [col_hit, jnp.zeros((wide - tall, per_tile * LANES), jnp.bfloat16)], axis=0
        )
        x = flat(values[0:per_tile, :])
        y = flat(values[per_tile : 2 * per_tile, :])
        x_high = x.astype(jnp.bfloat16).astype(jnp.float32)
        y_high = y.astype(jnp.bfloat16).astype(jnp.float32)
        for channel, parts in enumerate(((x_high, x - x_high), (y_high, y - y_high), (1.0,))):
            for part in parts:
                picked = jnp.where(row_hit, part, 0.0).astype(jnp.bfloat16)
                sum_ref[channel] += nt_dot(picked, col_hit)

    for channel in range(3):
        last = sum_ref[channel, :, pl.ds(side, wide - side)]
        turned = pltpu.roll(last, wide - side - 2 * halo, 1)
        lane = lax.broadcasted_iota(jnp.int32, last.shape, 1)
        sum_ref[channel, :, pl.ds(side, wide - side)] = jnp.where(
            lane < halo, last, jnp.where(lane >= wide - side - halo, turned, 0.0)
        )


def sums_kernel(side, halo, tile_cols, tiles, first, at_ref, points_ref, out_ref, sum_ref):
    vertex_sums(
        side, halo, tile_cols, at_ref[0], at_ref[1], tiles, points_ref.at[pl.ds(first, tiles)], sum_ref
    )
    out_ref[...] = sum_ref[:, pl.ds(0, out_ref.shape[1]), :]


def relax_kernel(
    side, halo, tile_cols, tiles, first, extent, at_ref, points_ref, mesh_ref, out_ref, sum_ref
):
    vertex_sums(
        side, halo, tile_cols, at_ref[0], at_ref[1], tiles, points_ref.at[pl.ds(first, tiles)], sum_ref
    )
    span = side + 2 * halo
    wide = sum_ref.shape[2]
    shape = (span, wide)
    row = lax.broadcasted_iota(jnp.int32, shape, 0)
    col = lax.broadcasted_iota(jnp.int32, shape, 1)
    row = jnp.where(row < side + halo, row, row - span) + at_ref[0]
    col = jnp.where(col < side + halo, col, col - wide) + at_ref[1]
    inside = (row >= 0) & (row < extent[0]) & (col >= 0) & (col < extent[1])
    own_pulled = (at_ref[2] == 0).astype(jnp.float32)
    linked = 1.0
    matched = sum_ref[2, pl.ds(0, span), :]
    moving, gains, has, step = [], [], [], []
    for part, pulled in enumerate((own_pulled, 1.0 - own_pulled)):
        gain = mesh_ref[part * 3 + 2]
        diagonal = 4.0 * gain + spring_sec * linked + spring_match * matched * pulled
        gains.append(gain)
        has.append(matched * pulled)
        step.append(jnp.where(inside, relax_rate / diagonal, 0.0))
        moving.append(
            [
                (mesh_ref[part * 3 + c], sum_ref[c, pl.ds(0, span), :] * pulled)
                for c in range(2)
            ]
        )
    for sweep in range(ITERS):
        later = []
        for part in range(2):
            row_of = []
            for c in range(2):
                u, pulled = moving[part][c]
                other = moving[1 - part][c][0]
                laplace = (
                    pltpu.roll(u, 1, 0)
                    + pltpu.roll(u, span - 1, 0)
                    + pltpu.roll(u, 1, 1)
                    + pltpu.roll(u, wide - 1, 1)
                    - 4.0 * u
                )
                force = (
                    gains[part] * laplace
                    + spring_sec * (other - linked * u)
                    + spring_match * (pulled - has[part] * u)
                )
                row_of.append((u + step[part] * force, pulled))
            later.append(row_of)
        moving = later
    for c in range(2):
        out_ref[c] = moving[0][c][0][0:side, 0:side]


def with_halo(value, halo, wide):
    side = value.shape[1]
    after = passed_along(value[:, :halo], "ty", -1)
    before = passed_along(value[:, side - halo :], "ty", 1)
    value = jnp.concatenate([value, after, before], axis=1)
    after = passed_along(value[:, :, :halo], "tx", -1)
    before = passed_along(value[:, :, side - halo :], "tx", 1)
    gap = jnp.zeros(value.shape[:2] + (wide - side - 2 * halo,), value.dtype)
    return jnp.concatenate([value, after, gap, before], axis=2)


def per_device(
    descriptors, positions, vertex_ids, candidate_blocks, candidate_count, displacement, stiffness
):
    point_total, width = descriptors.shape[3:]
    per_tile = point_total // BLK
    tile_rows, tile_cols = lax.axis_size("ty"), lax.axis_size("tx")
    sections = lax.axis_size("sec")
    tiles = tile_rows * tile_cols
    sec_index = lax.axis_index("sec")
    side = displacement.shape[3]
    halo = ITERS
    wide = 2 * LANES * (-(-side // LANES)) if side % LANES == 0 else side + 2 * LANES
    score_factor = 16.0 / width

    packed = jnp.concatenate(
        [descriptors[0, 0, 0], positions[0, 0, 0].reshape(2 * per_tile, BLK)], axis=0
    )
    whole = jnp.concatenate(
        [vertex_ids[0, 0, 0], candidate_blocks[0, 0, 0], candidate_count[0, 0, 0][None]]
    )
    keys = lax.all_gather(packed, ("ty", "tx"), axis=0, tiled=False)
    queries = passed_along(packed, "sec", 1)
    whole = passed_along(whole, "sec", 1)
    ids = whole[:point_total].reshape(per_tile, LANES)
    points = match(whole[point_total:], queries, ids, keys, score_factor)

    at = jnp.stack(
        [lax.axis_index("ty") * side, lax.axis_index("tx") * side, sec_index]
    ).astype(jnp.int32)
    extent = (side * tile_rows, side * tile_cols)
    own_mesh = jnp.concatenate([displacement[0], stiffness], axis=0)
    span = side + 2 * halo
    sum_shape = pltpu.VMEM((3, -(-span // 16) * 16, wide), jnp.float32)

    if sections == 2:
        other_mesh = lax.ppermute(own_mesh, "sec", [(0, 1), (1, 0)])
        mesh_values = with_halo(jnp.concatenate([own_mesh, other_mesh], axis=0), halo, wide)
        points = lax.all_gather(points, ("sec", "ty", "tx"), axis=0, tiled=False)
        relaxed = pl.pallas_call(
            functools.partial(relax_kernel, side, halo, tile_cols, tiles, tiles, extent),
            out_shape=jax.ShapeDtypeStruct((2, side, side), jnp.float32),
            in_specs=[
                pl.BlockSpec(memory_space=pltpu.SMEM),
                pl.BlockSpec(memory_space=pltpu.VMEM),
                pl.BlockSpec(memory_space=pltpu.VMEM),
            ],
            out_specs=pl.BlockSpec(memory_space=pltpu.VMEM),
            scratch_shapes=[sum_shape],
            compiler_params=pltpu.CompilerParams(vmem_limit_bytes=VMEM_BYTES),
            name="relax",
        )(at, points, mesh_values)
        return relaxed[None]

    mesh_values = with_halo(own_mesh, halo, wide)
    points = lax.all_gather(points, ("ty", "tx"), axis=0, tiled=False)
    points = passed_along(points, "sec", -1)
    sums = pl.pallas_call(
        functools.partial(sums_kernel, side, halo, tile_cols, tiles, 0),
        out_shape=jax.ShapeDtypeStruct((3, span, wide), jnp.float32),
        in_specs=[
            pl.BlockSpec(memory_space=pltpu.SMEM),
            pl.BlockSpec(memory_space=pltpu.VMEM),
        ],
        out_specs=pl.BlockSpec(memory_space=pltpu.VMEM),
        scratch_shapes=[sum_shape],
        compiler_params=pltpu.CompilerParams(vmem_limit_bytes=VMEM_BYTES),
        name="sums",
    )(at, points)
    has_next = (sec_index < sections - 1).astype(jnp.float32)
    linked = (sec_index > 0).astype(jnp.float32) + has_next
    pulled, matched = sums[0:2] * has_next, sums[2] * has_next
    moving, gains = mesh_values[0:2], mesh_values[2]
    row = jnp.arange(span)[:, None]
    col = jnp.arange(wide)[None, :]
    row = jnp.where(row < side + halo, row, row - span) + at[0]
    col = jnp.where(col < side + halo, col, col - wide) + at[1]
    inside = (row >= 0) & (row < extent[0]) & (col >= 0) & (col < extent[1])
    diagonal = 4.0 * gains + spring_sec * linked + spring_match * matched
    step = jnp.where(inside, relax_rate / jnp.where(inside, diagonal, 1.0), 0.0)
    for sweep in range(ITERS):
        lower_sec = passed_along(moving, "sec", 1)
        upper_sec = passed_along(moving, "sec", -1)
        laplace = (
            jnp.roll(moving, 1, 1)
            + jnp.roll(moving, -1, 1)
            + jnp.roll(moving, 1, 2)
            + jnp.roll(moving, -1, 2)
            - 4.0 * moving
        )
        force = (
            gains * laplace
            + spring_sec * (lower_sec + upper_sec - linked * moving)
            + spring_match * (pulled - matched * moving)
        )
        moving = moving + step * force
    return moving[None, :, :side, :side]


def solution(mesh):
    in_specs = (
        P("sec", "ty", "tx", None, None),
        P("sec", "ty", "tx", None, None),
        P("sec", "ty", "tx", None),
        P("sec", "ty", "tx", None),
        P("sec", "ty", "tx"),
        P("sec", None, "ty", "tx"),
        P("sec", "ty", "tx"),
    )
    out_specs = P("sec", None, "ty", "tx")
    return jax.shard_map(
        per_device, mesh=mesh, in_specs=in_specs, out_specs=out_specs, check_vma=False
    )
```

```python
import functools
import math

import jax
import jax.numpy as jnp
from jax import lax
from jax.experimental import pallas as pl
from jax.experimental.pallas import tpu as pltpu
from jax.sharding import PartitionSpec as P

BLK = 128
ITERS = 4
LANES = 128
PLACE_ROWS = 16
VMEM_BYTES = 24 * 1024 * 1024

spring_sec = 0.5
spring_match = 1.0
relax_rate = 0.8


def passed_along(value, axis, by):
    devices = lax.axis_size(axis)
    pairs = [(i, i + by) for i in range(devices) if 0 <= i + by < devices]
    return lax.ppermute(value, axis, pairs)


def exchanged(value, axes):
    return lax.all_to_all(value, axes, split_axis=0, concat_axis=0, tiled=True)


def spread(value, axes):
    copies = jnp.broadcast_to(value[None], (lax.axis_size(axes),) + value.shape)
    return exchanged(copies, axes)


def nt_dot(a, b):
    return lax.dot_general(a, b, (((1,), (1,)), ((), ())), preferred_element_type=jnp.float32)


def in_vmem(count):
    return [pl.BlockSpec(memory_space=pltpu.VMEM)] * count


def in_smem():
    return pl.BlockSpec(memory_space=pltpu.SMEM)


def match_kernel(scale, work_ref, query_ref, key_ref, out_ref, place_buf):
    shares, tile_rows, out_rows, _ = out_ref.shape
    rows = out_rows // 4
    point_total = shares * rows * LANES
    key_tiles = key_ref.shape[0]
    key_rows = key_ref.shape[1] - PLACE_ROWS
    part = key_rows // BLK
    total = key_tiles * part
    step = 256 if point_total % 256 == 0 else LANES

    row_at = lax.broadcasted_iota(jnp.int32, (PLACE_ROWS, LANES), 0)
    for tile in range(key_tiles):
        place = key_ref[tile, pl.ds(key_rows, PLACE_ROWS), :].astype(jnp.float32)
        for j in range(part):
            x, y = place[j : j + 1, :], place[part + j : part + j + 1, :]
            stacked = jnp.where(
                row_at == 0, x, jnp.where(row_at == 1, y, jnp.where(row_at == 2, 1.0, 0.0))
            )
            place_buf[tile * part + j] = stacked.astype(jnp.bfloat16)

    for tile in range(tile_rows):
        count = work_ref[tile, total]

        def body(pair, carry):
            tops, sums = carry
            live = 2 * pair + 1 < count
            first = work_ref[tile, 2 * pair]
            second = work_ref[tile, jnp.where(live, 2 * pair + 1, 2 * pair)]

            def keys_of(block):
                at = pl.multiple_of(lax.rem(block, part) * BLK, BLK)
                return key_ref[lax.div(block, part), pl.ds(at, BLK), :]

            keys = jnp.concatenate([keys_of(first), keys_of(second)], axis=0)
            kept = jnp.where(live, 1.0, 0.0).astype(jnp.bfloat16)
            place = jnp.concatenate([place_buf[first], place_buf[second] * kept], axis=1)
            new_tops, new_sums = [], []
            for c in range(point_total // step):
                queries = query_ref[tile, pl.ds(c * step, step), :]
                scores = nt_dot(keys, queries) * scale
                top = jnp.maximum(tops[c], jnp.max(scores, axis=0, keepdims=True))
                weights = jnp.exp2(scores - top).astype(jnp.bfloat16)
                added = jnp.dot(place, weights, preferred_element_type=jnp.float32)
                new_tops.append(top)
                new_sums.append(sums[c] * jnp.exp2(tops[c] - top) + added)
            return tuple(new_tops), tuple(new_sums)

        chunks = point_total // step
        tops, sums = lax.fori_loop(
            0,
            (count + 1) // 2,
            body,
            (
                tuple(jnp.full((1, step), -1e30, jnp.float32) for _ in range(chunks)),
                tuple(jnp.zeros((PLACE_ROWS, step), jnp.float32) for _ in range(chunks)),
            ),
        )
        per_chunk = step // LANES
        for row in range(shares * rows):
            c, lanes = row // per_chunk, slice((row % per_chunk) * LANES, (row % per_chunk + 1) * LANES)
            share, at = row // rows, row % rows
            for place, value in enumerate(
                (tops[c][:, lanes], sums[c][2:3, lanes], sums[c][0:1, lanes], sums[c][1:2, lanes])
            ):
                out_ref[share, tile, pl.ds(place * rows + at, 1), :] = value


def match(work, queries, keys, score_factor, shares, point_total):
    tile_rows = queries.shape[0]
    width = queries.shape[2]
    key_tiles = keys.shape[0]
    part = (keys.shape[1] - PLACE_ROWS) // BLK
    rows = point_total // LANES // shares
    pairs = tile_rows * key_tiles * part
    return pl.pallas_call(
        functools.partial(match_kernel, score_factor * math.log2(math.e)),
        out_shape=jax.ShapeDtypeStruct((shares, tile_rows, 4 * rows, LANES), jnp.float32),
        in_specs=[in_smem()] + in_vmem(2),
        out_specs=pl.BlockSpec(memory_space=pltpu.VMEM),
        scratch_shapes=[pltpu.VMEM((key_tiles * part, PLACE_ROWS, LANES), jnp.bfloat16)],
        compiler_params=pltpu.CompilerParams(vmem_limit_bytes=VMEM_BYTES),
        cost_estimate=pl.CostEstimate(
            flops=pairs * point_total * BLK * width,
            bytes_accessed=2 * (queries.size + keys.size),
            transcendentals=pairs * point_total * BLK // 4,
        ),
        name="match",
    )(work, queries, keys)


def combine_kernel(parts_ref, place_ref, out_ref):
    parts, out_rows, _ = parts_ref.shape
    rows = out_rows // 4
    tops = [parts_ref[i, 0:rows, :] for i in range(parts)]
    top = functools.reduce(jnp.maximum, tops)
    total = x = y = jnp.zeros_like(top)
    for i in range(parts):
        gain = jnp.exp2(tops[i] - top)
        total += gain * parts_ref[i, rows : 2 * rows, :]
        x += gain * parts_ref[i, 2 * rows : 3 * rows, :]
        y += gain * parts_ref[i, 3 * rows :, :]
    pull = jnp.concatenate([x / total, y / total], axis=0) - place_ref[...].astype(jnp.float32)
    for i in range(out_ref.shape[0]):
        out_ref[i] = pull


def combine(parts, place, copies):
    return pl.pallas_call(
        combine_kernel,
        out_shape=jax.ShapeDtypeStruct((copies,) + place.shape, jnp.float32),
        in_specs=in_vmem(2),
        out_specs=pl.BlockSpec(memory_space=pltpu.VMEM),
        name="combine",
    )(parts, place)


def vertex_sums(side, halo, tile_cols, at_ref, ids_ref, points_ref, sum_ref):
    span = side + 2 * halo
    tall = -(-span // 16) * 16
    wide = sum_ref.shape[2]
    shares, tiles, both_rows, _ = points_ref.shape
    rows = both_rows // 2
    along = functools.partial(jnp.concatenate, axis=1)

    def folded(at):
        return jnp.where(
            (at >= 0) & (at < side + halo), at, jnp.where((at < 0) & (at >= -halo), at + span, -1)
        )

    sum_ref[...] = jnp.zeros_like(sum_ref)

    @pl.loop(0, tiles)
    def _(tile):
        ids = ids_ref[tile]
        tile_of = lax.div(ids, side * side)
        within = lax.rem(ids, side * side)
        row = folded(lax.div(tile_of, tile_cols) * side + lax.div(within, side) - at_ref[0])
        col = folded(lax.rem(tile_of, tile_cols) * side + lax.rem(within, side) - at_ref[1])
        values = [points_ref[share, tile] for share in range(shares)]
        x = along([v[i : i + 1, :] for v in values for i in range(rows)])
        y = along([v[i : i + 1, :] for v in values for i in range(rows, 2 * rows)])
        row, col = (along([v[i : i + 1, :] for i in range(shares * rows)]) for v in (row, col))
        count = row.shape[1]
        at = lax.broadcasted_iota(jnp.int32, (tall, count), 0)
        row_hit = at == row
        col_hit = jnp.where(at == col, 1.0, 0.0).astype(jnp.bfloat16)
        col_hit = jnp.concatenate(
            [col_hit, jnp.zeros((wide - tall, count), jnp.bfloat16)], axis=0
        )
        x_high = x.astype(jnp.bfloat16).astype(jnp.float32)
        y_high = y.astype(jnp.bfloat16).astype(jnp.float32)
        picked = jnp.concatenate(
            [
                jnp.where(row_hit, part, 0.0).astype(jnp.bfloat16)
                for part in (x_high, x - x_high, y_high, y - y_high, 1.0)
            ],
            axis=0,
        )
        summed = nt_dot(picked, col_hit)
        sum_ref[0] += summed[0:tall] + summed[tall : 2 * tall]
        sum_ref[1] += summed[2 * tall : 3 * tall] + summed[3 * tall : 4 * tall]
        sum_ref[2] += summed[4 * tall :]

    for channel in range(3):
        last = sum_ref[channel, :, pl.ds(side, wide - side)]
        turned = pltpu.roll(last, wide - side - 2 * halo, 1)
        lane = lax.broadcasted_iota(jnp.int32, last.shape, 1)
        sum_ref[channel, :, pl.ds(side, wide - side)] = jnp.where(
            lane < halo, last, jnp.where(lane >= wide - side - halo, turned, 0.0)
        )


def sums_kernel(side, halo, tile_cols, at_ref, ids_ref, points_ref, out_ref, sum_ref):
    vertex_sums(side, halo, tile_cols, at_ref, ids_ref, points_ref, sum_ref)
    out_ref[...] = sum_ref[:, pl.ds(0, out_ref.shape[1]), :]


def relax_kernel(
    side, halo, tile_cols, extent, at_ref, ids_ref, points_ref, mesh_ref, out_ref, sum_ref
):
    vertex_sums(side, halo, tile_cols, at_ref, ids_ref, points_ref, sum_ref)
    span = side + 2 * halo
    wide = sum_ref.shape[2]
    shape = (span, wide)
    row = lax.broadcasted_iota(jnp.int32, shape, 0)
    col = lax.broadcasted_iota(jnp.int32, shape, 1)
    row = jnp.where(row < side + halo, row, row - span) + at_ref[0]
    col = jnp.where(col < side + halo, col, col - wide) + at_ref[1]
    inside = (row >= 0) & (row < extent[0]) & (col >= 0) & (col < extent[1])
    own_pulled = (at_ref[2] == 0).astype(jnp.float32)
    linked = 1.0
    matched = sum_ref[2, pl.ds(0, span), :]
    moving, gains, has, step = [], [], [], []
    for part, pulled in enumerate((own_pulled, 1.0 - own_pulled)):
        gain = mesh_ref[part * 3 + 2]
        diagonal = 4.0 * gain + spring_sec * linked + spring_match * matched * pulled
        gains.append(gain)
        has.append(matched * pulled)
        step.append(jnp.where(inside, relax_rate / diagonal, 0.0))
        moving.append(
            [
                (mesh_ref[part * 3 + c], sum_ref[c, pl.ds(0, span), :] * pulled)
                for c in range(2)
            ]
        )
    for sweep in range(ITERS):
        later = []
        for part in range(2):
            row_of = []
            for c in range(2):
                u, pulled = moving[part][c]
                other = moving[1 - part][c][0]
                laplace = (
                    pltpu.roll(u, 1, 0)
                    + pltpu.roll(u, span - 1, 0)
                    + pltpu.roll(u, 1, 1)
                    + pltpu.roll(u, wide - 1, 1)
                    - 4.0 * u
                )
                force = (
                    gains[part] * laplace
                    + spring_sec * (other - linked * u)
                    + spring_match * (pulled - has[part] * u)
                )
                row_of.append((u + step[part] * force, pulled))
            later.append(row_of)
        moving = later
    for c in range(2):
        out_ref[c] = moving[0][c][0][0:side, 0:side]


def with_halo(value, halo, wide):
    side = value.shape[1]
    after = passed_along(value[:, :halo], "ty", -1)
    before = passed_along(value[:, side - halo :], "ty", 1)
    value = jnp.concatenate([value, after, before], axis=1)
    after = passed_along(value[:, :, :halo], "tx", -1)
    before = passed_along(value[:, :, side - halo :], "tx", 1)
    gap = jnp.zeros(value.shape[:2] + (wide - side - 2 * halo,), value.dtype)
    return jnp.concatenate([value, after, gap, before], axis=2)


def sweeps(moving, gains, sums, at, side, halo, extent):
    sections = lax.axis_size("sec")
    sec_index = at[2]
    has_next = (sec_index < sections - 1).astype(jnp.float32)
    linked = (sec_index > 0).astype(jnp.float32) + has_next
    pulled, matched = sums[0:2] * has_next, sums[2] * has_next
    span, wide = moving.shape[1:]
    row = jnp.arange(span)[:, None]
    col = jnp.arange(wide)[None, :]
    row = jnp.where(row < side + halo, row, row - span) + at[0]
    col = jnp.where(col < side + halo, col, col - wide) + at[1]
    inside = (row >= 0) & (row < extent[0]) & (col >= 0) & (col < extent[1])
    diagonal = 4.0 * gains + spring_sec * linked + spring_match * matched
    step = jnp.where(inside, relax_rate / jnp.where(inside, diagonal, 1.0), 0.0)
    for sweep in range(ITERS):
        lower_sec = passed_along(moving, "sec", 1)
        upper_sec = passed_along(moving, "sec", -1)
        laplace = (
            jnp.roll(moving, 1, 1)
            + jnp.roll(moving, -1, 1)
            + jnp.roll(moving, 1, 2)
            + jnp.roll(moving, -1, 2)
            - 4.0 * moving
        )
        force = (
            gains * laplace
            + spring_sec * (lower_sec + upper_sec - linked * moving)
            + spring_match * (pulled - matched * moving)
        )
        moving = moving + step * force
    return moving[:, :side, :side]


def local_work(lists, counts, blocks):
    total = blocks.shape[0]
    is_live = jnp.arange(lists.shape[1])[None, :] < counts[:, None]
    hit = (lists[:, :, None] == blocks[None, None, :]) & is_live[:, :, None]
    live = jnp.any(hit, axis=1)
    spot = jnp.arange(total)
    rank = jnp.sum(live[:, None, :] & (spot[None, :] < spot[:, None])[None], axis=2)
    taken = live[:, None, :] & (rank[:, None, :] == spot[None, :, None])
    packed = jnp.sum(jnp.where(taken, spot[None, None, :], 0), axis=2)
    number = jnp.sum(live, axis=1)
    return jnp.concatenate([packed, number[:, None]], axis=1).astype(jnp.int32)


def per_device(
    descriptors, positions, vertex_ids, candidate_blocks, candidate_count, displacement, stiffness
):
    point_total, width = descriptors.shape[3:]
    per_tile = point_total // BLK
    tile_rows, tile_cols = lax.axis_size("ty"), lax.axis_size("tx")
    sections = lax.axis_size("sec")
    sec_index = lax.axis_index("sec")
    tiles = tile_rows * tile_cols
    side = displacement.shape[3]
    halo = ITERS
    span = side + 2 * halo
    wide = -(-span // LANES) * LANES
    shares = 2 if sections == 2 and per_tile % 2 == 0 else 1
    part = per_tile // shares
    key_rows = part * BLK

    own_desc = descriptors[0, 0, 0]
    own_place = positions[0, 0, 0].reshape(2, per_tile, BLK)

    def key_part(share):
        blocks = slice(share * part, (share + 1) * part)
        place = own_place[:, blocks].reshape(2 * part, BLK)
        filler = jnp.zeros((PLACE_ROWS - 2 * part, BLK), place.dtype)
        desc = own_desc[share * key_rows : (share + 1) * key_rows]
        return jnp.concatenate([desc, place, filler], axis=0)

    query = jnp.concatenate([own_desc, own_place.reshape(2 * per_tile, BLK)], axis=0)
    whole = jnp.concatenate(
        [vertex_ids[0, 0, 0], candidate_blocks[0, 0, 0], candidate_count[0, 0, 0][None]]
    )
    if shares == 2:
        first = sec_index == 0
        key = jnp.where(first, passed_along(key_part(0), "sec", -1), key_part(1))
        query = jnp.where(first, query, passed_along(query, "sec", 1))
        whole = jnp.where(first, whole, passed_along(whole, "sec", 1))
        share = sec_index
    else:
        key = key_part(0)
        query = passed_along(query, "sec", 1)
        whole = passed_along(whole, "sec", 1)
        share = 0
    keys = spread(key, "tx")
    queries = spread(query, "ty")
    ids = spread(whole[:point_total].reshape(per_tile, LANES), ("ty", "tx"))
    lists = spread(whole[point_total:], "ty")

    key_tile = lax.axis_index("ty") * tile_cols + jnp.arange(tile_cols)
    blocks = (key_tile[:, None] * per_tile + share * part + jnp.arange(part)[None, :]).reshape(-1)
    work = local_work(lists[:, :-1], lists[:, -1], blocks)
    parts = match(work, queries, keys, 16.0 / width, shares, point_total)

    place = query[point_total:].reshape(2, shares, part, LANES)
    place = lax.dynamic_index_in_dim(place, share, 1, keepdims=False).reshape(2 * part, LANES)
    at = jnp.stack(
        [lax.axis_index("ty") * side, lax.axis_index("tx") * side, sec_index]
    ).astype(jnp.int32)
    extent = (side * tile_rows, side * tile_cols)
    own_mesh = jnp.concatenate([displacement[0], stiffness], axis=0)
    sum_shape = pltpu.VMEM((3, -(-span // 16) * 16, wide), jnp.float32)

    if shares == 2:
        other_mesh = lax.ppermute(own_mesh, "sec", [(0, 1), (1, 0)])
        mesh_values = with_halo(jnp.concatenate([own_mesh, other_mesh], axis=0), halo, wide)
        parts = exchanged(parts.reshape((-1,) + parts.shape[2:]), ("sec", "ty"))
        points = exchanged(combine(parts, place, 2 * tiles), ("sec", "ty", "tx"))
        relaxed = pl.pallas_call(
            functools.partial(relax_kernel, side, halo, tile_cols, extent),
            out_shape=jax.ShapeDtypeStruct((2, side, side), jnp.float32),
            in_specs=[in_smem()] + in_vmem(3),
            out_specs=pl.BlockSpec(memory_space=pltpu.VMEM),
            scratch_shapes=[sum_shape],
            compiler_params=pltpu.CompilerParams(vmem_limit_bytes=VMEM_BYTES),
            name="relax",
        )(at, ids, points.reshape(2, tiles, 2 * part, LANES), mesh_values)
        return relaxed[None]

    mesh_values = with_halo(own_mesh, halo, wide)
    parts = exchanged(parts[0], "ty")
    points = passed_along(exchanged(combine(parts, place, tiles), ("ty", "tx")), "sec", -1)
    ids = passed_along(ids, "sec", -1)
    sums = pl.pallas_call(
        functools.partial(sums_kernel, side, halo, tile_cols),
        out_shape=jax.ShapeDtypeStruct((3, span, wide), jnp.float32),
        in_specs=[in_smem()] + in_vmem(2),
        out_specs=pl.BlockSpec(memory_space=pltpu.VMEM),
        scratch_shapes=[sum_shape],
        compiler_params=pltpu.CompilerParams(vmem_limit_bytes=VMEM_BYTES),
        name="sums",
    )(at, ids, points[None])
    return sweeps(mesh_values[0:2], mesh_values[2], sums, at, side, halo, extent)[None]


def solution(mesh):
    in_specs = (
        P("sec", "ty", "tx", None, None),
        P("sec", "ty", "tx", None, None),
        P("sec", "ty", "tx", None),
        P("sec", "ty", "tx", None),
        P("sec", "ty", "tx"),
        P("sec", None, "ty", "tx"),
        P("sec", "ty", "tx"),
    )
    out_specs = P("sec", None, "ty", "tx")
    return jax.shard_map(
        per_device, mesh=mesh, in_specs=in_specs, out_specs=out_specs, check_vma=False
    )
```

```python
import functools
import math

import jax
import jax.numpy as jnp
from jax import lax
from jax.experimental import pallas as pl
from jax.experimental.pallas import tpu as pltpu
from jax.sharding import PartitionSpec as P

BLK = 128
ITERS = 4
LANES = 128
PLACE_ROWS = 16
VMEM_BYTES = 24 * 1024 * 1024

spring_sec = 0.5
spring_match = 1.0
relax_rate = 0.8


def passed_along(value, axis, by):
    devices = lax.axis_size(axis)
    pairs = [(i, i + by) for i in range(devices) if 0 <= i + by < devices]
    return lax.ppermute(value, axis, pairs)


def exchanged(value, axes):
    return lax.all_to_all(value, axes, split_axis=0, concat_axis=0, tiled=True)


def spread(value, axes):
    copies = jnp.broadcast_to(value[None], (lax.axis_size(axes),) + value.shape)
    return exchanged(copies, axes)


def nt_dot(a, b):
    return lax.dot_general(a, b, (((1,), (1,)), ((), ())), preferred_element_type=jnp.float32)


def in_vmem(count):
    return [pl.BlockSpec(memory_space=pltpu.VMEM)] * count


def in_smem():
    return pl.BlockSpec(memory_space=pltpu.SMEM)


def match_kernel(scale, key_tiles, work_ref, query_ref, *refs):
    key_refs, (out_ref, key_buf, place_buf) = refs[:key_tiles], refs[key_tiles:]
    shares, tile_rows, out_rows, _ = out_ref.shape
    rows = out_rows // 4
    point_total = shares * rows * LANES
    width = key_buf.shape[2]
    key_rows = key_buf.shape[1]
    part = key_rows // BLK
    total = key_tiles * part
    step = 256 if point_total % 256 == 0 else LANES

    row_at = lax.broadcasted_iota(jnp.int32, (PLACE_ROWS, LANES), 0)
    for tile, key_ref in enumerate(key_refs):
        key_buf[tile] = key_ref[pl.ds(0, key_rows), :]
        place = key_ref[pl.ds(key_rows, PLACE_ROWS), :].astype(jnp.float32)
        for j in range(part):
            x, y = place[j : j + 1, :], place[part + j : part + j + 1, :]
            stacked = jnp.where(
                row_at == 0, x, jnp.where(row_at == 1, y, jnp.where(row_at == 2, 1.0, 0.0))
            )
            place_buf[tile * part + j] = stacked.astype(jnp.bfloat16)

    for tile in range(tile_rows):
        count = work_ref[tile, total]

        def body(pair, carry):
            tops, sums = carry
            live = 2 * pair + 1 < count
            first = work_ref[tile, 2 * pair]
            second = work_ref[tile, jnp.where(live, 2 * pair + 1, 2 * pair)]

            def keys_of(block):
                at = pl.multiple_of(lax.rem(block, part) * BLK, BLK)
                return key_buf[lax.div(block, part), pl.ds(at, BLK), :]

            keys = jnp.concatenate([keys_of(first), keys_of(second)], axis=0)
            kept = jnp.where(live, 1.0, 0.0).astype(jnp.bfloat16)
            place = jnp.concatenate([place_buf[first], place_buf[second] * kept], axis=1)
            new_tops, new_sums = [], []
            for c in range(point_total // step):
                queries = query_ref[tile, pl.ds(0, width), pl.ds(c * step, step)]
                scores = jnp.dot(keys, queries, preferred_element_type=jnp.float32) * scale
                top = jnp.maximum(tops[c], jnp.max(scores, axis=0, keepdims=True))
                weights = jnp.exp2(scores - top).astype(jnp.bfloat16)
                added = jnp.dot(place, weights, preferred_element_type=jnp.float32)
                new_tops.append(top)
                new_sums.append(sums[c] * jnp.exp2(tops[c] - top) + added)
            return tuple(new_tops), tuple(new_sums)

        chunks = point_total // step
        tops, sums = lax.fori_loop(
            0,
            (count + 1) // 2,
            body,
            (
                tuple(jnp.full((1, step), -1e30, jnp.float32) for _ in range(chunks)),
                tuple(jnp.zeros((PLACE_ROWS, step), jnp.float32) for _ in range(chunks)),
            ),
        )
        per_chunk = step // LANES
        for row in range(shares * rows):
            c, lanes = row // per_chunk, slice((row % per_chunk) * LANES, (row % per_chunk + 1) * LANES)
            share, at = row // rows, row % rows
            for place, value in enumerate(
                (tops[c][:, lanes], sums[c][2:3, lanes], sums[c][0:1, lanes], sums[c][1:2, lanes])
            ):
                out_ref[share, tile, pl.ds(place * rows + at, 1), :] = value


def match(work, queries, keys, score_factor, shares, point_total):
    tile_rows = queries.shape[0]
    key_tiles = len(keys)
    key_rows, width = keys[0].shape[0] - PLACE_ROWS, keys[0].shape[1]
    part = key_rows // BLK
    rows = point_total // LANES // shares
    pairs = tile_rows * key_tiles * part
    return pl.pallas_call(
        functools.partial(match_kernel, score_factor * math.log2(math.e), key_tiles),
        out_shape=jax.ShapeDtypeStruct((shares, tile_rows, 4 * rows, LANES), jnp.float32),
        in_specs=[in_smem()] + in_vmem(1 + key_tiles),
        out_specs=pl.BlockSpec(memory_space=pltpu.VMEM),
        scratch_shapes=[
            pltpu.VMEM((key_tiles, key_rows, width), jnp.bfloat16),
            pltpu.VMEM((key_tiles * part, PLACE_ROWS, LANES), jnp.bfloat16),
        ],
        compiler_params=pltpu.CompilerParams(vmem_limit_bytes=VMEM_BYTES),
        cost_estimate=pl.CostEstimate(
            flops=pairs * point_total * BLK * width,
            bytes_accessed=2 * (queries.size + key_tiles * keys[0].size),
            transcendentals=pairs * point_total * BLK // 4,
        ),
        name="match",
    )(work, queries, *keys)


def combine_kernel(parts_ref, place_ref, out_ref):
    parts, out_rows, _ = parts_ref.shape
    rows = out_rows // 4
    tops = [parts_ref[i, 0:rows, :] for i in range(parts)]
    top = functools.reduce(jnp.maximum, tops)
    total = x = y = jnp.zeros_like(top)
    for i in range(parts):
        gain = jnp.exp2(tops[i] - top)
        total += gain * parts_ref[i, rows : 2 * rows, :]
        x += gain * parts_ref[i, 2 * rows : 3 * rows, :]
        y += gain * parts_ref[i, 3 * rows :, :]
    pull = jnp.concatenate([x / total, y / total], axis=0) - place_ref[...].astype(jnp.float32)
    for i in range(out_ref.shape[0]):
        out_ref[i] = pull


def combine(parts, place, copies):
    return pl.pallas_call(
        combine_kernel,
        out_shape=jax.ShapeDtypeStruct((copies,) + place.shape, jnp.float32),
        in_specs=in_vmem(2),
        out_specs=pl.BlockSpec(memory_space=pltpu.VMEM),
        compiler_params=pltpu.CompilerParams(vmem_limit_bytes=VMEM_BYTES),
        name="combine",
    )(parts, place)


def spots_kernel(side, halo, tile_cols, at_ref, ids_ref, row_ref, col_ref, count_ref):
    tiles, tall, count = row_ref.shape
    wide = col_ref.shape[2]
    span = side + 2 * halo

    def folded(at, length):
        return jnp.where(
            (at >= 0) & (at < side + halo), at, jnp.where((at < 0) & (at >= -halo), at + length, -1)
        )

    count_ref[...] = jnp.zeros_like(count_ref)

    @pl.loop(0, tiles)
    def _(tile):
        ids = ids_ref[tile]
        tile_of = lax.div(ids, side * side)
        within = lax.rem(ids, side * side)
        row = lax.div(tile_of, tile_cols) * side + lax.div(within, side) - at_ref[0]
        col = lax.rem(tile_of, tile_cols) * side + lax.rem(within, side) - at_ref[1]
        row, col = folded(row, span), folded(col, wide)
        for i in range(count // LANES):
            here = slice(i * LANES, (i + 1) * LANES)
            at = lax.broadcasted_iota(jnp.int32, (tall, LANES), 0)
            row_ref[tile, :, here] = jnp.where(at == row[i : i + 1, :], 1.0, 0.0).astype(jnp.bfloat16)
            turned = jnp.broadcast_to(col[i : i + 1, :].astype(jnp.float32), (LANES, LANES)).T
            at = lax.broadcasted_iota(jnp.int32, (LANES, LANES), 1)
            for j in range(wide // LANES):
                lane = (at + j * LANES).astype(jnp.float32)
                col_ref[tile, here, pl.ds(j * LANES, LANES)] = jnp.where(
                    turned == lane, 1.0, 0.0
                ).astype(jnp.bfloat16)
        count_ref[...] += jnp.dot(
            row_ref[tile], col_ref[tile], preferred_element_type=jnp.float32
        )


def spots(side, halo, tile_cols, wide, at, ids):
    tiles = ids.shape[0]
    count = ids.shape[1] * ids.shape[2]
    tall = -(-(side + 2 * halo) // 16) * 16
    return pl.pallas_call(
        functools.partial(spots_kernel, side, halo, tile_cols),
        out_shape=(
            jax.ShapeDtypeStruct((tiles, tall, count), jnp.bfloat16),
            jax.ShapeDtypeStruct((tiles, count, wide), jnp.bfloat16),
            jax.ShapeDtypeStruct((tall, wide), jnp.float32),
        ),
        in_specs=[in_smem()] + in_vmem(1),
        out_specs=(pl.BlockSpec(memory_space=pltpu.VMEM),) * 3,
        compiler_params=pltpu.CompilerParams(vmem_limit_bytes=VMEM_BYTES),
        cost_estimate=pl.CostEstimate(
            flops=2 * tiles * tall * count * wide,
            bytes_accessed=2 * tiles * count * (tall + wide),
            transcendentals=0,
        ),
        name="spots",
    )(at, ids)


def vertex_sums(row_ref, col_ref, points_ref, sum_ref):
    tall = row_ref.shape[1]
    shares, tiles, both_rows, _ = points_ref.shape
    rows = both_rows // 2
    along = functools.partial(jnp.concatenate, axis=1)
    sum_ref[...] = jnp.zeros_like(sum_ref)

    @pl.loop(0, tiles)
    def _(tile):
        values = [points_ref[share, tile] for share in range(shares)]
        x = along([v[i : i + 1, :] for v in values for i in range(rows)])
        y = along([v[i : i + 1, :] for v in values for i in range(rows, 2 * rows)])
        hit = row_ref[tile]
        parts = []
        for value in (x, y):
            high = value.astype(jnp.bfloat16)
            low = (value - high.astype(jnp.float32)).astype(jnp.bfloat16)
            parts += [hit * high, hit * low]
        summed = jnp.dot(
            jnp.concatenate(parts, axis=0), col_ref[tile], preferred_element_type=jnp.float32
        )
        sum_ref[0] += summed[0:tall] + summed[tall : 2 * tall]
        sum_ref[1] += summed[2 * tall : 3 * tall] + summed[3 * tall :]


def sums_kernel(row_ref, col_ref, points_ref, out_ref, sum_ref):
    vertex_sums(row_ref, col_ref, points_ref, sum_ref)
    out_ref[...] = sum_ref[:, pl.ds(0, out_ref.shape[1]), :]


def relax_kernel(
    side, halo, extent, at_ref, row_ref, col_ref, count_ref, points_ref, mesh_ref, out_ref, sum_ref
):
    vertex_sums(row_ref, col_ref, points_ref, sum_ref)
    span = side + 2 * halo
    wide = sum_ref.shape[2]
    shape = (span, wide)
    row = lax.broadcasted_iota(jnp.int32, shape, 0)
    col = lax.broadcasted_iota(jnp.int32, shape, 1)
    row = jnp.where(row < side + halo, row, row - span) + at_ref[0]
    col = jnp.where(col < side + halo, col, col - wide) + at_ref[1]
    inside = (row >= 0) & (row < extent[0]) & (col >= 0) & (col < extent[1])
    own_pulled = (at_ref[2] == 0).astype(jnp.float32)
    linked = 1.0
    matched = count_ref[pl.ds(0, span), :]
    moving, gains, has, step = [], [], [], []
    for part, pulled in enumerate((own_pulled, 1.0 - own_pulled)):
        gain = mesh_ref[part * 3 + 2]
        diagonal = 4.0 * gain + spring_sec * linked + spring_match * matched * pulled
        gains.append(gain)
        has.append(matched * pulled)
        step.append(jnp.where(inside, relax_rate / diagonal, 0.0))
        moving.append(
            [
                (mesh_ref[part * 3 + c], sum_ref[c, pl.ds(0, span), :] * pulled)
                for c in range(2)
            ]
        )
    for sweep in range(ITERS):
        later = []
        for part in range(2):
            row_of = []
            for c in range(2):
                u, pulled = moving[part][c]
                other = moving[1 - part][c][0]
                laplace = (
                    pltpu.roll(u, 1, 0)
                    + pltpu.roll(u, span - 1, 0)
                    + pltpu.roll(u, 1, 1)
                    + pltpu.roll(u, wide - 1, 1)
                    - 4.0 * u
                )
                force = (
                    gains[part] * laplace
                    + spring_sec * (other - linked * u)
                    + spring_match * (pulled - has[part] * u)
                )
                row_of.append((u + step[part] * force, pulled))
            later.append(row_of)
        moving = later
    for c in range(2):
        out_ref[c] = moving[0][c][0][0:side, 0:side]


def with_halo(value, halo, wide):
    side = value.shape[1]
    after = passed_along(value[:, :halo], "ty", -1)
    before = passed_along(value[:, side - halo :], "ty", 1)
    value = jnp.concatenate([value, after, before], axis=1)
    after = passed_along(value[:, :, :halo], "tx", -1)
    before = passed_along(value[:, :, side - halo :], "tx", 1)
    gap = jnp.zeros(value.shape[:2] + (wide - side - 2 * halo,), value.dtype)
    return jnp.concatenate([value, after, gap, before], axis=2)


def sweeps(moving, gains, sums, number, at, side, halo, extent):
    sections = lax.axis_size("sec")
    sec_index = at[2]
    has_next = (sec_index < sections - 1).astype(jnp.float32)
    linked = (sec_index > 0).astype(jnp.float32) + has_next
    pulled, matched = sums * has_next, number * has_next
    span, wide = moving.shape[1:]
    row = jnp.arange(span)[:, None]
    col = jnp.arange(wide)[None, :]
    row = jnp.where(row < side + halo, row, row - span) + at[0]
    col = jnp.where(col < side + halo, col, col - wide) + at[1]
    inside = (row >= 0) & (row < extent[0]) & (col >= 0) & (col < extent[1])
    diagonal = 4.0 * gains + spring_sec * linked + spring_match * matched
    step = jnp.where(inside, relax_rate / jnp.where(inside, diagonal, 1.0), 0.0)
    for sweep in range(ITERS):
        lower_sec = passed_along(moving, "sec", 1)
        upper_sec = passed_along(moving, "sec", -1)
        laplace = (
            jnp.roll(moving, 1, 1)
            + jnp.roll(moving, -1, 1)
            + jnp.roll(moving, 1, 2)
            + jnp.roll(moving, -1, 2)
            - 4.0 * moving
        )
        force = (
            gains * laplace
            + spring_sec * (lower_sec + upper_sec - linked * moving)
            + spring_match * (pulled - matched * moving)
        )
        moving = moving + step * force
    return moving[:, :side, :side]


def local_work(lists, counts, blocks):
    total = blocks.shape[0]
    is_live = jnp.arange(lists.shape[1])[None, :] < counts[:, None]
    hit = (lists[:, :, None] == blocks[None, None, :]) & is_live[:, :, None]
    live = jnp.any(hit, axis=1)
    spot = jnp.arange(total)
    rank = jnp.sum(live[:, None, :] & (spot[None, :] < spot[:, None])[None], axis=2)
    taken = live[:, None, :] & (rank[:, None, :] == spot[None, :, None])
    packed = jnp.sum(jnp.where(taken, spot[None, None, :], 0), axis=2)
    number = jnp.sum(live, axis=1)
    return jnp.concatenate([packed, number[:, None]], axis=1).astype(jnp.int32)


def per_device(
    descriptors, positions, vertex_ids, candidate_blocks, candidate_count, displacement, stiffness
):
    point_total, width = descriptors.shape[3:]
    per_tile = point_total // BLK
    tile_rows, tile_cols = lax.axis_size("ty"), lax.axis_size("tx")
    sections = lax.axis_size("sec")
    sec_index = lax.axis_index("sec")
    tiles = tile_rows * tile_cols
    side = displacement.shape[3]
    halo = ITERS
    span = side + 2 * halo
    wide = -(-span // LANES) * LANES
    shares = 2 if sections == 2 and per_tile % 2 == 0 else 1
    part = per_tile // shares
    key_rows = part * BLK

    own_desc = descriptors[0, 0, 0]
    own_place = positions[0, 0, 0].reshape(2, per_tile, BLK)

    def key_part(share):
        blocks = slice(share * part, (share + 1) * part)
        place = own_place[:, blocks].reshape(2 * part, BLK)
        filler = jnp.zeros((PLACE_ROWS - 2 * part, BLK), place.dtype)
        desc = own_desc[share * key_rows : (share + 1) * key_rows]
        return jnp.concatenate([desc, place, filler], axis=0)

    filler = jnp.zeros((PLACE_ROWS - 2, point_total), own_desc.dtype)
    query = jnp.concatenate([own_desc.T, positions[0, 0, 0], filler], axis=0)
    whole = jnp.concatenate(
        [vertex_ids[0, 0, 0], candidate_blocks[0, 0, 0], candidate_count[0, 0, 0][None]]
    )
    whole = jnp.pad(whole, (0, -whole.shape[0] % (8 * LANES))).reshape(-1, LANES)
    if shares == 2:
        first = sec_index == 0
        key = jnp.where(first, passed_along(key_part(0), "sec", -1), key_part(1))
        query = jnp.where(first, query, passed_along(query, "sec", 1))
        whole = spread(whole, ("sec", "ty", "tx"))[:tiles]
        share = sec_index
    else:
        key = key_part(0)
        query = passed_along(query, "sec", 1)
        whole = spread(passed_along(whole, "sec", 1), ("ty", "tx"))
        share = 0
    keys = [key]
    for j in range(1, tile_cols):
        turn = [(i, (i + j) % tile_cols) for i in range(tile_cols)]
        keys.append(lax.ppermute(key, "tx", turn))
    queries = spread(query, "ty")

    ids = whole[:, :per_tile]
    lists = whole[:, per_tile:].reshape(tile_rows, tile_cols, -1)
    lists = lax.dynamic_index_in_dim(lists, lax.axis_index("tx"), 1, keepdims=False)
    cand = candidate_blocks.shape[3]
    key_tile = lax.axis_index("ty") * tile_cols + jnp.mod(
        lax.axis_index("tx") - jnp.arange(tile_cols), tile_cols
    )
    blocks = (key_tile[:, None] * per_tile + share * part + jnp.arange(part)[None, :]).reshape(-1)
    work = local_work(lists[:, :cand], lists[:, cand], blocks)

    place = query[width : width + 2].reshape(2, shares, part, LANES)
    place = lax.dynamic_index_in_dim(place, share, 1, keepdims=False).reshape(2 * part, LANES)
    at = jnp.stack(
        [lax.axis_index("ty") * side, lax.axis_index("tx") * side, sec_index]
    ).astype(jnp.int32)
    extent = (side * tile_rows, side * tile_cols)
    own_mesh = jnp.concatenate([displacement[0], stiffness], axis=0)
    sum_shape = pltpu.VMEM((2, -(-span // 16) * 16, wide), jnp.float32)

    if shares == 2:
        row_hit, col_hit, number = spots(side, halo, tile_cols, wide, at, ids)
        other_mesh = lax.ppermute(own_mesh, "sec", [(0, 1), (1, 0)])
        mesh_values = with_halo(jnp.concatenate([own_mesh, other_mesh], axis=0), halo, wide)
        parts = match(work, queries, keys, 16.0 / width, shares, point_total)
        parts = exchanged(parts.reshape((-1,) + parts.shape[2:]), ("sec", "ty"))
        points = exchanged(combine(parts, place, 2 * tiles), ("sec", "ty", "tx"))
        relaxed = pl.pallas_call(
            functools.partial(relax_kernel, side, halo, extent),
            out_shape=jax.ShapeDtypeStruct((2, side, side), jnp.float32),
            in_specs=[in_smem()] + in_vmem(5),
            out_specs=pl.BlockSpec(memory_space=pltpu.VMEM),
            scratch_shapes=[sum_shape],
            compiler_params=pltpu.CompilerParams(vmem_limit_bytes=VMEM_BYTES),
            name="relax",
        )(at, row_hit, col_hit, number, points.reshape(2, tiles, 2 * part, LANES), mesh_values)
        return relaxed[None]

    ids = passed_along(ids, "sec", -1)
    row_hit, col_hit, number = spots(side, halo, tile_cols, wide, at, ids)
    mesh_values = with_halo(own_mesh, halo, wide)
    parts = match(work, queries, keys, 16.0 / width, shares, point_total)
    parts = exchanged(parts[0], "ty")
    points = passed_along(exchanged(combine(parts, place, tiles), ("ty", "tx")), "sec", -1)
    sums = pl.pallas_call(
        sums_kernel,
        out_shape=jax.ShapeDtypeStruct((2, span, wide), jnp.float32),
        in_specs=in_vmem(3),
        out_specs=pl.BlockSpec(memory_space=pltpu.VMEM),
        scratch_shapes=[sum_shape],
        compiler_params=pltpu.CompilerParams(vmem_limit_bytes=VMEM_BYTES),
        name="sums",
    )(row_hit, col_hit, points[None])
    moving, gains = mesh_values[0:2], mesh_values[2]
    return sweeps(moving, gains, sums, number[:span], at, side, halo, extent)[None]


def solution(mesh):
    in_specs = (
        P("sec", "ty", "tx", None, None),
        P("sec", "ty", "tx", None, None),
        P("sec", "ty", "tx", None),
        P("sec", "ty", "tx", None),
        P("sec", "ty", "tx"),
        P("sec", None, "ty", "tx"),
        P("sec", "ty", "tx"),
    )
    out_specs = P("sec", None, "ty", "tx")
    return jax.shard_map(
        per_device, mesh=mesh, in_specs=in_specs, out_specs=out_specs, check_vma=False
    )
```

```python
import functools
import math

import jax
import jax.numpy as jnp
from jax import lax
from jax.experimental import pallas as pl
from jax.experimental.pallas import tpu as pltpu
from jax.sharding import PartitionSpec as P

BLK = 128
ITERS = 4
LANES = 128
PLACE_ROWS = 16
GROUP = 2
VMEM_BYTES = 24 * 1024 * 1024

spring_sec = 0.5
spring_match = 1.0
relax_rate = 0.8


def passed_along(value, axis, by):
    devices = lax.axis_size(axis)
    pairs = [(i, i + by) for i in range(devices) if 0 <= i + by < devices]
    return lax.ppermute(value, axis, pairs)


def exchanged(value, axes):
    return lax.all_to_all(value, axes, split_axis=0, concat_axis=0, tiled=True)


def spread(value, axes):
    copies = jnp.broadcast_to(value[None], (lax.axis_size(axes),) + value.shape)
    return exchanged(copies, axes)


def nt_dot(a, b):
    return lax.dot_general(a, b, (((1,), (1,)), ((), ())), preferred_element_type=jnp.float32)


def in_vmem(count):
    return [pl.BlockSpec(memory_space=pltpu.VMEM)] * count


def in_smem():
    return pl.BlockSpec(memory_space=pltpu.SMEM)


def match_kernel(scale, tile_rows, key_tiles, work_ref, *refs):
    query_refs, key_refs = refs[:tile_rows], refs[tile_rows : tile_rows + key_tiles]
    out_ref, query_buf, key_buf, place_buf, state_buf = refs[tile_rows + key_tiles :]
    shares, _, out_rows, _ = out_ref.shape
    rows = out_rows // 4
    point_total = query_buf.shape[1]
    key_rows = key_buf.shape[1]
    part = key_rows // BLK

    row_at = lax.broadcasted_iota(jnp.int32, (PLACE_ROWS, LANES), 0)
    for tile, query_ref in enumerate(query_refs):
        query_buf[tile] = query_ref[...]
    for tile, key_ref in enumerate(key_refs):
        key_buf[tile] = key_ref[pl.ds(0, key_rows), :]
        place = key_ref[pl.ds(key_rows, PLACE_ROWS), :].astype(jnp.float32)
        for j in range(part):
            x, y = place[j : j + 1, :], place[part + j : part + j + 1, :]
            stacked = jnp.where(
                row_at == 0, x, jnp.where(row_at == 1, y, jnp.where(row_at == 2, 1.0, 0.0))
            )
            place_buf[tile * part + j] = stacked.astype(jnp.bfloat16)

    state_row = lax.broadcasted_iota(jnp.int32, state_buf.shape[1:], 0)
    for tile in range(tile_rows):
        state_buf[tile] = jnp.where(state_row == 3, -1e30, 0.0)

    def item(at):
        tile, first, second, live = (work_ref[at * 4 + i] for i in range(4))

        def keys_of(block):
            start = pl.multiple_of(lax.rem(block, part) * BLK, BLK)
            return key_buf[lax.div(block, part), pl.ds(start, BLK), :]

        def place_of(block, number):
            kept = jnp.where(live >= number, 1.0, 0.0).astype(jnp.bfloat16)
            return place_buf[block] * kept

        keys = jnp.concatenate([keys_of(first), keys_of(second)], axis=0)
        place = jnp.concatenate([place_of(first, 1), place_of(second, 2)], axis=1)
        return tile, live, keys, place

    @pl.loop(0, work_ref[work_ref.shape[0] - 1])
    def _(group):
        items = [item(group * GROUP + i) for i in range(GROUP)]
        scores = [nt_dot(keys, query_buf[tile]) * scale for tile, _, keys, _ in items]
        tops = [jnp.max(score, axis=0, keepdims=True) for score in scores]
        weights = [jnp.exp2(s - top).astype(jnp.bfloat16) for s, top in zip(scores, tops)]
        sums = [
            jnp.dot(place, weight, preferred_element_type=jnp.float32)[0:8]
            for (_, _, _, place), weight in zip(items, weights)
        ]
        for (tile, live, _, _), top, added in zip(items, tops, sums):
            top = jnp.where(live > 0, top, -1e30)
            state = state_buf[tile]
            before = state[3:4, :]
            both = jnp.maximum(before, top)
            state = state * jnp.exp2(before - both) + added * jnp.exp2(top - both)
            state_buf[tile] = jnp.where(state_row == 3, both, state)

    for tile in range(tile_rows):
        to = work_ref[work_ref.shape[0] - 2 - tile]
        for row in range(shares * rows):
            lanes = pl.ds(row * LANES, LANES)
            for place, held in enumerate((3, 2, 0, 1)):
                out_ref[row // rows, to, pl.ds(place * rows + row % rows, 1), :] = state_buf[
                    tile, pl.ds(held, 1), lanes
                ]


def match(work, queries, keys, score_factor, shares):
    tile_rows, key_tiles = len(queries), len(keys)
    point_total, width = queries[0].shape
    key_rows = keys[0].shape[0] - PLACE_ROWS
    part = key_rows // BLK
    rows = point_total // LANES // shares
    return pl.pallas_call(
        functools.partial(
            match_kernel, score_factor * math.log2(math.e), tile_rows, key_tiles
        ),
        out_shape=jax.ShapeDtypeStruct((shares, tile_rows, 4 * rows, LANES), jnp.float32),
        in_specs=[in_smem()] + in_vmem(tile_rows + key_tiles),
        out_specs=pl.BlockSpec(memory_space=pltpu.VMEM),
        scratch_shapes=[
            pltpu.VMEM((tile_rows, point_total, width), jnp.bfloat16),
            pltpu.VMEM((key_tiles, key_rows, width), jnp.bfloat16),
            pltpu.VMEM((key_tiles * part, PLACE_ROWS, LANES), jnp.bfloat16),
            pltpu.VMEM((tile_rows, 8, point_total), jnp.float32),
        ],
        compiler_params=pltpu.CompilerParams(vmem_limit_bytes=VMEM_BYTES),
        cost_estimate=pl.CostEstimate(
            flops=tile_rows * key_tiles * part * point_total * BLK * width,
            bytes_accessed=2 * (tile_rows * queries[0].size + key_tiles * keys[0].size),
            transcendentals=tile_rows * key_tiles * part * point_total * BLK // 4,
        ),
        name="match",
    )(work, *queries, *keys)


def combine_kernel(parts_ref, place_ref, out_ref):
    parts, out_rows, _ = parts_ref.shape
    rows = out_rows // 4
    tops = [parts_ref[i, 0:rows, :] for i in range(parts)]
    top = functools.reduce(jnp.maximum, tops)
    total = x = y = jnp.zeros_like(top)
    for i in range(parts):
        gain = jnp.exp2(tops[i] - top)
        total += gain * parts_ref[i, rows : 2 * rows, :]
        x += gain * parts_ref[i, 2 * rows : 3 * rows, :]
        y += gain * parts_ref[i, 3 * rows :, :]
    pull = jnp.concatenate([x / total, y / total], axis=0) - place_ref[...].astype(jnp.float32)
    for i in range(out_ref.shape[0]):
        out_ref[i] = pull


def combine(parts, place, copies):
    return pl.pallas_call(
        combine_kernel,
        out_shape=jax.ShapeDtypeStruct((copies,) + place.shape, jnp.float32),
        in_specs=in_vmem(2),
        out_specs=pl.BlockSpec(memory_space=pltpu.VMEM),
        compiler_params=pltpu.CompilerParams(vmem_limit_bytes=VMEM_BYTES),
        name="combine",
    )(parts, place)


def one_hot(at, length, limits):
    count = at.shape[1]
    parts, done = [], 0
    for low, high in limits:
        spot = lax.broadcasted_iota(jnp.int32, (high - low, count), 0) + low
        if low > done:
            parts.append(jnp.zeros((low - done, count), jnp.bfloat16))
        parts.append(jnp.where(spot == at, 1.0, 0.0).astype(jnp.bfloat16))
        done = high
    if length > done:
        parts.append(jnp.zeros((length - done, count), jnp.bfloat16))
    return jnp.concatenate(parts, axis=0)


def flat(value):
    return jnp.concatenate([value[i : i + 1, :] for i in range(value.shape[0])], axis=1)


def hits(side, halo, tall, wide, row, col):
    up = lambda n: -(-n // 16) * 16
    limits = ((0, up(side + halo)), (wide - up(halo), wide))
    return one_hot(flat(row), tall, ((0, tall),)), one_hot(flat(col), wide, limits)


def spots_kernel(
    side, halo, tile_cols, at_ref, ids_ref, rounds_ref, spot_ref, count_ref, hit_buf
):
    tiles = ids_ref.shape[0]
    tall, wide = count_ref.shape

    def folded(at, length):
        return jnp.where(
            (at >= 0) & (at < side + halo), at, jnp.where((at < 0) & (at >= -halo), at + length, -1)
        )

    number = jnp.zeros(ids_ref.shape[1:], jnp.int32)
    for tile in range(tiles):
        ids = ids_ref[tile]
        tile_of = lax.div(ids, side * side)
        within = lax.rem(ids, side * side)
        row = lax.div(tile_of, tile_cols) * side + lax.div(within, side) - at_ref[0]
        col = lax.rem(tile_of, tile_cols) * side + lax.rem(within, side) - at_ref[1]
        row, col = folded(row, side + 2 * halo), folded(col, wide)
        here = (row >= 0) & (col >= 0)
        hit_buf[0, tile] = jnp.where(here, number, -1)
        hit_buf[1, tile] = row
        hit_buf[2, tile] = col
        number = number + here.astype(jnp.int32)
    rounds = jnp.max(number)
    rounds_ref[0] = rounds
    count_ref[...] = jnp.zeros_like(count_ref)

    @pl.loop(0, rounds)
    def _(k):
        tile_of = row = col = jnp.full(number.shape, -1, jnp.int32)
        for tile in range(tiles):
            here = hit_buf[0, tile] == k
            tile_of = jnp.where(here, tile, tile_of)
            row = jnp.where(here, hit_buf[1, tile], row)
            col = jnp.where(here, hit_buf[2, tile], col)
        spot_ref[k, 0] = tile_of
        spot_ref[k, 1] = row
        spot_ref[k, 2] = col
        row_hit, col_hit = hits(side, halo, tall, wide, row, col)
        count_ref[...] += nt_dot(row_hit, col_hit)


def spots(side, halo, tile_cols, wide, at, ids):
    tall = -(-(side + 2 * halo) // 16) * 16
    return pl.pallas_call(
        functools.partial(spots_kernel, side, halo, tile_cols),
        out_shape=(
            jax.ShapeDtypeStruct((1,), jnp.int32),
            jax.ShapeDtypeStruct((ids.shape[0], 3) + ids.shape[1:], jnp.int32),
            jax.ShapeDtypeStruct((tall, wide), jnp.float32),
        ),
        in_specs=[in_smem()] + in_vmem(1),
        out_specs=(in_smem(),) + (pl.BlockSpec(memory_space=pltpu.VMEM),) * 2,
        scratch_shapes=[pltpu.VMEM((3,) + ids.shape, jnp.int32)],
        compiler_params=pltpu.CompilerParams(vmem_limit_bytes=VMEM_BYTES),
        cost_estimate=pl.CostEstimate(
            flops=10 * tall * ids.shape[1] * LANES * wide,
            bytes_accessed=16 * ids.size,
            transcendentals=0,
        ),
        name="spots",
    )(at, ids)


def vertex_sums(side, halo, rounds_ref, spot_ref, points_ref, sum_ref):
    _, tall, wide = sum_ref.shape
    shares, tiles, both_rows, _ = points_ref.shape
    rows = both_rows // 2
    sum_ref[...] = jnp.zeros_like(sum_ref)

    @pl.loop(0, rounds_ref[0])
    def _(k):
        tile_of = spot_ref[k, 0]
        x = y = jnp.zeros(tile_of.shape, jnp.float32)
        for tile in range(tiles):
            here = tile_of == tile
            values = [points_ref[share, tile] for share in range(shares)]
            x = jnp.where(here, jnp.concatenate([v[:rows] for v in values], axis=0), x)
            y = jnp.where(here, jnp.concatenate([v[rows:] for v in values], axis=0), y)
        row_hit, col_hit = hits(side, halo, tall, wide, spot_ref[k, 1], spot_ref[k, 2])
        parts = []
        for value in (flat(x), flat(y)):
            high = value.astype(jnp.bfloat16)
            low = (value - high.astype(jnp.float32)).astype(jnp.bfloat16)
            parts += [row_hit * high, row_hit * low]
        summed = nt_dot(jnp.concatenate(parts, axis=0), col_hit)
        sum_ref[0] += summed[0:tall] + summed[tall : 2 * tall]
        sum_ref[1] += summed[2 * tall : 3 * tall] + summed[3 * tall :]


def sums_kernel(side, halo, rounds_ref, spot_ref, points_ref, out_ref, sum_ref):
    vertex_sums(side, halo, rounds_ref, spot_ref, points_ref, sum_ref)
    out_ref[...] = sum_ref[:, pl.ds(0, out_ref.shape[1]), :]


def relax_kernel(
    side,
    halo,
    extent,
    at_ref,
    rounds_ref,
    spot_ref,
    count_ref,
    points_ref,
    own_ref,
    other_ref,
    out_ref,
    sum_ref,
):
    vertex_sums(side, halo, rounds_ref, spot_ref, points_ref, sum_ref)
    span = side + 2 * halo
    wide = sum_ref.shape[2]
    shape = (span, wide)
    row = lax.broadcasted_iota(jnp.int32, shape, 0)
    col = lax.broadcasted_iota(jnp.int32, shape, 1)
    row = jnp.where(row < side + halo, row, row - span) + at_ref[0]
    col = jnp.where(col < side + halo, col, col - wide) + at_ref[1]
    inside = (row >= 0) & (row < extent[0]) & (col >= 0) & (col < extent[1])
    own_pulled = (at_ref[2] == 0).astype(jnp.float32)
    linked = 1.0
    matched = count_ref[pl.ds(0, span), :]
    moving, gains, has, step = [], [], [], []
    for mesh_ref, pulled in ((own_ref, own_pulled), (other_ref, 1.0 - own_pulled)):
        gain = mesh_ref[2]
        diagonal = 4.0 * gain + spring_sec * linked + spring_match * matched * pulled
        gains.append(gain)
        has.append(matched * pulled)
        step.append(jnp.where(inside, relax_rate / diagonal, 0.0))
        moving.append(
            [(mesh_ref[c], sum_ref[c, pl.ds(0, span), :] * pulled) for c in range(2)]
        )
    for sweep in range(ITERS):
        later = []
        for part in range(2):
            row_of = []
            for c in range(2):
                u, pulled = moving[part][c]
                other = moving[1 - part][c][0]
                laplace = (
                    pltpu.roll(u, 1, 0)
                    + pltpu.roll(u, span - 1, 0)
                    + pltpu.roll(u, 1, 1)
                    + pltpu.roll(u, wide - 1, 1)
                    - 4.0 * u
                )
                force = (
                    gains[part] * laplace
                    + spring_sec * (other - linked * u)
                    + spring_match * (pulled - has[part] * u)
                )
                row_of.append((u + step[part] * force, pulled))
            later.append(row_of)
        moving = later
    for c in range(2):
        out_ref[c] = moving[0][c][0][0:side, 0:side]


def with_halo(value, halo, wide):
    side = value.shape[1]
    after = passed_along(value[:, :halo], "ty", -1)
    before = passed_along(value[:, side - halo :], "ty", 1)
    value = jnp.concatenate([value, after, before], axis=1)
    after = passed_along(value[:, :, :halo], "tx", -1)
    before = passed_along(value[:, :, side - halo :], "tx", 1)
    gap = jnp.zeros(value.shape[:2] + (wide - side - 2 * halo,), value.dtype)
    return jnp.concatenate([value, after, gap, before], axis=2)


def sweeps(moving, gains, sums, number, at, side, halo, extent):
    sections = lax.axis_size("sec")
    sec_index = at[2]
    has_next = (sec_index < sections - 1).astype(jnp.float32)
    linked = (sec_index > 0).astype(jnp.float32) + has_next
    pulled, matched = sums * has_next, number * has_next
    span, wide = moving.shape[1:]
    row = jnp.arange(span)[:, None]
    col = jnp.arange(wide)[None, :]
    row = jnp.where(row < side + halo, row, row - span) + at[0]
    col = jnp.where(col < side + halo, col, col - wide) + at[1]
    inside = (row >= 0) & (row < extent[0]) & (col >= 0) & (col < extent[1])
    diagonal = 4.0 * gains + spring_sec * linked + spring_match * matched
    step = jnp.where(inside, relax_rate / jnp.where(inside, diagonal, 1.0), 0.0)
    for sweep in range(ITERS):
        lower_sec = passed_along(moving, "sec", 1)
        upper_sec = passed_along(moving, "sec", -1)
        laplace = (
            jnp.roll(moving, 1, 1)
            + jnp.roll(moving, -1, 1)
            + jnp.roll(moving, 1, 2)
            + jnp.roll(moving, -1, 2)
            - 4.0 * moving
        )
        force = (
            gains * laplace
            + spring_sec * (lower_sec + upper_sec - linked * moving)
            + spring_match * (pulled - matched * moving)
        )
        moving = moving + step * force
    return moving[:, :side, :side]


def local_work(lists, counts, blocks, rows):
    tiles, total = lists.shape[0], blocks.shape[0]
    is_live = jnp.arange(lists.shape[1])[None, :] < counts[:, None]
    hit = (lists[:, :, None] == blocks[None, None, :]) & is_live[:, :, None]
    live = jnp.any(hit, axis=1)
    spot = jnp.arange(total)
    rank = jnp.sum(live[:, None, :] & (spot[None, :] < spot[:, None])[None], axis=2)
    taken = live[:, None, :] & (rank[:, None, :] == spot[None, :, None])
    packed = jnp.sum(jnp.where(taken, spot[None, None, :], 0), axis=2)
    number = jnp.sum(live, axis=1)
    pairs = (number + 1) // 2
    tile = jnp.arange(tiles)
    before = jnp.sum(jnp.where(tile[None, :] < tile[:, None], pairs[None, :], 0), axis=1)
    most = tiles * -(-total // 2)
    item = jnp.arange(-(-most // GROUP) * GROUP)[:, None]
    mine = (item >= before[None, :]) & (item < (before + pairs)[None, :])
    place = 2 * (item - before[None, :])

    def chosen(at, values):
        there = mine[:, :, None] & (at[:, :, None] == spot[None, None, :])
        return jnp.sum(jnp.where(there, values, 0), axis=(1, 2))

    second = jnp.where(place + 1 < number[None, :], place + 1, place)
    full = jnp.where(place + 1 < number[None, :], 2, 1)
    work = jnp.stack(
        [
            jnp.sum(jnp.where(mine, tile[None, :], 0), axis=1),
            chosen(place, packed[None]),
            chosen(second, packed[None]),
            jnp.sum(jnp.where(mine, full, 0), axis=1),
        ],
        axis=1,
    )
    groups = (jnp.sum(pairs) + GROUP - 1) // GROUP
    return jnp.concatenate([work.reshape(-1), rows[::-1], groups[None]]).astype(jnp.int32)


def doubled(value, axis):
    devices, index = lax.axis_size(axis), lax.axis_index(axis)
    if devices & (devices - 1):
        turns = range(1, devices)
        moved = [
            lax.ppermute(value, axis, [(i, (i + j) % devices) for i in range(devices)])
            for j in turns
        ]
        return [value] + moved, jnp.mod(index - jnp.arange(devices), devices)
    held, steps = {0: value}, devices // 2
    near = lambda v, by: lax.ppermute(v, axis, [(i, i ^ by) for i in range(devices)])
    while steps:
        held.update({at | steps: near(v, steps) for at, v in list(held.items())})
        steps //= 2
    return [held[i] for i in range(devices)], index ^ jnp.arange(devices)


def per_device(
    descriptors, positions, vertex_ids, candidate_blocks, candidate_count, displacement, stiffness
):
    point_total, width = descriptors.shape[3:]
    per_tile = point_total // BLK
    tile_rows, tile_cols = lax.axis_size("ty"), lax.axis_size("tx")
    sections = lax.axis_size("sec")
    sec_index = lax.axis_index("sec")
    tiles = tile_rows * tile_cols
    side = displacement.shape[3]
    halo = ITERS
    span = side + 2 * halo
    wide = -(-span // LANES) * LANES
    shares = 2 if sections == 2 and per_tile % 2 == 0 else 1
    part = per_tile // shares
    key_rows = part * BLK

    own_desc = descriptors[0, 0, 0]
    own_place = positions[0, 0, 0].reshape(2 * per_tile, BLK)
    swap = [(i, 1 - i) for i in range(2)]
    query = passed_along(own_desc, "sec", 1)
    whole = jnp.concatenate(
        [vertex_ids[0, 0, 0], candidate_blocks[0, 0, 0], candidate_count[0, 0, 0][None]]
    )
    whole = jnp.pad(whole, (0, -whole.shape[0] % (8 * LANES))).reshape(-1, LANES)
    if shares == 2:
        first = sec_index == 0
        key = passed_along(own_desc[:key_rows], "sec", -1)
        other_place = lax.ppermute(own_place, "sec", swap)
        query = jnp.where(first, own_desc, query)
        key = jnp.where(first, key, own_desc[key_rows:])
        key_place = jnp.where(first, other_place, own_place).reshape(2, shares, part, BLK)
        key_place = jnp.where(first, key_place[:, 0], key_place[:, 1]).reshape(2 * part, BLK)
        place = jnp.where(first, own_place, other_place).reshape(2, shares, part, BLK)
        place = jnp.where(first, place[:, 0], place[:, 1]).reshape(2 * part, BLK)
        whole = spread(whole, ("sec", "ty", "tx"))[:tiles]
        share = sec_index
    else:
        key, key_place = own_desc, own_place
        place = passed_along(own_place, "sec", 1)
        whole = spread(passed_along(whole, "sec", 1), ("ty", "tx"))
        share = 0
    filler = jnp.zeros((PLACE_ROWS - 2 * part, BLK), key_place.dtype)
    key = jnp.concatenate([key, key_place, filler], axis=0)
    queries, query_row = doubled(query, "ty")
    keys = [key]
    for j in range(1, tile_cols):
        turn = [(i, (i + j) % tile_cols) for i in range(tile_cols)]
        keys.append(lax.ppermute(key, "tx", turn))

    ids = whole[:, :per_tile]
    lists = whole[:, per_tile].reshape(tile_rows, tile_cols, -1)
    lists = lax.dynamic_index_in_dim(lists, lax.axis_index("tx"), 1, keepdims=False)
    turned = query_row[:, None] == jnp.arange(tile_rows)[None, :]
    lists = jnp.sum(jnp.where(turned[:, :, None], lists[None], 0), axis=1)
    cand = candidate_blocks.shape[3]
    key_tile = lax.axis_index("ty") * tile_cols + jnp.mod(
        lax.axis_index("tx") - jnp.arange(tile_cols), tile_cols
    )
    blocks = (key_tile[:, None] * per_tile + share * part + jnp.arange(part)[None, :]).reshape(-1)
    work = local_work(lists[:, :cand], lists[:, cand], blocks, query_row)

    at = jnp.stack(
        [lax.axis_index("ty") * side, lax.axis_index("tx") * side, sec_index]
    ).astype(jnp.int32)
    extent = (side * tile_rows, side * tile_cols)
    own_mesh = with_halo(jnp.concatenate([displacement[0], stiffness], axis=0), halo, wide)
    sum_shape = pltpu.VMEM((2, -(-span // 16) * 16, wide), jnp.float32)

    if shares == 2:
        rounds, spot, number = spots(side, halo, tile_cols, wide, at, ids)
        other_mesh = lax.ppermute(own_mesh, "sec", swap)
        work = jnp.concatenate([work[: -1 - tile_rows], rounds, work[-1 - tile_rows :]])
        parts = match(work, queries, keys, 16.0 / width, shares)
        parts = exchanged(parts.reshape((-1,) + parts.shape[2:]), ("sec", "ty"))
        points = exchanged(combine(parts, place, 2 * tiles), ("sec", "ty", "tx"))
        relaxed = pl.pallas_call(
            functools.partial(relax_kernel, side, halo, extent),
            out_shape=jax.ShapeDtypeStruct((2, side, side), jnp.float32),
            in_specs=[in_smem()] * 2 + in_vmem(5),
            out_specs=pl.BlockSpec(memory_space=pltpu.VMEM),
            scratch_shapes=[sum_shape],
            compiler_params=pltpu.CompilerParams(vmem_limit_bytes=VMEM_BYTES),
            name="relax",
        )(at, rounds, spot, number, points.reshape(2, tiles, -1, LANES), own_mesh, other_mesh)
        return relaxed[None]

    ids = passed_along(ids, "sec", -1)
    rounds, spot, number = spots(side, halo, tile_cols, wide, at, ids)
    parts = match(work, queries, keys, 16.0 / width, shares)
    parts = exchanged(parts[0], "ty")
    points = passed_along(exchanged(combine(parts, place, tiles), ("ty", "tx")), "sec", -1)
    sums = pl.pallas_call(
        functools.partial(sums_kernel, side, halo),
        out_shape=jax.ShapeDtypeStruct((2, span, wide), jnp.float32),
        in_specs=[in_smem()] + in_vmem(2),
        out_specs=pl.BlockSpec(memory_space=pltpu.VMEM),
        scratch_shapes=[sum_shape],
        compiler_params=pltpu.CompilerParams(vmem_limit_bytes=VMEM_BYTES),
        name="sums",
    )(rounds, spot, points[None])
    moving, gains = own_mesh[0:2], own_mesh[2]
    return sweeps(moving, gains, sums, number[:span], at, side, halo, extent)[None]


def solution(mesh):
    in_specs = (
        P("sec", "ty", "tx", None, None),
        P("sec", "ty", "tx", None, None),
        P("sec", "ty", "tx", None),
        P("sec", "ty", "tx", None),
        P("sec", "ty", "tx"),
        P("sec", None, "ty", "tx"),
        P("sec", "ty", "tx"),
    )
    out_specs = P("sec", None, "ty", "tx")
    return jax.shard_map(
        per_device, mesh=mesh, in_specs=in_specs, out_specs=out_specs, check_vma=False
    )
```

```python
import functools
import math

import jax
import jax.numpy as jnp
from jax import lax
from jax.experimental import pallas as pl
from jax.experimental.pallas import tpu as pltpu
from jax.sharding import PartitionSpec as P

BLK = 128
ITERS = 4
LANES = 128
PLACE_ROWS = 16
GROUP = 2
VMEM_BYTES = 24 * 1024 * 1024

spring_sec = 0.5
spring_match = 1.0
relax_rate = 0.8


def passed_along(value, axis, by):
    devices = lax.axis_size(axis)
    pairs = [(i, i + by) for i in range(devices) if 0 <= i + by < devices]
    return lax.ppermute(value, axis, pairs)


def exchanged(value, axes):
    return lax.all_to_all(value, axes, split_axis=0, concat_axis=0, tiled=True)


def spread(value, axes):
    copies = jnp.broadcast_to(value[None], (lax.axis_size(axes),) + value.shape)
    return exchanged(copies, axes)


def nt_dot(a, b):
    return lax.dot_general(a, b, (((1,), (1,)), ((), ())), preferred_element_type=jnp.float32)


def in_vmem(count):
    return [pl.BlockSpec(memory_space=pltpu.VMEM)] * count


def in_smem():
    return pl.BlockSpec(memory_space=pltpu.SMEM)


def match_kernel(scale, tile_rows, key_tiles, work_ref, *refs):
    query_refs, key_refs = refs[:tile_rows], refs[tile_rows : tile_rows + key_tiles]
    out_ref, query_buf, key_buf, place_buf, state_buf = refs[tile_rows + key_tiles :]
    shares, _, out_rows, _ = out_ref.shape
    rows = out_rows // 4
    point_total = query_buf.shape[1]
    key_rows = key_buf.shape[1]
    part = key_rows // BLK

    row_at = lax.broadcasted_iota(jnp.int32, (PLACE_ROWS, LANES), 0)
    for tile, query_ref in enumerate(query_refs):
        query_buf[tile] = query_ref[...]
    for tile, key_ref in enumerate(key_refs):
        key_buf[tile] = key_ref[pl.ds(0, key_rows), :]
        place = key_ref[pl.ds(key_rows, PLACE_ROWS), :].astype(jnp.float32)
        for j in range(part):
            x, y = place[j : j + 1, :], place[part + j : part + j + 1, :]
            stacked = jnp.where(
                row_at == 0, x, jnp.where(row_at == 1, y, jnp.where(row_at == 2, 1.0, 0.0))
            )
            place_buf[tile * part + j] = stacked.astype(jnp.bfloat16)

    state_row = lax.broadcasted_iota(jnp.int32, state_buf.shape[1:], 0)
    for tile in range(tile_rows):
        state_buf[tile] = jnp.where(state_row == 3, -1e30, 0.0)

    def item(at):
        tile, first, second, live = (work_ref[at * 4 + i] for i in range(4))

        def keys_of(block):
            start = pl.multiple_of(lax.rem(block, part) * BLK, BLK)
            return key_buf[lax.div(block, part), pl.ds(start, BLK), :]

        def place_of(block, number):
            kept = jnp.where(live >= number, 1.0, 0.0).astype(jnp.bfloat16)
            return place_buf[block] * kept

        keys = jnp.concatenate([keys_of(first), keys_of(second)], axis=0)
        place = jnp.concatenate([place_of(first, 1), place_of(second, 2)], axis=1)
        return tile, live, keys, place

    @pl.loop(0, work_ref[work_ref.shape[0] - 1])
    def _(group):
        items = [item(group * GROUP + i) for i in range(GROUP)]
        scores = [nt_dot(keys, query_buf[tile]) * scale for tile, _, keys, _ in items]
        tops = [jnp.max(score, axis=0, keepdims=True) for score in scores]
        weights = [jnp.exp2(s - top).astype(jnp.bfloat16) for s, top in zip(scores, tops)]
        sums = [
            jnp.dot(place, weight, preferred_element_type=jnp.float32)[0:8]
            for (_, _, _, place), weight in zip(items, weights)
        ]
        for (tile, live, _, _), top, added in zip(items, tops, sums):
            top = jnp.where(live > 0, top, -1e30)
            state = state_buf[tile]
            before = state[3:4, :]
            both = jnp.maximum(before, top)
            state = state * jnp.exp2(before - both) + added * jnp.exp2(top - both)
            state_buf[tile] = jnp.where(state_row == 3, both, state)

    for tile in range(tile_rows):
        to = work_ref[work_ref.shape[0] - 2 - tile]
        for row in range(shares * rows):
            lanes = pl.ds(row * LANES, LANES)
            for place, held in enumerate((3, 2, 0, 1)):
                out_ref[row // rows, to, pl.ds(place * rows + row % rows, 1), :] = state_buf[
                    tile, pl.ds(held, 1), lanes
                ]


def match(work, queries, keys, score_factor, shares):
    tile_rows, key_tiles = len(queries), len(keys)
    point_total, width = queries[0].shape
    key_rows = keys[0].shape[0] - PLACE_ROWS
    part = key_rows // BLK
    rows = point_total // LANES // shares
    return pl.pallas_call(
        functools.partial(
            match_kernel, score_factor * math.log2(math.e), tile_rows, key_tiles
        ),
        out_shape=jax.ShapeDtypeStruct((shares, tile_rows, 4 * rows, LANES), jnp.float32),
        in_specs=[in_smem()] + in_vmem(tile_rows + key_tiles),
        out_specs=pl.BlockSpec(memory_space=pltpu.VMEM),
        scratch_shapes=[
            pltpu.VMEM((tile_rows, point_total, width), jnp.bfloat16),
            pltpu.VMEM((key_tiles, key_rows, width), jnp.bfloat16),
            pltpu.VMEM((key_tiles * part, PLACE_ROWS, LANES), jnp.bfloat16),
            pltpu.VMEM((tile_rows, 8, point_total), jnp.float32),
        ],
        compiler_params=pltpu.CompilerParams(vmem_limit_bytes=VMEM_BYTES),
        cost_estimate=pl.CostEstimate(
            flops=tile_rows * key_tiles * part * point_total * BLK * width,
            bytes_accessed=2 * (tile_rows * queries[0].size + key_tiles * keys[0].size),
            transcendentals=tile_rows * key_tiles * part * point_total * BLK // 4,
        ),
        name="match",
    )(work, *queries, *keys)


def combine_kernel(parts_ref, place_ref, out_ref):
    parts, out_rows, _ = parts_ref.shape
    rows = out_rows // 4
    tops = [parts_ref[i, 0:rows, :] for i in range(parts)]
    top = functools.reduce(jnp.maximum, tops)
    total = x = y = jnp.zeros_like(top)
    for i in range(parts):
        gain = jnp.exp2(tops[i] - top)
        total += gain * parts_ref[i, rows : 2 * rows, :]
        x += gain * parts_ref[i, 2 * rows : 3 * rows, :]
        y += gain * parts_ref[i, 3 * rows :, :]
    pull = jnp.concatenate([x / total, y / total], axis=0) - place_ref[...].astype(jnp.float32)
    for i in range(out_ref.shape[0]):
        out_ref[i] = pull


def combine(parts, place, copies):
    return pl.pallas_call(
        combine_kernel,
        out_shape=jax.ShapeDtypeStruct((copies,) + place.shape, jnp.float32),
        in_specs=in_vmem(2),
        out_specs=pl.BlockSpec(memory_space=pltpu.VMEM),
        compiler_params=pltpu.CompilerParams(vmem_limit_bytes=VMEM_BYTES),
        name="combine",
    )(parts, place)


def one_hot(at, length, limits):
    count = at.shape[1]
    parts, done = [], 0
    for low, high in limits:
        spot = lax.broadcasted_iota(jnp.int32, (high - low, count), 0) + low
        if low > done:
            parts.append(jnp.zeros((low - done, count), jnp.bfloat16))
        parts.append(jnp.where(spot == at, 1.0, 0.0).astype(jnp.bfloat16))
        done = high
    if length > done:
        parts.append(jnp.zeros((length - done, count), jnp.bfloat16))
    return jnp.concatenate(parts, axis=0)


def flat(value):
    return jnp.concatenate([value[i : i + 1, :] for i in range(value.shape[0])], axis=1)


def hits(side, halo, tall, wide, row, col):
    up = lambda n: -(-n // 16) * 16
    limits = ((0, up(side + halo)), (wide - up(halo), wide))
    return one_hot(flat(row), tall, ((0, tall),)), one_hot(flat(col), wide, limits)


def spots_kernel(
    side, halo, tile_cols, at_ref, ids_ref, rounds_ref, spot_ref, count_ref, hit_buf
):
    tiles = ids_ref.shape[0]
    tall, wide = count_ref.shape

    def folded(at, length):
        return jnp.where(
            (at >= 0) & (at < side + halo), at, jnp.where((at < 0) & (at >= -halo), at + length, -1)
        )

    number = jnp.zeros(ids_ref.shape[1:], jnp.int32)
    for tile in range(tiles):
        ids = ids_ref[tile]
        tile_of = lax.div(ids, side * side)
        within = lax.rem(ids, side * side)
        row = lax.div(tile_of, tile_cols) * side + lax.div(within, side) - at_ref[0]
        col = lax.rem(tile_of, tile_cols) * side + lax.rem(within, side) - at_ref[1]
        row, col = folded(row, side + 2 * halo), folded(col, wide)
        here = (row >= 0) & (col >= 0)
        hit_buf[0, tile] = jnp.where(here, number, -1)
        hit_buf[1, tile] = row
        hit_buf[2, tile] = col
        number = number + here.astype(jnp.int32)
    rounds = jnp.max(number)
    rounds_ref[0] = rounds
    count_ref[...] = jnp.zeros_like(count_ref)

    @pl.loop(0, rounds)
    def _(k):
        tile_of = row = col = jnp.full(number.shape, -1, jnp.int32)
        for tile in range(tiles):
            here = hit_buf[0, tile] == k
            tile_of = jnp.where(here, tile, tile_of)
            row = jnp.where(here, hit_buf[1, tile], row)
            col = jnp.where(here, hit_buf[2, tile], col)
        spot_ref[k, 0] = tile_of
        spot_ref[k, 1] = row
        spot_ref[k, 2] = col
        row_hit, col_hit = hits(side, halo, tall, wide, row, col)
        count_ref[...] += nt_dot(row_hit, col_hit)


def spots(side, halo, tile_cols, wide, at, ids):
    tall = -(-(side + 2 * halo) // 16) * 16
    return pl.pallas_call(
        functools.partial(spots_kernel, side, halo, tile_cols),
        out_shape=(
            jax.ShapeDtypeStruct((1,), jnp.int32),
            jax.ShapeDtypeStruct((ids.shape[0], 3) + ids.shape[1:], jnp.int32),
            jax.ShapeDtypeStruct((tall, wide), jnp.float32),
        ),
        in_specs=[in_smem()] + in_vmem(1),
        out_specs=(in_smem(),) + (pl.BlockSpec(memory_space=pltpu.VMEM),) * 2,
        scratch_shapes=[pltpu.VMEM((3,) + ids.shape, jnp.int32)],
        compiler_params=pltpu.CompilerParams(vmem_limit_bytes=VMEM_BYTES),
        cost_estimate=pl.CostEstimate(
            flops=10 * tall * ids.shape[1] * LANES * wide,
            bytes_accessed=16 * ids.size,
            transcendentals=0,
        ),
        name="spots",
    )(at, ids)


def vertex_sums(side, halo, rounds_ref, spot_ref, points_ref, sum_ref):
    _, tall, wide = sum_ref.shape
    shares, tiles, both_rows, _ = points_ref.shape
    rows = both_rows // 2
    sum_ref[...] = jnp.zeros_like(sum_ref)

    @pl.loop(0, rounds_ref[0])
    def _(k):
        tile_of = spot_ref[k, 0]
        x = y = jnp.zeros(tile_of.shape, jnp.float32)
        for tile in range(tiles):
            here = tile_of == tile
            values = [points_ref[share, tile] for share in range(shares)]
            x = jnp.where(here, jnp.concatenate([v[:rows] for v in values], axis=0), x)
            y = jnp.where(here, jnp.concatenate([v[rows:] for v in values], axis=0), y)
        row_hit, col_hit = hits(side, halo, tall, wide, spot_ref[k, 1], spot_ref[k, 2])
        parts = []
        for value in (flat(x), flat(y)):
            high = value.astype(jnp.bfloat16)
            low = (value - high.astype(jnp.float32)).astype(jnp.bfloat16)
            parts += [row_hit * high, row_hit * low]
        summed = nt_dot(jnp.concatenate(parts, axis=0), col_hit)
        sum_ref[0] += summed[0:tall] + summed[tall : 2 * tall]
        sum_ref[1] += summed[2 * tall : 3 * tall] + summed[3 * tall :]


def sums_kernel(side, halo, rounds_ref, spot_ref, points_ref, out_ref, sum_ref):
    vertex_sums(side, halo, rounds_ref, spot_ref, points_ref, sum_ref)
    out_ref[...] = sum_ref[:, pl.ds(0, out_ref.shape[1]), :]


def relax_kernel(
    side,
    halo,
    extent,
    at_ref,
    rounds_ref,
    spot_ref,
    count_ref,
    points_ref,
    mesh_ref,
    out_ref,
    sum_ref,
):
    vertex_sums(side, halo, rounds_ref, spot_ref, points_ref, sum_ref)
    span = side + 2 * halo
    wide = sum_ref.shape[2]
    shape = (span, wide)
    row = lax.broadcasted_iota(jnp.int32, shape, 0)
    col = lax.broadcasted_iota(jnp.int32, shape, 1)
    row = jnp.where(row < side + halo, row, row - span) + at_ref[0]
    col = jnp.where(col < side + halo, col, col - wide) + at_ref[1]
    inside = (row >= 0) & (row < extent[0]) & (col >= 0) & (col < extent[1])
    own_pulled = (at_ref[2] == 0).astype(jnp.float32)
    linked = 1.0
    matched = count_ref[pl.ds(0, span), :]
    moving, gains, has, step = [], [], [], []
    for part, pulled in enumerate((own_pulled, 1.0 - own_pulled)):
        gain = mesh_ref[part * 3 + 2]
        diagonal = 4.0 * gain + spring_sec * linked + spring_match * matched * pulled
        gains.append(gain)
        has.append(matched * pulled)
        step.append(jnp.where(inside, relax_rate / diagonal, 0.0))
        moving.append(
            [(mesh_ref[part * 3 + c], sum_ref[c, pl.ds(0, span), :] * pulled) for c in range(2)]
        )
    for sweep in range(ITERS):
        later = []
        for part in range(2):
            row_of = []
            for c in range(2):
                u, pulled = moving[part][c]
                other = moving[1 - part][c][0]
                laplace = (
                    pltpu.roll(u, 1, 0)
                    + pltpu.roll(u, span - 1, 0)
                    + pltpu.roll(u, 1, 1)
                    + pltpu.roll(u, wide - 1, 1)
                    - 4.0 * u
                )
                force = (
                    gains[part] * laplace
                    + spring_sec * (other - linked * u)
                    + spring_match * (pulled - has[part] * u)
                )
                row_of.append((u + step[part] * force, pulled))
            later.append(row_of)
        moving = later
    for c in range(2):
        out_ref[c] = moving[0][c][0][0:side, 0:side]


def with_halo(value, halo, wide):
    side = value.shape[1]
    after = passed_along(value[:, :halo], "ty", -1)
    before = passed_along(value[:, side - halo :], "ty", 1)
    value = jnp.concatenate([value, after, before], axis=1)
    after = passed_along(value[:, :, :halo].swapaxes(1, 2), "tx", -1).swapaxes(1, 2)
    before = passed_along(value[:, :, side - halo :].swapaxes(1, 2), "tx", 1).swapaxes(1, 2)
    gap = jnp.zeros(value.shape[:2] + (wide - side - 2 * halo,), value.dtype)
    return jnp.concatenate([value, after, gap, before], axis=2)


def sweeps(moving, gains, sums, number, at, side, halo, extent):
    sections = lax.axis_size("sec")
    sec_index = at[2]
    has_next = (sec_index < sections - 1).astype(jnp.float32)
    linked = (sec_index > 0).astype(jnp.float32) + has_next
    pulled, matched = sums * has_next, number * has_next
    span, wide = moving.shape[1:]
    row = jnp.arange(span)[:, None]
    col = jnp.arange(wide)[None, :]
    row = jnp.where(row < side + halo, row, row - span) + at[0]
    col = jnp.where(col < side + halo, col, col - wide) + at[1]
    inside = (row >= 0) & (row < extent[0]) & (col >= 0) & (col < extent[1])
    diagonal = 4.0 * gains + spring_sec * linked + spring_match * matched
    step = jnp.where(inside, relax_rate / jnp.where(inside, diagonal, 1.0), 0.0)
    for sweep in range(ITERS):
        lower_sec = passed_along(moving, "sec", 1)
        upper_sec = passed_along(moving, "sec", -1)
        laplace = (
            jnp.roll(moving, 1, 1)
            + jnp.roll(moving, -1, 1)
            + jnp.roll(moving, 1, 2)
            + jnp.roll(moving, -1, 2)
            - 4.0 * moving
        )
        force = (
            gains * laplace
            + spring_sec * (lower_sec + upper_sec - linked * moving)
            + spring_match * (pulled - matched * moving)
        )
        moving = moving + step * force
    return moving[:, :side, :side]


def local_work(lists, counts, blocks, rows):
    tiles, total = lists.shape[0], blocks.shape[0]
    is_live = jnp.arange(lists.shape[1])[None, :] < counts[:, None]
    hit = (lists[:, :, None] == blocks[None, None, :]) & is_live[:, :, None]
    live = jnp.any(hit, axis=1)
    spot = jnp.arange(total)
    rank = jnp.sum(live[:, None, :] & (spot[None, :] < spot[:, None])[None], axis=2)
    taken = live[:, None, :] & (rank[:, None, :] == spot[None, :, None])
    packed = jnp.sum(jnp.where(taken, spot[None, None, :], 0), axis=2)
    number = jnp.sum(live, axis=1)
    pairs = (number + 1) // 2
    tile = jnp.arange(tiles)
    before = jnp.sum(jnp.where(tile[None, :] < tile[:, None], pairs[None, :], 0), axis=1)
    most = tiles * -(-total // 2)
    item = jnp.arange(-(-most // GROUP) * GROUP)[:, None]
    mine = (item >= before[None, :]) & (item < (before + pairs)[None, :])
    place = 2 * (item - before[None, :])

    def chosen(at, values):
        there = mine[:, :, None] & (at[:, :, None] == spot[None, None, :])
        return jnp.sum(jnp.where(there, values, 0), axis=(1, 2))

    second = jnp.where(place + 1 < number[None, :], place + 1, place)
    full = jnp.where(place + 1 < number[None, :], 2, 1)
    work = jnp.stack(
        [
            jnp.sum(jnp.where(mine, tile[None, :], 0), axis=1),
            chosen(place, packed[None]),
            chosen(second, packed[None]),
            jnp.sum(jnp.where(mine, full, 0), axis=1),
        ],
        axis=1,
    )
    groups = (jnp.sum(pairs) + GROUP - 1) // GROUP
    return jnp.concatenate([work.reshape(-1), rows[::-1], groups[None]]).astype(jnp.int32)


def gathered(values, axes):
    held, steps, index = [], [], []
    for value, axis in zip(values, axes):
        devices, here = lax.axis_size(axis), lax.axis_index(axis)
        if devices & (devices - 1):
            turns = [[(i, (i + j) % devices) for i in range(devices)] for j in range(1, devices)]
            moved = [lax.ppermute(value, axis, turn) for turn in turns]
            held.append(dict(enumerate([value] + moved)))
            steps.append(0)
            index.append(jnp.mod(here - jnp.arange(devices), devices))
        else:
            held.append({0: value})
            steps.append(devices.bit_length() - 1)
            index.append(here ^ jnp.arange(devices))
    for step in range(1, max(steps) + 1):
        for i, axis in enumerate(axes):
            devices = lax.axis_size(axis)
            for at in range(devices - 1, 0, -1):
                if steps[i] and at.bit_count() == step:
                    by = at & -at
                    pairs = [(j, j ^ by) for j in range(devices)]
                    held[i][at] = lax.ppermute(held[i][at ^ by], axis, pairs)
        if step < max(steps):
            held = lax.optimization_barrier(held)
    return [[h[i] for i in range(len(h))] for h in held], index


def per_device(
    descriptors, positions, vertex_ids, candidate_blocks, candidate_count, displacement, stiffness
):
    point_total, width = descriptors.shape[3:]
    per_tile = point_total // BLK
    tile_rows, tile_cols = lax.axis_size("ty"), lax.axis_size("tx")
    sections = lax.axis_size("sec")
    sec_index = lax.axis_index("sec")
    tiles = tile_rows * tile_cols
    side = displacement.shape[3]
    halo = ITERS
    span = side + 2 * halo
    wide = -(-span // LANES) * LANES
    shares = 2 if sections == 2 and per_tile % 2 == 0 else 1
    part = per_tile // shares
    key_rows = part * BLK

    own_desc = descriptors[0, 0, 0]
    own_place = positions[0, 0, 0].reshape(2 * per_tile, BLK)
    swap = [(i, 1 - i) for i in range(2)]
    query = passed_along(own_desc, "sec", 1)
    whole = jnp.concatenate(
        [vertex_ids[0, 0, 0], candidate_blocks[0, 0, 0], candidate_count[0, 0, 0][None]]
    )
    whole = jnp.pad(whole, (0, -whole.shape[0] % (8 * LANES))).reshape(-1, LANES)
    if shares == 2:
        first = sec_index == 0
        key = passed_along(own_desc[:key_rows], "sec", -1)
        other_place = lax.ppermute(own_place, "sec", swap)
        query = jnp.where(first, own_desc, query)
        key = jnp.where(first, key, own_desc[key_rows:])
        key_place = jnp.where(first, other_place, own_place).reshape(2, shares, part, BLK)
        key_place = jnp.where(first, key_place[:, 0], key_place[:, 1]).reshape(2 * part, BLK)
        place = jnp.where(first, own_place, other_place).reshape(2, shares, part, BLK)
        place = jnp.where(first, place[:, 0], place[:, 1]).reshape(2 * part, BLK)
        whole = jnp.where(first, whole, passed_along(whole, "sec", 1))
        share = sec_index
    else:
        key, key_place = own_desc, own_place
        place = passed_along(own_place, "sec", 1)
        whole = passed_along(whole, "sec", 1)
        share = 0
    whole = spread(whole, ("ty", "tx"))
    filler = jnp.zeros((PLACE_ROWS - 2 * part, BLK), key_place.dtype)
    key = jnp.concatenate([key, key_place, filler], axis=0)
    (queries, keys), (query_row, key_col) = gathered((query, key), ("ty", "tx"))

    ids = whole[:, :per_tile]
    lists = whole[:, per_tile].reshape(tile_rows, tile_cols, -1)
    lists = lax.dynamic_index_in_dim(lists, lax.axis_index("tx"), 1, keepdims=False)
    turned = query_row[:, None] == jnp.arange(tile_rows)[None, :]
    lists = jnp.sum(jnp.where(turned[:, :, None], lists[None], 0), axis=1)
    cand = candidate_blocks.shape[3]
    key_tile = lax.axis_index("ty") * tile_cols + key_col
    blocks = (key_tile[:, None] * per_tile + share * part + jnp.arange(part)[None, :]).reshape(-1)
    work = local_work(lists[:, :cand], lists[:, cand], blocks, query_row)

    at = jnp.stack(
        [lax.axis_index("ty") * side, lax.axis_index("tx") * side, sec_index]
    ).astype(jnp.int32)
    extent = (side * tile_rows, side * tile_cols)
    own_mesh = jnp.concatenate([displacement[0], stiffness], axis=0)
    far = tile_rows // 2
    own_mesh, queries[far] = lax.optimization_barrier((own_mesh, queries[far]))
    sum_shape = pltpu.VMEM((2, -(-span // 16) * 16, wide), jnp.float32)

    if shares == 2:
        other_mesh = lax.ppermute(own_mesh, "sec", swap)
        both = jnp.concatenate([own_mesh, other_mesh], axis=0)
        both, queries, keys = lax.optimization_barrier((both, queries, keys))
        mesh_values = with_halo(both, halo, wide)
        parts = match(work, queries, keys, 16.0 / width, shares)
        ids, parts = lax.optimization_barrier((ids, parts))
        rounds, spot, number = spots(side, halo, tile_cols, wide, at, ids)
        parts = exchanged(parts.reshape((-1,) + parts.shape[2:]), ("sec", "ty"))
        points = exchanged(combine(parts, place, 2 * tiles), ("sec", "ty", "tx"))
        relaxed = pl.pallas_call(
            functools.partial(relax_kernel, side, halo, extent),
            out_shape=jax.ShapeDtypeStruct((2, side, side), jnp.float32),
            in_specs=[in_smem()] * 2 + in_vmem(4),
            out_specs=pl.BlockSpec(memory_space=pltpu.VMEM),
            scratch_shapes=[sum_shape],
            compiler_params=pltpu.CompilerParams(vmem_limit_bytes=VMEM_BYTES),
            name="relax",
        )(at, rounds, spot, number, points.reshape(2, tiles, -1, LANES), mesh_values)
        return relaxed[None]

    ids = passed_along(ids, "sec", -1)
    rounds, spot, number = spots(side, halo, tile_cols, wide, at, ids)
    parts = match(work, queries, keys, 16.0 / width, shares)
    parts = exchanged(parts[0], "ty")
    points = passed_along(exchanged(combine(parts, place, tiles), ("ty", "tx")), "sec", -1)
    sums = pl.pallas_call(
        functools.partial(sums_kernel, side, halo),
        out_shape=jax.ShapeDtypeStruct((2, span, wide), jnp.float32),
        in_specs=[in_smem()] + in_vmem(2),
        out_specs=pl.BlockSpec(memory_space=pltpu.VMEM),
        scratch_shapes=[sum_shape],
        compiler_params=pltpu.CompilerParams(vmem_limit_bytes=VMEM_BYTES),
        name="sums",
    )(rounds, spot, points[None])
    own_mesh = with_halo(own_mesh, halo, wide)
    moving, gains = own_mesh[0:2], own_mesh[2]
    return sweeps(moving, gains, sums, number[:span], at, side, halo, extent)[None]


def solution(mesh):
    in_specs = (
        P("sec", "ty", "tx", None, None),
        P("sec", "ty", "tx", None, None),
        P("sec", "ty", "tx", None),
        P("sec", "ty", "tx", None),
        P("sec", "ty", "tx"),
        P("sec", None, "ty", "tx"),
        P("sec", "ty", "tx"),
    )
    out_specs = P("sec", None, "ty", "tx")
    return jax.shard_map(
        per_device, mesh=mesh, in_specs=in_specs, out_specs=out_specs, check_vma=False
    )
```

```python
import functools
import math

import jax
import jax.numpy as jnp
from jax import lax
from jax.experimental import pallas as pl
from jax.experimental.pallas import tpu as pltpu
from jax.sharding import PartitionSpec as P

BLK = 128
ITERS = 4
LANES = 128
PLACE_ROWS = 16
GROUP = 2
BASE = 256
DIGITS = 3
VMEM_BYTES = 24 * 1024 * 1024

spring_sec = 0.5
spring_match = 1.0
relax_rate = 0.8


def passed_along(value, axis, by):
    devices = lax.axis_size(axis)
    pairs = [(i, i + by) for i in range(devices) if 0 <= i + by < devices]
    return lax.ppermute(value, axis, pairs)


def exchanged(value, axes):
    return lax.all_to_all(value, axes, split_axis=0, concat_axis=0, tiled=True)


def spread(value, axes):
    copies = jnp.broadcast_to(value[None], (lax.axis_size(axes),) + value.shape)
    return exchanged(copies, axes)


def nt_dot(a, b):
    return lax.dot_general(a, b, (((1,), (1,)), ((), ())), preferred_element_type=jnp.float32)


def in_vmem(count):
    return [pl.BlockSpec(memory_space=pltpu.VMEM)] * count


def in_smem():
    return pl.BlockSpec(memory_space=pltpu.SMEM)


def match_kernel(scale, part, tile_rows, work_ref, key_ref, *refs):
    query_refs = refs[:tile_rows]
    out_ref, query_buf, place_buf, state_buf, list_buf = refs[tile_rows:]
    shares = out_ref.shape[0]
    key_tiles, key_total, _ = key_ref.shape
    point_total = query_buf.shape[1]
    rows = point_total // LANES // shares
    key_rows = part * BLK
    total = key_tiles * part
    cand = (work_ref.shape[0] - tile_rows) // tile_rows

    number = 0
    for tile in range(tile_rows):
        for i in range(cand):
            place = work_ref[tile * cand + i]
            list_buf[number] = tile * total + place
            number = number + jnp.where(place >= 0, 1, 0)
        list_buf[number] = -1
        number = number + lax.rem(number, 2)
    for i in range(2 * GROUP):
        list_buf[number + i] = -1
    groups = lax.div(number + 2 * GROUP - 1, 2 * GROUP)

    row_at = lax.broadcasted_iota(jnp.int32, (PLACE_ROWS, LANES), 0)
    for tile, query_ref in enumerate(query_refs):
        query_buf[tile] = query_ref[pl.ds(0, point_total), :]
    ids = []
    for tile in range(key_tiles):
        rest = key_ref[tile, pl.ds(key_rows, key_total - key_rows), :].astype(jnp.float32)
        for j in range(part):
            x, y = rest[j : j + 1, :], rest[part + j : part + j + 1, :]
            stacked = jnp.where(
                row_at == 0, x, jnp.where(row_at == 1, y, jnp.where(row_at == 2, 1.0, 0.0))
            )
            place_buf[tile * part + j] = stacked.astype(jnp.bfloat16)
        digits = [rest[2 * part + i * rows : 2 * part + (i + 1) * rows] for i in range(DIGITS)]
        ids.append(sum(digit * float(BASE**i) for i, digit in enumerate(digits)))

    state_row = lax.broadcasted_iota(jnp.int32, state_buf.shape[1:], 0)
    for tile in range(tile_rows):
        state_buf[tile] = jnp.where(state_row == 3, -1e30, 0.0)

    def item(at):
        codes = [list_buf[2 * at + i] for i in range(2)]
        tile = lax.div(jnp.maximum(codes[0], 0), total)
        keys, places = [], []
        for code in codes:
            block = lax.rem(jnp.maximum(code, 0), total)
            start = pl.multiple_of(lax.rem(block, part) * BLK, BLK)
            keys.append(key_ref[lax.div(block, part), pl.ds(start, BLK), :])
            kept = jnp.where(code >= 0, 1.0, 0.0).astype(jnp.bfloat16)
            places.append(place_buf[block] * kept)
        return tile, codes[0] >= 0, jnp.concatenate(keys, axis=0), jnp.concatenate(places, axis=1)

    @pl.loop(0, groups)
    def _(group):
        items = [item(group * GROUP + i) for i in range(GROUP)]
        scores = [nt_dot(keys, query_buf[tile]) * scale for tile, _, keys, _ in items]
        tops = [jnp.max(score, axis=0, keepdims=True) for score in scores]
        weights = [jnp.exp2(s - top).astype(jnp.bfloat16) for s, top in zip(scores, tops)]
        sums = [
            jnp.dot(place, weight, preferred_element_type=jnp.float32)[0:8]
            for (_, _, _, place), weight in zip(items, weights)
        ]
        for (tile, live, _, _), top, added in zip(items, tops, sums):
            top = jnp.where(live, top, -1e30)
            state = state_buf[tile]
            before = state[3:4, :]
            both = jnp.maximum(before, top)
            state = state * jnp.exp2(before - both) + added * jnp.exp2(top - both)
            state_buf[tile] = jnp.where(state_row == 3, both, state)

    for tile in range(tile_rows):
        to = work_ref[tile_rows * cand + tile]
        for row in range(shares * rows):
            lanes = pl.ds(row * LANES, LANES)
            for place, held in enumerate((3, 2, 0, 1)):
                out_ref[row // rows, to, pl.ds(place * rows + row % rows, 1), :] = state_buf[
                    tile, pl.ds(held, 1), lanes
                ]
        for share in range(shares):
            out_ref[share, tile, pl.ds(4 * rows, key_tiles * rows), :] = jnp.concatenate(ids, axis=0)


def match(work, queries, keys, score_factor, shares, point_total, part):
    tile_rows, key_tiles = len(queries), keys.shape[0]
    width = keys.shape[2]
    rows = point_total // LANES // shares
    return pl.pallas_call(
        functools.partial(match_kernel, score_factor * math.log2(math.e), part, tile_rows),
        out_shape=jax.ShapeDtypeStruct(
            (shares, tile_rows, (4 + key_tiles) * rows, LANES), jnp.float32
        ),
        in_specs=[in_smem()] + in_vmem(1 + tile_rows),
        out_specs=pl.BlockSpec(memory_space=pltpu.VMEM),
        scratch_shapes=[
            pltpu.VMEM((tile_rows, point_total, width), jnp.bfloat16),
            pltpu.VMEM((key_tiles * part, PLACE_ROWS, LANES), jnp.bfloat16),
            pltpu.VMEM((tile_rows, 8, point_total), jnp.float32),
            pltpu.SMEM((work.shape[0] + 2 * GROUP + tile_rows,), jnp.int32),
        ],
        compiler_params=pltpu.CompilerParams(vmem_limit_bytes=VMEM_BYTES),
        cost_estimate=pl.CostEstimate(
            flops=tile_rows * key_tiles * part * point_total * BLK * width,
            bytes_accessed=2 * (tile_rows * queries[0].size + keys.size),
            transcendentals=tile_rows * key_tiles * part * point_total * BLK // 4,
        ),
        name="match",
    )(work, keys, *queries)


def combine_kernel(parts_ref, place_ref, out_ref):
    parts = parts_ref.shape[0]
    rows = place_ref.shape[0] // 2
    tops = [parts_ref[i, 0:rows, :] for i in range(parts)]
    top = functools.reduce(jnp.maximum, tops)
    total = x = y = jnp.zeros_like(top)
    for i in range(parts):
        gain = jnp.exp2(tops[i] - top)
        total += gain * parts_ref[i, rows : 2 * rows, :]
        x += gain * parts_ref[i, 2 * rows : 3 * rows, :]
        y += gain * parts_ref[i, 3 * rows : 4 * rows, :]
    pull = jnp.concatenate([x / total, y / total], axis=0) - place_ref[...].astype(jnp.float32)
    for i in range(out_ref.shape[0]):
        out_ref[i] = pull


def combine(parts, place, copies):
    return pl.pallas_call(
        combine_kernel,
        out_shape=jax.ShapeDtypeStruct((copies,) + place.shape, jnp.float32),
        in_specs=in_vmem(2),
        out_specs=pl.BlockSpec(memory_space=pltpu.VMEM),
        compiler_params=pltpu.CompilerParams(vmem_limit_bytes=VMEM_BYTES),
        name="combine",
    )(parts, place)


def one_hot(at, length, limits):
    count = at.shape[1]
    parts, done = [], 0
    for low, high in limits:
        spot = lax.broadcasted_iota(jnp.int32, (high - low, count), 0) + low
        if low > done:
            parts.append(jnp.zeros((low - done, count), jnp.bfloat16))
        parts.append(jnp.where(spot == at, 1.0, 0.0).astype(jnp.bfloat16))
        done = high
    if length > done:
        parts.append(jnp.zeros((length - done, count), jnp.bfloat16))
    return jnp.concatenate(parts, axis=0)


def flat(value):
    return jnp.concatenate([value[i : i + 1, :] for i in range(value.shape[0])], axis=1)


def hits(side, halo, tall, wide, row, col):
    up = lambda n: -(-n // 16) * 16
    limits = ((0, up(side + halo)), (wide - up(halo), wide))
    return one_hot(flat(row), tall, ((0, tall),)), one_hot(flat(col), wide, limits)


def spots_kernel(
    side, halo, key_tiles, at_ref, parts_ref, rounds_ref, spot_ref, count_ref, hit_buf
):
    shares, tile_rows, _, _ = parts_ref.shape
    rows = hit_buf.shape[2] // shares
    tall, wide = count_ref.shape

    def folded(at, length):
        return jnp.where(
            (at >= 0) & (at < side + halo), at, jnp.where((at < 0) & (at >= -halo), at + length, -1)
        )

    number = jnp.zeros(hit_buf.shape[2:], jnp.int32)
    tiles = [(i, j) for i in range(tile_rows) for j in range(key_tiles)]
    for at, (i, j) in enumerate(tiles):
        ids = jnp.concatenate(
            [parts_ref[k, i, pl.ds((4 + j) * rows, rows), :] for k in range(shares)], axis=0
        ).astype(jnp.int32)
        tile_of = lax.div(ids, side * side)
        within = lax.rem(ids, side * side)
        row = lax.div(tile_of, key_tiles) * side + lax.div(within, side) - at_ref[0]
        col = lax.rem(tile_of, key_tiles) * side + lax.rem(within, side) - at_ref[1]
        row, col = folded(row, side + 2 * halo), folded(col, wide)
        here = (row >= 0) & (col >= 0)
        hit_buf[0, at] = jnp.where(here, number, -1)
        hit_buf[1, at] = row
        hit_buf[2, at] = col
        number = number + here.astype(jnp.int32)
    rounds = jnp.max(number)
    rounds_ref[0] = rounds
    count_ref[...] = jnp.zeros_like(count_ref)

    @pl.loop(0, rounds)
    def _(k):
        tile_of = row = col = jnp.full(number.shape, -1, jnp.int32)
        for at, (i, j) in enumerate(tiles):
            here = hit_buf[0, at] == k
            tile_of = jnp.where(here, at, tile_of)
            row = jnp.where(here, hit_buf[1, at], row)
            col = jnp.where(here, hit_buf[2, at], col)
        spot_ref[k, 0] = tile_of
        spot_ref[k, 1] = row
        spot_ref[k, 2] = col
        row_hit, col_hit = hits(side, halo, tall, wide, row, col)
        count_ref[...] += nt_dot(row_hit, col_hit)


def spots(side, halo, key_tiles, wide, at, parts, rows):
    tall = -(-(side + 2 * halo) // 16) * 16
    points = (parts.shape[0] * rows, LANES)
    tiles = parts.shape[1] * key_tiles
    return pl.pallas_call(
        functools.partial(spots_kernel, side, halo, key_tiles),
        out_shape=(
            jax.ShapeDtypeStruct((1,), jnp.int32),
            jax.ShapeDtypeStruct((tiles, 3) + points, jnp.int32),
            jax.ShapeDtypeStruct((tall, wide), jnp.float32),
        ),
        in_specs=[in_smem()] + in_vmem(1),
        out_specs=(in_smem(),) + (pl.BlockSpec(memory_space=pltpu.VMEM),) * 2,
        scratch_shapes=[pltpu.VMEM((3, tiles) + points, jnp.int32)],
        compiler_params=pltpu.CompilerParams(vmem_limit_bytes=VMEM_BYTES),
        cost_estimate=pl.CostEstimate(
            flops=10 * tall * points[0] * LANES * wide,
            bytes_accessed=8 * parts.size,
            transcendentals=0,
        ),
        name="spots",
    )(at, parts)


def vertex_sums(side, halo, rounds_ref, spot_ref, points_ref, sum_ref):
    _, tall, wide = sum_ref.shape
    shares, tiles, both_rows, _ = points_ref.shape
    rows = both_rows // 2
    sum_ref[...] = jnp.zeros_like(sum_ref)

    @pl.loop(0, rounds_ref[0])
    def _(k):
        tile_of = spot_ref[k, 0]
        x = y = jnp.zeros(tile_of.shape, jnp.float32)
        for tile in range(tiles):
            here = tile_of == tile
            values = [points_ref[share, tile] for share in range(shares)]
            x = jnp.where(here, jnp.concatenate([v[:rows] for v in values], axis=0), x)
            y = jnp.where(here, jnp.concatenate([v[rows:] for v in values], axis=0), y)
        row_hit, col_hit = hits(side, halo, tall, wide, spot_ref[k, 1], spot_ref[k, 2])
        parts = []
        for value in (flat(x), flat(y)):
            high = value.astype(jnp.bfloat16)
            low = (value - high.astype(jnp.float32)).astype(jnp.bfloat16)
            parts += [row_hit * high, row_hit * low]
        summed = nt_dot(jnp.concatenate(parts, axis=0), col_hit)
        sum_ref[0] += summed[0:tall] + summed[tall : 2 * tall]
        sum_ref[1] += summed[2 * tall : 3 * tall] + summed[3 * tall :]


def sums_kernel(side, halo, rounds_ref, spot_ref, points_ref, out_ref, sum_ref):
    vertex_sums(side, halo, rounds_ref, spot_ref, points_ref, sum_ref)
    out_ref[...] = sum_ref[:, pl.ds(0, out_ref.shape[1]), :]


def relax_kernel(
    side,
    halo,
    extent,
    at_ref,
    rounds_ref,
    spot_ref,
    count_ref,
    points_ref,
    mesh_ref,
    out_ref,
    sum_ref,
):
    vertex_sums(side, halo, rounds_ref, spot_ref, points_ref, sum_ref)
    span = side + 2 * halo
    wide = sum_ref.shape[2]
    shape = (span, wide)
    row = lax.broadcasted_iota(jnp.int32, shape, 0)
    col = lax.broadcasted_iota(jnp.int32, shape, 1)
    row = jnp.where(row < side + halo, row, row - span) + at_ref[0]
    col = jnp.where(col < side + halo, col, col - wide) + at_ref[1]
    inside = (row >= 0) & (row < extent[0]) & (col >= 0) & (col < extent[1])
    own_pulled = (at_ref[2] == 0).astype(jnp.float32)
    linked = 1.0
    matched = count_ref[pl.ds(0, span), :]
    moving, gains, has, step = [], [], [], []
    for part, pulled in enumerate((own_pulled, 1.0 - own_pulled)):
        gain = mesh_ref[part * 3 + 2]
        diagonal = 4.0 * gain + spring_sec * linked + spring_match * matched * pulled
        gains.append(gain)
        has.append(matched * pulled)
        step.append(jnp.where(inside, relax_rate / diagonal, 0.0))
        moving.append(
            [(mesh_ref[part * 3 + c], sum_ref[c, pl.ds(0, span), :] * pulled) for c in range(2)]
        )
    for sweep in range(ITERS):
        later = []
        for part in range(2):
            row_of = []
            for c in range(2):
                u, pulled = moving[part][c]
                other = moving[1 - part][c][0]
                laplace = (
                    pltpu.roll(u, 1, 0)
                    + pltpu.roll(u, span - 1, 0)
                    + pltpu.roll(u, 1, 1)
                    + pltpu.roll(u, wide - 1, 1)
                    - 4.0 * u
                )
                force = (
                    gains[part] * laplace
                    + spring_sec * (other - linked * u)
                    + spring_match * (pulled - has[part] * u)
                )
                row_of.append((u + step[part] * force, pulled))
            later.append(row_of)
        moving = later
    for c in range(2):
        out_ref[c] = moving[0][c][0][0:side, 0:side]


def row_edges(value, halo):
    after = passed_along(value[:, :halo], "ty", -1)
    before = passed_along(value[:, value.shape[1] - halo :], "ty", 1)
    return jnp.concatenate([after, before], axis=1)


def col_edges(value, halo):
    after = passed_along(value[:, :, :halo].swapaxes(1, 2), "tx", -1)
    before = passed_along(value[:, :, value.shape[2] - halo :].swapaxes(1, 2), "tx", 1)
    return jnp.concatenate([after, before], axis=1)


def framed(value, cols, wide):
    halo = cols.shape[1] // 2
    cols = cols.swapaxes(1, 2)
    gap = jnp.zeros(value.shape[:2] + (wide - value.shape[2] - 2 * halo,), value.dtype)
    return jnp.concatenate([value, cols[:, :, :halo], gap, cols[:, :, halo:]], axis=2)


def sweeps(moving, gains, sums, number, at, side, halo, extent):
    sections = lax.axis_size("sec")
    sec_index = at[2]
    has_next = (sec_index < sections - 1).astype(jnp.float32)
    linked = (sec_index > 0).astype(jnp.float32) + has_next
    pulled, matched = sums * has_next, number * has_next
    span, wide = moving.shape[1:]
    row = jnp.arange(span)[:, None]
    col = jnp.arange(wide)[None, :]
    row = jnp.where(row < side + halo, row, row - span) + at[0]
    col = jnp.where(col < side + halo, col, col - wide) + at[1]
    inside = (row >= 0) & (row < extent[0]) & (col >= 0) & (col < extent[1])
    diagonal = 4.0 * gains + spring_sec * linked + spring_match * matched
    step = jnp.where(inside, relax_rate / jnp.where(inside, diagonal, 1.0), 0.0)
    for sweep in range(ITERS):
        lower_sec = passed_along(moving, "sec", 1)
        upper_sec = passed_along(moving, "sec", -1)
        laplace = (
            jnp.roll(moving, 1, 1)
            + jnp.roll(moving, -1, 1)
            + jnp.roll(moving, 1, 2)
            + jnp.roll(moving, -1, 2)
            - 4.0 * moving
        )
        force = (
            gains * laplace
            + spring_sec * (lower_sec + upper_sec - linked * moving)
            + spring_match * (pulled - matched * moving)
        )
        moving = moving + step * force
    return moving[:, :side, :side]


def pack_kernel(place_ref, ids_ref, list_ref, out_ref):
    def digit(value, i):
        return ((value >> (i * BASE.bit_length() - i)) & (BASE - 1)).astype(jnp.float32)

    def cut(row):
        return [row[:, i : i + LANES] for i in range(0, row.shape[1], LANES)]

    place, ids, listed = place_ref[...].astype(jnp.float32), ids_ref[...], list_ref[...]
    rows = cut(place[0:1]) + cut(place[1:2])
    for i in range(DIGITS):
        rows += cut(digit(ids, i))
    last = [digit(listed, 0), digit(listed, 1)]
    gap = jnp.zeros((out_ref.shape[0] - len(rows) - PLACE_ROWS, LANES), jnp.float32)
    end = jnp.zeros((PLACE_ROWS - len(last), LANES), jnp.float32)
    rows += ([gap] if gap.shape[0] else []) + last + [end]
    out_ref[...] = jnp.concatenate(rows, axis=0).astype(jnp.bfloat16)


def pack(place, ids, listed):
    per_tile = ids.shape[1] // LANES
    rows = -(-(2 + DIGITS) * per_tile // 16) * 16 + PLACE_ROWS
    return pl.pallas_call(
        pack_kernel,
        out_shape=jax.ShapeDtypeStruct((rows, LANES), jnp.bfloat16),
        in_specs=in_vmem(3),
        out_specs=pl.BlockSpec(memory_space=pltpu.VMEM),
        compiler_params=pltpu.CompilerParams(vmem_limit_bytes=VMEM_BYTES),
        name="pack",
    )(place, ids, listed)


def gathered(value, axis):
    devices, here = lax.axis_size(axis), lax.axis_index(axis)
    if devices & (devices - 1):
        partners = [[(i, (i + j) % devices) for i in range(devices)] for j in range(1, devices)]
        place = jnp.mod(here - jnp.arange(devices), devices)
    else:
        partners = [[(i, i ^ j) for i in range(devices)] for j in range(1, devices)]
        place = here ^ jnp.arange(devices)
    return [value] + [lax.ppermute(value, axis, pairs) for pairs in partners], place


def per_device(
    descriptors, positions, vertex_ids, candidate_blocks, candidate_count, displacement, stiffness
):
    point_total, width = descriptors.shape[3:]
    per_tile = point_total // BLK
    tile_rows, tile_cols = lax.axis_size("ty"), lax.axis_size("tx")
    sections = lax.axis_size("sec")
    sec_index = lax.axis_index("sec")
    tiles = tile_rows * tile_cols
    side = displacement.shape[3]
    halo = ITERS
    span = side + 2 * halo
    wide = -(-span // LANES) * LANES
    cand = candidate_blocks.shape[3]
    shares = 2 if sections == 2 and per_tile % 2 == 0 else 1
    part = per_tile // shares
    key_rows = part * BLK

    own_desc = descriptors[0, 0, 0]
    listed = jnp.concatenate([candidate_blocks[0, 0, 0], candidate_count[0, 0, 0][None]])
    listed = jnp.pad(listed, (0, LANES - cand - 1))[None]
    own_rest = pack(positions[0, 0, 0], vertex_ids[0, 0], listed)
    own_mesh = jnp.concatenate([displacement[0], stiffness], axis=0)
    swap = [(i, 1 - i) for i in range(2)]

    def of_share(rows):
        rows = rows.reshape(-1, shares, part, LANES)
        if shares == 2:
            rows = jnp.where(sec_index == 0, rows[:, 0], rows[:, 1])
        return rows.reshape(-1, LANES)

    if shares == 2:
        first = sec_index == 0
        share = sec_index
        desc = lax.ppermute(own_desc, "sec", swap)
        rest = lax.ppermute(own_rest, "sec", swap)
        query = jnp.where(first, own_desc, desc)
        key = jnp.where(first, desc[:key_rows], own_desc[key_rows:])
        query_rest = jnp.where(first, own_rest, rest)
        key_rest = jnp.where(first, rest, own_rest)
    else:
        share = 0
        key, key_rest = own_desc, own_rest
        query = passed_along(own_desc, "sec", 1)
        query_rest = passed_along(own_rest, "sec", 1)
    place = of_share(query_rest[: 2 * per_tile])
    ids = of_share(query_rest[2 * per_tile : (2 + DIGITS) * per_tile])
    filler = jnp.zeros((-(2 + DIGITS) * part % 16, LANES), jnp.bfloat16)
    key = jnp.concatenate([key, of_share(key_rest[: 2 * per_tile]), ids, filler], axis=0)
    query = jnp.concatenate([query, query_rest[-PLACE_ROWS:]], axis=0)

    queries, query_row = gathered(query, "ty")
    keys = spread(key, "tx")

    lists = jnp.stack([v[point_total : point_total + 2] for v in queries]).astype(jnp.int32)
    lists = lists[:, 0] + BASE * lists[:, 1]
    blocks, counts = lists[:, :cand], lists[:, cand : cand + 1]
    tile_of, within = blocks // per_tile, blocks % per_tile
    here = (
        (jnp.arange(cand)[None, :] < counts)
        & (tile_of // tile_cols == lax.axis_index("ty"))
        & (within // part == share)
    )
    work = jnp.where(here, tile_of % tile_cols * part + within % part, -1)
    work = jnp.concatenate([work.reshape(-1), query_row]).astype(jnp.int32)
    at = jnp.stack(
        [lax.axis_index("ty") * side, lax.axis_index("tx") * side, sec_index]
    ).astype(jnp.int32)
    extent = (side * tile_rows, side * tile_cols)
    sum_shape = pltpu.VMEM((2, -(-span // 16) * 16, wide), jnp.float32)

    tied, rest = lax.optimization_barrier((own_mesh, query_rest))
    rows = row_edges(tied, halo)
    rows, tied, queries[1] = lax.optimization_barrier((rows, own_mesh, queries[1]))
    tall_mesh = jnp.concatenate([own_mesh, rows], axis=1)
    cols = col_edges(tall_mesh, halo)

    if shares == 2:
        other = lax.ppermute(tied, "sec", swap)
        other, cols, work = lax.optimization_barrier((other, cols, work))
    parts = match(work, queries, keys, 16.0 / width, shares, point_total, part)
    if shares == 2:
        edges = jnp.concatenate(
            [jnp.pad(rows, ((0, 0), (0, 0), (0, span - side))), cols], axis=1
        )
        edges = lax.ppermute(edges, "sec", swap)
        other = jnp.concatenate([other, edges[:, : 2 * halo, :side]], axis=1)
        mesh_values = framed(
            jnp.concatenate([tall_mesh, other], axis=0),
            jnp.concatenate([cols, edges[:, 2 * halo :]], axis=0),
            wide,
        )
        shape = parts.shape
        parts = exchanged(parts.reshape((-1,) + shape[2:]), ("sec", "ty"))
        points = exchanged(combine(parts, place, 2 * tiles), ("sec", "ty", "tx"))
        rounds, spot, number = spots(side, halo, tile_cols, wide, at, parts.reshape(shape), part)
        relaxed = pl.pallas_call(
            functools.partial(relax_kernel, side, halo, extent),
            out_shape=jax.ShapeDtypeStruct((2, side, side), jnp.float32),
            in_specs=[in_smem()] * 2 + in_vmem(4),
            out_specs=pl.BlockSpec(memory_space=pltpu.VMEM),
            scratch_shapes=[sum_shape],
            compiler_params=pltpu.CompilerParams(vmem_limit_bytes=VMEM_BYTES),
            name="relax",
        )(at, rounds, spot, number, points.reshape(2, tiles, -1, LANES), mesh_values)
        return relaxed[None]

    parts = exchanged(parts[0], "ty")
    points = passed_along(exchanged(combine(parts, place, tiles), ("ty", "tx")), "sec", -1)
    parts = passed_along(parts, "sec", -1)
    rounds, spot, number = spots(side, halo, tile_cols, wide, at, parts[None], part)
    sums = pl.pallas_call(
        functools.partial(sums_kernel, side, halo),
        out_shape=jax.ShapeDtypeStruct((2, span, wide), jnp.float32),
        in_specs=[in_smem()] + in_vmem(2),
        out_specs=pl.BlockSpec(memory_space=pltpu.VMEM),
        scratch_shapes=[sum_shape],
        compiler_params=pltpu.CompilerParams(vmem_limit_bytes=VMEM_BYTES),
        name="sums",
    )(rounds, spot, points[None])
    mesh_values = framed(tall_mesh, cols, wide)
    moving, gains = mesh_values[0:2], mesh_values[2]
    return sweeps(moving, gains, sums, number[:span], at, side, halo, extent)[None]


def solution(mesh):
    in_specs = (
        P("sec", "ty", "tx", None, None),
        P("sec", "ty", "tx", None, None),
        P("sec", "ty", "tx", None),
        P("sec", "ty", "tx", None),
        P("sec", "ty", "tx"),
        P("sec", None, "ty", "tx"),
        P("sec", "ty", "tx"),
    )
    out_specs = P("sec", None, "ty", "tx")
    return jax.shard_map(
        per_device, mesh=mesh, in_specs=in_specs, out_specs=out_specs, check_vma=False
    )
```

```python
import functools
import math

import jax
import jax.numpy as jnp
from jax import lax
from jax.experimental import pallas as pl
from jax.experimental.pallas import tpu as pltpu
from jax.sharding import PartitionSpec as P

BLK = 128
ITERS = 4
LANES = 128
PLACE_ROWS = 16
GROUP = 2
BASE = 256
DIGITS = 3
VMEM_BYTES = 24 * 1024 * 1024

spring_sec = 0.5
spring_match = 1.0
relax_rate = 0.8


def passed_along(value, axis, by):
    devices = lax.axis_size(axis)
    pairs = [(i, i + by) for i in range(devices) if 0 <= i + by < devices]
    return lax.ppermute(value, axis, pairs)


def exchanged(value, axes):
    return lax.all_to_all(value, axes, split_axis=0, concat_axis=0, tiled=True)


def spread(value, axes):
    copies = jnp.broadcast_to(value[None], (lax.axis_size(axes),) + value.shape)
    return exchanged(copies, axes)


def nt_dot(a, b):
    return lax.dot_general(a, b, (((1,), (1,)), ((), ())), preferred_element_type=jnp.float32)


def in_vmem(count):
    return [pl.BlockSpec(memory_space=pltpu.VMEM)] * count


def in_smem():
    return pl.BlockSpec(memory_space=pltpu.SMEM)


def match_kernel(scale, key_tiles, work_ref, query_ref, *refs):
    key_refs = refs[:key_tiles]
    out_ref, key_buf, place_buf, state_buf, list_buf = refs[key_tiles:]
    shares, tile_rows = out_ref.shape[:2]
    point_total = state_buf.shape[2]
    rows = point_total // LANES // shares
    key_rows = key_buf.shape[1]
    part = key_rows // BLK
    total = key_tiles * part
    cand = work_ref.shape[0] // tile_rows

    number = 0
    for tile in range(tile_rows):
        for i in range(cand):
            place = work_ref[tile * cand + i]
            list_buf[number] = tile * total + place
            number = number + jnp.where(place >= 0, 1, 0)
        list_buf[number] = -1
        number = number + lax.rem(number, 2)
    for i in range(2 * GROUP):
        list_buf[number + i] = -1
    groups = lax.div(number + 2 * GROUP - 1, 2 * GROUP)

    row_at = lax.broadcasted_iota(jnp.int32, (PLACE_ROWS, LANES), 0)
    ids = []
    for tile, key_ref in enumerate(key_refs):
        key_buf[tile] = key_ref[pl.ds(0, key_rows), :]
        rest = key_ref[pl.ds(key_rows, key_ref.shape[0] - key_rows), :].astype(jnp.float32)
        for j in range(part):
            x, y = rest[j : j + 1, :], rest[part + j : part + j + 1, :]
            stacked = jnp.where(
                row_at == 0, x, jnp.where(row_at == 1, y, jnp.where(row_at == 2, 1.0, 0.0))
            )
            place_buf[tile * part + j] = stacked.astype(jnp.bfloat16)
        digits = [rest[2 * part + i * rows : 2 * part + (i + 1) * rows] for i in range(DIGITS)]
        ids.append(sum(digit * float(BASE**i) for i, digit in enumerate(digits)))

    state_row = lax.broadcasted_iota(jnp.int32, state_buf.shape[1:], 0)
    for tile in range(tile_rows):
        state_buf[tile] = jnp.where(state_row == 3, -1e30, 0.0)

    def item(at):
        codes = [list_buf[2 * at + i] for i in range(2)]
        tile = lax.div(jnp.maximum(codes[0], 0), total)
        keys, places = [], []
        for code in codes:
            block = lax.rem(jnp.maximum(code, 0), total)
            start = pl.multiple_of(lax.rem(block, part) * BLK, BLK)
            keys.append(key_buf[lax.div(block, part), pl.ds(start, BLK), :])
            kept = jnp.where(code >= 0, 1.0, 0.0).astype(jnp.bfloat16)
            places.append(place_buf[block] * kept)
        return tile, codes[0] >= 0, jnp.concatenate(keys, axis=0), jnp.concatenate(places, axis=1)

    @pl.loop(0, groups)
    def _(group):
        items = [item(group * GROUP + i) for i in range(GROUP)]
        scores = [
            nt_dot(keys, query_ref[tile, pl.ds(0, point_total), :]) * scale
            for tile, _, keys, _ in items
        ]
        tops = [jnp.max(score, axis=0, keepdims=True) for score in scores]
        weights = [jnp.exp2(s - top).astype(jnp.bfloat16) for s, top in zip(scores, tops)]
        sums = [
            jnp.dot(place, weight, preferred_element_type=jnp.float32)[0:8]
            for (_, _, _, place), weight in zip(items, weights)
        ]
        for (tile, live, _, _), top, added in zip(items, tops, sums):
            top = jnp.where(live, top, -1e30)
            state = state_buf[tile]
            before = state[3:4, :]
            both = jnp.maximum(before, top)
            state = state * jnp.exp2(before - both) + added * jnp.exp2(top - both)
            state_buf[tile] = jnp.where(state_row == 3, both, state)

    for tile in range(tile_rows):
        for row in range(shares * rows):
            lanes = pl.ds(row * LANES, LANES)
            for place, held in enumerate((3, 2, 0, 1)):
                out_ref[row // rows, tile, pl.ds(place * rows + row % rows, 1), :] = state_buf[
                    tile, pl.ds(held, 1), lanes
                ]
        for share in range(shares):
            out_ref[share, tile, pl.ds(4 * rows, key_tiles * rows), :] = jnp.concatenate(ids, axis=0)


def match(work, queries, keys, score_factor, shares, point_total, part):
    tile_rows, key_tiles = queries.shape[0], len(keys)
    width = queries.shape[2]
    rows = point_total // LANES // shares
    return pl.pallas_call(
        functools.partial(match_kernel, score_factor * math.log2(math.e), key_tiles),
        out_shape=jax.ShapeDtypeStruct(
            (shares, tile_rows, (4 + key_tiles) * rows, LANES), jnp.float32
        ),
        in_specs=[in_smem()] + in_vmem(1 + key_tiles),
        out_specs=pl.BlockSpec(memory_space=pltpu.VMEM),
        scratch_shapes=[
            pltpu.VMEM((key_tiles, part * BLK, width), jnp.bfloat16),
            pltpu.VMEM((key_tiles * part, PLACE_ROWS, LANES), jnp.bfloat16),
            pltpu.VMEM((tile_rows, 8, point_total), jnp.float32),
            pltpu.SMEM((work.shape[0] + 2 * GROUP + tile_rows,), jnp.int32),
        ],
        compiler_params=pltpu.CompilerParams(vmem_limit_bytes=VMEM_BYTES),
        cost_estimate=pl.CostEstimate(
            flops=tile_rows * key_tiles * part * point_total * BLK * width,
            bytes_accessed=2 * (queries.size + key_tiles * keys[0].size),
            transcendentals=tile_rows * key_tiles * part * point_total * BLK // 4,
        ),
        name="match",
    )(work, queries, *keys)


def combine_kernel(parts_ref, place_ref, out_ref):
    parts = parts_ref.shape[0]
    rows = place_ref.shape[0] // 2
    tops = [parts_ref[i, 0:rows, :] for i in range(parts)]
    top = functools.reduce(jnp.maximum, tops)
    total = x = y = jnp.zeros_like(top)
    for i in range(parts):
        gain = jnp.exp2(tops[i] - top)
        total += gain * parts_ref[i, rows : 2 * rows, :]
        x += gain * parts_ref[i, 2 * rows : 3 * rows, :]
        y += gain * parts_ref[i, 3 * rows : 4 * rows, :]
    pull = jnp.concatenate([x / total, y / total], axis=0) - place_ref[...].astype(jnp.float32)
    for i in range(out_ref.shape[0]):
        out_ref[i] = pull


def combine(parts, place, copies):
    return pl.pallas_call(
        combine_kernel,
        out_shape=jax.ShapeDtypeStruct((copies,) + place.shape, jnp.float32),
        in_specs=in_vmem(2),
        out_specs=pl.BlockSpec(memory_space=pltpu.VMEM),
        compiler_params=pltpu.CompilerParams(vmem_limit_bytes=VMEM_BYTES),
        name="combine",
    )(parts, place)


def one_hot(at, length, limits):
    count = at.shape[1]
    parts, done = [], 0
    for low, high in limits:
        spot = lax.broadcasted_iota(jnp.int32, (high - low, count), 0) + low
        if low > done:
            parts.append(jnp.zeros((low - done, count), jnp.bfloat16))
        parts.append(jnp.where(spot == at, 1.0, 0.0).astype(jnp.bfloat16))
        done = high
    if length > done:
        parts.append(jnp.zeros((length - done, count), jnp.bfloat16))
    return jnp.concatenate(parts, axis=0)


def flat(value):
    return jnp.concatenate([value[i : i + 1, :] for i in range(value.shape[0])], axis=1)


def hits(side, halo, tall, wide, row, col):
    up = lambda n: -(-n // 16) * 16
    limits = ((0, up(side + halo)), (wide - up(halo), wide))
    return one_hot(flat(row), tall, ((0, tall),)), one_hot(flat(col), wide, limits)


def spots_kernel(
    side, halo, key_tiles, at_ref, parts_ref, rounds_ref, spot_ref, count_ref, hit_buf
):
    shares, tile_rows, _, _ = parts_ref.shape
    rows = hit_buf.shape[2] // shares
    tall, wide = count_ref.shape

    def folded(at, length):
        return jnp.where(
            (at >= 0) & (at < side + halo), at, jnp.where((at < 0) & (at >= -halo), at + length, -1)
        )

    number = jnp.zeros(hit_buf.shape[2:], jnp.int32)
    tiles = [(i, j) for i in range(tile_rows) for j in range(key_tiles)]
    for at, (i, j) in enumerate(tiles):
        ids = jnp.concatenate(
            [parts_ref[k, i, pl.ds((4 + j) * rows, rows), :] for k in range(shares)], axis=0
        ).astype(jnp.int32)
        tile_of = lax.div(ids, side * side)
        within = lax.rem(ids, side * side)
        row = lax.div(tile_of, key_tiles) * side + lax.div(within, side) - at_ref[0]
        col = lax.rem(tile_of, key_tiles) * side + lax.rem(within, side) - at_ref[1]
        row, col = folded(row, side + 2 * halo), folded(col, wide)
        here = (row >= 0) & (col >= 0)
        hit_buf[0, at] = jnp.where(here, number, -1)
        hit_buf[1, at] = row
        hit_buf[2, at] = col
        number = number + here.astype(jnp.int32)
    rounds = jnp.max(number)
    rounds_ref[0] = rounds
    count_ref[...] = jnp.zeros_like(count_ref)

    @pl.loop(0, rounds)
    def _(k):
        tile_of = row = col = jnp.full(number.shape, -1, jnp.int32)
        for at, (i, j) in enumerate(tiles):
            here = hit_buf[0, at] == k
            tile_of = jnp.where(here, i * key_tiles + at_ref[3 + j], tile_of)
            row = jnp.where(here, hit_buf[1, at], row)
            col = jnp.where(here, hit_buf[2, at], col)
        spot_ref[k, 0] = tile_of
        spot_ref[k, 1] = row
        spot_ref[k, 2] = col
        row_hit, col_hit = hits(side, halo, tall, wide, row, col)
        count_ref[...] += nt_dot(row_hit, col_hit)


def spots(side, halo, key_tiles, wide, at, parts, rows):
    tall = -(-(side + 2 * halo) // 16) * 16
    points = (parts.shape[0] * rows, LANES)
    tiles = parts.shape[1] * key_tiles
    return pl.pallas_call(
        functools.partial(spots_kernel, side, halo, key_tiles),
        out_shape=(
            jax.ShapeDtypeStruct((1,), jnp.int32),
            jax.ShapeDtypeStruct((tiles, 3) + points, jnp.int32),
            jax.ShapeDtypeStruct((tall, wide), jnp.float32),
        ),
        in_specs=[in_smem()] + in_vmem(1),
        out_specs=(in_smem(),) + (pl.BlockSpec(memory_space=pltpu.VMEM),) * 2,
        scratch_shapes=[pltpu.VMEM((3, tiles) + points, jnp.int32)],
        compiler_params=pltpu.CompilerParams(vmem_limit_bytes=VMEM_BYTES),
        cost_estimate=pl.CostEstimate(
            flops=10 * tall * points[0] * LANES * wide,
            bytes_accessed=8 * parts.size,
            transcendentals=0,
        ),
        name="spots",
    )(at, parts)


def vertex_sums(side, halo, rounds_ref, spot_ref, points_ref, sum_ref):
    _, tall, wide = sum_ref.shape
    shares, tiles, both_rows, _ = points_ref.shape
    rows = both_rows // 2
    sum_ref[...] = jnp.zeros_like(sum_ref)

    @pl.loop(0, rounds_ref[0])
    def _(k):
        tile_of = spot_ref[k, 0]
        x = y = jnp.zeros(tile_of.shape, jnp.float32)
        for tile in range(tiles):
            here = tile_of == tile
            values = [points_ref[share, tile] for share in range(shares)]
            x = jnp.where(here, jnp.concatenate([v[:rows] for v in values], axis=0), x)
            y = jnp.where(here, jnp.concatenate([v[rows:] for v in values], axis=0), y)
        row_hit, col_hit = hits(side, halo, tall, wide, spot_ref[k, 1], spot_ref[k, 2])
        parts = []
        for value in (flat(x), flat(y)):
            high = value.astype(jnp.bfloat16)
            low = (value - high.astype(jnp.float32)).astype(jnp.bfloat16)
            parts += [row_hit * high, row_hit * low]
        summed = nt_dot(jnp.concatenate(parts, axis=0), col_hit)
        sum_ref[0] += summed[0:tall] + summed[tall : 2 * tall]
        sum_ref[1] += summed[2 * tall : 3 * tall] + summed[3 * tall :]


def sums_kernel(side, halo, rounds_ref, spot_ref, points_ref, out_ref, sum_ref):
    vertex_sums(side, halo, rounds_ref, spot_ref, points_ref, sum_ref)
    out_ref[...] = sum_ref[:, pl.ds(0, out_ref.shape[1]), :]


def relax_kernel(
    side,
    halo,
    extent,
    at_ref,
    rounds_ref,
    spot_ref,
    count_ref,
    points_ref,
    mesh_ref,
    out_ref,
    sum_ref,
):
    vertex_sums(side, halo, rounds_ref, spot_ref, points_ref, sum_ref)
    span = side + 2 * halo
    wide = sum_ref.shape[2]
    shape = (span, wide)
    row = lax.broadcasted_iota(jnp.int32, shape, 0)
    col = lax.broadcasted_iota(jnp.int32, shape, 1)
    row = jnp.where(row < side + halo, row, row - span) + at_ref[0]
    col = jnp.where(col < side + halo, col, col - wide) + at_ref[1]
    inside = (row >= 0) & (row < extent[0]) & (col >= 0) & (col < extent[1])
    own_pulled = (at_ref[2] == 0).astype(jnp.float32)
    linked = 1.0
    matched = count_ref[pl.ds(0, span), :]
    moving, gains, has, step = [], [], [], []
    for part, pulled in enumerate((own_pulled, 1.0 - own_pulled)):
        gain = mesh_ref[part * 3 + 2]
        diagonal = 4.0 * gain + spring_sec * linked + spring_match * matched * pulled
        gains.append(gain)
        has.append(matched * pulled)
        step.append(jnp.where(inside, relax_rate / diagonal, 0.0))
        moving.append(
            [(mesh_ref[part * 3 + c], sum_ref[c, pl.ds(0, span), :] * pulled) for c in range(2)]
        )
    for sweep in range(ITERS):
        later = []
        for part in range(2):
            row_of = []
            for c in range(2):
                u, pulled = moving[part][c]
                other = moving[1 - part][c][0]
                laplace = (
                    pltpu.roll(u, 1, 0)
                    + pltpu.roll(u, span - 1, 0)
                    + pltpu.roll(u, 1, 1)
                    + pltpu.roll(u, wide - 1, 1)
                    - 4.0 * u
                )
                force = (
                    gains[part] * laplace
                    + spring_sec * (other - linked * u)
                    + spring_match * (pulled - has[part] * u)
                )
                row_of.append((u + step[part] * force, pulled))
            later.append(row_of)
        moving = later
    for c in range(2):
        out_ref[c] = moving[0][c][0][0:side, 0:side]


def with_halo(value, halo, wide):
    side = value.shape[1]
    after = passed_along(value[:, :halo], "ty", -1)
    before = passed_along(value[:, side - halo :], "ty", 1)
    value = jnp.concatenate([value, after, before], axis=1)
    after = passed_along(value[:, :, :halo].swapaxes(1, 2), "tx", -1).swapaxes(1, 2)
    before = passed_along(value[:, :, side - halo :].swapaxes(1, 2), "tx", 1).swapaxes(1, 2)
    gap = jnp.zeros(value.shape[:2] + (wide - side - 2 * halo,), value.dtype)
    return jnp.concatenate([value, after, gap, before], axis=2)


def sweeps(moving, gains, sums, number, at, side, halo, extent):
    sections = lax.axis_size("sec")
    sec_index = at[2]
    has_next = (sec_index < sections - 1).astype(jnp.float32)
    linked = (sec_index > 0).astype(jnp.float32) + has_next
    pulled, matched = sums * has_next, number * has_next
    span, wide = moving.shape[1:]
    row = jnp.arange(span)[:, None]
    col = jnp.arange(wide)[None, :]
    row = jnp.where(row < side + halo, row, row - span) + at[0]
    col = jnp.where(col < side + halo, col, col - wide) + at[1]
    inside = (row >= 0) & (row < extent[0]) & (col >= 0) & (col < extent[1])
    diagonal = 4.0 * gains + spring_sec * linked + spring_match * matched
    step = jnp.where(inside, relax_rate / jnp.where(inside, diagonal, 1.0), 0.0)
    for sweep in range(ITERS):
        lower_sec = passed_along(moving, "sec", 1)
        upper_sec = passed_along(moving, "sec", -1)
        laplace = (
            jnp.roll(moving, 1, 1)
            + jnp.roll(moving, -1, 1)
            + jnp.roll(moving, 1, 2)
            + jnp.roll(moving, -1, 2)
            - 4.0 * moving
        )
        force = (
            gains * laplace
            + spring_sec * (lower_sec + upper_sec - linked * moving)
            + spring_match * (pulled - matched * moving)
        )
        moving = moving + step * force
    return moving[:, :side, :side]


def pack_kernel(desc_hbm, place_ref, ids_ref, list_ref, out_ref, sem):
    points = desc_hbm.shape[0]
    copy = pltpu.make_async_copy(desc_hbm, out_ref.at[pl.ds(0, points), :], sem)
    copy.start()

    def digit(value, i):
        return ((value >> (i * BASE.bit_length() - i)) & (BASE - 1)).astype(jnp.float32)

    def cut(row):
        return [row[:, i : i + LANES] for i in range(0, row.shape[1], LANES)]

    place, ids, listed = place_ref[...].astype(jnp.float32), ids_ref[...], list_ref[...]
    rows = cut(place[0:1]) + cut(place[1:2])
    for i in range(DIGITS):
        rows += cut(digit(ids, i))
    last = [digit(listed, 0), digit(listed, 1)]
    count = out_ref.shape[0] - points
    gap = jnp.zeros((count - len(rows) - PLACE_ROWS, LANES), jnp.float32)
    end = jnp.zeros((PLACE_ROWS - len(last), LANES), jnp.float32)
    rows += ([gap] if gap.shape[0] else []) + last + [end]
    out_ref[pl.ds(points, count), :] = jnp.concatenate(rows, axis=0).astype(jnp.bfloat16)
    copy.wait()


def pack(desc, place, ids, listed):
    per_tile = ids.shape[1] // LANES
    rows = -(-(2 + DIGITS) * per_tile // 16) * 16 + PLACE_ROWS
    return pl.pallas_call(
        pack_kernel,
        out_shape=jax.ShapeDtypeStruct((desc.shape[0] + rows, LANES), jnp.bfloat16),
        in_specs=[pl.BlockSpec(memory_space=pl.ANY)] + in_vmem(3),
        out_specs=pl.BlockSpec(memory_space=pltpu.VMEM),
        scratch_shapes=[pltpu.SemaphoreType.DMA],
        compiler_params=pltpu.CompilerParams(vmem_limit_bytes=VMEM_BYTES),
        name="pack",
    )(desc, place, ids, listed)


def gathered(value, axis):
    devices, here = lax.axis_size(axis), lax.axis_index(axis)
    if devices & (devices - 1):
        partners = [[(i, (i + j) % devices) for i in range(devices)] for j in range(1, devices)]
        place = jnp.mod(here - jnp.arange(devices), devices)
    else:
        partners = [[(i, i ^ j) for i in range(devices)] for j in range(1, devices)]
        place = here ^ jnp.arange(devices)
    return [value] + [lax.ppermute(value, axis, pairs) for pairs in partners], place


def per_device(
    descriptors, positions, vertex_ids, candidate_blocks, candidate_count, displacement, stiffness
):
    point_total, width = descriptors.shape[3:]
    per_tile = point_total // BLK
    tile_rows, tile_cols = lax.axis_size("ty"), lax.axis_size("tx")
    sections = lax.axis_size("sec")
    sec_index = lax.axis_index("sec")
    tiles = tile_rows * tile_cols
    side = displacement.shape[3]
    halo = ITERS
    span = side + 2 * halo
    wide = -(-span // LANES) * LANES
    cand = candidate_blocks.shape[3]
    shares = 2 if sections == 2 and per_tile % 2 == 0 else 1
    part = per_tile // shares
    key_rows = part * BLK

    listed = jnp.concatenate([candidate_blocks[0, 0, 0], candidate_count[0, 0, 0][None]])
    listed = jnp.pad(listed, (0, LANES - cand - 1))[None]
    own = pack(descriptors[0, 0, 0], positions[0, 0, 0], vertex_ids[0, 0], listed)
    own_mesh = jnp.concatenate([displacement[0], stiffness], axis=0)
    swap = [(i, 1 - i) for i in range(2)]

    def of_share(rows):
        rows = rows.reshape(-1, shares, part, LANES)
        if shares == 2:
            rows = jnp.where(sec_index == 0, rows[:, 0], rows[:, 1])
        return rows.reshape(-1, LANES)

    if shares == 2:
        first = sec_index == 0
        share = sec_index
        other = lax.ppermute(own, "sec", swap)
        query = jnp.where(first, own, other)
        key = jnp.where(first, other[:key_rows], own[key_rows:point_total])
        key_place = jnp.where(
            first,
            other[point_total : point_total + 2 * per_tile],
            own[point_total : point_total + 2 * per_tile],
        )
    else:
        share = 0
        query = passed_along(own, "sec", 1)
        key, key_place = own[:point_total], own[point_total : point_total + 2 * per_tile]
    rest = query[point_total:]
    place = of_share(rest[: 2 * per_tile])
    ids = of_share(rest[2 * per_tile : (2 + DIGITS) * per_tile])
    filler = jnp.zeros((-(2 + DIGITS) * part % 16, LANES), jnp.bfloat16)
    key = jnp.concatenate([key, of_share(key_place), ids, filler], axis=0)
    query = jnp.concatenate([query[:point_total], rest[-PLACE_ROWS:]], axis=0)

    keys, key_col = gathered(key, "tx")
    queries = spread(query, "ty")

    lists = queries[:, point_total : point_total + 2].astype(jnp.int32)
    lists = lists[:, 0] + BASE * lists[:, 1]
    blocks, counts = lists[:, :cand], lists[:, cand : cand + 1]
    tile_of, within = blocks // per_tile, blocks % per_tile
    slot_of = jnp.zeros_like(tile_of)
    for i in range(tile_cols):
        slot_of = jnp.where(tile_of % tile_cols == key_col[i], i, slot_of)
    here = (
        (jnp.arange(cand)[None, :] < counts)
        & (tile_of // tile_cols == lax.axis_index("ty"))
        & (within // part == share)
    )
    work = jnp.where(here, slot_of * part + within % part, -1).reshape(-1).astype(jnp.int32)
    at = jnp.concatenate(
        [
            jnp.stack([lax.axis_index("ty") * side, lax.axis_index("tx") * side, sec_index]),
            key_col,
        ]
    ).astype(jnp.int32)
    extent = (side * tile_rows, side * tile_cols)
    sum_shape = pltpu.VMEM((2, -(-span // 16) * 16, wide), jnp.float32)

    if shares == 2:
        tied, keys[1] = lax.optimization_barrier((own_mesh, keys[1]))
        own_mesh = jnp.concatenate([own_mesh, lax.ppermute(tied, "sec", swap)], axis=0)
    parts = match(work, queries, keys, 16.0 / width, shares, point_total, part)
    own_mesh, parts = lax.optimization_barrier((own_mesh, parts))
    mesh_values = with_halo(own_mesh, halo, wide)
    if shares == 2:
        shape = parts.shape
        parts = exchanged(parts.reshape((-1,) + shape[2:]), ("sec", "ty"))
        points = exchanged(combine(parts, place, 2 * tiles), ("sec", "ty", "tx"))
        rounds, spot, number = spots(side, halo, tile_cols, wide, at, parts.reshape(shape), part)
        relaxed = pl.pallas_call(
            functools.partial(relax_kernel, side, halo, extent),
            out_shape=jax.ShapeDtypeStruct((2, side, side), jnp.float32),
            in_specs=[in_smem()] * 2 + in_vmem(4),
            out_specs=pl.BlockSpec(memory_space=pltpu.VMEM),
            scratch_shapes=[sum_shape],
            compiler_params=pltpu.CompilerParams(vmem_limit_bytes=VMEM_BYTES),
            name="relax",
        )(at, rounds, spot, number, points.reshape(2, tiles, -1, LANES), mesh_values)
        return relaxed[None]

    parts = exchanged(parts[0], "ty")
    points = passed_along(exchanged(combine(parts, place, tiles), ("ty", "tx")), "sec", -1)
    parts = passed_along(parts, "sec", -1)
    rounds, spot, number = spots(side, halo, tile_cols, wide, at, parts[None], part)
    sums = pl.pallas_call(
        functools.partial(sums_kernel, side, halo),
        out_shape=jax.ShapeDtypeStruct((2, span, wide), jnp.float32),
        in_specs=[in_smem()] + in_vmem(2),
        out_specs=pl.BlockSpec(memory_space=pltpu.VMEM),
        scratch_shapes=[sum_shape],
        compiler_params=pltpu.CompilerParams(vmem_limit_bytes=VMEM_BYTES),
        name="sums",
    )(rounds, spot, points[None])
    moving, gains = mesh_values[0:2], mesh_values[2]
    return sweeps(moving, gains, sums, number[:span], at, side, halo, extent)[None]


def solution(mesh):
    in_specs = (
        P("sec", "ty", "tx", None, None),
        P("sec", "ty", "tx", None, None),
        P("sec", "ty", "tx", None),
        P("sec", "ty", "tx", None),
        P("sec", "ty", "tx"),
        P("sec", None, "ty", "tx"),
        P("sec", "ty", "tx"),
    )
    out_specs = P("sec", None, "ty", "tx")
    return jax.shard_map(
        per_device, mesh=mesh, in_specs=in_specs, out_specs=out_specs, check_vma=False
    )
```

```python
import functools
import math

import jax
import jax.numpy as jnp
from jax import lax
from jax.experimental import pallas as pl
from jax.experimental.pallas import tpu as pltpu
from jax.sharding import PartitionSpec as P

BLK = 128
ITERS = 4
LANES = 128
PLACE_ROWS = 16
GROUP = 2
BASE = 256
DIGITS = 3
VMEM_BYTES = 24 * 1024 * 1024

spring_sec = 0.5
spring_match = 1.0
relax_rate = 0.8


def passed_along(value, axis, by):
    devices = lax.axis_size(axis)
    pairs = [(i, i + by) for i in range(devices) if 0 <= i + by < devices]
    return lax.ppermute(value, axis, pairs)


def exchanged(value, axes):
    return lax.all_to_all(value, axes, split_axis=0, concat_axis=0, tiled=True)


def spread(value, axes):
    copies = jnp.broadcast_to(value[None], (lax.axis_size(axes),) + value.shape)
    return exchanged(copies, axes)


def nt_dot(a, b):
    return lax.dot_general(a, b, (((1,), (1,)), ((), ())), preferred_element_type=jnp.float32)


def in_vmem(count):
    return [pl.BlockSpec(memory_space=pltpu.VMEM)] * count


def in_smem():
    return pl.BlockSpec(memory_space=pltpu.SMEM)


def match_kernel(scale, tile_rows, key_tiles, cand, at_ref, *refs):
    query_refs, key_refs = refs[:tile_rows], refs[tile_rows : tile_rows + key_tiles]
    (edge_ref, out_ref, query_buf, key_buf, place_buf, state_buf, found_buf, work_ref, list_buf, sem) = (
        refs[tile_rows + key_tiles :]
    )
    shares = out_ref.shape[0]
    point_total = state_buf.shape[2]
    rows = point_total // LANES // shares
    key_rows = key_buf.shape[1]
    part = key_rows // BLK
    total = key_tiles * part
    own_row, share = at_ref[3], at_ref[4]

    for tile, query_ref in enumerate(query_refs):
        last = query_ref[pl.ds(point_total, PLACE_ROWS), :].astype(jnp.float32).astype(jnp.int32)
        here = last[0:1] == own_row * shares + share
        found_buf[pl.ds(tile, 1), :] = jnp.where(here, last[1:2], -1)
    found = pltpu.make_async_copy(found_buf, work_ref, sem)
    found.start()

    row_at = lax.broadcasted_iota(jnp.int32, (PLACE_ROWS, LANES), 0)
    ids = []
    for tile, key_ref in enumerate(key_refs):
        col = at_ref[5 + tile_rows + tile]
        key_buf[col] = key_ref[pl.ds(0, key_rows), :]
        rest = key_ref[pl.ds(key_rows, key_ref.shape[0] - key_rows), :].astype(jnp.float32)
        for j in range(part):
            x, y = rest[j : j + 1, :], rest[part + j : part + j + 1, :]
            stacked = jnp.where(
                row_at == 0, x, jnp.where(row_at == 1, y, jnp.where(row_at == 2, 1.0, 0.0))
            )
            place_buf[col * part + j] = stacked.astype(jnp.bfloat16)
        digits = [rest[2 * part + i * rows : 2 * part + (i + 1) * rows] for i in range(DIGITS)]
        ids.append(sum(digit * float(BASE**i) for i, digit in enumerate(digits)))

    for tile, query_ref in enumerate(query_refs):
        query_buf[tile] = query_ref[pl.ds(0, point_total), :]
    found.wait()

    number = 0
    for tile in range(tile_rows):
        for i in range(cand):
            place = work_ref[tile, i]
            list_buf[number] = tile * total + place
            number = number + jnp.where(place >= 0, 1, 0)
        list_buf[number] = -1
        number = number + lax.rem(number, 2)
    for i in range(2 * GROUP):
        list_buf[number + i] = -1
    groups = lax.div(number + 2 * GROUP - 1, 2 * GROUP)

    state_row = lax.broadcasted_iota(jnp.int32, state_buf.shape[1:], 0)
    for tile in range(tile_rows):
        state_buf[tile] = jnp.where(state_row == 3, -1e30, 0.0)

    def item(at):
        codes = [list_buf[2 * at + i] for i in range(2)]
        tile = lax.div(jnp.maximum(codes[0], 0), total)
        keys, places = [], []
        for code in codes:
            block = lax.rem(jnp.maximum(code, 0), total)
            start = pl.multiple_of(lax.rem(block, part) * BLK, BLK)
            keys.append(key_buf[lax.div(block, part), pl.ds(start, BLK), :])
            kept = jnp.where(code >= 0, 1.0, 0.0).astype(jnp.bfloat16)
            places.append(place_buf[block] * kept)
        return tile, codes[0] >= 0, jnp.concatenate(keys, axis=0), jnp.concatenate(places, axis=1)

    @pl.loop(0, groups)
    def _(group):
        items = [item(group * GROUP + i) for i in range(GROUP)]
        scores = [
            nt_dot(keys, query_buf[tile]) * scale
            for tile, _, keys, _ in items
        ]
        tops = [jnp.max(score, axis=0, keepdims=True) for score in scores]
        weights = [jnp.exp2(s - top).astype(jnp.bfloat16) for s, top in zip(scores, tops)]
        sums = [
            jnp.dot(place, weight, preferred_element_type=jnp.float32)[0:8]
            for (_, _, _, place), weight in zip(items, weights)
        ]
        for (tile, live, _, _), top, added in zip(items, tops, sums):
            top = jnp.where(live, top, -1e30)
            state = state_buf[tile]
            before = state[3:4, :]
            both = jnp.maximum(before, top)
            state = state * jnp.exp2(before - both) + added * jnp.exp2(top - both)
            state_buf[tile] = jnp.where(state_row == 3, both, state)

    edge_rows = edge_ref.shape[1]
    for tile in range(tile_rows):
        to = at_ref[5 + tile]
        for row in range(shares * rows):
            lanes = pl.ds(row * LANES, LANES)
            for place, held in enumerate((3, 2, 0, 1)):
                out_ref[row // rows, to, pl.ds(place * rows + row % rows, 1), :] = state_buf[
                    tile, pl.ds(held, 1), lanes
                ]
        for share in range(shares):
            out_ref[share, tile, pl.ds(4 * rows, key_tiles * rows), :] = jnp.concatenate(ids, axis=0)
            out_ref[share, tile, pl.ds((4 + key_tiles) * rows, edge_rows), :] = jnp.where(
                tile > own_row, edge_ref[1], edge_ref[0]
            )


def match(at, queries, keys, edges, score_factor, shares, point_total, part, cand):
    tile_rows, key_tiles = len(queries), len(keys)
    width = queries[0].shape[1]
    rows = point_total // LANES // shares
    total = key_tiles * part
    return pl.pallas_call(
        functools.partial(
            match_kernel, score_factor * math.log2(math.e), tile_rows, key_tiles, cand
        ),
        out_shape=jax.ShapeDtypeStruct(
            (shares, tile_rows, (4 + key_tiles) * rows + edges.shape[1], LANES), jnp.float32
        ),
        in_specs=[in_smem()] + in_vmem(tile_rows + key_tiles + 1),
        out_specs=pl.BlockSpec(memory_space=pltpu.VMEM),
        scratch_shapes=[
            pltpu.VMEM((tile_rows, point_total, width), jnp.bfloat16),
            pltpu.VMEM((key_tiles, part * BLK, width), jnp.bfloat16),
            pltpu.VMEM((total, PLACE_ROWS, LANES), jnp.bfloat16),
            pltpu.VMEM((tile_rows, 8, point_total), jnp.float32),
            pltpu.VMEM((tile_rows, LANES), jnp.int32),
            pltpu.SMEM((tile_rows, LANES), jnp.int32),
            pltpu.SMEM((tile_rows * (cand + 1) + 2 * GROUP + 1,), jnp.int32),
            pltpu.SemaphoreType.DMA,
        ],
        compiler_params=pltpu.CompilerParams(vmem_limit_bytes=VMEM_BYTES),
        cost_estimate=pl.CostEstimate(
            flops=tile_rows * total * point_total * BLK * width,
            bytes_accessed=2 * (tile_rows * queries[0].size + key_tiles * keys[0].size),
            transcendentals=tile_rows * total * point_total * BLK // 4,
        ),
        name="match",
    )(at, *queries, *keys, edges)


def combine_kernel(parts_ref, place_ref, out_ref):
    parts = parts_ref.shape[0]
    rows = place_ref.shape[0] // 2
    tops = [parts_ref[i, 0:rows, :] for i in range(parts)]
    top = functools.reduce(jnp.maximum, tops)
    total = x = y = jnp.zeros_like(top)
    for i in range(parts):
        gain = jnp.exp2(tops[i] - top)
        total += gain * parts_ref[i, rows : 2 * rows, :]
        x += gain * parts_ref[i, 2 * rows : 3 * rows, :]
        y += gain * parts_ref[i, 3 * rows : 4 * rows, :]
    pull = jnp.concatenate([x / total, y / total], axis=0) - place_ref[...].astype(jnp.float32)
    for i in range(out_ref.shape[0]):
        out_ref[i] = pull


def combine(parts, place, copies):
    return pl.pallas_call(
        combine_kernel,
        out_shape=jax.ShapeDtypeStruct((copies,) + place.shape, jnp.float32),
        in_specs=in_vmem(2),
        out_specs=pl.BlockSpec(memory_space=pltpu.VMEM),
        compiler_params=pltpu.CompilerParams(vmem_limit_bytes=VMEM_BYTES),
        name="combine",
    )(parts, place)


def one_hot(at, length, limits):
    count = at.shape[1]
    parts, done = [], 0
    for low, high in limits:
        spot = lax.broadcasted_iota(jnp.int32, (high - low, count), 0) + low
        if low > done:
            parts.append(jnp.zeros((low - done, count), jnp.bfloat16))
        parts.append(jnp.where(spot == at, 1.0, 0.0).astype(jnp.bfloat16))
        done = high
    if length > done:
        parts.append(jnp.zeros((length - done, count), jnp.bfloat16))
    return jnp.concatenate(parts, axis=0)


def flat(value):
    return jnp.concatenate([value[i : i + 1, :] for i in range(value.shape[0])], axis=1)


def hits(side, halo, tall, wide, row, col):
    up = lambda n: -(-n // 16) * 16
    limits = ((0, up(side + halo)), (wide - up(halo), wide))
    return one_hot(flat(row), tall, ((0, tall),)), one_hot(flat(col), wide, limits)


def spots_kernel(
    side, halo, key_tiles, at_ref, parts_ref, rounds_ref, spot_ref, count_ref, hit_buf
):
    shares, tile_rows, _, _ = parts_ref.shape
    rows = hit_buf.shape[2] // shares
    tall, wide = count_ref.shape

    def folded(at, length):
        return jnp.where(
            (at >= 0) & (at < side + halo), at, jnp.where((at < 0) & (at >= -halo), at + length, -1)
        )

    number = jnp.zeros(hit_buf.shape[2:], jnp.int32)
    tiles = [(i, j) for i in range(tile_rows) for j in range(key_tiles)]
    for at, (i, j) in enumerate(tiles):
        ids = jnp.concatenate(
            [parts_ref[k, i, pl.ds((4 + j) * rows, rows), :] for k in range(shares)], axis=0
        ).astype(jnp.int32)
        tile_of = lax.div(ids, side * side)
        within = lax.rem(ids, side * side)
        row = lax.div(tile_of, key_tiles) * side + lax.div(within, side) - at_ref[0]
        col = lax.rem(tile_of, key_tiles) * side + lax.rem(within, side) - at_ref[1]
        row, col = folded(row, side + 2 * halo), folded(col, wide)
        here = (row >= 0) & (col >= 0)
        hit_buf[0, at] = jnp.where(here, number, -1)
        hit_buf[1, at] = row
        hit_buf[2, at] = col
        number = number + here.astype(jnp.int32)
    rounds = jnp.max(number)
    rounds_ref[0] = rounds
    count_ref[...] = jnp.zeros_like(count_ref)

    @pl.loop(0, rounds)
    def _(k):
        tile_of = row = col = jnp.full(number.shape, -1, jnp.int32)
        for at, (i, j) in enumerate(tiles):
            here = hit_buf[0, at] == k
            tile_of = jnp.where(here, i * key_tiles + at_ref[5 + tile_rows + j], tile_of)
            row = jnp.where(here, hit_buf[1, at], row)
            col = jnp.where(here, hit_buf[2, at], col)
        spot_ref[k, 0] = tile_of
        spot_ref[k, 1] = row
        spot_ref[k, 2] = col
        row_hit, col_hit = hits(side, halo, tall, wide, row, col)
        count_ref[...] += nt_dot(row_hit, col_hit)


def spots(side, halo, key_tiles, wide, at, parts, rows):
    tall = -(-(side + 2 * halo) // 16) * 16
    points = (parts.shape[0] * rows, LANES)
    tiles = parts.shape[1] * key_tiles
    return pl.pallas_call(
        functools.partial(spots_kernel, side, halo, key_tiles),
        out_shape=(
            jax.ShapeDtypeStruct((1,), jnp.int32),
            jax.ShapeDtypeStruct((tiles, 3) + points, jnp.int32),
            jax.ShapeDtypeStruct((tall, wide), jnp.float32),
        ),
        in_specs=[in_smem()] + in_vmem(1),
        out_specs=(in_smem(),) + (pl.BlockSpec(memory_space=pltpu.VMEM),) * 2,
        scratch_shapes=[pltpu.VMEM((3, tiles) + points, jnp.int32)],
        compiler_params=pltpu.CompilerParams(vmem_limit_bytes=VMEM_BYTES),
        cost_estimate=pl.CostEstimate(
            flops=10 * tall * points[0] * LANES * wide,
            bytes_accessed=8 * parts.size,
            transcendentals=0,
        ),
        name="spots",
    )(at, parts)


def vertex_sums(side, halo, rounds_ref, spot_ref, points_ref, sum_ref):
    _, tall, wide = sum_ref.shape
    shares, tiles, both_rows, _ = points_ref.shape
    rows = both_rows // 2
    sum_ref[...] = jnp.zeros_like(sum_ref)

    @pl.loop(0, rounds_ref[0])
    def _(k):
        tile_of = spot_ref[k, 0]
        x = y = jnp.zeros(tile_of.shape, jnp.float32)
        for tile in range(tiles):
            here = tile_of == tile
            values = [points_ref[share, tile] for share in range(shares)]
            x = jnp.where(here, jnp.concatenate([v[:rows] for v in values], axis=0), x)
            y = jnp.where(here, jnp.concatenate([v[rows:] for v in values], axis=0), y)
        row_hit, col_hit = hits(side, halo, tall, wide, spot_ref[k, 1], spot_ref[k, 2])
        parts = []
        for value in (flat(x), flat(y)):
            high = value.astype(jnp.bfloat16)
            low = (value - high.astype(jnp.float32)).astype(jnp.bfloat16)
            parts += [row_hit * high, row_hit * low]
        summed = nt_dot(jnp.concatenate(parts, axis=0), col_hit)
        sum_ref[0] += summed[0:tall] + summed[tall : 2 * tall]
        sum_ref[1] += summed[2 * tall : 3 * tall] + summed[3 * tall :]


def sums_kernel(side, halo, rounds_ref, spot_ref, points_ref, out_ref, sum_ref):
    vertex_sums(side, halo, rounds_ref, spot_ref, points_ref, sum_ref)
    out_ref[...] = sum_ref[:, pl.ds(0, out_ref.shape[1]), :]


def relax_kernel(
    side,
    halo,
    extent,
    at_ref,
    rounds_ref,
    spot_ref,
    count_ref,
    points_ref,
    mesh_ref,
    out_ref,
    sum_ref,
):
    vertex_sums(side, halo, rounds_ref, spot_ref, points_ref, sum_ref)
    span = side + 2 * halo
    wide = sum_ref.shape[2]
    shape = (span, wide)
    row = lax.broadcasted_iota(jnp.int32, shape, 0)
    col = lax.broadcasted_iota(jnp.int32, shape, 1)
    row = jnp.where(row < side + halo, row, row - span) + at_ref[0]
    col = jnp.where(col < side + halo, col, col - wide) + at_ref[1]
    inside = (row >= 0) & (row < extent[0]) & (col >= 0) & (col < extent[1])
    own_pulled = (at_ref[2] == 0).astype(jnp.float32)
    linked = 1.0
    matched = count_ref[pl.ds(0, span), :]
    moving, gains, has, step = [], [], [], []
    for part, pulled in enumerate((own_pulled, 1.0 - own_pulled)):
        gain = mesh_ref[part * 3 + 2]
        diagonal = 4.0 * gain + spring_sec * linked + spring_match * matched * pulled
        gains.append(gain)
        has.append(matched * pulled)
        step.append(jnp.where(inside, relax_rate / diagonal, 0.0))
        moving.append(
            [(mesh_ref[part * 3 + c], sum_ref[c, pl.ds(0, span), :] * pulled) for c in range(2)]
        )
    for sweep in range(ITERS):
        later = []
        for part in range(2):
            row_of = []
            for c in range(2):
                u, pulled = moving[part][c]
                other = moving[1 - part][c][0]
                laplace = (
                    pltpu.roll(u, 1, 0)
                    + pltpu.roll(u, span - 1, 0)
                    + pltpu.roll(u, 1, 1)
                    + pltpu.roll(u, wide - 1, 1)
                    - 4.0 * u
                )
                force = (
                    gains[part] * laplace
                    + spring_sec * (other - linked * u)
                    + spring_match * (pulled - has[part] * u)
                )
                row_of.append((u + step[part] * force, pulled))
            later.append(row_of)
        moving = later
    for c in range(2):
        out_ref[c] = moving[0][c][0][0:side, 0:side]


def col_edges(value, halo):
    after = passed_along(value[:, :, :halo].swapaxes(1, 2), "tx", -1)
    before = passed_along(value[:, :, value.shape[2] - halo :].swapaxes(1, 2), "tx", 1)
    return jnp.concatenate([after, before], axis=1)


def sweeps(moving, gains, sums, number, at, side, halo, extent):
    sections = lax.axis_size("sec")
    sec_index = at[2]
    has_next = (sec_index < sections - 1).astype(jnp.float32)
    linked = (sec_index > 0).astype(jnp.float32) + has_next
    pulled, matched = sums * has_next, number * has_next
    span, wide = moving.shape[1:]
    row = jnp.arange(span)[:, None]
    col = jnp.arange(wide)[None, :]
    row = jnp.where(row < side + halo, row, row - span) + at[0]
    col = jnp.where(col < side + halo, col, col - wide) + at[1]
    inside = (row >= 0) & (row < extent[0]) & (col >= 0) & (col < extent[1])
    diagonal = 4.0 * gains + spring_sec * linked + spring_match * matched
    step = jnp.where(inside, relax_rate / jnp.where(inside, diagonal, 1.0), 0.0)
    for sweep in range(ITERS):
        lower_sec = passed_along(moving, "sec", 1)
        upper_sec = passed_along(moving, "sec", -1)
        laplace = (
            jnp.roll(moving, 1, 1)
            + jnp.roll(moving, -1, 1)
            + jnp.roll(moving, 1, 2)
            + jnp.roll(moving, -1, 2)
            - 4.0 * moving
        )
        force = (
            gains * laplace
            + spring_sec * (lower_sec + upper_sec - linked * moving)
            + spring_match * (pulled - matched * moving)
        )
        moving = moving + step * force
    return moving[:, :side, :side]


def pack_kernel(
    shares,
    tile_cols,
    desc_hbm,
    place_hbm,
    ids_hbm,
    list_hbm,
    count_hbm,
    first_ref,
    second_ref,
    place_ref,
    ids_ref,
    list_ref,
    count_ref,
    sems,
):
    half = second_ref.shape[0]
    copies = [
        pltpu.make_async_copy(source, target, sems.at[i])
        for i, (source, target) in enumerate(
            (
                (place_hbm, place_ref),
                (ids_hbm, ids_ref),
                (list_hbm, list_ref),
                (count_hbm, count_ref),
                (desc_hbm.at[pl.ds(0, half), :], first_ref.at[pl.ds(0, half), :]),
                (desc_hbm.at[pl.ds(half, half), :], second_ref),
            )
        )
    ]
    for copy in copies:
        copy.start()
    for copy in copies[:4]:
        copy.wait()

    def cut(row):
        return [row[:, i : i + LANES] for i in range(0, row.shape[1], LANES)]

    place, ids, blocks = place_ref[...].astype(jnp.float32), ids_ref[...], list_ref[...]
    rows = cut(place[0:1]) + cut(place[1:2])
    for i in range(DIGITS):
        digit = lax.rem(lax.div(ids, BASE**i), BASE)
        rows += cut(digit.astype(jnp.float32))
    per_tile = place.shape[1] // BLK
    part = per_tile // shares
    tile, within = lax.div(blocks, per_tile), lax.rem(blocks, per_tile)
    device = lax.div(tile, tile_cols) * shares + lax.div(within, part)
    spot = lax.rem(tile, tile_cols) * part + lax.rem(within, part)
    live = lax.broadcasted_iota(jnp.int32, blocks.shape, 1) < count_ref[0, 0]
    device = jnp.where(live, device, BASE - 1)
    count = first_ref.shape[0] - half
    gap = jnp.zeros((count - len(rows) - PLACE_ROWS, LANES), jnp.float32)
    end = jnp.zeros((PLACE_ROWS - 2, LANES), jnp.float32)
    rows += ([gap] if gap.shape[0] else []) + [v.astype(jnp.float32) for v in (device, spot)] + [end]
    first_ref[pl.ds(half, count), :] = jnp.concatenate(rows, axis=0).astype(jnp.bfloat16)
    for copy in copies[4:]:
        copy.wait()


def pack(desc, place, ids, blocks, count, shares, tile_cols):
    points, width = desc.shape
    half = points // 2
    rows = -(-(2 + DIGITS) * (points // LANES) // 16) * 16 + PLACE_ROWS
    return pl.pallas_call(
        functools.partial(pack_kernel, shares, tile_cols),
        out_shape=(
            jax.ShapeDtypeStruct((half + rows, width), jnp.bfloat16),
            jax.ShapeDtypeStruct((half, width), jnp.bfloat16),
        ),
        in_specs=[pl.BlockSpec(memory_space=pl.ANY)] * 5,
        out_specs=(pl.BlockSpec(memory_space=pltpu.VMEM),) * 2,
        scratch_shapes=[
            pltpu.VMEM(place.shape, place.dtype),
            pltpu.VMEM(ids.shape, ids.dtype),
            pltpu.VMEM(blocks.shape, blocks.dtype),
            pltpu.SMEM(count.shape, count.dtype),
            pltpu.SemaphoreType.DMA((6,)),
        ],
        compiler_params=pltpu.CompilerParams(vmem_limit_bytes=VMEM_BYTES),
        name="pack",
    )(desc, place, ids, blocks, count)


def turns(axis):
    devices, here = lax.axis_size(axis), lax.axis_index(axis)
    if devices & (devices - 1):
        pairs = [[(i, (i + j) % devices) for i in range(devices)] for j in range(1, devices)]
        return pairs, jnp.mod(here - jnp.arange(devices), devices)
    pairs = [[(i, i ^ j) for i in range(devices)] for j in range(1, devices)]
    return pairs, here ^ jnp.arange(devices)


def gathered(value, axis):
    return [value] + [lax.ppermute(value, axis, pairs) for pairs in turns(axis)[0]]


def handed_on(value, axis):
    devices = lax.axis_size(axis)
    if devices & (devices - 1):
        return gathered(value, axis)
    held = {0: value}
    for at in sorted(range(1, devices), key=lambda at: (at.bit_count(), -at)):
        by = at & -at
        held[at] = lax.ppermute(held[at ^ by], axis, [(i, i ^ by) for i in range(devices)])
    return [held[i] for i in range(devices)]


def per_device(
    descriptors, positions, vertex_ids, candidate_blocks, candidate_count, displacement, stiffness
):
    point_total, width = descriptors.shape[3:]
    per_tile = point_total // BLK
    tile_rows, tile_cols = lax.axis_size("ty"), lax.axis_size("tx")
    sections = lax.axis_size("sec")
    sec_index = lax.axis_index("sec")
    tiles = tile_rows * tile_cols
    side = displacement.shape[3]
    halo = ITERS
    span = side + 2 * halo
    wide = -(-span // LANES) * LANES
    cand = candidate_blocks.shape[3]
    shares = 2 if sections == 2 and per_tile % 2 == 0 else 1
    part = per_tile // shares
    key_rows = part * BLK

    first_half, second_half = pack(
        descriptors[0, 0, 0],
        positions[0, 0, 0],
        vertex_ids[0, 0],
        jnp.pad(candidate_blocks[0, 0], ((0, 0), (0, LANES - cand))),
        candidate_count[0, 0][None],
        shares,
        tile_cols,
    )
    half = point_total // 2
    swap = [(i, 1 - i) for i in range(2)]

    def of_share(rows):
        rows = rows.reshape(-1, shares, part, LANES)
        if shares == 2:
            rows = jnp.where(sec_index == 0, rows[:, 0], rows[:, 1])
        return rows.reshape(-1, LANES)

    place_rows = slice(half, half + 2 * per_tile)
    id_rows = slice(half + 2 * per_tile, half + (2 + DIGITS) * per_tile)
    if shares == 2:
        first = sec_index == 0
        share = sec_index
        other = lax.ppermute(first_half, "sec", swap)
        came = passed_along(second_half, "sec", 1)
        query = jnp.where(first, first_half, other)
        key = jnp.where(first, other[:half], second_half)
        key_place = jnp.where(first, other[place_rows], first_half[place_rows])
        rest = jnp.where(first, second_half, came)
    else:
        share = 0
        query, rest = (passed_along(v, "sec", 1) for v in (first_half, second_half))
        key = jnp.concatenate([first_half[:half], second_half], axis=0)
        key_place = first_half[place_rows]
    place, ids = of_share(query[place_rows]), of_share(query[id_rows])
    filler = jnp.zeros((-(2 + DIGITS) * part % 16, LANES), jnp.bfloat16)
    key = jnp.concatenate([key, of_share(key_place), ids, filler], axis=0)
    query = jnp.concatenate([query[:half], rest, query[-PLACE_ROWS:]], axis=0)
    keys = gathered(key, "tx")
    queries = handed_on(query, "ty")
    at = jnp.concatenate(
        [
            jnp.stack([lax.axis_index("ty") * side, lax.axis_index("tx") * side, sec_index]),
            jnp.stack([lax.axis_index("ty"), jnp.asarray(share)]),
            turns("ty")[1],
            turns("tx")[1],
        ]
    ).astype(jnp.int32)
    extent = (side * tile_rows, side * tile_cols)
    sum_shape = pltpu.VMEM((2, -(-span // 16) * 16, wide), jnp.float32)

    own_mesh = jnp.concatenate([displacement[0], stiffness], axis=0)
    cols = col_edges(own_mesh, halo)
    top, end = own_mesh[:, :halo], own_mesh[:, side - halo :]
    corners = [
        jnp.pad(v.swapaxes(1, 2), ((0, 0), (0, 0), (0, side - 2 * halo)))
        for v in (cols[:, :, :halo], cols[:, :, side - halo :])
    ]
    edges = jnp.stack([jnp.concatenate(v, axis=0) for v in ((top, corners[0]), (end, corners[1]))])
    edges = edges.reshape(2, -1, LANES)
    meshes = [jnp.concatenate([own_mesh, cols], axis=1)]
    if shares == 2:
        tied, queries[1] = lax.optimization_barrier((meshes[0], queries[1]))
        meshes.append(lax.ppermute(tied, "sec", swap))
    parts = match(at, queries, keys, edges, 16.0 / width, shares, point_total, part, cand)
    shape = parts.shape
    parts = exchanged(parts.reshape((-1,) + shape[2:]), ("sec", "ty") if shares == 2 else "ty")
    pulls = combine(parts, place, shares * tiles)
    parts, pulls = lax.optimization_barrier((parts, pulls))

    def edge_rows(by):
        near = lax.axis_index("ty") + by
        rows = parts.reshape(shape)[:, :, -edges.shape[1] :]
        rows = lax.dynamic_index_in_dim(rows, jnp.clip(near, 0, tile_rows - 1), 1, keepdims=False)
        rows = jnp.where((near >= 0) & (near < tile_rows), rows, 0.0)
        rows = rows.reshape(shares, 2, 3, halo, side)
        if shares == 2:
            rows = jnp.where(first, rows, rows[::-1])
        rows = rows.reshape(-1, 3, halo, side)
        return [
            jnp.concatenate([rows[2 * i], rows[2 * i + 1, :, :, : 2 * halo]], axis=2)
            for i in range(shares)
        ]

    after, before = edge_rows(1), edge_rows(-1)
    framed = []
    for i, mesh in enumerate(meshes):
        sides = mesh[:, side:].swapaxes(1, 2)
        whole = jnp.concatenate([mesh[:, :side], sides], axis=2)
        framed.append(jnp.concatenate([whole, after[i], before[i]], axis=1))
    framed = jnp.concatenate(framed, axis=0)
    gap = jnp.zeros(framed.shape[:2] + (wide - span,), framed.dtype)
    mesh_values = jnp.concatenate(
        [framed[:, :, : side + halo], gap, framed[:, :, side + halo :]], axis=2
    )
    if shares == 2:
        points = exchanged(pulls, ("sec", "ty", "tx"))
        rounds, spot, number = spots(side, halo, tile_cols, wide, at, parts.reshape(shape), part)
        relaxed = pl.pallas_call(
            functools.partial(relax_kernel, side, halo, extent),
            out_shape=jax.ShapeDtypeStruct((2, side, side), jnp.float32),
            in_specs=[in_smem()] * 2 + in_vmem(4),
            out_specs=pl.BlockSpec(memory_space=pltpu.VMEM),
            scratch_shapes=[sum_shape],
            compiler_params=pltpu.CompilerParams(vmem_limit_bytes=VMEM_BYTES),
            name="relax",
        )(at, rounds, spot, number, points.reshape(2, tiles, -1, LANES), mesh_values)
        return relaxed[None]

    points = passed_along(exchanged(pulls, ("ty", "tx")), "sec", -1)
    parts = passed_along(parts, "sec", -1)
    rounds, spot, number = spots(side, halo, tile_cols, wide, at, parts[None], part)
    sums = pl.pallas_call(
        functools.partial(sums_kernel, side, halo),
        out_shape=jax.ShapeDtypeStruct((2, span, wide), jnp.float32),
        in_specs=[in_smem()] + in_vmem(2),
        out_specs=pl.BlockSpec(memory_space=pltpu.VMEM),
        scratch_shapes=[sum_shape],
        compiler_params=pltpu.CompilerParams(vmem_limit_bytes=VMEM_BYTES),
        name="sums",
    )(rounds, spot, points[None])
    moving, gains = mesh_values[0:2], mesh_values[2]
    return sweeps(moving, gains, sums, number[:span], at, side, halo, extent)[None]


def solution(mesh):
    in_specs = (
        P("sec", "ty", "tx", None, None),
        P("sec", "ty", "tx", None, None),
        P("sec", "ty", "tx", None),
        P("sec", "ty", "tx", None),
        P("sec", "ty", "tx"),
        P("sec", None, "ty", "tx"),
        P("sec", "ty", "tx"),
    )
    out_specs = P("sec", None, "ty", "tx")
    return jax.shard_map(
        per_device, mesh=mesh, in_specs=in_specs, out_specs=out_specs, check_vma=False
    )
```

```python
import functools
import math

import jax
import jax.numpy as jnp
from jax import lax
from jax.experimental import pallas as pl
from jax.experimental.pallas import tpu as pltpu
from jax.sharding import PartitionSpec as P

BLK = 128
ITERS = 4
LANES = 128
PLACE_ROWS = 16
GROUP = 2
BASE = 256
DIGITS = 3
VMEM_BYTES = 24 * 1024 * 1024

spring_sec = 0.5
spring_match = 1.0
relax_rate = 0.8


def passed_along(value, axis, by):
    devices = lax.axis_size(axis)
    pairs = [(i, i + by) for i in range(devices) if 0 <= i + by < devices]
    return lax.ppermute(value, axis, pairs)


def exchanged(value, axes):
    return lax.all_to_all(value, axes, split_axis=0, concat_axis=0, tiled=True)


def spread(value, axes):
    copies = jnp.broadcast_to(value[None], (lax.axis_size(axes),) + value.shape)
    return exchanged(copies, axes)


def nt_dot(a, b):
    return lax.dot_general(a, b, (((1,), (1,)), ((), ())), preferred_element_type=jnp.float32)


def in_vmem(count):
    return [pl.BlockSpec(memory_space=pltpu.VMEM)] * count


def in_smem():
    return pl.BlockSpec(memory_space=pltpu.SMEM)


def match_kernel(scale, tile_rows, key_tiles, cand, at_ref, *refs):
    query_refs, key_refs = refs[:tile_rows], refs[tile_rows : tile_rows + key_tiles]
    (edge_ref, out_ref, query_buf, key_buf, place_buf, state_buf, found_buf, work_ref, list_buf, sem) = (
        refs[tile_rows + key_tiles :]
    )
    shares = out_ref.shape[0]
    point_total = state_buf.shape[2]
    rows = point_total // LANES // shares
    key_rows = key_buf.shape[1]
    part = key_rows // BLK
    total = key_tiles * part
    own_row, share = at_ref[3], at_ref[4]

    for tile, query_ref in enumerate(query_refs):
        last = query_ref[pl.ds(point_total, PLACE_ROWS), :].astype(jnp.float32).astype(jnp.int32)
        here = last[0:1] == own_row * shares + share
        found_buf[pl.ds(tile, 1), :] = jnp.where(here, last[1:2], -1)
    found = pltpu.make_async_copy(found_buf, work_ref, sem)
    found.start()

    row_at = lax.broadcasted_iota(jnp.int32, (PLACE_ROWS, LANES), 0)
    ids = []
    for tile, key_ref in enumerate(key_refs):
        col = at_ref[5 + tile_rows + tile]
        key_buf[col] = key_ref[pl.ds(0, key_rows), :]
        rest = key_ref[pl.ds(key_rows, key_ref.shape[0] - key_rows), :].astype(jnp.float32)
        for j in range(part):
            x, y = rest[j : j + 1, :], rest[part + j : part + j + 1, :]
            stacked = jnp.where(
                row_at == 0, x, jnp.where(row_at == 1, y, jnp.where(row_at == 2, 1.0, 0.0))
            )
            place_buf[col * part + j] = stacked.astype(jnp.bfloat16)
        digits = [rest[2 * part + i * rows : 2 * part + (i + 1) * rows] for i in range(DIGITS)]
        ids.append(sum(digit * float(BASE**i) for i, digit in enumerate(digits)))

    for tile, query_ref in enumerate(query_refs):
        query_buf[tile] = query_ref[pl.ds(0, point_total), :]
    found.wait()

    number = 0
    for tile in range(tile_rows):
        for i in range(cand):
            place = work_ref[tile, i]
            list_buf[number] = tile * total + place
            number = number + jnp.where(place >= 0, 1, 0)
        list_buf[number] = -1
        number = number + lax.rem(number, 2)
    for i in range(2 * GROUP):
        list_buf[number + i] = -1
    groups = lax.div(number + 2 * GROUP - 1, 2 * GROUP)

    state_row = lax.broadcasted_iota(jnp.int32, state_buf.shape[1:], 0)
    for tile in range(tile_rows):
        state_buf[tile] = jnp.where(state_row == 3, -1e30, 0.0)

    def item(at):
        codes = [list_buf[2 * at + i] for i in range(2)]
        tile = lax.div(jnp.maximum(codes[0], 0), total)
        keys, places = [], []
        for code in codes:
            block = lax.rem(jnp.maximum(code, 0), total)
            start = pl.multiple_of(lax.rem(block, part) * BLK, BLK)
            keys.append(key_buf[lax.div(block, part), pl.ds(start, BLK), :])
            kept = jnp.where(code >= 0, 1.0, 0.0).astype(jnp.bfloat16)
            places.append(place_buf[block] * kept)
        return tile, codes[0] >= 0, jnp.concatenate(keys, axis=0), jnp.concatenate(places, axis=1)

    @pl.loop(0, groups)
    def _(group):
        items = [item(group * GROUP + i) for i in range(GROUP)]
        scores = [
            nt_dot(keys, query_buf[tile]) * scale
            for tile, _, keys, _ in items
        ]
        tops = [jnp.max(score, axis=0, keepdims=True) for score in scores]
        weights = [jnp.exp2(s - top).astype(jnp.bfloat16) for s, top in zip(scores, tops)]
        sums = [
            jnp.dot(place, weight, preferred_element_type=jnp.float32)[0:8]
            for (_, _, _, place), weight in zip(items, weights)
        ]
        for (tile, live, _, _), top, added in zip(items, tops, sums):
            top = jnp.where(live, top, -1e30)
            state = state_buf[tile]
            before = state[3:4, :]
            both = jnp.maximum(before, top)
            state = state * jnp.exp2(before - both) + added * jnp.exp2(top - both)
            state_buf[tile] = jnp.where(state_row == 3, both, state)

    edge_rows = edge_ref.shape[1]
    for tile in range(tile_rows):
        to = at_ref[5 + tile]
        for row in range(shares * rows):
            lanes = pl.ds(row * LANES, LANES)
            for place, held in enumerate((3, 2, 0, 1)):
                out_ref[row // rows, to, pl.ds(place * rows + row % rows, 1), :] = state_buf[
                    tile, pl.ds(held, 1), lanes
                ]
        for share in range(shares):
            out_ref[share, tile, pl.ds(4 * rows, key_tiles * rows), :] = jnp.concatenate(ids, axis=0)
            out_ref[share, tile, pl.ds((4 + key_tiles) * rows, edge_rows), :] = jnp.where(
                tile > own_row, edge_ref[1], jnp.where(tile < own_row, edge_ref[0], edge_ref[2])
            )


def match(at, queries, keys, edges, score_factor, shares, point_total, part, cand):
    tile_rows, key_tiles = len(queries), len(keys)
    width = queries[0].shape[1]
    rows = point_total // LANES // shares
    total = key_tiles * part
    return pl.pallas_call(
        functools.partial(
            match_kernel, score_factor * math.log2(math.e), tile_rows, key_tiles, cand
        ),
        out_shape=jax.ShapeDtypeStruct(
            (shares, tile_rows, (4 + key_tiles) * rows + edges.shape[1], LANES), jnp.float32
        ),
        in_specs=[in_smem()] + in_vmem(tile_rows + key_tiles + 1),
        out_specs=pl.BlockSpec(memory_space=pltpu.VMEM),
        scratch_shapes=[
            pltpu.VMEM((tile_rows, point_total, width), jnp.bfloat16),
            pltpu.VMEM((key_tiles, part * BLK, width), jnp.bfloat16),
            pltpu.VMEM((total, PLACE_ROWS, LANES), jnp.bfloat16),
            pltpu.VMEM((tile_rows, 8, point_total), jnp.float32),
            pltpu.VMEM((tile_rows, LANES), jnp.int32),
            pltpu.SMEM((tile_rows, LANES), jnp.int32),
            pltpu.SMEM((tile_rows * (cand + 1) + 2 * GROUP + 1,), jnp.int32),
            pltpu.SemaphoreType.DMA,
        ],
        compiler_params=pltpu.CompilerParams(vmem_limit_bytes=VMEM_BYTES),
        cost_estimate=pl.CostEstimate(
            flops=tile_rows * total * point_total * BLK * width,
            bytes_accessed=2 * (tile_rows * queries[0].size + key_tiles * keys[0].size),
            transcendentals=tile_rows * total * point_total * BLK // 4,
        ),
        name="match",
    )(at, *queries, *keys, edges)


def combine_kernel(parts_ref, place_ref, out_ref):
    parts = parts_ref.shape[0]
    rows = place_ref.shape[0] // 2
    tops = [parts_ref[i, 0:rows, :] for i in range(parts)]
    top = functools.reduce(jnp.maximum, tops)
    total = x = y = jnp.zeros_like(top)
    for i in range(parts):
        gain = jnp.exp2(tops[i] - top)
        total += gain * parts_ref[i, rows : 2 * rows, :]
        x += gain * parts_ref[i, 2 * rows : 3 * rows, :]
        y += gain * parts_ref[i, 3 * rows : 4 * rows, :]
    pull = jnp.concatenate([x / total, y / total], axis=0) - place_ref[...]
    for i in range(out_ref.shape[0]):
        out_ref[i] = pull


def combine(parts, place, copies):
    return pl.pallas_call(
        combine_kernel,
        out_shape=jax.ShapeDtypeStruct((copies,) + place.shape, jnp.float32),
        in_specs=in_vmem(2),
        out_specs=pl.BlockSpec(memory_space=pltpu.VMEM),
        compiler_params=pltpu.CompilerParams(vmem_limit_bytes=VMEM_BYTES),
        name="combine",
    )(parts, place)


def one_hot(at, length, limits):
    count = at.shape[1]
    parts, done = [], 0
    for low, high in limits:
        spot = lax.broadcasted_iota(jnp.int32, (high - low, count), 0) + low
        if low > done:
            parts.append(jnp.zeros((low - done, count), jnp.bfloat16))
        parts.append(jnp.where(spot == at, 1.0, 0.0).astype(jnp.bfloat16))
        done = high
    if length > done:
        parts.append(jnp.zeros((length - done, count), jnp.bfloat16))
    return jnp.concatenate(parts, axis=0)


def flat(value):
    return jnp.concatenate([value[i : i + 1, :] for i in range(value.shape[0])], axis=1)


def hits(side, halo, tall, wide, row, col):
    up = lambda n: -(-n // 16) * 16
    limits = ((0, up(side + halo)), (wide - up(halo), wide))
    return one_hot(flat(row), tall, ((0, tall),)), one_hot(flat(col), wide, limits)


def spots_kernel(
    side, halo, key_tiles, at_ref, parts_ref, rounds_ref, spot_ref, count_ref, hit_buf
):
    shares, tile_rows, _, _ = parts_ref.shape
    rows = hit_buf.shape[2] // shares
    tall, wide = count_ref.shape

    def folded(at, length):
        return jnp.where(
            (at >= 0) & (at < side + halo), at, jnp.where((at < 0) & (at >= -halo), at + length, -1)
        )

    number = jnp.zeros(hit_buf.shape[2:], jnp.int32)
    tiles = [(i, j) for i in range(tile_rows) for j in range(key_tiles)]
    for at, (i, j) in enumerate(tiles):
        ids = jnp.concatenate(
            [parts_ref[k, i, pl.ds((4 + j) * rows, rows), :] for k in range(shares)], axis=0
        ).astype(jnp.int32)
        tile_of = lax.div(ids, side * side)
        within = lax.rem(ids, side * side)
        row = lax.div(tile_of, key_tiles) * side + lax.div(within, side) - at_ref[0]
        col = lax.rem(tile_of, key_tiles) * side + lax.rem(within, side) - at_ref[1]
        row, col = folded(row, side + 2 * halo), folded(col, wide)
        here = (row >= 0) & (col >= 0)
        hit_buf[0, at] = jnp.where(here, number, -1)
        hit_buf[1, at] = row
        hit_buf[2, at] = col
        number = number + here.astype(jnp.int32)
    rounds = jnp.max(number)
    rounds_ref[0] = rounds
    count_ref[...] = jnp.zeros_like(count_ref)

    @pl.loop(0, rounds)
    def _(k):
        tile_of = row = col = jnp.full(number.shape, -1, jnp.int32)
        for at, (i, j) in enumerate(tiles):
            here = hit_buf[0, at] == k
            tile_of = jnp.where(here, i * key_tiles + at_ref[5 + tile_rows + j], tile_of)
            row = jnp.where(here, hit_buf[1, at], row)
            col = jnp.where(here, hit_buf[2, at], col)
        spot_ref[k, 0] = tile_of
        spot_ref[k, 1] = row
        spot_ref[k, 2] = col
        row_hit, col_hit = hits(side, halo, tall, wide, row, col)
        count_ref[...] += nt_dot(row_hit, col_hit)


def spots(side, halo, key_tiles, wide, at, parts, rows):
    tall = -(-(side + 2 * halo) // 16) * 16
    points = (parts.shape[0] * rows, LANES)
    tiles = parts.shape[1] * key_tiles
    return pl.pallas_call(
        functools.partial(spots_kernel, side, halo, key_tiles),
        out_shape=(
            jax.ShapeDtypeStruct((1,), jnp.int32),
            jax.ShapeDtypeStruct((tiles, 3) + points, jnp.int32),
            jax.ShapeDtypeStruct((tall, wide), jnp.float32),
        ),
        in_specs=[in_smem()] + in_vmem(1),
        out_specs=(in_smem(),) + (pl.BlockSpec(memory_space=pltpu.VMEM),) * 2,
        scratch_shapes=[pltpu.VMEM((3, tiles) + points, jnp.int32)],
        compiler_params=pltpu.CompilerParams(vmem_limit_bytes=VMEM_BYTES),
        cost_estimate=pl.CostEstimate(
            flops=10 * tall * points[0] * LANES * wide,
            bytes_accessed=8 * parts.size,
            transcendentals=0,
        ),
        name="spots",
    )(at, parts)


def vertex_sums(side, halo, rounds_ref, spot_ref, points_ref, sum_ref):
    _, tall, wide = sum_ref.shape
    shares, tiles, both_rows, _ = points_ref.shape
    rows = both_rows // 2
    sum_ref[...] = jnp.zeros_like(sum_ref)

    @pl.loop(0, rounds_ref[0])
    def _(k):
        tile_of = spot_ref[k, 0]
        x = y = jnp.zeros(tile_of.shape, jnp.float32)
        for tile in range(tiles):
            here = tile_of == tile
            values = [points_ref[share, tile] for share in range(shares)]
            x = jnp.where(here, jnp.concatenate([v[:rows] for v in values], axis=0), x)
            y = jnp.where(here, jnp.concatenate([v[rows:] for v in values], axis=0), y)
        row_hit, col_hit = hits(side, halo, tall, wide, spot_ref[k, 1], spot_ref[k, 2])
        parts = []
        for value in (flat(x), flat(y)):
            high = value.astype(jnp.bfloat16)
            low = (value - high.astype(jnp.float32)).astype(jnp.bfloat16)
            parts += [row_hit * high, row_hit * low]
        summed = nt_dot(jnp.concatenate(parts, axis=0), col_hit)
        sum_ref[0] += summed[0:tall] + summed[tall : 2 * tall]
        sum_ref[1] += summed[2 * tall : 3 * tall] + summed[3 * tall :]


def sums_kernel(side, halo, rounds_ref, spot_ref, points_ref, out_ref, sum_ref):
    vertex_sums(side, halo, rounds_ref, spot_ref, points_ref, sum_ref)
    out_ref[...] = sum_ref[:, pl.ds(0, out_ref.shape[1]), :]


def relax_kernel(
    side,
    halo,
    extent,
    at_ref,
    rounds_ref,
    spot_ref,
    count_ref,
    points_ref,
    mesh_ref,
    out_ref,
    sum_ref,
):
    vertex_sums(side, halo, rounds_ref, spot_ref, points_ref, sum_ref)
    span = side + 2 * halo
    wide = sum_ref.shape[2]
    shape = (span, wide)
    row = lax.broadcasted_iota(jnp.int32, shape, 0)
    col = lax.broadcasted_iota(jnp.int32, shape, 1)
    row = jnp.where(row < side + halo, row, row - span) + at_ref[0]
    col = jnp.where(col < side + halo, col, col - wide) + at_ref[1]
    inside = (row >= 0) & (row < extent[0]) & (col >= 0) & (col < extent[1])
    own_pulled = (at_ref[2] == 0).astype(jnp.float32)
    linked = 1.0
    matched = count_ref[pl.ds(0, span), :]
    moving, gains, has, step = [], [], [], []
    for part, pulled in enumerate((own_pulled, 1.0 - own_pulled)):
        gain = mesh_ref[part * 3 + 2]
        diagonal = 4.0 * gain + spring_sec * linked + spring_match * matched * pulled
        gains.append(gain)
        has.append(matched * pulled)
        step.append(jnp.where(inside, relax_rate / diagonal, 0.0))
        moving.append(
            [(mesh_ref[part * 3 + c], sum_ref[c, pl.ds(0, span), :] * pulled) for c in range(2)]
        )
    for sweep in range(ITERS):
        later = []
        for part in range(2):
            row_of = []
            for c in range(2):
                u, pulled = moving[part][c]
                other = moving[1 - part][c][0]
                laplace = (
                    pltpu.roll(u, 1, 0)
                    + pltpu.roll(u, span - 1, 0)
                    + pltpu.roll(u, 1, 1)
                    + pltpu.roll(u, wide - 1, 1)
                    - 4.0 * u
                )
                force = (
                    gains[part] * laplace
                    + spring_sec * (other - linked * u)
                    + spring_match * (pulled - has[part] * u)
                )
                row_of.append((u + step[part] * force, pulled))
            later.append(row_of)
        moving = later
    for c in range(2):
        out_ref[c] = moving[0][c][0][0:side, 0:side]


def col_edges(value, halo):
    after = passed_along(value[:, :, :halo].swapaxes(1, 2), "tx", -1)
    before = passed_along(value[:, :, value.shape[2] - halo :].swapaxes(1, 2), "tx", 1)
    return jnp.concatenate([after, before], axis=1)


def sweeps(moving, gains, sums, number, at, side, halo, extent):
    sections = lax.axis_size("sec")
    sec_index = at[2]
    has_next = (sec_index < sections - 1).astype(jnp.float32)
    linked = (sec_index > 0).astype(jnp.float32) + has_next
    pulled, matched = sums * has_next, number * has_next
    span, wide = moving.shape[1:]
    row = jnp.arange(span)[:, None]
    col = jnp.arange(wide)[None, :]
    row = jnp.where(row < side + halo, row, row - span) + at[0]
    col = jnp.where(col < side + halo, col, col - wide) + at[1]
    inside = (row >= 0) & (row < extent[0]) & (col >= 0) & (col < extent[1])
    diagonal = 4.0 * gains + spring_sec * linked + spring_match * matched
    step = jnp.where(inside, relax_rate / jnp.where(inside, diagonal, 1.0), 0.0)
    for sweep in range(ITERS):
        lower_sec = passed_along(moving, "sec", 1)
        upper_sec = passed_along(moving, "sec", -1)
        laplace = (
            jnp.roll(moving, 1, 1)
            + jnp.roll(moving, -1, 1)
            + jnp.roll(moving, 1, 2)
            + jnp.roll(moving, -1, 2)
            - 4.0 * moving
        )
        force = (
            gains * laplace
            + spring_sec * (lower_sec + upper_sec - linked * moving)
            + spring_match * (pulled - matched * moving)
        )
        moving = moving + step * force
    return moving[:, :side, :side]


def pack_kernel(
    shares,
    tile_cols,
    desc_hbm,
    place_hbm,
    ids_hbm,
    list_hbm,
    count_hbm,
    first_ref,
    second_ref,
    place_ref,
    ids_ref,
    list_ref,
    count_ref,
    last_ref,
    sems,
):
    half = second_ref.shape[0]
    copies = [
        pltpu.make_async_copy(source, target, sems.at[i])
        for i, (source, target) in enumerate(
            (
                (place_hbm, place_ref),
                (ids_hbm, ids_ref),
                (list_hbm, list_ref),
                (count_hbm, count_ref),
                (desc_hbm.at[pl.ds(0, half), :], first_ref.at[pl.ds(0, half), :]),
                (desc_hbm.at[pl.ds(half, half), :], second_ref),
            )
        )
    ]
    for copy in copies:
        copy.start()
    for copy in copies[:4]:
        copy.wait()

    def cut(row):
        return [row[:, i : i + LANES] for i in range(0, row.shape[1], LANES)]

    place, ids, blocks = place_ref[...].astype(jnp.float32), ids_ref[...], list_ref[...]
    rows = cut(place[0:1]) + cut(place[1:2])
    for i in range(DIGITS):
        digit = lax.rem(lax.div(ids, BASE**i), BASE)
        rows += cut(digit.astype(jnp.float32))
    per_tile = place.shape[1] // BLK
    part = per_tile // shares
    tile, within = lax.div(blocks, per_tile), lax.rem(blocks, per_tile)
    device = lax.div(tile, tile_cols) * shares + lax.div(within, part)
    spot = lax.rem(tile, tile_cols) * part + lax.rem(within, part)
    live = lax.broadcasted_iota(jnp.int32, blocks.shape, 1) < count_ref[0, 0]
    last_ref[...] = jnp.full_like(last_ref, BASE - 1.0)
    last_ref[0:1, 0 : blocks.shape[1]] = jnp.where(live, device, BASE - 1).astype(jnp.float32)
    last_ref[1:2, 0 : blocks.shape[1]] = spot.astype(jnp.float32)
    count = first_ref.shape[0] - half
    gap = jnp.zeros((count - len(rows) - PLACE_ROWS, LANES), jnp.float32)
    rows += ([gap] if gap.shape[0] else []) + [last_ref[...]]
    first_ref[pl.ds(half, count), :] = jnp.concatenate(rows, axis=0).astype(jnp.bfloat16)
    for copy in copies[4:]:
        copy.wait()


def pack(desc, place, ids, blocks, count, shares, tile_cols):
    points, width = desc.shape
    half = points // 2
    rows = -(-(2 + DIGITS) * (points // LANES) // 16) * 16 + PLACE_ROWS
    return pl.pallas_call(
        functools.partial(pack_kernel, shares, tile_cols),
        out_shape=(
            jax.ShapeDtypeStruct((half + rows, width), jnp.bfloat16),
            jax.ShapeDtypeStruct((half, width), jnp.bfloat16),
        ),
        in_specs=[pl.BlockSpec(memory_space=pltpu.HBM)] * 5,
        out_specs=(pl.BlockSpec(memory_space=pltpu.VMEM),) * 2,
        scratch_shapes=[
            pltpu.VMEM(place.shape, place.dtype),
            pltpu.VMEM(ids.shape, ids.dtype),
            pltpu.VMEM(blocks.shape, blocks.dtype),
            pltpu.SMEM(count.shape, count.dtype),
            pltpu.VMEM((PLACE_ROWS, LANES), jnp.float32),
            pltpu.SemaphoreType.DMA((6,)),
        ],
        compiler_params=pltpu.CompilerParams(vmem_limit_bytes=VMEM_BYTES),
        name="pack",
    )(desc, place, ids, blocks, count)


def turns(axis):
    devices, here = lax.axis_size(axis), lax.axis_index(axis)
    if devices & (devices - 1):
        pairs = [[(i, (i + j) % devices) for i in range(devices)] for j in range(1, devices)]
        return pairs, jnp.mod(here - jnp.arange(devices), devices)
    pairs = [[(i, i ^ j) for i in range(devices)] for j in range(1, devices)]
    return pairs, here ^ jnp.arange(devices)


def key_kernel(shares, sec_ref, first_ref, second_ref, other_ref, key_ref, place_ref):
    half = second_ref.shape[0]
    per_tile = 2 * half // LANES
    part = per_tile // shares
    own, other = first_ref, first_ref
    if shares == 2:
        other = other_ref
    at_first = sec_ref[0] == 0

    def rest(ref, share):
        rows = ref[pl.ds(half, (2 + DIGITS) * per_tile), :].astype(jnp.float32)
        kept = [
            rows[i * per_tile + share * part : i * per_tile + (share + 1) * part]
            for i in range(2 + DIGITS)
        ]
        return jnp.concatenate(kept[:2], axis=0), kept[2:]

    if shares == 2:
        keys = jnp.where(at_first, other[pl.ds(0, half), :], second_ref[...])
        key_ref[pl.ds(0, half), :] = keys
        (own_0, ids_0), (own_1, _) = rest(own, 0), rest(own, 1)
        (other_0, _), (other_1, ids_1) = rest(other, 0), rest(other, 1)
        key_place = jnp.where(at_first, other_0, own_1)
        place_ref[...] = jnp.where(at_first, own_0, other_1)
        ids = [jnp.where(at_first, a, b) for a, b in zip(ids_0, ids_1)]
    else:
        key_ref[pl.ds(0, half), :] = own[pl.ds(0, half), :]
        key_ref[pl.ds(half, half), :] = second_ref[...]
        key_place, _ = rest(own, 0)
        place_ref[...], ids = rest(other_ref, 0)
    done = part * BLK
    filler = jnp.zeros((-(2 + DIGITS) * part % 16, LANES), jnp.float32)
    rows = [key_place] + ids + ([filler] if filler.shape[0] else [])
    key_ref[pl.ds(done, key_ref.shape[0] - done), :] = jnp.concatenate(rows, axis=0).astype(
        jnp.bfloat16
    )


def key_payload(sec, first_half, second_half, other, shares):
    half, width = second_half.shape
    part = 2 * half // LANES // shares
    rows = part * BLK + -(-(2 + DIGITS) * part // 16) * 16
    return pl.pallas_call(
        functools.partial(key_kernel, shares),
        out_shape=(
            jax.ShapeDtypeStruct((rows, width), jnp.bfloat16),
            jax.ShapeDtypeStruct((2 * part, LANES), jnp.float32),
        ),
        in_specs=[in_smem()] + in_vmem(3),
        out_specs=(pl.BlockSpec(memory_space=pltpu.VMEM),) * 2,
        compiler_params=pltpu.CompilerParams(vmem_limit_bytes=VMEM_BYTES),
        name="key_payload",
    )(sec, first_half, second_half, other)


def query_kernel(shares, sec_ref, first_ref, second_ref, other_ref, came_ref, out_ref):
    half = second_ref.shape[0]
    last = first_ref.shape[0] - PLACE_ROWS

    def chosen(own, other):
        return jnp.where(sec_ref[0] == 0, own, other) if shares == 2 else other

    for target, rows in ((0, pl.ds(0, half)), (2 * half, pl.ds(last, PLACE_ROWS))):
        out_ref[pl.ds(target, rows.size), :] = chosen(first_ref[rows, :], other_ref[rows, :])
    out_ref[pl.ds(half, half), :] = chosen(second_ref[...], came_ref[...])


def query_payload(sec, first_half, second_half, other, came, shares):
    half, width = second_half.shape
    return pl.pallas_call(
        functools.partial(query_kernel, shares),
        out_shape=jax.ShapeDtypeStruct((2 * half + PLACE_ROWS, width), jnp.bfloat16),
        in_specs=[in_smem()] + in_vmem(4),
        out_specs=pl.BlockSpec(memory_space=pltpu.VMEM),
        compiler_params=pltpu.CompilerParams(vmem_limit_bytes=VMEM_BYTES),
        name="query_payload",
    )(sec, first_half, second_half, other, came)


def gathered(values, axes, beside):
    held, steps = [], []
    for value, axis in zip(values, axes):
        devices = lax.axis_size(axis)
        if devices & (devices - 1):
            moved = [lax.ppermute(value, axis, pairs) for pairs in turns(axis)[0]]
            held.append(dict(enumerate([value] + moved)))
            steps.append(0)
        else:
            held.append({0: value})
            steps.append(devices.bit_length() - 1)
    for step in range(1, max(steps) + 1):
        for i, axis in enumerate(axes):
            devices = lax.axis_size(axis)
            for at in range(devices - 1, 0, -1):
                if steps[i] and at.bit_count() == step:
                    by = at & -at
                    pairs = [(j, j ^ by) for j in range(devices)]
                    held[i][at] = lax.ppermute(held[i][at ^ by], axis, pairs)
        if step == 1:
            held, beside = lax.optimization_barrier((held, beside))
    return [[h[i] for i in range(len(h))] for h in held], beside


def per_device(
    descriptors, positions, vertex_ids, candidate_blocks, candidate_count, displacement, stiffness
):
    point_total, width = descriptors.shape[3:]
    per_tile = point_total // BLK
    tile_rows, tile_cols = lax.axis_size("ty"), lax.axis_size("tx")
    sections = lax.axis_size("sec")
    sec_index = lax.axis_index("sec")
    tiles = tile_rows * tile_cols
    side = displacement.shape[3]
    halo = ITERS
    span = side + 2 * halo
    wide = -(-span // LANES) * LANES
    cand = candidate_blocks.shape[3]
    shares = 2 if sections == 2 and per_tile % 2 == 0 else 1
    part = per_tile // shares
    key_rows = part * BLK

    first_half, second_half = pack(
        descriptors[0, 0, 0],
        positions[0, 0, 0],
        vertex_ids[0, 0],
        candidate_blocks[0, 0],
        candidate_count[0, 0][None],
        shares,
        tile_cols,
    )
    half = point_total // 2
    swap = [(i, 1 - i) for i in range(2)]

    sec = jnp.asarray(sec_index, jnp.int32)[None]
    own_mesh = jnp.concatenate([displacement[0], stiffness], axis=0)
    if shares == 2:
        share = sec_index
        other = lax.ppermute(first_half, "sec", swap)
    else:
        share = 0
        other = passed_along(first_half, "sec", 1)
    came = passed_along(second_half, "sec", 1)
    cols = col_edges(own_mesh, halo)
    key, place = key_payload(sec, first_half, second_half, other, shares)
    meshes = [own_mesh]
    if shares == 2:
        tied, key = lax.optimization_barrier((own_mesh, key))
        meshes.append(lax.ppermute(tied, "sec", swap))
    query = query_payload(sec, first_half, second_half, other, came, shares)
    (queries, keys), cols = gathered((query, key), ("ty", "tx"), cols)
    at = jnp.concatenate(
        [
            jnp.stack([lax.axis_index("ty") * side, lax.axis_index("tx") * side, sec_index]),
            jnp.stack([lax.axis_index("ty"), jnp.asarray(share)]),
            turns("ty")[1],
            turns("tx")[1],
        ]
    ).astype(jnp.int32)
    extent = (side * tile_rows, side * tile_cols)
    sum_shape = pltpu.VMEM((2, -(-span // 16) * 16, wide), jnp.float32)

    top, end = own_mesh[:, :halo], own_mesh[:, side - halo :]
    corners = [
        jnp.pad(v.swapaxes(1, 2), ((0, 0), (0, 0), (0, side - 2 * halo)))
        for v in (cols[:, :, :halo], cols[:, :, side - halo :])
    ]
    edges = [jnp.concatenate(v, axis=0) for v in ((top, corners[0]), (end, corners[1]))]
    edges = jnp.stack([v.reshape(-1, LANES) for v in edges + [cols]])
    parts = match(at, queries, keys, edges, 16.0 / width, shares, point_total, part, cand)
    shape = parts.shape
    parts = exchanged(parts.reshape((-1,) + shape[2:]), ("sec", "ty") if shares == 2 else "ty")
    pulls = combine(parts, place, shares * tiles)
    parts, pulls, meshes = lax.optimization_barrier((parts, pulls, meshes))

    def edge_rows(by):
        near = lax.axis_index("ty") + by
        rows = parts.reshape(shape)[:, :, -edges.shape[1] :]
        rows = lax.dynamic_index_in_dim(rows, jnp.clip(near, 0, tile_rows - 1), 1, keepdims=False)
        rows = jnp.where((near >= 0) & (near < tile_rows), rows, 0.0)
        rows = rows.reshape(shares, 2, 3, halo, side)
        if shares == 2:
            rows = jnp.where(sec_index == 0, rows, rows[::-1])
        return [
            jnp.concatenate([rows[i, 0], rows[i, 1, :, :, : 2 * halo]], axis=2)
            for i in range(shares)
        ]

    after, before = edge_rows(1), edge_rows(-1)
    cols = [cols]
    if shares == 2:
        sent = parts.reshape(shape)[:, :, -edges.shape[1] :]
        sent = lax.dynamic_index_in_dim(sent, lax.axis_index("ty"), 1, keepdims=False)
        cols.append(jnp.where(sec_index == 0, sent[1], sent[0]).reshape(cols[0].shape))
    framed = []
    for i, mesh in enumerate(meshes):
        whole = jnp.concatenate([mesh, cols[i].swapaxes(1, 2)], axis=2)
        framed.append(jnp.concatenate([whole, after[i], before[i]], axis=1))
    framed = jnp.concatenate(framed, axis=0)
    gap = jnp.zeros(framed.shape[:2] + (wide - span,), framed.dtype)
    mesh_values = jnp.concatenate(
        [framed[:, :, : side + halo], gap, framed[:, :, side + halo :]], axis=2
    )
    if shares == 2:
        points = exchanged(pulls, ("sec", "ty", "tx"))
        rounds, spot, number = spots(side, halo, tile_cols, wide, at, parts.reshape(shape), part)
        relaxed = pl.pallas_call(
            functools.partial(relax_kernel, side, halo, extent),
            out_shape=jax.ShapeDtypeStruct((2, side, side), jnp.float32),
            in_specs=[in_smem()] * 2 + in_vmem(4),
            out_specs=pl.BlockSpec(memory_space=pltpu.VMEM),
            scratch_shapes=[sum_shape],
            compiler_params=pltpu.CompilerParams(vmem_limit_bytes=VMEM_BYTES),
            name="relax",
        )(at, rounds, spot, number, points.reshape(2, tiles, -1, LANES), mesh_values)
        return relaxed[None]

    points = passed_along(exchanged(pulls, ("ty", "tx")), "sec", -1)
    parts = passed_along(parts, "sec", -1)
    rounds, spot, number = spots(side, halo, tile_cols, wide, at, parts[None], part)
    sums = pl.pallas_call(
        functools.partial(sums_kernel, side, halo),
        out_shape=jax.ShapeDtypeStruct((2, span, wide), jnp.float32),
        in_specs=[in_smem()] + in_vmem(2),
        out_specs=pl.BlockSpec(memory_space=pltpu.VMEM),
        scratch_shapes=[sum_shape],
        compiler_params=pltpu.CompilerParams(vmem_limit_bytes=VMEM_BYTES),
        name="sums",
    )(rounds, spot, points[None])
    moving, gains = mesh_values[0:2], mesh_values[2]
    return sweeps(moving, gains, sums, number[:span], at, side, halo, extent)[None]


def solution(mesh):
    in_specs = (
        P("sec", "ty", "tx", None, None),
        P("sec", "ty", "tx", None, None),
        P("sec", "ty", "tx", None),
        P("sec", "ty", "tx", None),
        P("sec", "ty", "tx"),
        P("sec", None, "ty", "tx"),
        P("sec", "ty", "tx"),
    )
    out_specs = P("sec", None, "ty", "tx")
    return jax.shard_map(
        per_device, mesh=mesh, in_specs=in_specs, out_specs=out_specs, check_vma=False
    )
```

```python
import functools
import math

import jax
import jax.numpy as jnp
from jax import lax
from jax.experimental import pallas as pl
from jax.experimental.pallas import tpu as pltpu
from jax.sharding import PartitionSpec as P

BLK = 128
ITERS = 4
LANES = 128
PLACE_ROWS = 16
GROUP = 2
ROUND = 8
BASE = 256
DIGITS = 3
VMEM_BYTES = 24 * 1024 * 1024

spring_sec = 0.5
spring_match = 1.0
relax_rate = 0.8


def passed_along(value, axis, by):
    devices = lax.axis_size(axis)
    pairs = [(i, i + by) for i in range(devices) if 0 <= i + by < devices]
    return lax.ppermute(value, axis, pairs)


def exchanged(value, axes):
    return lax.all_to_all(value, axes, split_axis=0, concat_axis=0, tiled=True)


def spread(value, axes):
    copies = jnp.broadcast_to(value[None], (lax.axis_size(axes),) + value.shape)
    return exchanged(copies, axes)


def nt_dot(a, b):
    return lax.dot_general(a, b, (((1,), (1,)), ((), ())), preferred_element_type=jnp.float32)


def in_vmem(count):
    return [pl.BlockSpec(memory_space=pltpu.VMEM)] * count


def in_smem():
    return pl.BlockSpec(memory_space=pltpu.SMEM)


def match_kernel(scale, tile_rows, key_tiles, cand, at_ref, *refs):
    query_refs, key_refs = refs[:tile_rows], refs[tile_rows : tile_rows + key_tiles]
    (edge_ref, out_ref, query_buf, key_buf, place_buf, state_buf, found_buf, work_ref, list_buf, sem) = (
        refs[tile_rows + key_tiles :]
    )
    shares = out_ref.shape[0]
    point_total = state_buf.shape[2]
    rows = point_total // LANES // shares
    key_rows = key_buf.shape[1]
    part = key_rows // BLK
    total = key_tiles * part
    own_row, share = at_ref[3], at_ref[4]

    for tile, query_ref in enumerate(query_refs):
        last = query_ref[pl.ds(point_total, PLACE_ROWS), :].astype(jnp.float32).astype(jnp.int32)
        here = last[0:1] == own_row * shares + share
        found_buf[pl.ds(tile, 1), :] = jnp.where(here, last[1:2], -1)
    found = pltpu.make_async_copy(found_buf, work_ref, sem)
    found.start()

    row_at = lax.broadcasted_iota(jnp.int32, (PLACE_ROWS, LANES), 0)
    ids = []
    for tile, key_ref in enumerate(key_refs):
        col = at_ref[5 + tile_rows + tile]
        key_buf[col] = key_ref[pl.ds(0, key_rows), :]
        rest = key_ref[pl.ds(key_rows, key_ref.shape[0] - key_rows), :].astype(jnp.float32)
        for j in range(part):
            x, y = rest[j : j + 1, :], rest[part + j : part + j + 1, :]
            stacked = jnp.where(
                row_at == 0, x, jnp.where(row_at == 1, y, jnp.where(row_at == 2, 1.0, 0.0))
            )
            place_buf[col * part + j] = stacked.astype(jnp.bfloat16)
        digits = [rest[2 * part + i * rows : 2 * part + (i + 1) * rows] for i in range(DIGITS)]
        ids.append(sum(digit * float(BASE**i) for i, digit in enumerate(digits)))

    for tile, query_ref in enumerate(query_refs):
        query_buf[tile] = query_ref[pl.ds(0, point_total), :]
    found.wait()

    number = 0
    for tile in range(tile_rows):
        for i in range(cand):
            place = work_ref[tile, i]
            list_buf[number] = tile * total + place
            number = number + jnp.where(place >= 0, 1, 0)
        list_buf[number] = -1
        number = number + lax.rem(number, 2)
    for i in range(2 * GROUP):
        list_buf[number + i] = -1
    groups = lax.div(number + 2 * GROUP - 1, 2 * GROUP)

    state_row = lax.broadcasted_iota(jnp.int32, state_buf.shape[1:], 0)
    for tile in range(tile_rows):
        state_buf[tile] = jnp.where(state_row == 3, -1e30, 0.0)

    def item(at):
        codes = [list_buf[2 * at + i] for i in range(2)]
        tile = lax.div(jnp.maximum(codes[0], 0), total)
        keys, places = [], []
        for code in codes:
            block = lax.rem(jnp.maximum(code, 0), total)
            start = pl.multiple_of(lax.rem(block, part) * BLK, BLK)
            keys.append(key_buf[lax.div(block, part), pl.ds(start, BLK), :])
            kept = jnp.where(code >= 0, 1.0, 0.0).astype(jnp.bfloat16)
            places.append(place_buf[block] * kept)
        return tile, codes[0] >= 0, jnp.concatenate(keys, axis=0), jnp.concatenate(places, axis=1)

    @pl.loop(0, groups)
    def _(group):
        items = [item(group * GROUP + i) for i in range(GROUP)]
        scores = [
            nt_dot(keys, query_buf[tile]) * scale
            for tile, _, keys, _ in items
        ]
        tops = [jnp.max(score, axis=0, keepdims=True) for score in scores]
        weights = [jnp.exp2(s - top).astype(jnp.bfloat16) for s, top in zip(scores, tops)]
        sums = [
            jnp.dot(place, weight, preferred_element_type=jnp.float32)[0:8]
            for (_, _, _, place), weight in zip(items, weights)
        ]
        for (tile, live, _, _), top, added in zip(items, tops, sums):
            top = jnp.where(live, top, -1e30)
            state = state_buf[tile]
            before = state[3:4, :]
            both = jnp.maximum(before, top)
            state = state * jnp.exp2(before - both) + added * jnp.exp2(top - both)
            state_buf[tile] = jnp.where(state_row == 3, both, state)

    edge_rows = edge_ref.shape[1]
    for tile in range(tile_rows):
        to = at_ref[5 + tile]
        for row in range(shares * rows):
            lanes = pl.ds(row * LANES, LANES)
            for place, held in enumerate((3, 2, 0, 1)):
                out_ref[row // rows, to, pl.ds(place * rows + row % rows, 1), :] = state_buf[
                    tile, pl.ds(held, 1), lanes
                ]
        for share in range(shares):
            out_ref[share, tile, pl.ds(4 * rows, key_tiles * rows), :] = jnp.concatenate(ids, axis=0)
            out_ref[share, tile, pl.ds((4 + key_tiles) * rows, edge_rows), :] = jnp.where(
                tile > own_row, edge_ref[1], jnp.where(tile < own_row, edge_ref[0], edge_ref[2])
            )


def match(at, queries, keys, edges, score_factor, shares, point_total, part, cand):
    tile_rows, key_tiles = len(queries), len(keys)
    width = queries[0].shape[1]
    rows = point_total // LANES // shares
    total = key_tiles * part
    return pl.pallas_call(
        functools.partial(
            match_kernel, score_factor * math.log2(math.e), tile_rows, key_tiles, cand
        ),
        out_shape=jax.ShapeDtypeStruct(
            (shares, tile_rows, (4 + key_tiles) * rows + edges.shape[1], LANES), jnp.float32
        ),
        in_specs=[in_smem()] + in_vmem(tile_rows + key_tiles + 1),
        out_specs=pl.BlockSpec(memory_space=pltpu.VMEM),
        scratch_shapes=[
            pltpu.VMEM((tile_rows, point_total, width), jnp.bfloat16),
            pltpu.VMEM((key_tiles, part * BLK, width), jnp.bfloat16),
            pltpu.VMEM((total, PLACE_ROWS, LANES), jnp.bfloat16),
            pltpu.VMEM((tile_rows, 8, point_total), jnp.float32),
            pltpu.VMEM((tile_rows, LANES), jnp.int32),
            pltpu.SMEM((tile_rows, LANES), jnp.int32),
            pltpu.SMEM((tile_rows * (cand + 1) + 2 * GROUP + 1,), jnp.int32),
            pltpu.SemaphoreType.DMA,
        ],
        compiler_params=pltpu.CompilerParams(vmem_limit_bytes=VMEM_BYTES),
        cost_estimate=pl.CostEstimate(
            flops=tile_rows * total * point_total * BLK * width,
            bytes_accessed=2 * (tile_rows * queries[0].size + key_tiles * keys[0].size),
            transcendentals=tile_rows * total * point_total * BLK // 4,
        ),
        name="match",
    )(at, *queries, *keys, edges)


def combine_kernel(parts_ref, place_ref, out_ref):
    parts = parts_ref.shape[0]
    rows = place_ref.shape[0] // 2
    tops = [parts_ref[i, 0:rows, :] for i in range(parts)]
    top = functools.reduce(jnp.maximum, tops)
    total = x = y = jnp.zeros_like(top)
    for i in range(parts):
        gain = jnp.exp2(tops[i] - top)
        total += gain * parts_ref[i, rows : 2 * rows, :]
        x += gain * parts_ref[i, 2 * rows : 3 * rows, :]
        y += gain * parts_ref[i, 3 * rows : 4 * rows, :]
    pull = jnp.concatenate([x / total, y / total], axis=0) - place_ref[...]
    for i in range(out_ref.shape[0]):
        out_ref[i] = pull


def combine(parts, place, copies):
    return pl.pallas_call(
        combine_kernel,
        out_shape=jax.ShapeDtypeStruct((copies,) + place.shape, jnp.float32),
        in_specs=in_vmem(2),
        out_specs=pl.BlockSpec(memory_space=pltpu.VMEM),
        compiler_params=pltpu.CompilerParams(vmem_limit_bytes=VMEM_BYTES),
        name="combine",
    )(parts, place)


def one_hot(at, length, limits):
    count = at.shape[1]
    parts, done = [], 0
    for low, high in limits:
        spot = lax.broadcasted_iota(jnp.int32, (high - low, count), 0) + low
        if low > done:
            parts.append(jnp.zeros((low - done, count), jnp.bfloat16))
        parts.append(jnp.where(spot == at, 1.0, 0.0).astype(jnp.bfloat16))
        done = high
    if length > done:
        parts.append(jnp.zeros((length - done, count), jnp.bfloat16))
    return jnp.concatenate(parts, axis=0)


def flat(value):
    return jnp.concatenate([value[i : i + 1, :] for i in range(value.shape[0])], axis=1)


def hits(side, halo, tall, wide, row, col):
    up = lambda n: -(-n // 16) * 16
    limits = ((0, up(side + halo)), (wide - up(halo), wide))
    return one_hot(flat(row), tall, ((0, tall),)), one_hot(flat(col), wide, limits)


def ranked(rank, row, values):
    sums = [0.0] * len(values)
    for tile in range(rank.shape[0]):
        here = rank[tile] == row
        sums = [total + jnp.where(here, v[tile], 0.0) for total, v in zip(sums, values)]
    return [jnp.sum(total, axis=0, keepdims=True) for total in sums]


def spots_kernel(
    side, halo, key_tiles, at_ref, parts_ref, rounds_ref, rank_ref, spot_ref, count_ref, hit_buf
):
    shares, tile_rows, _, _ = parts_ref.shape
    count = rank_ref.shape[1]
    rows = count // shares
    tall, wide = count_ref.shape

    def folded(at, length):
        return jnp.where(
            (at >= 0) & (at < side + halo), at, jnp.where((at < 0) & (at >= -halo), at + length, -1)
        )

    number = jnp.zeros((1, LANES), jnp.int32)
    point_row = lax.broadcasted_iota(jnp.int32, (count, LANES), 0)
    for i in range(tile_rows):
        for j in range(key_tiles):
            ids = jnp.concatenate(
                [parts_ref[k, i, pl.ds((4 + j) * rows, rows), :] for k in range(shares)], axis=0
            ).astype(jnp.int32)
            tile_of = lax.div(ids, side * side)
            within = lax.rem(ids, side * side)
            row = lax.div(tile_of, key_tiles) * side + lax.div(within, side) - at_ref[0]
            col = lax.rem(tile_of, key_tiles) * side + lax.rem(within, side) - at_ref[1]
            row, col = folded(row, side + 2 * halo), folded(col, wide)
            here = (row >= 0) & (col >= 0)
            hit = here.astype(jnp.int32)
            by = 1
            while by < count:
                hit = hit + jnp.where(point_row >= by, pltpu.roll(hit, by, 0), 0)
                by *= 2
            tile = i * key_tiles + at_ref[5 + tile_rows + j]
            rank_ref[tile] = jnp.where(here, number + hit - 1, -1)
            hit_buf[0, tile] = row.astype(jnp.float32) + 1.0
            hit_buf[1, tile] = col.astype(jnp.float32) + 1.0
            number = number + hit[count - 1 : count, :]
    rounds = lax.div(jnp.max(number) + ROUND - 1, ROUND)
    rounds_ref[0] = rounds
    count_ref[...] = jnp.zeros_like(count_ref)

    @pl.loop(0, rounds)
    def _(k):
        found = [ranked(rank_ref, k * ROUND + r, (hit_buf.at[0], hit_buf.at[1])) for r in range(ROUND)]
        row, col = (jnp.concatenate(v, axis=0).astype(jnp.int32) - 1 for v in zip(*found))
        spot_ref[k, 0] = row
        spot_ref[k, 1] = col
        row_hit, col_hit = hits(side, halo, tall, wide, row, col)
        count_ref[...] += nt_dot(row_hit, col_hit)


def spots(side, halo, key_tiles, wide, at, parts, rows):
    tall = -(-(side + 2 * halo) // 16) * 16
    count = parts.shape[0] * rows
    tiles = parts.shape[1] * key_tiles
    rounds = -(-tiles * count // ROUND)
    return pl.pallas_call(
        functools.partial(spots_kernel, side, halo, key_tiles),
        out_shape=(
            jax.ShapeDtypeStruct((1,), jnp.int32),
            jax.ShapeDtypeStruct((tiles, count, LANES), jnp.int32),
            jax.ShapeDtypeStruct((rounds, 2, ROUND, LANES), jnp.int32),
            jax.ShapeDtypeStruct((tall, wide), jnp.float32),
        ),
        in_specs=[in_smem()] + in_vmem(1),
        out_specs=(in_smem(),) + (pl.BlockSpec(memory_space=pltpu.VMEM),) * 3,
        scratch_shapes=[pltpu.VMEM((2, tiles, count, LANES), jnp.float32)],
        compiler_params=pltpu.CompilerParams(vmem_limit_bytes=VMEM_BYTES),
        cost_estimate=pl.CostEstimate(
            flops=8 * tall * ROUND * LANES * wide,
            bytes_accessed=8 * parts.size,
            transcendentals=0,
        ),
        name="spots",
    )(at, parts)


def vertex_sums(side, halo, rounds_ref, rank_ref, spot_ref, points_ref, sum_ref, point_buf):
    _, tall, wide = sum_ref.shape
    shares, tiles, both_rows, _ = points_ref.shape
    rows = both_rows // 2
    sum_ref[...] = jnp.zeros_like(sum_ref)
    for tile in range(tiles):
        for share in range(shares):
            for c in range(2):
                point_buf[c, tile, pl.ds(share * rows, rows), :] = points_ref[
                    share, tile, pl.ds(c * rows, rows), :
                ]

    @pl.loop(0, rounds_ref[0])
    def _(k):
        found = [
            ranked(rank_ref, k * ROUND + r, (point_buf.at[0], point_buf.at[1])) for r in range(ROUND)
        ]
        row_hit, col_hit = hits(side, halo, tall, wide, spot_ref[k, 0], spot_ref[k, 1])
        parts = []
        for value in zip(*found):
            value = jnp.concatenate(value, axis=1)
            high = value.astype(jnp.bfloat16)
            low = (value - high.astype(jnp.float32)).astype(jnp.bfloat16)
            parts += [row_hit * high, row_hit * low]
        summed = nt_dot(jnp.concatenate(parts, axis=0), col_hit)
        sum_ref[0] += summed[0:tall] + summed[tall : 2 * tall]
        sum_ref[1] += summed[2 * tall : 3 * tall] + summed[3 * tall :]


def sums_kernel(side, halo, rounds_ref, rank_ref, spot_ref, points_ref, out_ref, sum_ref, point_buf):
    vertex_sums(side, halo, rounds_ref, rank_ref, spot_ref, points_ref, sum_ref, point_buf)
    out_ref[...] = sum_ref[:, pl.ds(0, out_ref.shape[1]), :]


def relax_kernel(
    side,
    halo,
    extent,
    at_ref,
    rounds_ref,
    rank_ref,
    spot_ref,
    count_ref,
    points_ref,
    mesh_ref,
    out_ref,
    sum_ref,
    point_buf,
):
    vertex_sums(side, halo, rounds_ref, rank_ref, spot_ref, points_ref, sum_ref, point_buf)
    span = side + 2 * halo
    wide = sum_ref.shape[2]
    shape = (span, wide)
    row = lax.broadcasted_iota(jnp.int32, shape, 0)
    col = lax.broadcasted_iota(jnp.int32, shape, 1)
    row = jnp.where(row < side + halo, row, row - span) + at_ref[0]
    col = jnp.where(col < side + halo, col, col - wide) + at_ref[1]
    inside = (row >= 0) & (row < extent[0]) & (col >= 0) & (col < extent[1])
    own_pulled = (at_ref[2] == 0).astype(jnp.float32)
    linked = 1.0
    matched = count_ref[pl.ds(0, span), :]
    moving, gains, has, step = [], [], [], []
    for part, pulled in enumerate((own_pulled, 1.0 - own_pulled)):
        gain = mesh_ref[part * 3 + 2]
        diagonal = 4.0 * gain + spring_sec * linked + spring_match * matched * pulled
        gains.append(gain)
        has.append(matched * pulled)
        step.append(jnp.where(inside, relax_rate / diagonal, 0.0))
        moving.append(
            [(mesh_ref[part * 3 + c], sum_ref[c, pl.ds(0, span), :] * pulled) for c in range(2)]
        )
    for sweep in range(ITERS):
        later = []
        for part in range(2):
            row_of = []
            for c in range(2):
                u, pulled = moving[part][c]
                other = moving[1 - part][c][0]
                laplace = (
                    pltpu.roll(u, 1, 0)
                    + pltpu.roll(u, span - 1, 0)
                    + pltpu.roll(u, 1, 1)
                    + pltpu.roll(u, wide - 1, 1)
                    - 4.0 * u
                )
                force = (
                    gains[part] * laplace
                    + spring_sec * (other - linked * u)
                    + spring_match * (pulled - has[part] * u)
                )
                row_of.append((u + step[part] * force, pulled))
            later.append(row_of)
        moving = later
    for c in range(2):
        out_ref[c] = moving[0][c][0][0:side, 0:side]


def col_edges(value, halo):
    after = passed_along(value[:, :, :halo].swapaxes(1, 2), "tx", -1)
    before = passed_along(value[:, :, value.shape[2] - halo :].swapaxes(1, 2), "tx", 1)
    return jnp.concatenate([after, before], axis=1)


def sweeps(moving, gains, sums, number, at, side, halo, extent):
    sections = lax.axis_size("sec")
    sec_index = at[2]
    has_next = (sec_index < sections - 1).astype(jnp.float32)
    linked = (sec_index > 0).astype(jnp.float32) + has_next
    pulled, matched = sums * has_next, number * has_next
    span, wide = moving.shape[1:]
    row = jnp.arange(span)[:, None]
    col = jnp.arange(wide)[None, :]
    row = jnp.where(row < side + halo, row, row - span) + at[0]
    col = jnp.where(col < side + halo, col, col - wide) + at[1]
    inside = (row >= 0) & (row < extent[0]) & (col >= 0) & (col < extent[1])
    diagonal = 4.0 * gains + spring_sec * linked + spring_match * matched
    step = jnp.where(inside, relax_rate / jnp.where(inside, diagonal, 1.0), 0.0)
    for sweep in range(ITERS):
        lower_sec = passed_along(moving, "sec", 1)
        upper_sec = passed_along(moving, "sec", -1)
        laplace = (
            jnp.roll(moving, 1, 1)
            + jnp.roll(moving, -1, 1)
            + jnp.roll(moving, 1, 2)
            + jnp.roll(moving, -1, 2)
            - 4.0 * moving
        )
        force = (
            gains * laplace
            + spring_sec * (lower_sec + upper_sec - linked * moving)
            + spring_match * (pulled - matched * moving)
        )
        moving = moving + step * force
    return moving[:, :side, :side]


def pack_kernel(
    shares,
    tile_cols,
    desc_hbm,
    place_hbm,
    ids_hbm,
    list_hbm,
    count_hbm,
    first_ref,
    second_ref,
    place_ref,
    ids_ref,
    list_ref,
    count_ref,
    last_ref,
    sems,
):
    half = second_ref.shape[0]
    copies = [
        pltpu.make_async_copy(source, target, sems.at[i])
        for i, (source, target) in enumerate(
            (
                (place_hbm, place_ref),
                (ids_hbm, ids_ref),
                (list_hbm, list_ref),
                (count_hbm, count_ref),
                (desc_hbm.at[pl.ds(0, half), :], first_ref.at[pl.ds(0, half), :]),
                (desc_hbm.at[pl.ds(half, half), :], second_ref),
            )
        )
    ]
    for copy in copies:
        copy.start()
    for copy in copies[:4]:
        copy.wait()

    def cut(row):
        return [row[:, i : i + LANES] for i in range(0, row.shape[1], LANES)]

    place, ids, blocks = place_ref[...].astype(jnp.float32), ids_ref[...], list_ref[...]
    rows = cut(place[0:1]) + cut(place[1:2])
    for i in range(DIGITS):
        digit = lax.rem(lax.div(ids, BASE**i), BASE)
        rows += cut(digit.astype(jnp.float32))
    per_tile = place.shape[1] // BLK
    part = per_tile // shares
    tile, within = lax.div(blocks, per_tile), lax.rem(blocks, per_tile)
    device = lax.div(tile, tile_cols) * shares + lax.div(within, part)
    spot = lax.rem(tile, tile_cols) * part + lax.rem(within, part)
    live = lax.broadcasted_iota(jnp.int32, blocks.shape, 1) < count_ref[0, 0]
    last_ref[...] = jnp.full_like(last_ref, BASE - 1.0)
    last_ref[0:1, 0 : blocks.shape[1]] = jnp.where(live, device, BASE - 1).astype(jnp.float32)
    last_ref[1:2, 0 : blocks.shape[1]] = spot.astype(jnp.float32)
    count = first_ref.shape[0] - half
    gap = jnp.zeros((count - len(rows) - PLACE_ROWS, LANES), jnp.float32)
    rows += ([gap] if gap.shape[0] else []) + [last_ref[...]]
    first_ref[pl.ds(half, count), :] = jnp.concatenate(rows, axis=0).astype(jnp.bfloat16)
    for copy in copies[4:]:
        copy.wait()


def pack(desc, place, ids, blocks, count, shares, tile_cols):
    points, width = desc.shape
    half = points // 2
    rows = -(-(2 + DIGITS) * (points // LANES) // 16) * 16 + PLACE_ROWS
    return pl.pallas_call(
        functools.partial(pack_kernel, shares, tile_cols),
        out_shape=(
            jax.ShapeDtypeStruct((half + rows, width), jnp.bfloat16),
            jax.ShapeDtypeStruct((half, width), jnp.bfloat16),
        ),
        in_specs=[pl.BlockSpec(memory_space=pltpu.HBM)] * 5,
        out_specs=(pl.BlockSpec(memory_space=pltpu.VMEM),) * 2,
        scratch_shapes=[
            pltpu.VMEM(place.shape, place.dtype),
            pltpu.VMEM(ids.shape, ids.dtype),
            pltpu.VMEM(blocks.shape, blocks.dtype),
            pltpu.SMEM(count.shape, count.dtype),
            pltpu.VMEM((PLACE_ROWS, LANES), jnp.float32),
            pltpu.SemaphoreType.DMA((6,)),
        ],
        name="pack",
    )(desc, place, ids, blocks, count)


def turns(axis):
    devices, here = lax.axis_size(axis), lax.axis_index(axis)
    if devices & (devices - 1):
        pairs = [[(i, (i + j) % devices) for i in range(devices)] for j in range(1, devices)]
        return pairs, jnp.mod(here - jnp.arange(devices), devices)
    pairs = [[(i, i ^ j) for i in range(devices)] for j in range(1, devices)]
    return pairs, here ^ jnp.arange(devices)


def key_kernel(shares, sec_ref, first_ref, second_ref, other_ref, key_ref, place_ref):
    half = second_ref.shape[0]
    per_tile = 2 * half // LANES
    part = per_tile // shares
    own, other = first_ref, first_ref
    if shares == 2:
        other = other_ref
    at_first = sec_ref[0] == 0

    def rest(ref, share):
        rows = ref[pl.ds(half, (2 + DIGITS) * per_tile), :].astype(jnp.float32)
        kept = [
            rows[i * per_tile + share * part : i * per_tile + (share + 1) * part]
            for i in range(2 + DIGITS)
        ]
        return jnp.concatenate(kept[:2], axis=0), kept[2:]

    if shares == 2:
        keys = jnp.where(at_first, other[pl.ds(0, half), :], second_ref[...])
        key_ref[pl.ds(0, half), :] = keys
        (own_0, ids_0), (own_1, _) = rest(own, 0), rest(own, 1)
        (other_0, _), (other_1, ids_1) = rest(other, 0), rest(other, 1)
        key_place = jnp.where(at_first, other_0, own_1)
        place_ref[...] = jnp.where(at_first, own_0, other_1)
        ids = [jnp.where(at_first, a, b) for a, b in zip(ids_0, ids_1)]
    else:
        key_ref[pl.ds(0, half), :] = own[pl.ds(0, half), :]
        key_ref[pl.ds(half, half), :] = second_ref[...]
        key_place, _ = rest(own, 0)
        place_ref[...], ids = rest(other_ref, 0)
    done = part * BLK
    filler = jnp.zeros((-(2 + DIGITS) * part % 16, LANES), jnp.float32)
    rows = [key_place] + ids + ([filler] if filler.shape[0] else [])
    key_ref[pl.ds(done, key_ref.shape[0] - done), :] = jnp.concatenate(rows, axis=0).astype(
        jnp.bfloat16
    )


def key_payload(sec, first_half, second_half, other, shares):
    half, width = second_half.shape
    part = 2 * half // LANES // shares
    rows = part * BLK + -(-(2 + DIGITS) * part // 16) * 16
    return pl.pallas_call(
        functools.partial(key_kernel, shares),
        out_shape=(
            jax.ShapeDtypeStruct((rows, width), jnp.bfloat16),
            jax.ShapeDtypeStruct((2 * part, LANES), jnp.float32),
        ),
        in_specs=[in_smem()] + in_vmem(3),
        out_specs=(pl.BlockSpec(memory_space=pltpu.VMEM),) * 2,
        compiler_params=pltpu.CompilerParams(vmem_limit_bytes=VMEM_BYTES),
        name="key_payload",
    )(sec, first_half, second_half, other)


def query_kernel(shares, sec_ref, first_ref, second_ref, other_ref, came_ref, out_ref):
    half = second_ref.shape[0]
    last = first_ref.shape[0] - PLACE_ROWS

    def chosen(own, other):
        return jnp.where(sec_ref[0] == 0, own, other) if shares == 2 else other

    for target, rows in ((0, pl.ds(0, half)), (2 * half, pl.ds(last, PLACE_ROWS))):
        out_ref[pl.ds(target, rows.size), :] = chosen(first_ref[rows, :], other_ref[rows, :])
    out_ref[pl.ds(half, half), :] = chosen(second_ref[...], came_ref[...])


def query_payload(sec, first_half, second_half, other, came, shares):
    half, width = second_half.shape
    return pl.pallas_call(
        functools.partial(query_kernel, shares),
        out_shape=jax.ShapeDtypeStruct((2 * half + PLACE_ROWS, width), jnp.bfloat16),
        in_specs=[in_smem()] + in_vmem(4),
        out_specs=pl.BlockSpec(memory_space=pltpu.VMEM),
        compiler_params=pltpu.CompilerParams(vmem_limit_bytes=VMEM_BYTES),
        name="query_payload",
    )(sec, first_half, second_half, other, came)


def gathered(values, axes, beside):
    held, steps = [], []
    for value, axis in zip(values, axes):
        devices = lax.axis_size(axis)
        if devices & (devices - 1):
            moved = [lax.ppermute(value, axis, pairs) for pairs in turns(axis)[0]]
            held.append(dict(enumerate([value] + moved)))
            steps.append(0)
        else:
            held.append({0: value})
            steps.append(devices.bit_length() - 1)
    for step in range(1, max(steps) + 1):
        for i, axis in enumerate(axes):
            devices = lax.axis_size(axis)
            for at in range(devices - 1, 0, -1):
                if steps[i] and at.bit_count() == step:
                    by = at & -at
                    pairs = [(j, j ^ by) for j in range(devices)]
                    held[i][at] = lax.ppermute(held[i][at ^ by], axis, pairs)
        if step == 1:
            held, beside = lax.optimization_barrier((held, beside))
    return [[h[i] for i in range(len(h))] for h in held], beside


def per_device(
    descriptors, positions, vertex_ids, candidate_blocks, candidate_count, displacement, stiffness
):
    point_total, width = descriptors.shape[3:]
    per_tile = point_total // BLK
    tile_rows, tile_cols = lax.axis_size("ty"), lax.axis_size("tx")
    sections = lax.axis_size("sec")
    sec_index = lax.axis_index("sec")
    tiles = tile_rows * tile_cols
    side = displacement.shape[3]
    halo = ITERS
    span = side + 2 * halo
    wide = -(-span // LANES) * LANES
    cand = candidate_blocks.shape[3]
    shares = 2 if sections == 2 and per_tile % 2 == 0 else 1
    part = per_tile // shares
    key_rows = part * BLK

    first_half, second_half = pack(
        descriptors[0, 0, 0],
        positions[0, 0, 0],
        vertex_ids[0, 0],
        candidate_blocks[0, 0],
        candidate_count[0, 0][None],
        shares,
        tile_cols,
    )
    half = point_total // 2
    swap = [(i, 1 - i) for i in range(2)]

    sec = jnp.asarray(sec_index, jnp.int32)[None]
    own_mesh = jnp.concatenate([displacement[0], stiffness], axis=0)
    if shares == 2:
        share = sec_index
        other = lax.ppermute(first_half, "sec", swap)
    else:
        share = 0
        other = passed_along(first_half, "sec", 1)
    came = passed_along(second_half, "sec", 1)
    cols = col_edges(own_mesh, halo)
    key, place = key_payload(sec, first_half, second_half, other, shares)
    meshes = [own_mesh]
    if shares == 2:
        tied, key = lax.optimization_barrier((own_mesh, key))
        meshes.append(lax.ppermute(tied, "sec", swap))
    query = query_payload(sec, first_half, second_half, other, came, shares)
    (queries, keys), (cols, meshes) = gathered((query, key), ("ty", "tx"), (cols, meshes))
    at = jnp.concatenate(
        [
            jnp.stack([lax.axis_index("ty") * side, lax.axis_index("tx") * side, sec_index]),
            jnp.stack([lax.axis_index("ty"), jnp.asarray(share)]),
            turns("ty")[1],
            turns("tx")[1],
        ]
    ).astype(jnp.int32)
    extent = (side * tile_rows, side * tile_cols)
    sum_shapes = [
        pltpu.VMEM((2, -(-span // 16) * 16, wide), jnp.float32),
        pltpu.VMEM((2, tiles, per_tile, LANES), jnp.float32),
    ]

    top, end = own_mesh[:, :halo], own_mesh[:, side - halo :]
    corners = [
        jnp.pad(v.swapaxes(1, 2), ((0, 0), (0, 0), (0, side - 2 * halo)))
        for v in (cols[:, :, :halo], cols[:, :, side - halo :])
    ]
    edges = [jnp.concatenate(v, axis=0) for v in ((top, corners[0]), (end, corners[1]))]
    edges = jnp.stack([v.reshape(-1, LANES) for v in edges + [cols]])
    parts = match(at, queries, keys, edges, 16.0 / width, shares, point_total, part, cand)
    shape = parts.shape
    parts = exchanged(parts.reshape((-1,) + shape[2:]), ("sec", "ty") if shares == 2 else "ty")
    pulls = combine(parts, place, shares * tiles)
    parts, pulls, meshes = lax.optimization_barrier((parts, pulls, meshes))

    def edge_rows(by):
        near = lax.axis_index("ty") + by
        rows = parts.reshape(shape)[:, :, -edges.shape[1] :]
        rows = lax.dynamic_index_in_dim(rows, jnp.clip(near, 0, tile_rows - 1), 1, keepdims=False)
        rows = jnp.where((near >= 0) & (near < tile_rows), rows, 0.0)
        rows = rows.reshape(shares, 2, 3, halo, side)
        if shares == 2:
            rows = jnp.where(sec_index == 0, rows, rows[::-1])
        return [
            jnp.concatenate([rows[i, 0], rows[i, 1, :, :, : 2 * halo]], axis=2)
            for i in range(shares)
        ]

    after, before = edge_rows(1), edge_rows(-1)
    cols = [cols]
    if shares == 2:
        sent = parts.reshape(shape)[:, :, -edges.shape[1] :]
        sent = lax.dynamic_index_in_dim(sent, lax.axis_index("ty"), 1, keepdims=False)
        cols.append(jnp.where(sec_index == 0, sent[1], sent[0]).reshape(cols[0].shape))
    framed = []
    for i, mesh in enumerate(meshes):
        whole = jnp.concatenate([mesh, cols[i].swapaxes(1, 2)], axis=2)
        framed.append(jnp.concatenate([whole, after[i], before[i]], axis=1))
    framed = jnp.concatenate(framed, axis=0)
    gap = jnp.zeros(framed.shape[:2] + (wide - span,), framed.dtype)
    mesh_values = jnp.concatenate(
        [framed[:, :, : side + halo], gap, framed[:, :, side + halo :]], axis=2
    )
    if shares == 2:
        points = exchanged(pulls, ("sec", "ty", "tx"))
        rounds, rank, spot, number = spots(side, halo, tile_cols, wide, at, parts.reshape(shape), part)
        relaxed = pl.pallas_call(
            functools.partial(relax_kernel, side, halo, extent),
            out_shape=jax.ShapeDtypeStruct((2, side, side), jnp.float32),
            in_specs=[in_smem()] * 2 + in_vmem(5),
            out_specs=pl.BlockSpec(memory_space=pltpu.VMEM),
            scratch_shapes=sum_shapes,
            compiler_params=pltpu.CompilerParams(vmem_limit_bytes=VMEM_BYTES),
            name="relax",
        )(at, rounds, rank, spot, number, points.reshape(2, tiles, -1, LANES), mesh_values)
        return relaxed[None]

    points = passed_along(exchanged(pulls, ("ty", "tx")), "sec", -1)
    parts = passed_along(parts, "sec", -1)
    rounds, rank, spot, number = spots(side, halo, tile_cols, wide, at, parts[None], part)
    sums = pl.pallas_call(
        functools.partial(sums_kernel, side, halo),
        out_shape=jax.ShapeDtypeStruct((2, span, wide), jnp.float32),
        in_specs=[in_smem()] + in_vmem(3),
        out_specs=pl.BlockSpec(memory_space=pltpu.VMEM),
        scratch_shapes=sum_shapes,
        compiler_params=pltpu.CompilerParams(vmem_limit_bytes=VMEM_BYTES),
        name="sums",
    )(rounds, rank, spot, points[None])
    moving, gains = mesh_values[0:2], mesh_values[2]
    return sweeps(moving, gains, sums, number[:span], at, side, halo, extent)[None]


def solution(mesh):
    in_specs = (
        P("sec", "ty", "tx", None, None),
        P("sec", "ty", "tx", None, None),
        P("sec", "ty", "tx", None),
        P("sec", "ty", "tx", None),
        P("sec", "ty", "tx"),
        P("sec", None, "ty", "tx"),
        P("sec", "ty", "tx"),
    )
    out_specs = P("sec", None, "ty", "tx")
    return jax.shard_map(
        per_device, mesh=mesh, in_specs=in_specs, out_specs=out_specs, check_vma=False
    )
```

```python
import functools
import math

import jax
import jax.numpy as jnp
from jax import lax
from jax.experimental import pallas as pl
from jax.experimental.pallas import tpu as pltpu
from jax.sharding import PartitionSpec as P

BLK = 128
ITERS = 4
LANES = 128
PLACE_ROWS = 16
GROUP = 2
ROUND = 8
BASE = 256
DIGITS = 3
VMEM_BYTES = 24 * 1024 * 1024

spring_sec = 0.5
spring_match = 1.0
relax_rate = 0.8


def passed_along(value, axis, by):
    devices = lax.axis_size(axis)
    pairs = [(i, i + by) for i in range(devices) if 0 <= i + by < devices]
    return lax.ppermute(value, axis, pairs)


def exchanged(value, axes):
    return lax.all_to_all(value, axes, split_axis=0, concat_axis=0, tiled=True)


def spread(value, axes):
    copies = jnp.broadcast_to(value[None], (lax.axis_size(axes),) + value.shape)
    return exchanged(copies, axes)


def nt_dot(a, b):
    return lax.dot_general(a, b, (((1,), (1,)), ((), ())), preferred_element_type=jnp.float32)


def in_vmem(count):
    return [pl.BlockSpec(memory_space=pltpu.VMEM)] * count


def in_smem():
    return pl.BlockSpec(memory_space=pltpu.SMEM)


def match_kernel(scale, plan, last, at_ref, *refs):
    tile_rows = max(i for i, _ in plan) + 1
    key_tiles = max(max(among) for _, among in plan if among) + 1
    query_refs, refs = refs[:tile_rows], refs[tile_rows:]
    key_refs, refs = refs[:key_tiles], refs[key_tiles:]
    if last:
        before_ref, edge_ref, out_ref = refs[:3]
        refs = refs[3:]
    else:
        (out_ref,) = refs[:1]
        refs = refs[1:]
    query_buf, key_buf, place_buf, state_buf, list_buf = refs
    point_total = state_buf.shape[2]
    all_tiles, key_rows = key_buf.shape[:2]
    part = key_rows // BLK
    total = all_tiles * part
    own_row, share, shares = at_ref[3], at_ref[4], at_ref[5]
    rows_at, cols_at = 6, 6 + query_buf.shape[0]

    number = 0
    for tile, among in plan:
        met = [at_ref[cols_at + i] for i in among]
        listed = query_refs[tile][pl.ds(point_total, PLACE_ROWS), :]
        listed = listed.astype(jnp.float32).astype(jnp.int32)
        here = listed[0:1] == own_row * shares + share
        for low in range(0, total, 16):
            place = listed[1:2] - low
            bits = jnp.where(here & (place >= 0) & (place < 16), 1 << jnp.clip(place, 0, 15), 0)
            bits = jnp.sum(bits)
            for i in range(low, min(low + 16, total)):
                allowed = functools.reduce(jnp.logical_or, [col == i // part for col in met])
                list_buf[number] = tile * total + i
                number = number + jnp.where(allowed, (bits >> (i - low)) & 1, 0)
        list_buf[number] = -1
        number = number + lax.rem(number, 2)
    for i in range(2 * GROUP):
        list_buf[number + i] = -1
    groups = lax.div(number + 2 * GROUP - 1, 2 * GROUP)

    row_at = lax.broadcasted_iota(jnp.int32, (PLACE_ROWS, LANES), 0)
    ids = []
    for tile, key_ref in enumerate(key_refs):
        col = at_ref[cols_at + tile]
        key_buf[col] = key_ref[pl.ds(0, key_rows), :]
        rest = key_ref[pl.ds(key_rows, key_ref.shape[0] - key_rows), :].astype(jnp.float32)
        for j in range(part):
            x, y = rest[j : j + 1, :], rest[part + j : part + j + 1, :]
            stacked = jnp.where(
                row_at == 0, x, jnp.where(row_at == 1, y, jnp.where(row_at == 2, 1.0, 0.0))
            )
            place_buf[col * part + j] = stacked.astype(jnp.bfloat16)
        digits = [rest[(2 + i) * part : (3 + i) * part] for i in range(DIGITS)]
        ids.append(sum(digit * float(BASE**i) for i, digit in enumerate(digits)))
    for tile, query_ref in enumerate(query_refs):
        query_buf[tile] = query_ref[pl.ds(0, point_total), :]

    state_row = lax.broadcasted_iota(jnp.int32, state_buf.shape[1:], 0)
    for tile in range(tile_rows):
        if last and tile < before_ref.shape[0]:
            state_buf[tile] = before_ref[tile]
        else:
            state_buf[tile] = jnp.where(state_row == 3, -1e30, 0.0)

    def item(at):
        codes = [list_buf[2 * at + i] for i in range(2)]
        tile = lax.div(jnp.maximum(codes[0], 0), total)
        keys, places = [], []
        for i, code in enumerate(codes):
            block = lax.rem(jnp.maximum(jnp.where(code >= 0, code, codes[0]), 0), total)
            block = jnp.where(codes[0] >= 0, block, at_ref[cols_at] * part)
            start = pl.multiple_of(lax.rem(block, part) * BLK, BLK)
            keys.append(key_buf[lax.div(block, part), pl.ds(start, BLK), :])
            kept = jnp.where(code >= 0, 1.0, 0.0).astype(jnp.bfloat16)
            places.append(place_buf[block] * kept)
        return tile, codes[0] >= 0, jnp.concatenate(keys, axis=0), jnp.concatenate(places, axis=1)

    @pl.loop(0, groups)
    def _(group):
        items = [item(group * GROUP + i) for i in range(GROUP)]
        scores = [nt_dot(keys, query_buf[tile]) * scale for tile, _, keys, _ in items]
        tops = [jnp.max(score, axis=0, keepdims=True) for score in scores]
        weights = [jnp.exp2(s - top).astype(jnp.bfloat16) for s, top in zip(scores, tops)]
        sums = [
            jnp.dot(place, weight, preferred_element_type=jnp.float32)[0:8]
            for (_, _, _, place), weight in zip(items, weights)
        ]
        for (tile, live, _, _), top, added in zip(items, tops, sums):
            top = jnp.where(live, top, -1e30)
            state = state_buf[tile]
            before = state[3:4, :]
            both = jnp.maximum(before, top)
            state = state * jnp.exp2(before - both) + added * jnp.exp2(top - both)
            state_buf[tile] = jnp.where(state_row == 3, both, state)

    if not last:
        out_ref[...] = state_buf[pl.ds(0, tile_rows)]
        return
    edge_rows = edge_ref.shape[1]
    for tile in range(tile_rows):
        to = at_ref[rows_at + tile]
        for row in range(point_total // LANES):
            lanes = pl.ds(row * LANES, LANES)
            for place, held in enumerate((3, 2, 0, 1)):
                out_ref[row // part, to, pl.ds(place * part + row % part, 1), :] = state_buf[
                    tile, pl.ds(held, 1), lanes
                ]
        for share in range(out_ref.shape[0]):
            out_ref[share, tile, pl.ds(4 * part, key_tiles * part), :] = jnp.concatenate(ids, axis=0)
            out_ref[share, tile, pl.ds((4 + key_tiles) * part, edge_rows), :] = jnp.where(
                tile > own_row, edge_ref[1], jnp.where(tile < own_row, edge_ref[0], edge_ref[2])
            )


def match(at, queries, keys, edges, score_factor, shares, part):
    tile_rows, key_tiles = len(queries), len(keys)
    point_total, width = queries[0].shape[0] - PLACE_ROWS, queries[0].shape[1]
    total = key_tiles * part

    def call(plan, out_shape, *more):
        many_rows = max(i for i, _ in plan) + 1
        many_keys = max(max(among) for _, among in plan if among) + 1
        scores = sum(len(among) for _, among in plan) * part * point_total * BLK
        return pl.pallas_call(
            functools.partial(
                match_kernel, score_factor * math.log2(math.e), plan, len(more) > 0
            ),
            out_shape=jax.ShapeDtypeStruct(out_shape, jnp.float32),
            in_specs=[in_smem()] + in_vmem(many_rows + many_keys + len(more)),
            out_specs=pl.BlockSpec(memory_space=pltpu.VMEM),
            scratch_shapes=[
                pltpu.VMEM((tile_rows, point_total, width), jnp.bfloat16),
                pltpu.VMEM((key_tiles, part * BLK, width), jnp.bfloat16),
                pltpu.VMEM((total, PLACE_ROWS, LANES), jnp.bfloat16),
                pltpu.VMEM((tile_rows, 8, point_total), jnp.float32),
                pltpu.SMEM((tile_rows * (total + 1) + 2 * GROUP + 1,), jnp.int32),
            ],
            compiler_params=pltpu.CompilerParams(vmem_limit_bytes=VMEM_BYTES),
            cost_estimate=pl.CostEstimate(
                flops=scores * width, bytes_accessed=4 * scores // BLK, transcendentals=scores // 4
            ),
            name="match_rest" if more else "match",
        )(at, *queries[:many_rows], *keys[:many_keys], *more)

    there = [
        [i for i in range(n) if i.bit_count() < 2 or n & (n - 1)] for n in (tile_rows, key_tiles)
    ]
    first = [(i, tuple(there[1])) for i in there[0]]
    rest = [(i, tuple(j for j in range(key_tiles) if j not in there[1])) for i in there[0]]
    rest = [v for v in rest if v[1]]
    rest += [(i, tuple(range(key_tiles))) for i in range(tile_rows) if i not in there[0]]
    if rest:
        state = call(first, (len(first), 8, point_total))
    else:
        rest, row = first, jnp.arange(8)[None, :, None]
        state = jnp.where(row == 3, -1e30, jnp.zeros((tile_rows, 8, point_total), jnp.float32))
    shape = (shares, tile_rows, (4 + key_tiles) * part + edges.shape[1], LANES)
    return call(rest, shape, state, edges)


def combine_kernel(parts_ref, place_ref, out_ref):
    parts = parts_ref.shape[0]
    rows = place_ref.shape[0] // 2
    tops = [parts_ref[i, 0:rows, :] for i in range(parts)]
    top = functools.reduce(jnp.maximum, tops)
    total = x = y = jnp.zeros_like(top)
    for i in range(parts):
        gain = jnp.exp2(tops[i] - top)
        total += gain * parts_ref[i, rows : 2 * rows, :]
        x += gain * parts_ref[i, 2 * rows : 3 * rows, :]
        y += gain * parts_ref[i, 3 * rows : 4 * rows, :]
    pull = jnp.concatenate([x / total, y / total], axis=0) - place_ref[...]
    for i in range(out_ref.shape[0]):
        out_ref[i] = pull


def combine(parts, place, copies):
    return pl.pallas_call(
        combine_kernel,
        out_shape=jax.ShapeDtypeStruct((copies,) + place.shape, jnp.float32),
        in_specs=in_vmem(2),
        out_specs=pl.BlockSpec(memory_space=pltpu.VMEM),
        compiler_params=pltpu.CompilerParams(vmem_limit_bytes=VMEM_BYTES),
        name="combine",
    )(parts, place)


def one_hot(at, length, limits):
    count = at.shape[1]
    parts, done = [], 0
    for low, high in limits:
        spot = lax.broadcasted_iota(jnp.int32, (high - low, count), 0) + low
        if low > done:
            parts.append(jnp.zeros((low - done, count), jnp.bfloat16))
        parts.append(jnp.where(spot == at, 1.0, 0.0).astype(jnp.bfloat16))
        done = high
    if length > done:
        parts.append(jnp.zeros((length - done, count), jnp.bfloat16))
    return jnp.concatenate(parts, axis=0)


def flat(value):
    return jnp.concatenate([value[i : i + 1, :] for i in range(value.shape[0])], axis=1)


def hits(side, halo, tall, wide, row, col):
    up = lambda n: -(-n // 16) * 16
    limits = ((0, up(side + halo)), (wide - up(halo), wide))
    return one_hot(flat(row), tall, ((0, tall),)), one_hot(flat(col), wide, limits)


def ranked(rank, row, values):
    sums = [0.0] * len(values)
    for tile in range(rank.shape[0]):
        here = rank[tile] == row
        sums = [total + jnp.where(here, v[tile], 0.0) for total, v in zip(sums, values)]
    return [jnp.sum(total, axis=0, keepdims=True) for total in sums]


def spots_kernel(
    side, halo, key_tiles, at_ref, parts_ref, rounds_ref, rank_ref, spot_ref, count_ref, hit_buf
):
    shares, tile_rows, _, _ = parts_ref.shape
    count = rank_ref.shape[1]
    rows = count // shares
    tall, wide = count_ref.shape

    def folded(at, length):
        return jnp.where(
            (at >= 0) & (at < side + halo), at, jnp.where((at < 0) & (at >= -halo), at + length, -1)
        )

    number = jnp.zeros((1, LANES), jnp.int32)
    point_row = lax.broadcasted_iota(jnp.int32, (count, LANES), 0)
    for i in range(tile_rows):
        for j in range(key_tiles):
            ids = jnp.concatenate(
                [parts_ref[k, i, pl.ds((4 + j) * rows, rows), :] for k in range(shares)], axis=0
            ).astype(jnp.int32)
            tile_of = lax.div(ids, side * side)
            within = lax.rem(ids, side * side)
            row = lax.div(tile_of, key_tiles) * side + lax.div(within, side) - at_ref[0]
            col = lax.rem(tile_of, key_tiles) * side + lax.rem(within, side) - at_ref[1]
            row, col = folded(row, side + 2 * halo), folded(col, wide)
            here = (row >= 0) & (col >= 0)
            hit = here.astype(jnp.int32)
            by = 1
            while by < count:
                hit = hit + jnp.where(point_row >= by, pltpu.roll(hit, by, 0), 0)
                by *= 2
            tile = i * key_tiles + at_ref[6 + tile_rows + j]
            rank_ref[tile] = jnp.where(here, number + hit - 1, -1)
            hit_buf[0, tile] = row.astype(jnp.float32) + 1.0
            hit_buf[1, tile] = col.astype(jnp.float32) + 1.0
            number = number + hit[count - 1 : count, :]
    rounds = lax.div(jnp.max(number) + ROUND - 1, ROUND)
    rounds_ref[0] = rounds
    count_ref[...] = jnp.zeros_like(count_ref)

    @pl.loop(0, rounds)
    def _(k):
        found = [ranked(rank_ref, k * ROUND + r, (hit_buf.at[0], hit_buf.at[1])) for r in range(ROUND)]
        row, col = (jnp.concatenate(v, axis=0).astype(jnp.int32) - 1 for v in zip(*found))
        spot_ref[k, 0] = row
        spot_ref[k, 1] = col
        row_hit, col_hit = hits(side, halo, tall, wide, row, col)
        count_ref[...] += nt_dot(row_hit, col_hit)


def spots(side, halo, key_tiles, wide, at, parts, rows):
    tall = -(-(side + 2 * halo) // 16) * 16
    count = parts.shape[0] * rows
    tiles = parts.shape[1] * key_tiles
    rounds = -(-tiles * count // ROUND)
    return pl.pallas_call(
        functools.partial(spots_kernel, side, halo, key_tiles),
        out_shape=(
            jax.ShapeDtypeStruct((1,), jnp.int32),
            jax.ShapeDtypeStruct((tiles, count, LANES), jnp.int32),
            jax.ShapeDtypeStruct((rounds, 2, ROUND, LANES), jnp.int32),
            jax.ShapeDtypeStruct((tall, wide), jnp.float32),
        ),
        in_specs=[in_smem()] + in_vmem(1),
        out_specs=(in_smem(),) + (pl.BlockSpec(memory_space=pltpu.VMEM),) * 3,
        scratch_shapes=[pltpu.VMEM((2, tiles, count, LANES), jnp.float32)],
        compiler_params=pltpu.CompilerParams(vmem_limit_bytes=VMEM_BYTES),
        cost_estimate=pl.CostEstimate(
            flops=8 * tall * ROUND * LANES * wide,
            bytes_accessed=8 * parts.size,
            transcendentals=0,
        ),
        name="spots",
    )(at, parts)


def vertex_sums(side, halo, rounds_ref, rank_ref, spot_ref, points_ref, sum_ref, point_buf):
    _, tall, wide = sum_ref.shape
    shares, tiles, both_rows, _ = points_ref.shape
    rows = both_rows // 2
    sum_ref[...] = jnp.zeros_like(sum_ref)
    for tile in range(tiles):
        for share in range(shares):
            for c in range(2):
                point_buf[c, tile, pl.ds(share * rows, rows), :] = points_ref[
                    share, tile, pl.ds(c * rows, rows), :
                ]

    @pl.loop(0, rounds_ref[0])
    def _(k):
        found = [
            ranked(rank_ref, k * ROUND + r, (point_buf.at[0], point_buf.at[1])) for r in range(ROUND)
        ]
        row_hit, col_hit = hits(side, halo, tall, wide, spot_ref[k, 0], spot_ref[k, 1])
        parts = []
        for value in zip(*found):
            value = jnp.concatenate(value, axis=1)
            high = value.astype(jnp.bfloat16)
            low = (value - high.astype(jnp.float32)).astype(jnp.bfloat16)
            parts += [row_hit * high, row_hit * low]
        summed = nt_dot(jnp.concatenate(parts, axis=0), col_hit)
        sum_ref[0] += summed[0:tall] + summed[tall : 2 * tall]
        sum_ref[1] += summed[2 * tall : 3 * tall] + summed[3 * tall :]


def sums_kernel(side, halo, rounds_ref, rank_ref, spot_ref, points_ref, out_ref, sum_ref, point_buf):
    vertex_sums(side, halo, rounds_ref, rank_ref, spot_ref, points_ref, sum_ref, point_buf)
    out_ref[...] = sum_ref[:, pl.ds(0, out_ref.shape[1]), :]


def relax_kernel(
    side,
    halo,
    extent,
    at_ref,
    rounds_ref,
    rank_ref,
    spot_ref,
    count_ref,
    points_ref,
    mesh_ref,
    out_ref,
    sum_ref,
    point_buf,
):
    vertex_sums(side, halo, rounds_ref, rank_ref, spot_ref, points_ref, sum_ref, point_buf)
    span = side + 2 * halo
    wide = sum_ref.shape[2]
    shape = (span, wide)
    row = lax.broadcasted_iota(jnp.int32, shape, 0)
    col = lax.broadcasted_iota(jnp.int32, shape, 1)
    row = jnp.where(row < side + halo, row, row - span) + at_ref[0]
    col = jnp.where(col < side + halo, col, col - wide) + at_ref[1]
    inside = (row >= 0) & (row < extent[0]) & (col >= 0) & (col < extent[1])
    own_pulled = (at_ref[2] == 0).astype(jnp.float32)
    linked = 1.0
    matched = count_ref[pl.ds(0, span), :]
    moving, gains, has, step = [], [], [], []
    for part, pulled in enumerate((own_pulled, 1.0 - own_pulled)):
        gain = mesh_ref[part * 3 + 2]
        diagonal = 4.0 * gain + spring_sec * linked + spring_match * matched * pulled
        gains.append(gain)
        has.append(matched * pulled)
        step.append(jnp.where(inside, relax_rate / diagonal, 0.0))
        moving.append(
            [(mesh_ref[part * 3 + c], sum_ref[c, pl.ds(0, span), :] * pulled) for c in range(2)]
        )
    for sweep in range(ITERS):
        later = []
        for part in range(2):
            row_of = []
            for c in range(2):
                u, pulled = moving[part][c]
                other = moving[1 - part][c][0]
                laplace = (
                    pltpu.roll(u, 1, 0)
                    + pltpu.roll(u, span - 1, 0)
                    + pltpu.roll(u, 1, 1)
                    + pltpu.roll(u, wide - 1, 1)
                    - 4.0 * u
                )
                force = (
                    gains[part] * laplace
                    + spring_sec * (other - linked * u)
                    + spring_match * (pulled - has[part] * u)
                )
                row_of.append((u + step[part] * force, pulled))
            later.append(row_of)
        moving = later
    for c in range(2):
        out_ref[c] = moving[0][c][0][0:side, 0:side]


def col_edges(value, halo):
    after = passed_along(value[:, :, :halo].swapaxes(1, 2), "tx", -1)
    before = passed_along(value[:, :, value.shape[2] - halo :].swapaxes(1, 2), "tx", 1)
    return jnp.concatenate([after, before], axis=1)


def sweeps(moving, gains, sums, number, at, side, halo, extent):
    sections = lax.axis_size("sec")
    sec_index = at[2]
    has_next = (sec_index < sections - 1).astype(jnp.float32)
    linked = (sec_index > 0).astype(jnp.float32) + has_next
    pulled, matched = sums * has_next, number * has_next
    span, wide = moving.shape[1:]
    row = jnp.arange(span)[:, None]
    col = jnp.arange(wide)[None, :]
    row = jnp.where(row < side + halo, row, row - span) + at[0]
    col = jnp.where(col < side + halo, col, col - wide) + at[1]
    inside = (row >= 0) & (row < extent[0]) & (col >= 0) & (col < extent[1])
    diagonal = 4.0 * gains + spring_sec * linked + spring_match * matched
    step = jnp.where(inside, relax_rate / jnp.where(inside, diagonal, 1.0), 0.0)
    for sweep in range(ITERS):
        lower_sec = passed_along(moving, "sec", 1)
        upper_sec = passed_along(moving, "sec", -1)
        laplace = (
            jnp.roll(moving, 1, 1)
            + jnp.roll(moving, -1, 1)
            + jnp.roll(moving, 1, 2)
            + jnp.roll(moving, -1, 2)
            - 4.0 * moving
        )
        force = (
            gains * laplace
            + spring_sec * (lower_sec + upper_sec - linked * moving)
            + spring_match * (pulled - matched * moving)
        )
        moving = moving + step * force
    return moving[:, :side, :side]


def pack_kernel(
    shares,
    tile_cols,
    desc_hbm,
    place_hbm,
    ids_hbm,
    list_hbm,
    count_hbm,
    first_ref,
    second_ref,
    place_ref,
    ids_ref,
    list_ref,
    count_ref,
    last_ref,
    sems,
):
    half = second_ref.shape[0]
    copies = [
        pltpu.make_async_copy(source, target, sems.at[i])
        for i, (source, target) in enumerate(
            (
                (place_hbm, place_ref),
                (ids_hbm, ids_ref),
                (list_hbm, list_ref),
                (count_hbm, count_ref),
                (desc_hbm.at[pl.ds(0, half), :], first_ref.at[pl.ds(0, half), :]),
                (desc_hbm.at[pl.ds(half, half), :], second_ref),
            )
        )
    ]
    for copy in copies:
        copy.start()
    for copy in copies[:4]:
        copy.wait()

    def cut(row):
        return [row[:, i : i + LANES] for i in range(0, row.shape[1], LANES)]

    place, ids, blocks = place_ref[...].astype(jnp.float32), ids_ref[...], list_ref[...]
    rows = cut(place[0:1]) + cut(place[1:2])
    for i in range(DIGITS):
        digit = lax.rem(lax.div(ids, BASE**i), BASE)
        rows += cut(digit.astype(jnp.float32))
    per_tile = place.shape[1] // BLK
    part = per_tile // shares
    tile, within = lax.div(blocks, per_tile), lax.rem(blocks, per_tile)
    device = lax.div(tile, tile_cols) * shares + lax.div(within, part)
    spot = lax.rem(tile, tile_cols) * part + lax.rem(within, part)
    live = lax.broadcasted_iota(jnp.int32, blocks.shape, 1) < count_ref[0, 0]
    last_ref[...] = jnp.full_like(last_ref, BASE - 1.0)
    last_ref[0:1, 0 : blocks.shape[1]] = jnp.where(live, device, BASE - 1).astype(jnp.float32)
    last_ref[1:2, 0 : blocks.shape[1]] = spot.astype(jnp.float32)
    count = first_ref.shape[0] - half
    gap = jnp.zeros((count - len(rows) - PLACE_ROWS, LANES), jnp.float32)
    rows += ([gap] if gap.shape[0] else []) + [last_ref[...]]
    first_ref[pl.ds(half, count), :] = jnp.concatenate(rows, axis=0).astype(jnp.bfloat16)
    for copy in copies[4:]:
        copy.wait()


def pack(desc, place, ids, blocks, count, shares, tile_cols):
    points, width = desc.shape
    half = points // 2
    rows = -(-(2 + DIGITS) * (points // LANES) // 16) * 16 + PLACE_ROWS
    return pl.pallas_call(
        functools.partial(pack_kernel, shares, tile_cols),
        out_shape=(
            jax.ShapeDtypeStruct((half + rows, width), jnp.bfloat16),
            jax.ShapeDtypeStruct((half, width), jnp.bfloat16),
        ),
        in_specs=[pl.BlockSpec(memory_space=pltpu.HBM)] * 5,
        out_specs=(pl.BlockSpec(memory_space=pltpu.VMEM),) * 2,
        scratch_shapes=[
            pltpu.VMEM(place.shape, place.dtype),
            pltpu.VMEM(ids.shape, ids.dtype),
            pltpu.VMEM(blocks.shape, blocks.dtype),
            pltpu.SMEM(count.shape, count.dtype),
            pltpu.VMEM((PLACE_ROWS, LANES), jnp.float32),
            pltpu.SemaphoreType.DMA((6,)),
        ],
        name="pack",
    )(desc, place, ids, blocks, count)


def turns(axis):
    devices, here = lax.axis_size(axis), lax.axis_index(axis)
    if devices & (devices - 1):
        pairs = [[(i, (i + j) % devices) for i in range(devices)] for j in range(1, devices)]
        return pairs, jnp.mod(here - jnp.arange(devices), devices)
    pairs = [[(i, i ^ j) for i in range(devices)] for j in range(1, devices)]
    return pairs, here ^ jnp.arange(devices)


def key_kernel(shares, sec_ref, first_ref, second_ref, other_ref, key_ref, place_ref):
    half = second_ref.shape[0]
    per_tile = 2 * half // LANES
    part = per_tile // shares
    own, other = first_ref, first_ref
    if shares == 2:
        other = other_ref
    at_first = sec_ref[0] == 0

    def rest(ref, share):
        rows = ref[pl.ds(half, (2 + DIGITS) * per_tile), :].astype(jnp.float32)
        kept = [
            rows[i * per_tile + share * part : i * per_tile + (share + 1) * part]
            for i in range(2 + DIGITS)
        ]
        return jnp.concatenate(kept[:2], axis=0), kept[2:]

    if shares == 2:
        keys = jnp.where(at_first, other[pl.ds(0, half), :], second_ref[...])
        key_ref[pl.ds(0, half), :] = keys
        (own_0, ids_0), (own_1, _) = rest(own, 0), rest(own, 1)
        (other_0, _), (other_1, ids_1) = rest(other, 0), rest(other, 1)
        key_place = jnp.where(at_first, other_0, own_1)
        place_ref[...] = jnp.where(at_first, own_0, other_1)
        ids = [jnp.where(at_first, a, b) for a, b in zip(ids_0, ids_1)]
    else:
        key_ref[pl.ds(0, half), :] = own[pl.ds(0, half), :]
        key_ref[pl.ds(half, half), :] = second_ref[...]
        key_place, _ = rest(own, 0)
        place_ref[...], ids = rest(other_ref, 0)
    done = part * BLK
    filler = jnp.zeros((-(2 + DIGITS) * part % 16, LANES), jnp.float32)
    rows = [key_place] + ids + ([filler] if filler.shape[0] else [])
    key_ref[pl.ds(done, key_ref.shape[0] - done), :] = jnp.concatenate(rows, axis=0).astype(
        jnp.bfloat16
    )


def key_payload(sec, first_half, second_half, other, shares):
    half, width = second_half.shape
    part = 2 * half // LANES // shares
    rows = part * BLK + -(-(2 + DIGITS) * part // 16) * 16
    return pl.pallas_call(
        functools.partial(key_kernel, shares),
        out_shape=(
            jax.ShapeDtypeStruct((rows, width), jnp.bfloat16),
            jax.ShapeDtypeStruct((2 * part, LANES), jnp.float32),
        ),
        in_specs=[in_smem()] + in_vmem(3),
        out_specs=(pl.BlockSpec(memory_space=pltpu.VMEM),) * 2,
        compiler_params=pltpu.CompilerParams(vmem_limit_bytes=VMEM_BYTES),
        name="key_payload",
    )(sec, first_half, second_half, other)


def query_kernel(shares, sec_ref, first_ref, second_ref, other_ref, came_ref, out_ref):
    half = second_ref.shape[0]
    last = first_ref.shape[0] - PLACE_ROWS

    def chosen(own, other):
        return jnp.where(sec_ref[0] == 0, own, other) if shares == 2 else other

    for target, rows in ((0, pl.ds(0, half)), (2 * half, pl.ds(last, PLACE_ROWS))):
        out_ref[pl.ds(target, rows.size), :] = chosen(first_ref[rows, :], other_ref[rows, :])
    out_ref[pl.ds(half, half), :] = chosen(second_ref[...], came_ref[...])


def query_payload(sec, first_half, second_half, other, came, shares):
    half, width = second_half.shape
    return pl.pallas_call(
        functools.partial(query_kernel, shares),
        out_shape=jax.ShapeDtypeStruct((2 * half + PLACE_ROWS, width), jnp.bfloat16),
        in_specs=[in_smem()] + in_vmem(4),
        out_specs=pl.BlockSpec(memory_space=pltpu.VMEM),
        compiler_params=pltpu.CompilerParams(vmem_limit_bytes=VMEM_BYTES),
        name="query_payload",
    )(sec, first_half, second_half, other, came)


def gathered(values, axes, beside):
    held, steps = [], []
    for value, axis in zip(values, axes):
        devices = lax.axis_size(axis)
        if devices & (devices - 1):
            moved = [lax.ppermute(value, axis, pairs) for pairs in turns(axis)[0]]
            held.append(dict(enumerate([value] + moved)))
            steps.append(0)
        else:
            held.append({0: value})
            steps.append(devices.bit_length() - 1)
    for step in range(1, max(steps) + 1):
        for i, axis in enumerate(axes):
            devices = lax.axis_size(axis)
            for at in range(devices - 1, 0, -1):
                if steps[i] and at.bit_count() == step:
                    by = at & -at
                    pairs = [(j, j ^ by) for j in range(devices)]
                    held[i][at] = lax.ppermute(held[i][at ^ by], axis, pairs)
        if step == 1:
            held, beside = lax.optimization_barrier((held, beside))
    return [[h[i] for i in range(len(h))] for h in held], beside


def per_device(
    descriptors, positions, vertex_ids, candidate_blocks, candidate_count, displacement, stiffness
):
    point_total, width = descriptors.shape[3:]
    per_tile = point_total // BLK
    tile_rows, tile_cols = lax.axis_size("ty"), lax.axis_size("tx")
    sections = lax.axis_size("sec")
    sec_index = lax.axis_index("sec")
    tiles = tile_rows * tile_cols
    side = displacement.shape[3]
    halo = ITERS
    span = side + 2 * halo
    wide = -(-span // LANES) * LANES
    cand = candidate_blocks.shape[3]
    shares = 2 if sections == 2 and per_tile % 2 == 0 else 1
    part = per_tile // shares
    key_rows = part * BLK

    first_half, second_half = pack(
        descriptors[0, 0, 0],
        positions[0, 0, 0],
        vertex_ids[0, 0],
        candidate_blocks[0, 0],
        candidate_count[0, 0][None],
        shares,
        tile_cols,
    )
    half = point_total // 2
    swap = [(i, 1 - i) for i in range(2)]

    sec = jnp.asarray(sec_index, jnp.int32)[None]
    own_mesh = jnp.concatenate([displacement[0], stiffness], axis=0)
    if shares == 2:
        share = sec_index
        other = lax.ppermute(first_half, "sec", swap)
    else:
        share = 0
        other = passed_along(first_half, "sec", 1)
    came = passed_along(second_half, "sec", 1)
    cols = col_edges(own_mesh, halo)
    key, place = key_payload(sec, first_half, second_half, other, shares)
    meshes = [own_mesh]
    if shares == 2:
        tied, key = lax.optimization_barrier((own_mesh, key))
        meshes.append(lax.ppermute(tied, "sec", swap))
    query = query_payload(sec, first_half, second_half, other, came, shares)
    (queries, keys), (cols, meshes) = gathered((query, key), ("ty", "tx"), (cols, meshes))
    at = jnp.concatenate(
        [
            jnp.stack([lax.axis_index("ty") * side, lax.axis_index("tx") * side, sec_index]),
            jnp.stack([lax.axis_index("ty"), jnp.asarray(share), jnp.asarray(shares)]),
            turns("ty")[1],
            turns("tx")[1],
        ]
    ).astype(jnp.int32)
    extent = (side * tile_rows, side * tile_cols)
    sum_shapes = [
        pltpu.VMEM((2, -(-span // 16) * 16, wide), jnp.float32),
        pltpu.VMEM((2, tiles, per_tile, LANES), jnp.float32),
    ]

    top, end = own_mesh[:, :halo], own_mesh[:, side - halo :]
    corners = [
        jnp.pad(v.swapaxes(1, 2), ((0, 0), (0, 0), (0, side - 2 * halo)))
        for v in (cols[:, :, :halo], cols[:, :, side - halo :])
    ]
    edges = [jnp.concatenate(v, axis=0) for v in ((top, corners[0]), (end, corners[1]))]
    edges = jnp.stack([v.reshape(-1, LANES) for v in edges + [cols]])
    parts = match(at, queries, keys, edges, 16.0 / width, shares, part)
    shape = parts.shape
    parts = exchanged(parts.reshape((-1,) + shape[2:]), ("sec", "ty") if shares == 2 else "ty")
    pulls = combine(parts, place, shares * tiles)
    parts, pulls, meshes = lax.optimization_barrier((parts, pulls, meshes))

    def edge_rows(by):
        near = lax.axis_index("ty") + by
        rows = parts.reshape(shape)[:, :, -edges.shape[1] :]
        rows = lax.dynamic_index_in_dim(rows, jnp.clip(near, 0, tile_rows - 1), 1, keepdims=False)
        rows = jnp.where((near >= 0) & (near < tile_rows), rows, 0.0)
        rows = rows.reshape(shares, 2, 3, halo, side)
        if shares == 2:
            rows = jnp.where(sec_index == 0, rows, rows[::-1])
        return [
            jnp.concatenate([rows[i, 0], rows[i, 1, :, :, : 2 * halo]], axis=2)
            for i in range(shares)
        ]

    after, before = edge_rows(1), edge_rows(-1)
    cols = [cols]
    if shares == 2:
        sent = parts.reshape(shape)[:, :, -edges.shape[1] :]
        sent = lax.dynamic_index_in_dim(sent, lax.axis_index("ty"), 1, keepdims=False)
        cols.append(jnp.where(sec_index == 0, sent[1], sent[0]).reshape(cols[0].shape))
    framed = []
    for i, mesh in enumerate(meshes):
        whole = jnp.concatenate([mesh, cols[i].swapaxes(1, 2)], axis=2)
        framed.append(jnp.concatenate([whole, after[i], before[i]], axis=1))
    framed = jnp.concatenate(framed, axis=0)
    gap = jnp.zeros(framed.shape[:2] + (wide - span,), framed.dtype)
    mesh_values = jnp.concatenate(
        [framed[:, :, : side + halo], gap, framed[:, :, side + halo :]], axis=2
    )
    if shares == 2:
        points = exchanged(pulls, ("sec", "ty", "tx"))
        rounds, rank, spot, number = spots(side, halo, tile_cols, wide, at, parts.reshape(shape), part)
        relaxed = pl.pallas_call(
            functools.partial(relax_kernel, side, halo, extent),
            out_shape=jax.ShapeDtypeStruct((2, side, side), jnp.float32),
            in_specs=[in_smem()] * 2 + in_vmem(5),
            out_specs=pl.BlockSpec(memory_space=pltpu.VMEM),
            scratch_shapes=sum_shapes,
            compiler_params=pltpu.CompilerParams(vmem_limit_bytes=VMEM_BYTES),
            name="relax",
        )(at, rounds, rank, spot, number, points.reshape(2, tiles, -1, LANES), mesh_values)
        return relaxed[None]

    points = passed_along(exchanged(pulls, ("ty", "tx")), "sec", -1)
    parts = passed_along(parts, "sec", -1)
    rounds, rank, spot, number = spots(side, halo, tile_cols, wide, at, parts[None], part)
    sums = pl.pallas_call(
        functools.partial(sums_kernel, side, halo),
        out_shape=jax.ShapeDtypeStruct((2, span, wide), jnp.float32),
        in_specs=[in_smem()] + in_vmem(3),
        out_specs=pl.BlockSpec(memory_space=pltpu.VMEM),
        scratch_shapes=sum_shapes,
        compiler_params=pltpu.CompilerParams(vmem_limit_bytes=VMEM_BYTES),
        name="sums",
    )(rounds, rank, spot, points[None])
    moving, gains = mesh_values[0:2], mesh_values[2]
    return sweeps(moving, gains, sums, number[:span], at, side, halo, extent)[None]


def solution(mesh):
    in_specs = (
        P("sec", "ty", "tx", None, None),
        P("sec", "ty", "tx", None, None),
        P("sec", "ty", "tx", None),
        P("sec", "ty", "tx", None),
        P("sec", "ty", "tx"),
        P("sec", None, "ty", "tx"),
        P("sec", "ty", "tx"),
    )
    out_specs = P("sec", None, "ty", "tx")
    return jax.shard_map(
        per_device, mesh=mesh, in_specs=in_specs, out_specs=out_specs, check_vma=False
    )
```

```python
import functools
import math

import jax
import jax.numpy as jnp
from jax import lax
from jax.experimental import pallas as pl
from jax.experimental.pallas import tpu as pltpu
from jax.sharding import PartitionSpec as P

BLK = 128
ITERS = 4
LANES = 128
PLACE_ROWS = 16
GROUP = 2
ROUND = 8
BASE = 256
DIGITS = 3
VMEM_BYTES = 24 * 1024 * 1024

spring_sec = 0.5
spring_match = 1.0
relax_rate = 0.8


def passed_along(value, axis, by):
    devices = lax.axis_size(axis)
    pairs = [(i, i + by) for i in range(devices) if 0 <= i + by < devices]
    return lax.ppermute(value, axis, pairs)


def exchanged(value, axes):
    return lax.all_to_all(value, axes, split_axis=0, concat_axis=0, tiled=True)


def spread(value, axes):
    copies = jnp.broadcast_to(value[None], (lax.axis_size(axes),) + value.shape)
    return exchanged(copies, axes)


def nt_dot(a, b):
    return lax.dot_general(a, b, (((1,), (1,)), ((), ())), preferred_element_type=jnp.float32)


def in_vmem(count):
    return [pl.BlockSpec(memory_space=pltpu.VMEM)] * count


def in_smem():
    return pl.BlockSpec(memory_space=pltpu.SMEM)


def match_kernel(scale, plan, last, at_ref, *refs):
    tile_rows = max(i for i, _ in plan) + 1
    key_tiles = max(max(among) for _, among in plan if among) + 1
    query_refs, refs = refs[:tile_rows], refs[tile_rows:]
    rest_refs, refs = refs[:tile_rows], refs[tile_rows:]
    key_refs, refs = refs[:key_tiles], refs[key_tiles:]
    if last:
        before_ref, edge_ref, out_ref = refs[:3]
        refs = refs[3:]
    else:
        (out_ref,) = refs[:1]
        refs = refs[1:]
    query_buf, key_buf, place_buf, state_buf, list_buf = refs
    point_total = state_buf.shape[2]
    all_tiles, key_rows = key_buf.shape[:2]
    part = key_rows // BLK
    total = all_tiles * part
    own_row, share, shares = at_ref[3], at_ref[4], at_ref[5]
    rows_at, cols_at = 6, 6 + query_buf.shape[0]

    number = 0
    for tile, among in plan:
        met = [at_ref[cols_at + i] for i in among]
        listed = rest_refs[tile][pl.ds(point_total // 2, PLACE_ROWS), :]
        listed = listed.astype(jnp.float32).astype(jnp.int32)
        here = listed[0:1] == own_row * shares + share
        for low in range(0, total, 16):
            place = listed[1:2] - low
            bits = jnp.where(here & (place >= 0) & (place < 16), 1 << jnp.clip(place, 0, 15), 0)
            bits = jnp.sum(bits)
            for i in range(low, min(low + 16, total)):
                allowed = functools.reduce(jnp.logical_or, [col == i // part for col in met])
                list_buf[number] = tile * total + i
                number = number + jnp.where(allowed, (bits >> (i - low)) & 1, 0)
        list_buf[number] = -1
        number = number + lax.rem(number, 2)
    for i in range(2 * GROUP):
        list_buf[number + i] = -1
    groups = lax.div(number + 2 * GROUP - 1, 2 * GROUP)

    row_at = lax.broadcasted_iota(jnp.int32, (PLACE_ROWS, LANES), 0)
    ids = []
    for tile, key_ref in enumerate(key_refs):
        col = at_ref[cols_at + tile]
        key_buf[col] = key_ref[pl.ds(0, key_rows), :]
        rest = key_ref[pl.ds(key_rows, key_ref.shape[0] - key_rows), :].astype(jnp.float32)
        for j in range(part):
            x, y = rest[j : j + 1, :], rest[part + j : part + j + 1, :]
            stacked = jnp.where(
                row_at == 0, x, jnp.where(row_at == 1, y, jnp.where(row_at == 2, 1.0, 0.0))
            )
            place_buf[col * part + j] = stacked.astype(jnp.bfloat16)
        digits = [rest[(2 + i) * part : (3 + i) * part] for i in range(DIGITS)]
        ids.append(sum(digit * float(BASE**i) for i, digit in enumerate(digits)))
    half = point_total // 2
    for tile in range(tile_rows):
        query_buf[tile, pl.ds(0, half), :] = query_refs[tile][...]
        query_buf[tile, pl.ds(half, half), :] = rest_refs[tile][pl.ds(0, half), :]

    state_row = lax.broadcasted_iota(jnp.int32, state_buf.shape[1:], 0)
    for tile in range(tile_rows):
        if last and tile < before_ref.shape[0]:
            state_buf[tile] = before_ref[tile]
        else:
            state_buf[tile] = jnp.where(state_row == 3, -1e30, 0.0)

    def item(at):
        codes = [list_buf[2 * at + i] for i in range(2)]
        tile = lax.div(jnp.maximum(codes[0], 0), total)
        keys, places = [], []
        for i, code in enumerate(codes):
            block = lax.rem(jnp.maximum(jnp.where(code >= 0, code, codes[0]), 0), total)
            block = jnp.where(codes[0] >= 0, block, at_ref[cols_at] * part)
            start = pl.multiple_of(lax.rem(block, part) * BLK, BLK)
            keys.append(key_buf[lax.div(block, part), pl.ds(start, BLK), :])
            kept = jnp.where(code >= 0, 1.0, 0.0).astype(jnp.bfloat16)
            places.append(place_buf[block] * kept)
        return tile, codes[0] >= 0, jnp.concatenate(keys, axis=0), jnp.concatenate(places, axis=1)

    @pl.loop(0, groups)
    def _(group):
        items = [item(group * GROUP + i) for i in range(GROUP)]
        scores = [nt_dot(keys, query_buf[tile]) * scale for tile, _, keys, _ in items]
        tops = [jnp.max(score, axis=0, keepdims=True) for score in scores]
        weights = [jnp.exp2((s - top).astype(jnp.bfloat16)) for s, top in zip(scores, tops)]
        sums = [
            jnp.dot(place, weight, preferred_element_type=jnp.float32)[0:8]
            for (_, _, _, place), weight in zip(items, weights)
        ]
        for (tile, live, _, _), top, added in zip(items, tops, sums):
            top = jnp.where(live, top, -1e30)
            state = state_buf[tile]
            before = state[3:4, :]
            both = jnp.maximum(before, top)
            state = state * jnp.exp2(before - both) + added * jnp.exp2(top - both)
            state_buf[tile] = jnp.where(state_row == 3, both, state)

    if not last:
        out_ref[...] = state_buf[pl.ds(0, tile_rows)]
        return
    edge_rows = edge_ref.shape[1]
    for tile in range(tile_rows):
        to = at_ref[rows_at + tile]
        for row in range(point_total // LANES):
            lanes = pl.ds(row * LANES, LANES)
            for place, held in enumerate((3, 2, 0, 1)):
                out_ref[row // part, to, pl.ds(place * part + row % part, 1), :] = state_buf[
                    tile, pl.ds(held, 1), lanes
                ]
        for share in range(out_ref.shape[0]):
            out_ref[share, tile, pl.ds(4 * part, key_tiles * part), :] = jnp.concatenate(ids, axis=0)
            out_ref[share, tile, pl.ds((4 + key_tiles) * part, edge_rows), :] = jnp.where(
                tile > own_row, edge_ref[1], jnp.where(tile < own_row, edge_ref[0], edge_ref[2])
            )


def match(at, queries, rests, keys, edges, score_factor, shares, part):
    tile_rows, key_tiles = len(queries), len(keys)
    point_total, width = 2 * queries[0].shape[0], queries[0].shape[1]
    total = key_tiles * part

    def call(plan, out_shape, *more):
        many_rows = max(i for i, _ in plan) + 1
        many_keys = max(max(among) for _, among in plan if among) + 1
        scores = sum(len(among) for _, among in plan) * part * point_total * BLK
        return pl.pallas_call(
            functools.partial(
                match_kernel, score_factor * math.log2(math.e), plan, len(more) > 0
            ),
            out_shape=jax.ShapeDtypeStruct(out_shape, jnp.float32),
            in_specs=[in_smem()] + in_vmem(2 * many_rows + many_keys + len(more)),
            out_specs=pl.BlockSpec(memory_space=pltpu.VMEM),
            scratch_shapes=[
                pltpu.VMEM((tile_rows, point_total, width), jnp.bfloat16),
                pltpu.VMEM((key_tiles, part * BLK, width), jnp.bfloat16),
                pltpu.VMEM((total, PLACE_ROWS, LANES), jnp.bfloat16),
                pltpu.VMEM((tile_rows, 8, point_total), jnp.float32),
                pltpu.SMEM((tile_rows * (total + 1) + 2 * GROUP + 1,), jnp.int32),
            ],
            compiler_params=pltpu.CompilerParams(vmem_limit_bytes=VMEM_BYTES),
            cost_estimate=pl.CostEstimate(
                flops=scores * width, bytes_accessed=4 * scores // BLK, transcendentals=scores // 4
            ),
            name="match_rest" if more else "match",
        )(at, *queries[:many_rows], *rests[:many_rows], *keys[:many_keys], *more)

    there = [
        [i for i in range(n) if i.bit_count() < 2 or n & (n - 1)] for n in (tile_rows, key_tiles)
    ]
    first = [(i, tuple(there[1])) for i in there[0]]
    rest = [(i, tuple(j for j in range(key_tiles) if j not in there[1])) for i in there[0]]
    rest = [v for v in rest if v[1]]
    rest += [(i, tuple(range(key_tiles))) for i in range(tile_rows) if i not in there[0]]
    if rest:
        state = call(first, (len(first), 8, point_total))
    else:
        rest, row = first, jnp.arange(8)[None, :, None]
        state = jnp.where(row == 3, -1e30, jnp.zeros((tile_rows, 8, point_total), jnp.float32))
    shape = (shares, tile_rows, (4 + key_tiles) * part + edges.shape[1], LANES)
    return call(rest, shape, state, edges)


def combine_kernel(parts_ref, place_ref, out_ref):
    parts = parts_ref.shape[0]
    rows = place_ref.shape[0] // 2
    tops = [parts_ref[i, 0:rows, :] for i in range(parts)]
    top = functools.reduce(jnp.maximum, tops)
    total = x = y = jnp.zeros_like(top)
    for i in range(parts):
        gain = jnp.exp2(tops[i] - top)
        total += gain * parts_ref[i, rows : 2 * rows, :]
        x += gain * parts_ref[i, 2 * rows : 3 * rows, :]
        y += gain * parts_ref[i, 3 * rows : 4 * rows, :]
    pull = jnp.concatenate([x / total, y / total], axis=0) - place_ref[...]
    for i in range(out_ref.shape[0]):
        out_ref[i] = pull


def combine(parts, place, copies):
    return pl.pallas_call(
        combine_kernel,
        out_shape=jax.ShapeDtypeStruct((copies,) + place.shape, jnp.float32),
        in_specs=in_vmem(2),
        out_specs=pl.BlockSpec(memory_space=pltpu.VMEM),
        compiler_params=pltpu.CompilerParams(vmem_limit_bytes=VMEM_BYTES),
        name="combine",
    )(parts, place)


def one_hot(at, length, limits):
    count = at.shape[1]
    parts, done = [], 0
    for low, high in limits:
        spot = lax.broadcasted_iota(jnp.int32, (high - low, count), 0) + low
        if low > done:
            parts.append(jnp.zeros((low - done, count), jnp.bfloat16))
        parts.append(jnp.where(spot == at, 1.0, 0.0).astype(jnp.bfloat16))
        done = high
    if length > done:
        parts.append(jnp.zeros((length - done, count), jnp.bfloat16))
    return jnp.concatenate(parts, axis=0)


def flat(value):
    return jnp.concatenate([value[i : i + 1, :] for i in range(value.shape[0])], axis=1)


def hits(side, halo, tall, wide, row, col):
    up = lambda n: -(-n // 16) * 16
    limits = ((0, up(side + halo)), (wide - up(halo), wide))
    return one_hot(flat(row), tall, ((0, tall),)), one_hot(flat(col), wide, limits)


def ranked(rank, row, values):
    sums = [0.0] * len(values)
    for tile in range(rank.shape[0]):
        here = rank[tile] == row
        sums = [total + jnp.where(here, v[tile], 0.0) for total, v in zip(sums, values)]
    return [jnp.sum(total, axis=0, keepdims=True) for total in sums]


def spots_kernel(
    side, halo, key_tiles, at_ref, parts_ref, rounds_ref, rank_ref, spot_ref, count_ref, hit_buf
):
    shares, tile_rows, _, _ = parts_ref.shape
    count = rank_ref.shape[1]
    rows = count // shares
    tall, wide = count_ref.shape

    def folded(at, length):
        return jnp.where(
            (at >= 0) & (at < side + halo), at, jnp.where((at < 0) & (at >= -halo), at + length, -1)
        )

    number = jnp.zeros((1, LANES), jnp.int32)
    point_row = lax.broadcasted_iota(jnp.int32, (count, LANES), 0)
    for i in range(tile_rows):
        for j in range(key_tiles):
            ids = jnp.concatenate(
                [parts_ref[k, i, pl.ds((4 + j) * rows, rows), :] for k in range(shares)], axis=0
            ).astype(jnp.int32)
            tile_of = lax.div(ids, side * side)
            within = lax.rem(ids, side * side)
            row = lax.div(tile_of, key_tiles) * side + lax.div(within, side) - at_ref[0]
            col = lax.rem(tile_of, key_tiles) * side + lax.rem(within, side) - at_ref[1]
            row, col = folded(row, side + 2 * halo), folded(col, wide)
            here = (row >= 0) & (col >= 0)
            hit = here.astype(jnp.int32)
            by = 1
            while by < count:
                hit = hit + jnp.where(point_row >= by, pltpu.roll(hit, by, 0), 0)
                by *= 2
            tile = i * key_tiles + at_ref[6 + tile_rows + j]
            rank_ref[tile] = jnp.where(here, number + hit - 1, -1)
            hit_buf[0, tile] = row.astype(jnp.float32) + 1.0
            hit_buf[1, tile] = col.astype(jnp.float32) + 1.0
            number = number + hit[count - 1 : count, :]
    rounds = lax.div(jnp.max(number) + ROUND - 1, ROUND)
    rounds_ref[0] = rounds
    count_ref[...] = jnp.zeros_like(count_ref)

    @pl.loop(0, rounds)
    def _(k):
        found = [ranked(rank_ref, k * ROUND + r, (hit_buf.at[0], hit_buf.at[1])) for r in range(ROUND)]
        row, col = (jnp.concatenate(v, axis=0).astype(jnp.int32) - 1 for v in zip(*found))
        spot_ref[k, 0] = row
        spot_ref[k, 1] = col
        row_hit, col_hit = hits(side, halo, tall, wide, row, col)
        count_ref[...] += nt_dot(row_hit, col_hit)


def spots(side, halo, key_tiles, wide, at, parts, rows):
    tall = -(-(side + 2 * halo) // 16) * 16
    count = parts.shape[0] * rows
    tiles = parts.shape[1] * key_tiles
    rounds = -(-tiles * count // ROUND)
    return pl.pallas_call(
        functools.partial(spots_kernel, side, halo, key_tiles),
        out_shape=(
            jax.ShapeDtypeStruct((1,), jnp.int32),
            jax.ShapeDtypeStruct((tiles, count, LANES), jnp.int32),
            jax.ShapeDtypeStruct((rounds, 2, ROUND, LANES), jnp.int32),
            jax.ShapeDtypeStruct((tall, wide), jnp.float32),
        ),
        in_specs=[in_smem()] + in_vmem(1),
        out_specs=(in_smem(),) + (pl.BlockSpec(memory_space=pltpu.VMEM),) * 3,
        scratch_shapes=[pltpu.VMEM((2, tiles, count, LANES), jnp.float32)],
        compiler_params=pltpu.CompilerParams(vmem_limit_bytes=VMEM_BYTES),
        cost_estimate=pl.CostEstimate(
            flops=8 * tall * ROUND * LANES * wide,
            bytes_accessed=8 * parts.size,
            transcendentals=0,
        ),
        name="spots",
    )(at, parts)


def vertex_sums(side, halo, rounds_ref, rank_ref, spot_ref, points_ref, sum_ref, point_buf):
    _, tall, wide = sum_ref.shape
    shares, tiles, both_rows, _ = points_ref.shape
    rows = both_rows // 2
    sum_ref[...] = jnp.zeros_like(sum_ref)
    for tile in range(tiles):
        for share in range(shares):
            for c in range(2):
                point_buf[c, tile, pl.ds(share * rows, rows), :] = points_ref[
                    share, tile, pl.ds(c * rows, rows), :
                ]

    @pl.loop(0, rounds_ref[0])
    def _(k):
        found = [
            ranked(rank_ref, k * ROUND + r, (point_buf.at[0], point_buf.at[1])) for r in range(ROUND)
        ]
        row_hit, col_hit = hits(side, halo, tall, wide, spot_ref[k, 0], spot_ref[k, 1])
        parts = []
        for value in zip(*found):
            value = jnp.concatenate(value, axis=1)
            high = value.astype(jnp.bfloat16)
            low = (value - high.astype(jnp.float32)).astype(jnp.bfloat16)
            parts += [row_hit * high, row_hit * low]
        summed = nt_dot(jnp.concatenate(parts, axis=0), col_hit)
        sum_ref[0] += summed[0:tall] + summed[tall : 2 * tall]
        sum_ref[1] += summed[2 * tall : 3 * tall] + summed[3 * tall :]


def sums_kernel(side, halo, rounds_ref, rank_ref, spot_ref, points_ref, out_ref, sum_ref, point_buf):
    vertex_sums(side, halo, rounds_ref, rank_ref, spot_ref, points_ref, sum_ref, point_buf)
    out_ref[...] = sum_ref[:, pl.ds(0, out_ref.shape[1]), :]


def relax_kernel(
    side,
    halo,
    extent,
    at_ref,
    rounds_ref,
    rank_ref,
    spot_ref,
    count_ref,
    points_ref,
    mesh_ref,
    out_ref,
    sum_ref,
    point_buf,
):
    vertex_sums(side, halo, rounds_ref, rank_ref, spot_ref, points_ref, sum_ref, point_buf)
    span = side + 2 * halo
    wide = sum_ref.shape[2]
    shape = (span, wide)
    row = lax.broadcasted_iota(jnp.int32, shape, 0)
    col = lax.broadcasted_iota(jnp.int32, shape, 1)
    row = jnp.where(row < side + halo, row, row - span) + at_ref[0]
    col = jnp.where(col < side + halo, col, col - wide) + at_ref[1]
    inside = (row >= 0) & (row < extent[0]) & (col >= 0) & (col < extent[1])
    own_pulled = (at_ref[2] == 0).astype(jnp.float32)
    linked = 1.0
    matched = count_ref[pl.ds(0, span), :]
    moving, gains, has, step = [], [], [], []
    for part, pulled in enumerate((own_pulled, 1.0 - own_pulled)):
        gain = mesh_ref[part * 3 + 2]
        diagonal = 4.0 * gain + spring_sec * linked + spring_match * matched * pulled
        gains.append(gain)
        has.append(matched * pulled)
        step.append(jnp.where(inside, relax_rate / diagonal, 0.0))
        moving.append(
            [(mesh_ref[part * 3 + c], sum_ref[c, pl.ds(0, span), :] * pulled) for c in range(2)]
        )
    for sweep in range(ITERS):
        later = []
        for part in range(2):
            row_of = []
            for c in range(2):
                u, pulled = moving[part][c]
                other = moving[1 - part][c][0]
                laplace = (
                    pltpu.roll(u, 1, 0)
                    + pltpu.roll(u, span - 1, 0)
                    + pltpu.roll(u, 1, 1)
                    + pltpu.roll(u, wide - 1, 1)
                    - 4.0 * u
                )
                force = (
                    gains[part] * laplace
                    + spring_sec * (other - linked * u)
                    + spring_match * (pulled - has[part] * u)
                )
                row_of.append((u + step[part] * force, pulled))
            later.append(row_of)
        moving = later
    for c in range(2):
        out_ref[c] = moving[0][c][0][0:side, 0:side]


def col_edges(value, halo):
    after = passed_along(value[:, :, :halo].swapaxes(1, 2), "tx", -1)
    before = passed_along(value[:, :, value.shape[2] - halo :].swapaxes(1, 2), "tx", 1)
    return jnp.concatenate([after, before], axis=1)


def sweeps(moving, gains, sums, number, at, side, halo, extent):
    sections = lax.axis_size("sec")
    sec_index = at[2]
    has_next = (sec_index < sections - 1).astype(jnp.float32)
    linked = (sec_index > 0).astype(jnp.float32) + has_next
    pulled, matched = sums * has_next, number * has_next
    span, wide = moving.shape[1:]
    row = jnp.arange(span)[:, None]
    col = jnp.arange(wide)[None, :]
    row = jnp.where(row < side + halo, row, row - span) + at[0]
    col = jnp.where(col < side + halo, col, col - wide) + at[1]
    inside = (row >= 0) & (row < extent[0]) & (col >= 0) & (col < extent[1])
    diagonal = 4.0 * gains + spring_sec * linked + spring_match * matched
    step = jnp.where(inside, relax_rate / jnp.where(inside, diagonal, 1.0), 0.0)
    for sweep in range(ITERS):
        lower_sec = passed_along(moving, "sec", 1)
        upper_sec = passed_along(moving, "sec", -1)
        laplace = (
            jnp.roll(moving, 1, 1)
            + jnp.roll(moving, -1, 1)
            + jnp.roll(moving, 1, 2)
            + jnp.roll(moving, -1, 2)
            - 4.0 * moving
        )
        force = (
            gains * laplace
            + spring_sec * (lower_sec + upper_sec - linked * moving)
            + spring_match * (pulled - matched * moving)
        )
        moving = moving + step * force
    return moving[:, :side, :side]


def pack_kernel(
    shares,
    tile_cols,
    desc_hbm,
    place_hbm,
    ids_hbm,
    list_hbm,
    count_hbm,
    first_ref,
    second_ref,
    place_ref,
    ids_ref,
    list_ref,
    count_ref,
    last_ref,
    sems,
):
    half = second_ref.shape[0]
    copies = [
        pltpu.make_async_copy(source, target, sems.at[i])
        for i, (source, target) in enumerate(
            (
                (place_hbm, place_ref),
                (ids_hbm, ids_ref),
                (list_hbm, list_ref),
                (count_hbm, count_ref),
                (desc_hbm.at[pl.ds(0, half), :], first_ref.at[pl.ds(0, half), :]),
                (desc_hbm.at[pl.ds(half, half), :], second_ref),
            )
        )
    ]
    for copy in copies:
        copy.start()
    for copy in copies[:4]:
        copy.wait()

    def cut(row):
        return [row[:, i : i + LANES] for i in range(0, row.shape[1], LANES)]

    place, ids, blocks = place_ref[...].astype(jnp.float32), ids_ref[...], list_ref[...]
    rows = cut(place[0:1]) + cut(place[1:2])
    for i in range(DIGITS):
        digit = lax.rem(lax.div(ids, BASE**i), BASE)
        rows += cut(digit.astype(jnp.float32))
    per_tile = place.shape[1] // BLK
    part = per_tile // shares
    tile, within = lax.div(blocks, per_tile), lax.rem(blocks, per_tile)
    device = lax.div(tile, tile_cols) * shares + lax.div(within, part)
    spot = lax.rem(tile, tile_cols) * part + lax.rem(within, part)
    live = lax.broadcasted_iota(jnp.int32, blocks.shape, 1) < count_ref[0, 0]
    last_ref[...] = jnp.full_like(last_ref, BASE - 1.0)
    last_ref[0:1, 0 : blocks.shape[1]] = jnp.where(live, device, BASE - 1).astype(jnp.float32)
    last_ref[1:2, 0 : blocks.shape[1]] = spot.astype(jnp.float32)
    count = first_ref.shape[0] - half
    gap = jnp.zeros((count - len(rows) - PLACE_ROWS, LANES), jnp.float32)
    rows += ([gap] if gap.shape[0] else []) + [last_ref[...]]
    first_ref[pl.ds(half, count), :] = jnp.concatenate(rows, axis=0).astype(jnp.bfloat16)
    for copy in copies[4:]:
        copy.wait()


def pack(desc, place, ids, blocks, count, shares, tile_cols):
    points, width = desc.shape
    half = points // 2
    rows = -(-(2 + DIGITS) * (points // LANES) // 16) * 16 + PLACE_ROWS
    return pl.pallas_call(
        functools.partial(pack_kernel, shares, tile_cols),
        out_shape=(
            jax.ShapeDtypeStruct((half + rows, width), jnp.bfloat16),
            jax.ShapeDtypeStruct((half, width), jnp.bfloat16),
        ),
        in_specs=[pl.BlockSpec(memory_space=pltpu.HBM)] * 5,
        out_specs=(pl.BlockSpec(memory_space=pltpu.VMEM),) * 2,
        scratch_shapes=[
            pltpu.VMEM(place.shape, place.dtype),
            pltpu.VMEM(ids.shape, ids.dtype),
            pltpu.VMEM(blocks.shape, blocks.dtype),
            pltpu.SMEM(count.shape, count.dtype),
            pltpu.VMEM((PLACE_ROWS, LANES), jnp.float32),
            pltpu.SemaphoreType.DMA((6,)),
        ],
        name="pack",
    )(desc, place, ids, blocks, count)


def turns(axis):
    devices, here = lax.axis_size(axis), lax.axis_index(axis)
    if devices & (devices - 1):
        pairs = [[(i, (i + j) % devices) for i in range(devices)] for j in range(1, devices)]
        return pairs, jnp.mod(here - jnp.arange(devices), devices)
    pairs = [[(i, i ^ j) for i in range(devices)] for j in range(1, devices)]
    return pairs, here ^ jnp.arange(devices)


def key_kernel(
    shares, sec_ref, first_ref, second_ref, other_ref, key_ref, place_ref, query_ref
):
    half = second_ref.shape[0]
    per_tile = 2 * half // LANES
    part = per_tile // shares
    own, other = first_ref, first_ref
    if shares == 2:
        other = other_ref
    at_first = sec_ref[0] == 0

    def rest(ref, share):
        rows = ref[pl.ds(half, (2 + DIGITS) * per_tile), :].astype(jnp.float32)
        kept = [
            rows[i * per_tile + share * part : i * per_tile + (share + 1) * part]
            for i in range(2 + DIGITS)
        ]
        return jnp.concatenate(kept[:2], axis=0), kept[2:]

    queries = other_ref[pl.ds(0, half), :]
    if shares == 2:
        keys = jnp.where(at_first, queries, second_ref[...])
        key_ref[pl.ds(0, half), :] = keys
        queries = jnp.where(at_first, own[pl.ds(0, half), :], queries)
        (own_0, ids_0), (own_1, _) = rest(own, 0), rest(own, 1)
        (other_0, _), (other_1, ids_1) = rest(other, 0), rest(other, 1)
        key_place = jnp.where(at_first, other_0, own_1)
        place_ref[...] = jnp.where(at_first, own_0, other_1)
        ids = [jnp.where(at_first, a, b) for a, b in zip(ids_0, ids_1)]
    else:
        key_ref[pl.ds(0, half), :] = own[pl.ds(0, half), :]
        key_ref[pl.ds(half, half), :] = second_ref[...]
        key_place, _ = rest(own, 0)
        place_ref[...], ids = rest(other_ref, 0)
    query_ref[...] = queries
    done = part * BLK
    filler = jnp.zeros((-(2 + DIGITS) * part % 16, LANES), jnp.float32)
    rows = [key_place] + ids + ([filler] if filler.shape[0] else [])
    key_ref[pl.ds(done, key_ref.shape[0] - done), :] = jnp.concatenate(rows, axis=0).astype(
        jnp.bfloat16
    )


def key_payload(sec, first_half, second_half, other, shares):
    half, width = second_half.shape
    part = 2 * half // LANES // shares
    rows = part * BLK + -(-(2 + DIGITS) * part // 16) * 16
    return pl.pallas_call(
        functools.partial(key_kernel, shares),
        out_shape=(
            jax.ShapeDtypeStruct((rows, width), jnp.bfloat16),
            jax.ShapeDtypeStruct((2 * part, LANES), jnp.float32),
            jax.ShapeDtypeStruct((half, width), jnp.bfloat16),
        ),
        in_specs=[in_smem()] + in_vmem(3),
        out_specs=(pl.BlockSpec(memory_space=pltpu.VMEM),) * 3,
        compiler_params=pltpu.CompilerParams(vmem_limit_bytes=VMEM_BYTES),
        name="key_payload",
    )(sec, first_half, second_half, other)


def query_kernel(shares, sec_ref, first_ref, second_ref, other_ref, came_ref, out_ref):
    half = second_ref.shape[0]
    last = first_ref.shape[0] - PLACE_ROWS

    def chosen(own, other):
        return jnp.where(sec_ref[0] == 0, own, other) if shares == 2 else other

    rows = pl.ds(last, PLACE_ROWS)
    out_ref[pl.ds(0, half), :] = chosen(second_ref[...], came_ref[...])
    out_ref[pl.ds(half, PLACE_ROWS), :] = chosen(first_ref[rows, :], other_ref[rows, :])


def query_payload(sec, first_half, second_half, other, came, shares):
    half, width = second_half.shape
    return pl.pallas_call(
        functools.partial(query_kernel, shares),
        out_shape=jax.ShapeDtypeStruct((half + PLACE_ROWS, width), jnp.bfloat16),
        in_specs=[in_smem()] + in_vmem(4),
        out_specs=pl.BlockSpec(memory_space=pltpu.VMEM),
        compiler_params=pltpu.CompilerParams(vmem_limit_bytes=VMEM_BYTES),
        name="query_payload",
    )(sec, first_half, second_half, other, came)


def gathered(values, axes, beside):
    held, steps = [], []
    for value, axis in zip(values, axes):
        devices = lax.axis_size(axis)
        if devices & (devices - 1):
            moved = [lax.ppermute(value, axis, pairs) for pairs in turns(axis)[0]]
            held.append(dict(enumerate([value] + moved)))
            steps.append(0)
        else:
            held.append({0: value})
            steps.append(devices.bit_length() - 1)
    for step in range(1, max(steps) + 1):
        for i, axis in enumerate(axes):
            devices = lax.axis_size(axis)
            for at in range(devices - 1, 0, -1):
                if steps[i] and at.bit_count() == step:
                    by = at & -at
                    pairs = [(j, j ^ by) for j in range(devices)]
                    held[i][at] = lax.ppermute(held[i][at ^ by], axis, pairs)
        if step == 1:
            held, beside = lax.optimization_barrier((held, beside))
    return [[h[i] for i in range(len(h))] for h in held], beside


def per_device(
    descriptors, positions, vertex_ids, candidate_blocks, candidate_count, displacement, stiffness
):
    point_total, width = descriptors.shape[3:]
    per_tile = point_total // BLK
    tile_rows, tile_cols = lax.axis_size("ty"), lax.axis_size("tx")
    sections = lax.axis_size("sec")
    sec_index = lax.axis_index("sec")
    tiles = tile_rows * tile_cols
    side = displacement.shape[3]
    halo = ITERS
    span = side + 2 * halo
    wide = -(-span // LANES) * LANES
    cand = candidate_blocks.shape[3]
    shares = 2 if sections == 2 and per_tile % 2 == 0 else 1
    part = per_tile // shares
    key_rows = part * BLK

    first_half, second_half = pack(
        descriptors[0, 0, 0],
        positions[0, 0, 0],
        vertex_ids[0, 0],
        candidate_blocks[0, 0],
        candidate_count[0, 0][None],
        shares,
        tile_cols,
    )
    half = point_total // 2
    swap = [(i, 1 - i) for i in range(2)]

    sec = jnp.asarray(sec_index, jnp.int32)[None]
    own_mesh = jnp.concatenate([displacement[0], stiffness], axis=0)
    if shares == 2:
        share = sec_index
        other = lax.ppermute(first_half, "sec", swap)
    else:
        share = 0
        other = passed_along(first_half, "sec", 1)
    came = passed_along(second_half, "sec", 1)
    cols = col_edges(own_mesh, halo)
    key, place, query = key_payload(sec, first_half, second_half, other, shares)
    meshes = [own_mesh]
    if shares == 2:
        tied, key = lax.optimization_barrier((own_mesh, key))
        meshes.append(lax.ppermute(tied, "sec", swap))
    query_rest = query_payload(sec, first_half, second_half, other, came, shares)
    (keys, queries, rests), (cols, meshes) = gathered(
        (key, query, query_rest), ("tx", "ty", "ty"), (cols, meshes)
    )
    at = jnp.concatenate(
        [
            jnp.stack([lax.axis_index("ty") * side, lax.axis_index("tx") * side, sec_index]),
            jnp.stack([lax.axis_index("ty"), jnp.asarray(share), jnp.asarray(shares)]),
            turns("ty")[1],
            turns("tx")[1],
        ]
    ).astype(jnp.int32)
    extent = (side * tile_rows, side * tile_cols)
    sum_shapes = [
        pltpu.VMEM((2, -(-span // 16) * 16, wide), jnp.float32),
        pltpu.VMEM((2, tiles, per_tile, LANES), jnp.float32),
    ]

    top, end = own_mesh[:, :halo], own_mesh[:, side - halo :]
    corners = [
        jnp.pad(v.swapaxes(1, 2), ((0, 0), (0, 0), (0, side - 2 * halo)))
        for v in (cols[:, :, :halo], cols[:, :, side - halo :])
    ]
    edges = [jnp.concatenate(v, axis=0) for v in ((top, corners[0]), (end, corners[1]))]
    edges = jnp.stack([v.reshape(-1, LANES) for v in edges + [cols]])
    parts = match(at, queries, rests, keys, edges, 16.0 / width, shares, part)
    shape = parts.shape
    parts = exchanged(parts.reshape((-1,) + shape[2:]), ("sec", "ty") if shares == 2 else "ty")
    pulls = combine(parts, place, shares * tiles)
    parts, pulls, meshes = lax.optimization_barrier((parts, pulls, meshes))

    def edge_rows(by):
        near = lax.axis_index("ty") + by
        rows = parts.reshape(shape)[:, :, -edges.shape[1] :]
        rows = lax.dynamic_index_in_dim(rows, jnp.clip(near, 0, tile_rows - 1), 1, keepdims=False)
        rows = jnp.where((near >= 0) & (near < tile_rows), rows, 0.0)
        rows = rows.reshape(shares, 2, 3, halo, side)
        if shares == 2:
            rows = jnp.where(sec_index == 0, rows, rows[::-1])
        return [
            jnp.concatenate([rows[i, 0], rows[i, 1, :, :, : 2 * halo]], axis=2)
            for i in range(shares)
        ]

    after, before = edge_rows(1), edge_rows(-1)
    cols = [cols]
    if shares == 2:
        sent = parts.reshape(shape)[:, :, -edges.shape[1] :]
        sent = lax.dynamic_index_in_dim(sent, lax.axis_index("ty"), 1, keepdims=False)
        cols.append(jnp.where(sec_index == 0, sent[1], sent[0]).reshape(cols[0].shape))
    framed = []
    for i, mesh in enumerate(meshes):
        whole = jnp.concatenate([mesh, cols[i].swapaxes(1, 2)], axis=2)
        framed.append(jnp.concatenate([whole, after[i], before[i]], axis=1))
    framed = jnp.concatenate(framed, axis=0)
    gap = jnp.zeros(framed.shape[:2] + (wide - span,), framed.dtype)
    mesh_values = jnp.concatenate(
        [framed[:, :, : side + halo], gap, framed[:, :, side + halo :]], axis=2
    )
    if shares == 2:
        points = exchanged(pulls, ("sec", "ty", "tx"))
        rounds, rank, spot, number = spots(side, halo, tile_cols, wide, at, parts.reshape(shape), part)
        relaxed = pl.pallas_call(
            functools.partial(relax_kernel, side, halo, extent),
            out_shape=jax.ShapeDtypeStruct((2, side, side), jnp.float32),
            in_specs=[in_smem()] * 2 + in_vmem(5),
            out_specs=pl.BlockSpec(memory_space=pltpu.VMEM),
            scratch_shapes=sum_shapes,
            compiler_params=pltpu.CompilerParams(vmem_limit_bytes=VMEM_BYTES),
            name="relax",
        )(at, rounds, rank, spot, number, points.reshape(2, tiles, -1, LANES), mesh_values)
        return relaxed[None]

    points = passed_along(exchanged(pulls, ("ty", "tx")), "sec", -1)
    parts = passed_along(parts, "sec", -1)
    rounds, rank, spot, number = spots(side, halo, tile_cols, wide, at, parts[None], part)
    sums = pl.pallas_call(
        functools.partial(sums_kernel, side, halo),
        out_shape=jax.ShapeDtypeStruct((2, span, wide), jnp.float32),
        in_specs=[in_smem()] + in_vmem(3),
        out_specs=pl.BlockSpec(memory_space=pltpu.VMEM),
        scratch_shapes=sum_shapes,
        compiler_params=pltpu.CompilerParams(vmem_limit_bytes=VMEM_BYTES),
        name="sums",
    )(rounds, rank, spot, points[None])
    moving, gains = mesh_values[0:2], mesh_values[2]
    return sweeps(moving, gains, sums, number[:span], at, side, halo, extent)[None]


def solution(mesh):
    in_specs = (
        P("sec", "ty", "tx", None, None),
        P("sec", "ty", "tx", None, None),
        P("sec", "ty", "tx", None),
        P("sec", "ty", "tx", None),
        P("sec", "ty", "tx"),
        P("sec", None, "ty", "tx"),
        P("sec", "ty", "tx"),
    )
    out_specs = P("sec", None, "ty", "tx")
    return jax.shard_map(
        per_device, mesh=mesh, in_specs=in_specs, out_specs=out_specs, check_vma=False
    )
```

```python
import functools
import math

import jax
import jax.numpy as jnp
from jax import lax
from jax.experimental import pallas as pl
from jax.experimental.pallas import tpu as pltpu
from jax.sharding import PartitionSpec as P

BLK = 128
ITERS = 4
LANES = 128
PLACE_ROWS = 16
GROUP = 2
ROUND = 8
BASE = 256
DIGITS = 3
VMEM_BYTES = 24 * 1024 * 1024

spring_sec = 0.5
spring_match = 1.0
relax_rate = 0.8


def passed_along(value, axis, by):
    devices = lax.axis_size(axis)
    pairs = [(i, i + by) for i in range(devices) if 0 <= i + by < devices]
    return lax.ppermute(value, axis, pairs)


def exchanged(value, axes):
    return lax.all_to_all(value, axes, split_axis=0, concat_axis=0, tiled=True)


def spread(value, axes):
    copies = jnp.broadcast_to(value[None], (lax.axis_size(axes),) + value.shape)
    return exchanged(copies, axes)


def nt_dot(a, b):
    return lax.dot_general(a, b, (((1,), (1,)), ((), ())), preferred_element_type=jnp.float32)


def in_vmem(count):
    return [pl.BlockSpec(memory_space=pltpu.VMEM)] * count


def in_smem():
    return pl.BlockSpec(memory_space=pltpu.SMEM)


def match_kernel(scale, plan, last, at_ref, *refs):
    tile_rows = max(i for i, _ in plan) + 1
    key_tiles = max(max(among) for _, among in plan if among) + 1
    query_refs, refs = refs[:tile_rows], refs[tile_rows:]
    key_refs, refs = refs[:key_tiles], refs[key_tiles:]
    if last:
        before_ref, edge_ref, out_ref = refs[:3]
        refs = refs[3:]
    else:
        (out_ref,) = refs[:1]
        refs = refs[1:]
    query_buf, key_buf, place_buf, state_buf, list_buf = refs
    point_total = state_buf.shape[2]
    all_tiles, key_rows = key_buf.shape[:2]
    part = key_rows // BLK
    total = all_tiles * part
    own_row, share, shares = at_ref[3], at_ref[4], at_ref[5]
    rows_at, cols_at = 6, 6 + query_buf.shape[0]

    number = 0
    for tile, among in plan:
        met = [at_ref[cols_at + i] for i in among]
        listed = query_refs[tile][pl.ds(key_buf.shape[2], PLACE_ROWS), pl.ds(0, LANES)]
        listed = listed.astype(jnp.float32).astype(jnp.int32)
        here = listed[0:1] == own_row * shares + share
        for low in range(0, total, 16):
            place = listed[1:2] - low
            bits = jnp.where(here & (place >= 0) & (place < 16), 1 << jnp.clip(place, 0, 15), 0)
            bits = jnp.sum(bits)
            for i in range(low, min(low + 16, total)):
                allowed = functools.reduce(jnp.logical_or, [col == i // part for col in met])
                list_buf[number] = tile * total + i
                number = number + jnp.where(allowed, (bits >> (i - low)) & 1, 0)
        list_buf[number] = -1
        number = number + lax.rem(number, 2)
    for i in range(2 * GROUP):
        list_buf[number + i] = -1
    groups = lax.div(number + 2 * GROUP - 1, 2 * GROUP)

    row_at = lax.broadcasted_iota(jnp.int32, (PLACE_ROWS, LANES), 0)
    ids = []
    for tile, key_ref in enumerate(key_refs):
        col = at_ref[cols_at + tile]
        key_buf[col] = key_ref[pl.ds(0, key_rows), :]
        rest = key_ref[pl.ds(key_rows, key_ref.shape[0] - key_rows), :].astype(jnp.float32)
        for j in range(part):
            x, y = rest[j : j + 1, :], rest[part + j : part + j + 1, :]
            stacked = jnp.where(
                row_at == 0, x, jnp.where(row_at == 1, y, jnp.where(row_at == 2, 1.0, 0.0))
            )
            place_buf[col * part + j] = stacked.astype(jnp.bfloat16)
        digits = [rest[(2 + i) * part : (3 + i) * part] for i in range(DIGITS)]
        ids.append(sum(digit * float(BASE**i) for i, digit in enumerate(digits)))
    for tile, query_ref in enumerate(query_refs):
        query_buf[tile] = query_ref[pl.ds(0, key_buf.shape[2]), :]

    state_row = lax.broadcasted_iota(jnp.int32, state_buf.shape[1:], 0)
    for tile in range(tile_rows):
        if last and tile < before_ref.shape[0]:
            state_buf[tile] = before_ref[tile]
        else:
            state_buf[tile] = jnp.where(state_row == 3, -1e30, 0.0)

    def item(at):
        codes = [list_buf[2 * at + i] for i in range(2)]
        tile = lax.div(jnp.maximum(codes[0], 0), total)
        keys, places = [], []
        for i, code in enumerate(codes):
            block = lax.rem(jnp.maximum(jnp.where(code >= 0, code, codes[0]), 0), total)
            block = jnp.where(codes[0] >= 0, block, at_ref[cols_at] * part)
            start = pl.multiple_of(lax.rem(block, part) * BLK, BLK)
            keys.append(key_buf[lax.div(block, part), pl.ds(start, BLK), :])
            kept = jnp.where(code >= 0, 1.0, 0.0).astype(jnp.bfloat16)
            places.append(place_buf[block] * kept)
        return tile, codes[0] >= 0, jnp.concatenate(keys, axis=0), jnp.concatenate(places, axis=1)

    @pl.loop(0, groups)
    def _(group):
        items = [item(group * GROUP + i) for i in range(GROUP)]
        scores = [
            jnp.dot(keys, query_buf[tile], preferred_element_type=jnp.float32) * scale
            for tile, _, keys, _ in items
        ]
        tops = [jnp.max(score, axis=0, keepdims=True) for score in scores]
        weights = [jnp.exp2(s - top).astype(jnp.bfloat16) for s, top in zip(scores, tops)]
        sums = [
            jnp.dot(place, weight, preferred_element_type=jnp.float32)[0:8]
            for (_, _, _, place), weight in zip(items, weights)
        ]
        for (tile, live, _, _), top, added in zip(items, tops, sums):
            top = jnp.where(live, top, -1e30)
            state = state_buf[tile]
            before = state[3:4, :]
            both = jnp.maximum(before, top)
            state = state * jnp.exp2(before - both) + added * jnp.exp2(top - both)
            state_buf[tile] = jnp.where(state_row == 3, both, state)

    if not last:
        out_ref[...] = state_buf[pl.ds(0, tile_rows)]
        return
    edge_rows = edge_ref.shape[1]
    for tile in range(tile_rows):
        to = at_ref[rows_at + tile]
        for row in range(point_total // LANES):
            lanes = pl.ds(row * LANES, LANES)
            for place, held in enumerate((3, 2, 0, 1)):
                out_ref[row // part, to, pl.ds(place * part + row % part, 1), :] = state_buf[
                    tile, pl.ds(held, 1), lanes
                ]
        for share in range(out_ref.shape[0]):
            out_ref[share, tile, pl.ds(4 * part, key_tiles * part), :] = jnp.concatenate(ids, axis=0)
            out_ref[share, tile, pl.ds((4 + key_tiles) * part, edge_rows), :] = jnp.where(
                tile > own_row, edge_ref[1], jnp.where(tile < own_row, edge_ref[0], edge_ref[2])
            )


def match(at, queries, keys, edges, score_factor, shares, part):
    tile_rows, key_tiles = len(queries), len(keys)
    point_total, width = queries[0].shape[1], queries[0].shape[0] - PLACE_ROWS
    total = key_tiles * part

    def call(plan, out_shape, *more):
        many_rows = max(i for i, _ in plan) + 1
        many_keys = max(max(among) for _, among in plan if among) + 1
        scores = sum(len(among) for _, among in plan) * part * point_total * BLK
        return pl.pallas_call(
            functools.partial(
                match_kernel, score_factor * math.log2(math.e), plan, len(more) > 0
            ),
            out_shape=jax.ShapeDtypeStruct(out_shape, jnp.float32),
            in_specs=[in_smem()] + in_vmem(many_rows + many_keys + len(more)),
            out_specs=pl.BlockSpec(memory_space=pltpu.VMEM),
            scratch_shapes=[
                pltpu.VMEM((tile_rows, width, point_total), jnp.bfloat16),
                pltpu.VMEM((key_tiles, part * BLK, width), jnp.bfloat16),
                pltpu.VMEM((total, PLACE_ROWS, LANES), jnp.bfloat16),
                pltpu.VMEM((tile_rows, 8, point_total), jnp.float32),
                pltpu.SMEM((tile_rows * (total + 1) + 2 * GROUP + 1,), jnp.int32),
            ],
            compiler_params=pltpu.CompilerParams(vmem_limit_bytes=VMEM_BYTES),
            cost_estimate=pl.CostEstimate(
                flops=scores * width, bytes_accessed=4 * scores // BLK, transcendentals=scores // 4
            ),
            name="match_rest" if more else "match",
        )(at, *queries[:many_rows], *keys[:many_keys], *more)

    there = [
        [i for i in range(n) if i.bit_count() < 2 or n & (n - 1)] for n in (tile_rows, key_tiles)
    ]
    first = [(i, tuple(there[1])) for i in there[0]]
    rest = [(i, tuple(j for j in range(key_tiles) if j not in there[1])) for i in there[0]]
    rest = [v for v in rest if v[1]]
    rest += [(i, tuple(range(key_tiles))) for i in range(tile_rows) if i not in there[0]]
    if rest:
        state = call(first, (len(first), 8, point_total))
    else:
        rest, row = first, jnp.arange(8)[None, :, None]
        state = jnp.where(row == 3, -1e30, jnp.zeros((tile_rows, 8, point_total), jnp.float32))
    shape = (shares, tile_rows, (4 + key_tiles) * part + edges.shape[1], LANES)
    return call(rest, shape, state, edges)


def combine_kernel(parts_ref, place_ref, out_ref):
    parts = parts_ref.shape[0]
    rows = place_ref.shape[0] // 2
    tops = [parts_ref[i, 0:rows, :] for i in range(parts)]
    top = functools.reduce(jnp.maximum, tops)
    total = x = y = jnp.zeros_like(top)
    for i in range(parts):
        gain = jnp.exp2(tops[i] - top)
        total += gain * parts_ref[i, rows : 2 * rows, :]
        x += gain * parts_ref[i, 2 * rows : 3 * rows, :]
        y += gain * parts_ref[i, 3 * rows : 4 * rows, :]
    pull = jnp.concatenate([x / total, y / total], axis=0) - place_ref[...]
    for i in range(out_ref.shape[0]):
        out_ref[i] = pull


def combine(parts, place, copies):
    return pl.pallas_call(
        combine_kernel,
        out_shape=jax.ShapeDtypeStruct((copies,) + place.shape, jnp.float32),
        in_specs=in_vmem(2),
        out_specs=pl.BlockSpec(memory_space=pltpu.VMEM),
        compiler_params=pltpu.CompilerParams(vmem_limit_bytes=VMEM_BYTES),
        name="combine",
    )(parts, place)


def one_hot(at, length, limits):
    count = at.shape[1]
    parts, done = [], 0
    for low, high in limits:
        spot = lax.broadcasted_iota(jnp.int32, (high - low, count), 0) + low
        if low > done:
            parts.append(jnp.zeros((low - done, count), jnp.bfloat16))
        parts.append(jnp.where(spot == at, 1.0, 0.0).astype(jnp.bfloat16))
        done = high
    if length > done:
        parts.append(jnp.zeros((length - done, count), jnp.bfloat16))
    return jnp.concatenate(parts, axis=0)


def flat(value):
    return jnp.concatenate([value[i : i + 1, :] for i in range(value.shape[0])], axis=1)


def hits(side, halo, tall, wide, row, col):
    up = lambda n: -(-n // 16) * 16
    limits = ((0, up(side + halo)), (wide - up(halo), wide))
    return one_hot(flat(row), tall, ((0, tall),)), one_hot(flat(col), wide, limits)


def ranked(rank, row, values):
    sums = [0.0] * len(values)
    for tile in range(rank.shape[0]):
        here = rank[tile] == row
        sums = [total + jnp.where(here, v[tile], 0.0) for total, v in zip(sums, values)]
    return [jnp.sum(total, axis=0, keepdims=True) for total in sums]


def spots_kernel(
    side, halo, key_tiles, at_ref, parts_ref, rounds_ref, rank_ref, spot_ref, count_ref, hit_buf
):
    shares, tile_rows, _, _ = parts_ref.shape
    count = rank_ref.shape[1]
    rows = count // shares
    tall, wide = count_ref.shape

    def folded(at, length):
        return jnp.where(
            (at >= 0) & (at < side + halo), at, jnp.where((at < 0) & (at >= -halo), at + length, -1)
        )

    number = jnp.zeros((1, LANES), jnp.int32)
    point_row = lax.broadcasted_iota(jnp.int32, (count, LANES), 0)
    for i in range(tile_rows):
        for j in range(key_tiles):
            ids = jnp.concatenate(
                [parts_ref[k, i, pl.ds((4 + j) * rows, rows), :] for k in range(shares)], axis=0
            ).astype(jnp.int32)
            tile_of = lax.div(ids, side * side)
            within = lax.rem(ids, side * side)
            row = lax.div(tile_of, key_tiles) * side + lax.div(within, side) - at_ref[0]
            col = lax.rem(tile_of, key_tiles) * side + lax.rem(within, side) - at_ref[1]
            row, col = folded(row, side + 2 * halo), folded(col, wide)
            here = (row >= 0) & (col >= 0)
            hit = here.astype(jnp.int32)
            by = 1
            while by < count:
                hit = hit + jnp.where(point_row >= by, pltpu.roll(hit, by, 0), 0)
                by *= 2
            tile = i * key_tiles + at_ref[6 + tile_rows + j]
            rank_ref[tile] = jnp.where(here, number + hit - 1, -1)
            hit_buf[0, tile] = row.astype(jnp.float32) + 1.0
            hit_buf[1, tile] = col.astype(jnp.float32) + 1.0
            number = number + hit[count - 1 : count, :]
    rounds = lax.div(jnp.max(number) + ROUND - 1, ROUND)
    rounds_ref[0] = rounds
    count_ref[...] = jnp.zeros_like(count_ref)

    @pl.loop(0, rounds)
    def _(k):
        found = [ranked(rank_ref, k * ROUND + r, (hit_buf.at[0], hit_buf.at[1])) for r in range(ROUND)]
        row, col = (jnp.concatenate(v, axis=0).astype(jnp.int32) - 1 for v in zip(*found))
        spot_ref[k, 0] = row
        spot_ref[k, 1] = col
        row_hit, col_hit = hits(side, halo, tall, wide, row, col)
        count_ref[...] += nt_dot(row_hit, col_hit)


def spots(side, halo, key_tiles, wide, at, parts, rows):
    tall = -(-(side + 2 * halo) // 16) * 16
    count = parts.shape[0] * rows
    tiles = parts.shape[1] * key_tiles
    rounds = -(-tiles * count // ROUND)
    return pl.pallas_call(
        functools.partial(spots_kernel, side, halo, key_tiles),
        out_shape=(
            jax.ShapeDtypeStruct((1,), jnp.int32),
            jax.ShapeDtypeStruct((tiles, count, LANES), jnp.int32),
            jax.ShapeDtypeStruct((rounds, 2, ROUND, LANES), jnp.int32),
            jax.ShapeDtypeStruct((tall, wide), jnp.float32),
        ),
        in_specs=[in_smem()] + in_vmem(1),
        out_specs=(in_smem(),) + (pl.BlockSpec(memory_space=pltpu.VMEM),) * 3,
        scratch_shapes=[pltpu.VMEM((2, tiles, count, LANES), jnp.float32)],
        compiler_params=pltpu.CompilerParams(vmem_limit_bytes=VMEM_BYTES),
        cost_estimate=pl.CostEstimate(
            flops=8 * tall * ROUND * LANES * wide,
            bytes_accessed=8 * parts.size,
            transcendentals=0,
        ),
        name="spots",
    )(at, parts)


def vertex_sums(side, halo, rounds_ref, rank_ref, spot_ref, points_ref, sum_ref, point_buf):
    _, tall, wide = sum_ref.shape
    shares, tiles, both_rows, _ = points_ref.shape
    rows = both_rows // 2
    sum_ref[...] = jnp.zeros_like(sum_ref)
    for tile in range(tiles):
        for share in range(shares):
            for c in range(2):
                point_buf[c, tile, pl.ds(share * rows, rows), :] = points_ref[
                    share, tile, pl.ds(c * rows, rows), :
                ]

    @pl.loop(0, rounds_ref[0])
    def _(k):
        found = [
            ranked(rank_ref, k * ROUND + r, (point_buf.at[0], point_buf.at[1])) for r in range(ROUND)
        ]
        row_hit, col_hit = hits(side, halo, tall, wide, spot_ref[k, 0], spot_ref[k, 1])
        parts = []
        for value in zip(*found):
            value = jnp.concatenate(value, axis=1)
            high = value.astype(jnp.bfloat16)
            low = (value - high.astype(jnp.float32)).astype(jnp.bfloat16)
            parts += [row_hit * high, row_hit * low]
        summed = nt_dot(jnp.concatenate(parts, axis=0), col_hit)
        sum_ref[0] += summed[0:tall] + summed[tall : 2 * tall]
        sum_ref[1] += summed[2 * tall : 3 * tall] + summed[3 * tall :]


def sums_kernel(side, halo, rounds_ref, rank_ref, spot_ref, points_ref, out_ref, sum_ref, point_buf):
    vertex_sums(side, halo, rounds_ref, rank_ref, spot_ref, points_ref, sum_ref, point_buf)
    out_ref[...] = sum_ref[:, pl.ds(0, out_ref.shape[1]), :]


def relax_kernel(
    side,
    halo,
    extent,
    at_ref,
    rounds_ref,
    rank_ref,
    spot_ref,
    count_ref,
    points_ref,
    mesh_ref,
    out_ref,
    sum_ref,
    point_buf,
):
    vertex_sums(side, halo, rounds_ref, rank_ref, spot_ref, points_ref, sum_ref, point_buf)
    span = side + 2 * halo
    wide = sum_ref.shape[2]
    shape = (span, wide)
    row = lax.broadcasted_iota(jnp.int32, shape, 0)
    col = lax.broadcasted_iota(jnp.int32, shape, 1)
    row = jnp.where(row < side + halo, row, row - span) + at_ref[0]
    col = jnp.where(col < side + halo, col, col - wide) + at_ref[1]
    inside = (row >= 0) & (row < extent[0]) & (col >= 0) & (col < extent[1])
    own_pulled = (at_ref[2] == 0).astype(jnp.float32)
    linked = 1.0
    matched = count_ref[pl.ds(0, span), :]
    moving, gains, has, step = [], [], [], []
    for part, pulled in enumerate((own_pulled, 1.0 - own_pulled)):
        gain = mesh_ref[part * 3 + 2]
        diagonal = 4.0 * gain + spring_sec * linked + spring_match * matched * pulled
        gains.append(gain)
        has.append(matched * pulled)
        step.append(jnp.where(inside, relax_rate / diagonal, 0.0))
        moving.append(
            [(mesh_ref[part * 3 + c], sum_ref[c, pl.ds(0, span), :] * pulled) for c in range(2)]
        )
    for sweep in range(ITERS):
        later = []
        for part in range(2):
            row_of = []
            for c in range(2):
                u, pulled = moving[part][c]
                other = moving[1 - part][c][0]
                laplace = (
                    pltpu.roll(u, 1, 0)
                    + pltpu.roll(u, span - 1, 0)
                    + pltpu.roll(u, 1, 1)
                    + pltpu.roll(u, wide - 1, 1)
                    - 4.0 * u
                )
                force = (
                    gains[part] * laplace
                    + spring_sec * (other - linked * u)
                    + spring_match * (pulled - has[part] * u)
                )
                row_of.append((u + step[part] * force, pulled))
            later.append(row_of)
        moving = later
    for c in range(2):
        out_ref[c] = moving[0][c][0][0:side, 0:side]


def col_edges(value, halo):
    after = passed_along(value[:, :, :halo].swapaxes(1, 2), "tx", -1)
    before = passed_along(value[:, :, value.shape[2] - halo :].swapaxes(1, 2), "tx", 1)
    return jnp.concatenate([after, before], axis=1)


def sweeps(moving, gains, sums, number, at, side, halo, extent):
    sections = lax.axis_size("sec")
    sec_index = at[2]
    has_next = (sec_index < sections - 1).astype(jnp.float32)
    linked = (sec_index > 0).astype(jnp.float32) + has_next
    pulled, matched = sums * has_next, number * has_next
    span, wide = moving.shape[1:]
    row = jnp.arange(span)[:, None]
    col = jnp.arange(wide)[None, :]
    row = jnp.where(row < side + halo, row, row - span) + at[0]
    col = jnp.where(col < side + halo, col, col - wide) + at[1]
    inside = (row >= 0) & (row < extent[0]) & (col >= 0) & (col < extent[1])
    diagonal = 4.0 * gains + spring_sec * linked + spring_match * matched
    step = jnp.where(inside, relax_rate / jnp.where(inside, diagonal, 1.0), 0.0)
    for sweep in range(ITERS):
        lower_sec = passed_along(moving, "sec", 1)
        upper_sec = passed_along(moving, "sec", -1)
        laplace = (
            jnp.roll(moving, 1, 1)
            + jnp.roll(moving, -1, 1)
            + jnp.roll(moving, 1, 2)
            + jnp.roll(moving, -1, 2)
            - 4.0 * moving
        )
        force = (
            gains * laplace
            + spring_sec * (lower_sec + upper_sec - linked * moving)
            + spring_match * (pulled - matched * moving)
        )
        moving = moving + step * force
    return moving[:, :side, :side]


def pack_kernel(
    shares,
    tile_cols,
    desc_hbm,
    place_hbm,
    ids_hbm,
    list_hbm,
    count_hbm,
    first_ref,
    second_ref,
    place_ref,
    ids_ref,
    list_ref,
    count_ref,
    last_ref,
    sems,
):
    half = second_ref.shape[0]
    copies = [
        pltpu.make_async_copy(source, target, sems.at[i])
        for i, (source, target) in enumerate(
            (
                (place_hbm, place_ref),
                (ids_hbm, ids_ref),
                (list_hbm, list_ref),
                (count_hbm, count_ref),
                (desc_hbm.at[pl.ds(0, half), :], first_ref.at[pl.ds(0, half), :]),
                (desc_hbm.at[pl.ds(half, half), :], second_ref),
            )
        )
    ]
    for copy in copies:
        copy.start()
    for copy in copies[:4]:
        copy.wait()

    def cut(row):
        return [row[:, i : i + LANES] for i in range(0, row.shape[1], LANES)]

    place, ids, blocks = place_ref[...].astype(jnp.float32), ids_ref[...], list_ref[...]
    rows = cut(place[0:1]) + cut(place[1:2])
    for i in range(DIGITS):
        digit = lax.rem(lax.div(ids, BASE**i), BASE)
        rows += cut(digit.astype(jnp.float32))
    per_tile = place.shape[1] // BLK
    part = per_tile // shares
    tile, within = lax.div(blocks, per_tile), lax.rem(blocks, per_tile)
    device = lax.div(tile, tile_cols) * shares + lax.div(within, part)
    spot = lax.rem(tile, tile_cols) * part + lax.rem(within, part)
    live = lax.broadcasted_iota(jnp.int32, blocks.shape, 1) < count_ref[0, 0]
    last_ref[...] = jnp.full_like(last_ref, BASE - 1.0)
    last_ref[0:1, 0 : blocks.shape[1]] = jnp.where(live, device, BASE - 1).astype(jnp.float32)
    last_ref[1:2, 0 : blocks.shape[1]] = spot.astype(jnp.float32)
    count = first_ref.shape[0] - half
    gap = jnp.zeros((count - len(rows) - PLACE_ROWS, LANES), jnp.float32)
    rows += ([gap] if gap.shape[0] else []) + [last_ref[...]]
    first_ref[pl.ds(half, count), :] = jnp.concatenate(rows, axis=0).astype(jnp.bfloat16)
    for copy in copies[4:]:
        copy.wait()


def pack(desc, place, ids, blocks, count, shares, tile_cols):
    points, width = desc.shape
    half = points // 2
    rows = -(-(2 + DIGITS) * (points // LANES) // 16) * 16 + PLACE_ROWS
    return pl.pallas_call(
        functools.partial(pack_kernel, shares, tile_cols),
        out_shape=(
            jax.ShapeDtypeStruct((half + rows, width), jnp.bfloat16),
            jax.ShapeDtypeStruct((half, width), jnp.bfloat16),
        ),
        in_specs=[pl.BlockSpec(memory_space=pltpu.HBM)] * 5,
        out_specs=(pl.BlockSpec(memory_space=pltpu.VMEM),) * 2,
        scratch_shapes=[
            pltpu.VMEM(place.shape, place.dtype),
            pltpu.VMEM(ids.shape, ids.dtype),
            pltpu.VMEM(blocks.shape, blocks.dtype),
            pltpu.SMEM(count.shape, count.dtype),
            pltpu.VMEM((PLACE_ROWS, LANES), jnp.float32),
            pltpu.SemaphoreType.DMA((6,)),
        ],
        name="pack",
    )(desc, place, ids, blocks, count)


def turns(axis):
    devices, here = lax.axis_size(axis), lax.axis_index(axis)
    if devices & (devices - 1):
        pairs = [[(i, (i + j) % devices) for i in range(devices)] for j in range(1, devices)]
        return pairs, jnp.mod(here - jnp.arange(devices), devices)
    pairs = [[(i, i ^ j) for i in range(devices)] for j in range(1, devices)]
    return pairs, here ^ jnp.arange(devices)


def key_kernel(shares, sec_ref, first_ref, second_ref, other_ref, key_ref, place_ref):
    half = second_ref.shape[0]
    per_tile = 2 * half // LANES
    part = per_tile // shares
    own, other = first_ref, first_ref
    if shares == 2:
        other = other_ref
    at_first = sec_ref[0] == 0

    def rest(ref, share):
        rows = ref[pl.ds(half, (2 + DIGITS) * per_tile), :].astype(jnp.float32)
        kept = [
            rows[i * per_tile + share * part : i * per_tile + (share + 1) * part]
            for i in range(2 + DIGITS)
        ]
        return jnp.concatenate(kept[:2], axis=0), kept[2:]

    if shares == 2:
        keys = jnp.where(at_first, other[pl.ds(0, half), :], second_ref[...])
        key_ref[pl.ds(0, half), :] = keys
        (own_0, ids_0), (own_1, _) = rest(own, 0), rest(own, 1)
        (other_0, _), (other_1, ids_1) = rest(other, 0), rest(other, 1)
        key_place = jnp.where(at_first, other_0, own_1)
        place_ref[...] = jnp.where(at_first, own_0, other_1)
        ids = [jnp.where(at_first, a, b) for a, b in zip(ids_0, ids_1)]
    else:
        key_ref[pl.ds(0, half), :] = own[pl.ds(0, half), :]
        key_ref[pl.ds(half, half), :] = second_ref[...]
        key_place, _ = rest(own, 0)
        place_ref[...], ids = rest(other_ref, 0)
    done = part * BLK
    filler = jnp.zeros((-(2 + DIGITS) * part % 16, LANES), jnp.float32)
    rows = [key_place] + ids + ([filler] if filler.shape[0] else [])
    key_ref[pl.ds(done, key_ref.shape[0] - done), :] = jnp.concatenate(rows, axis=0).astype(
        jnp.bfloat16
    )


def key_payload(sec, first_half, second_half, other, shares):
    half, width = second_half.shape
    part = 2 * half // LANES // shares
    rows = part * BLK + -(-(2 + DIGITS) * part // 16) * 16
    return pl.pallas_call(
        functools.partial(key_kernel, shares),
        out_shape=(
            jax.ShapeDtypeStruct((rows, width), jnp.bfloat16),
            jax.ShapeDtypeStruct((2 * part, LANES), jnp.float32),
        ),
        in_specs=[in_smem()] + in_vmem(3),
        out_specs=(pl.BlockSpec(memory_space=pltpu.VMEM),) * 2,
        compiler_params=pltpu.CompilerParams(vmem_limit_bytes=VMEM_BYTES),
        name="key_payload",
    )(sec, first_half, second_half, other)


def query_kernel(shares, sec_ref, first_ref, second_ref, other_ref, came_ref, out_ref):
    half, width = second_ref.shape
    last = first_ref.shape[0] - PLACE_ROWS

    def chosen(own, other):
        return jnp.where(sec_ref[0] == 0, own, other) if shares == 2 else other

    rows = pl.ds(0, half)
    out_ref[pl.ds(0, width), pl.ds(0, half)] = chosen(first_ref[rows, :], other_ref[rows, :]).T
    out_ref[pl.ds(0, width), pl.ds(half, half)] = chosen(second_ref[...], came_ref[...]).T
    rows = pl.ds(last, PLACE_ROWS)
    out_ref[pl.ds(width, PLACE_ROWS), pl.ds(0, LANES)] = chosen(first_ref[rows, :], other_ref[rows, :])
    out_ref[pl.ds(width, PLACE_ROWS), pl.ds(LANES, 2 * half - LANES)] = jnp.zeros(
        (PLACE_ROWS, 2 * half - LANES), jnp.bfloat16
    )


def query_payload(sec, first_half, second_half, other, came, shares):
    half, width = second_half.shape
    return pl.pallas_call(
        functools.partial(query_kernel, shares),
        out_shape=jax.ShapeDtypeStruct((width + PLACE_ROWS, 2 * half), jnp.bfloat16),
        in_specs=[in_smem()] + in_vmem(4),
        out_specs=pl.BlockSpec(memory_space=pltpu.VMEM),
        compiler_params=pltpu.CompilerParams(vmem_limit_bytes=VMEM_BYTES),
        name="query_payload",
    )(sec, first_half, second_half, other, came)


def gathered(values, axes, beside):
    held, steps = [], []
    for value, axis in zip(values, axes):
        devices = lax.axis_size(axis)
        if devices & (devices - 1):
            moved = [lax.ppermute(value, axis, pairs) for pairs in turns(axis)[0]]
            held.append(dict(enumerate([value] + moved)))
            steps.append(0)
        else:
            held.append({0: value})
            steps.append(devices.bit_length() - 1)
    for step in range(1, max(steps) + 1):
        for i, axis in enumerate(axes):
            devices = lax.axis_size(axis)
            for at in range(devices - 1, 0, -1):
                if steps[i] and at.bit_count() == step:
                    by = at & -at
                    pairs = [(j, j ^ by) for j in range(devices)]
                    held[i][at] = lax.ppermute(held[i][at ^ by], axis, pairs)
        if step == 1:
            held, beside = lax.optimization_barrier((held, beside))
    return [[h[i] for i in range(len(h))] for h in held], beside


def per_device(
    descriptors, positions, vertex_ids, candidate_blocks, candidate_count, displacement, stiffness
):
    point_total, width = descriptors.shape[3:]
    per_tile = point_total // BLK
    tile_rows, tile_cols = lax.axis_size("ty"), lax.axis_size("tx")
    sections = lax.axis_size("sec")
    sec_index = lax.axis_index("sec")
    tiles = tile_rows * tile_cols
    side = displacement.shape[3]
    halo = ITERS
    span = side + 2 * halo
    wide = -(-span // LANES) * LANES
    cand = candidate_blocks.shape[3]
    shares = 2 if sections == 2 and per_tile % 2 == 0 else 1
    part = per_tile // shares
    key_rows = part * BLK

    first_half, second_half = pack(
        descriptors[0, 0, 0],
        positions[0, 0, 0],
        vertex_ids[0, 0],
        candidate_blocks[0, 0],
        candidate_count[0, 0][None],
        shares,
        tile_cols,
    )
    half = point_total // 2
    swap = [(i, 1 - i) for i in range(2)]

    sec = jnp.asarray(sec_index, jnp.int32)[None]
    own_mesh = jnp.concatenate([displacement[0], stiffness], axis=0)
    if shares == 2:
        share = sec_index
        other = lax.ppermute(first_half, "sec", swap)
    else:
        share = 0
        other = passed_along(first_half, "sec", 1)
    came = passed_along(second_half, "sec", 1)
    cols = col_edges(own_mesh, halo)
    key, place = key_payload(sec, first_half, second_half, other, shares)
    meshes = [own_mesh]
    if shares == 2:
        tied, key = lax.optimization_barrier((own_mesh, key))
        meshes.append(lax.ppermute(tied, "sec", swap))
    query = query_payload(sec, first_half, second_half, other, came, shares)
    (queries, keys), (cols, meshes) = gathered((query, key), ("ty", "tx"), (cols, meshes))
    at = jnp.concatenate(
        [
            jnp.stack([lax.axis_index("ty") * side, lax.axis_index("tx") * side, sec_index]),
            jnp.stack([lax.axis_index("ty"), jnp.asarray(share), jnp.asarray(shares)]),
            turns("ty")[1],
            turns("tx")[1],
        ]
    ).astype(jnp.int32)
    extent = (side * tile_rows, side * tile_cols)
    sum_shapes = [
        pltpu.VMEM((2, -(-span // 16) * 16, wide), jnp.float32),
        pltpu.VMEM((2, tiles, per_tile, LANES), jnp.float32),
    ]

    top, end = own_mesh[:, :halo], own_mesh[:, side - halo :]
    corners = [
        jnp.pad(v.swapaxes(1, 2), ((0, 0), (0, 0), (0, side - 2 * halo)))
        for v in (cols[:, :, :halo], cols[:, :, side - halo :])
    ]
    edges = [jnp.concatenate(v, axis=0) for v in ((top, corners[0]), (end, corners[1]))]
    edges = jnp.stack([v.reshape(-1, LANES) for v in edges + [cols]])
    parts = match(at, queries, keys, edges, 16.0 / width, shares, part)
    shape = parts.shape
    parts = exchanged(parts.reshape((-1,) + shape[2:]), ("sec", "ty") if shares == 2 else "ty")
    pulls = combine(parts, place, shares * tiles)
    parts, pulls, meshes = lax.optimization_barrier((parts, pulls, meshes))

    def edge_rows(by):
        near = lax.axis_index("ty") + by
        rows = parts.reshape(shape)[:, :, -edges.shape[1] :]
        rows = lax.dynamic_index_in_dim(rows, jnp.clip(near, 0, tile_rows - 1), 1, keepdims=False)
        rows = jnp.where((near >= 0) & (near < tile_rows), rows, 0.0)
        rows = rows.reshape(shares, 2, 3, halo, side)
        if shares == 2:
            rows = jnp.where(sec_index == 0, rows, rows[::-1])
        return [
            jnp.concatenate([rows[i, 0], rows[i, 1, :, :, : 2 * halo]], axis=2)
            for i in range(shares)
        ]

    after, before = edge_rows(1), edge_rows(-1)
    cols = [cols]
    if shares == 2:
        sent = parts.reshape(shape)[:, :, -edges.shape[1] :]
        sent = lax.dynamic_index_in_dim(sent, lax.axis_index("ty"), 1, keepdims=False)
        cols.append(jnp.where(sec_index == 0, sent[1], sent[0]).reshape(cols[0].shape))
    framed = []
    for i, mesh in enumerate(meshes):
        whole = jnp.concatenate([mesh, cols[i].swapaxes(1, 2)], axis=2)
        framed.append(jnp.concatenate([whole, after[i], before[i]], axis=1))
    framed = jnp.concatenate(framed, axis=0)
    gap = jnp.zeros(framed.shape[:2] + (wide - span,), framed.dtype)
    mesh_values = jnp.concatenate(
        [framed[:, :, : side + halo], gap, framed[:, :, side + halo :]], axis=2
    )
    if shares == 2:
        points = exchanged(pulls, ("sec", "ty", "tx"))
        rounds, rank, spot, number = spots(side, halo, tile_cols, wide, at, parts.reshape(shape), part)
        relaxed = pl.pallas_call(
            functools.partial(relax_kernel, side, halo, extent),
            out_shape=jax.ShapeDtypeStruct((2, side, side), jnp.float32),
            in_specs=[in_smem()] * 2 + in_vmem(5),
            out_specs=pl.BlockSpec(memory_space=pltpu.VMEM),
            scratch_shapes=sum_shapes,
            compiler_params=pltpu.CompilerParams(vmem_limit_bytes=VMEM_BYTES),
            name="relax",
        )(at, rounds, rank, spot, number, points.reshape(2, tiles, -1, LANES), mesh_values)
        return relaxed[None]

    points = passed_along(exchanged(pulls, ("ty", "tx")), "sec", -1)
    parts = passed_along(parts, "sec", -1)
    rounds, rank, spot, number = spots(side, halo, tile_cols, wide, at, parts[None], part)
    sums = pl.pallas_call(
        functools.partial(sums_kernel, side, halo),
        out_shape=jax.ShapeDtypeStruct((2, span, wide), jnp.float32),
        in_specs=[in_smem()] + in_vmem(3),
        out_specs=pl.BlockSpec(memory_space=pltpu.VMEM),
        scratch_shapes=sum_shapes,
        compiler_params=pltpu.CompilerParams(vmem_limit_bytes=VMEM_BYTES),
        name="sums",
    )(rounds, rank, spot, points[None])
    moving, gains = mesh_values[0:2], mesh_values[2]
    return sweeps(moving, gains, sums, number[:span], at, side, halo, extent)[None]


def solution(mesh):
    in_specs = (
        P("sec", "ty", "tx", None, None),
        P("sec", "ty", "tx", None, None),
        P("sec", "ty", "tx", None),
        P("sec", "ty", "tx", None),
        P("sec", "ty", "tx"),
        P("sec", None, "ty", "tx"),
        P("sec", "ty", "tx"),
    )
    out_specs = P("sec", None, "ty", "tx")
    return jax.shard_map(
        per_device, mesh=mesh, in_specs=in_specs, out_specs=out_specs, check_vma=False
    )
```

```python
import functools
import math

import jax
import jax.numpy as jnp
from jax import lax
from jax.experimental import pallas as pl
from jax.experimental.pallas import tpu as pltpu
from jax.sharding import PartitionSpec as P

BLK = 128
ITERS = 4
LANES = 128
PLACE_ROWS = 16
GROUP = 2
ROUND = 8
READY = 4
BASE = 256
DIGITS = 3
VMEM_BYTES = 24 * 1024 * 1024

spring_sec = 0.5
spring_match = 1.0
relax_rate = 0.8


def passed_along(value, axis, by):
    devices = lax.axis_size(axis)
    pairs = [(i, i + by) for i in range(devices) if 0 <= i + by < devices]
    return lax.ppermute(value, axis, pairs)


def exchanged(value, axes):
    return lax.all_to_all(value, axes, split_axis=0, concat_axis=0, tiled=True)


def spread(value, axes):
    copies = jnp.broadcast_to(value[None], (lax.axis_size(axes),) + value.shape)
    return exchanged(copies, axes)


def nt_dot(a, b):
    return lax.dot_general(a, b, (((1,), (1,)), ((), ())), preferred_element_type=jnp.float32)


def in_vmem(count):
    return [pl.BlockSpec(memory_space=pltpu.VMEM)] * count


def in_smem():
    return pl.BlockSpec(memory_space=pltpu.SMEM)


def match_kernel(scale, plan, last, at_ref, *refs):
    tile_rows = max(i for i, _ in plan) + 1
    key_tiles = max(max(among) for _, among in plan if among) + 1
    query_refs, refs = refs[:tile_rows], refs[tile_rows:]
    key_refs, refs = refs[:key_tiles], refs[key_tiles:]
    if last:
        before_ref, edge_ref, out_ref = refs[:3]
        refs = refs[3:]
    else:
        (out_ref,) = refs[:1]
        refs = refs[1:]
    query_buf, key_buf, place_buf, state_buf, list_buf = refs
    point_total = state_buf.shape[2]
    all_tiles, key_rows = key_buf.shape[:2]
    part = key_rows // BLK
    total = all_tiles * part
    own_row, share, shares = at_ref[3], at_ref[4], at_ref[5]
    rows_at, cols_at = 6, 6 + query_buf.shape[0]

    number = 0
    for tile, among in plan:
        met = [at_ref[cols_at + i] for i in among]
        listed = query_refs[tile][pl.ds(point_total, PLACE_ROWS), :]
        listed = listed.astype(jnp.float32).astype(jnp.int32)
        here = listed[0:1] == own_row * shares + share
        for low in range(0, total, 16):
            place = listed[1:2] - low
            bits = jnp.where(here & (place >= 0) & (place < 16), 1 << jnp.clip(place, 0, 15), 0)
            bits = jnp.sum(bits)
            for i in range(low, min(low + 16, total)):
                allowed = functools.reduce(jnp.logical_or, [col == i // part for col in met])
                list_buf[number] = tile * total + i
                number = number + jnp.where(allowed, (bits >> (i - low)) & 1, 0)
        list_buf[number] = -1
        number = number + lax.rem(number, 2)
    for i in range(2 * GROUP):
        list_buf[number + i] = -1
    groups = lax.div(number + 2 * GROUP - 1, 2 * GROUP)

    row_at = lax.broadcasted_iota(jnp.int32, (PLACE_ROWS, LANES), 0)
    ids = []
    for tile, key_ref in enumerate(key_refs):
        col = at_ref[cols_at + tile]
        key_buf[col] = key_ref[pl.ds(0, key_rows), :]
        rest = key_ref[pl.ds(key_rows, key_ref.shape[0] - key_rows), :].astype(jnp.float32)
        for j in range(part):
            x, y = rest[j : j + 1, :], rest[part + j : part + j + 1, :]
            stacked = jnp.where(
                row_at == 0, x, jnp.where(row_at == 1, y, jnp.where(row_at == 2, 1.0, 0.0))
            )
            place_buf[col * part + j] = stacked.astype(jnp.bfloat16)
        digits = [rest[(2 + i) * part : (3 + i) * part] for i in range(DIGITS)]
        ids.append(sum(digit * float(BASE**i) for i, digit in enumerate(digits)))
    for tile, query_ref in enumerate(query_refs):
        query_buf[tile] = query_ref[pl.ds(0, point_total), :]

    state_row = lax.broadcasted_iota(jnp.int32, state_buf.shape[1:], 0)
    for tile in range(tile_rows):
        if last and tile < before_ref.shape[0]:
            state_buf[tile] = before_ref[tile]
        else:
            state_buf[tile] = jnp.where(state_row == 3, -1e30, 0.0)

    def item(at):
        codes = [list_buf[2 * at + i] for i in range(2)]
        tile = lax.div(jnp.maximum(codes[0], 0), total)
        keys, places = [], []
        for i, code in enumerate(codes):
            block = lax.rem(jnp.maximum(jnp.where(code >= 0, code, codes[0]), 0), total)
            block = jnp.where(codes[0] >= 0, block, at_ref[cols_at] * part)
            start = pl.multiple_of(lax.rem(block, part) * BLK, BLK)
            keys.append(key_buf[lax.div(block, part), pl.ds(start, BLK), :])
            kept = jnp.where(code >= 0, 1.0, 0.0).astype(jnp.bfloat16)
            places.append(place_buf[block] * kept)
        return tile, codes[0] >= 0, jnp.concatenate(keys, axis=0), jnp.concatenate(places, axis=1)

    @pl.loop(0, groups)
    def _(group):
        items = [item(group * GROUP + i) for i in range(GROUP)]
        scores = [nt_dot(keys, query_buf[tile]) * scale for tile, _, keys, _ in items]
        tops = [jnp.max(score, axis=0, keepdims=True) for score in scores]
        weights = [jnp.exp2(s - top).astype(jnp.bfloat16) for s, top in zip(scores, tops)]
        sums = [
            jnp.dot(place, weight, preferred_element_type=jnp.float32)[0:8]
            for (_, _, _, place), weight in zip(items, weights)
        ]
        for (tile, live, _, _), top, added in zip(items, tops, sums):
            top = jnp.where(live, top, -1e30)
            state = state_buf[tile]
            before = state[3:4, :]
            both = jnp.maximum(before, top)
            state = state * jnp.exp2(before - both) + added * jnp.exp2(top - both)
            state_buf[tile] = jnp.where(state_row == 3, both, state)

    if not last:
        out_ref[...] = state_buf[pl.ds(0, tile_rows)]
        return
    edge_rows = edge_ref.shape[1]
    for tile in range(tile_rows):
        to = at_ref[rows_at + tile]
        for row in range(point_total // LANES):
            lanes = pl.ds(row * LANES, LANES)
            for place, held in enumerate((3, 2, 0, 1)):
                out_ref[row // part, to, pl.ds(place * part + row % part, 1), :] = state_buf[
                    tile, pl.ds(held, 1), lanes
                ]
        for share in range(out_ref.shape[0]):
            out_ref[share, tile, pl.ds(4 * part, key_tiles * part), :] = jnp.concatenate(ids, axis=0)
            out_ref[share, tile, pl.ds((4 + key_tiles) * part, edge_rows), :] = jnp.where(
                tile > own_row, edge_ref[1], jnp.where(tile < own_row, edge_ref[0], edge_ref[2])
            )


def match(at, queries, keys, edges, score_factor, shares, part):
    tile_rows, key_tiles = len(queries), len(keys)
    point_total, width = queries[0].shape[0] - PLACE_ROWS, queries[0].shape[1]
    total = key_tiles * part

    def call(plan, out_shape, *more):
        many_rows = max(i for i, _ in plan) + 1
        many_keys = max(max(among) for _, among in plan if among) + 1
        scores = sum(len(among) for _, among in plan) * part * point_total * BLK
        return pl.pallas_call(
            functools.partial(
                match_kernel, score_factor * math.log2(math.e), plan, len(more) > 0
            ),
            out_shape=jax.ShapeDtypeStruct(out_shape, jnp.float32),
            in_specs=[in_smem()] + in_vmem(many_rows + many_keys + len(more)),
            out_specs=pl.BlockSpec(memory_space=pltpu.VMEM),
            scratch_shapes=[
                pltpu.VMEM((tile_rows, point_total, width), jnp.bfloat16),
                pltpu.VMEM((key_tiles, part * BLK, width), jnp.bfloat16),
                pltpu.VMEM((total, PLACE_ROWS, LANES), jnp.bfloat16),
                pltpu.VMEM((tile_rows, 8, point_total), jnp.float32),
                pltpu.SMEM((tile_rows * (total + 1) + 2 * GROUP + 1,), jnp.int32),
            ],
            compiler_params=pltpu.CompilerParams(vmem_limit_bytes=VMEM_BYTES),
            cost_estimate=pl.CostEstimate(
                flops=scores * width, bytes_accessed=4 * scores // BLK, transcendentals=scores // 4
            ),
            name="match_rest" if more else "match",
        )(at, *queries[:many_rows], *keys[:many_keys], *more)

    there = [
        [i for i in range(n) if i.bit_count() < 2 or n & (n - 1)] for n in (tile_rows, key_tiles)
    ]
    first = [(i, tuple(there[1])) for i in there[0]]
    rest = [(i, tuple(j for j in range(key_tiles) if j not in there[1])) for i in there[0]]
    rest = [v for v in rest if v[1]]
    rest += [(i, tuple(range(key_tiles))) for i in range(tile_rows) if i not in there[0]]
    if rest:
        state = call(first, (len(first), 8, point_total))
    else:
        rest, row = first, jnp.arange(8)[None, :, None]
        state = jnp.where(row == 3, -1e30, jnp.zeros((tile_rows, 8, point_total), jnp.float32))
    shape = (shares, tile_rows, (4 + key_tiles) * part + edges.shape[1], LANES)
    return call(rest, shape, state, edges)


def combine_kernel(parts_ref, place_ref, out_ref):
    parts = parts_ref.shape[0]
    rows = place_ref.shape[0] // 2
    tops = [parts_ref[i, 0:rows, :] for i in range(parts)]
    top = functools.reduce(jnp.maximum, tops)
    total = x = y = jnp.zeros_like(top)
    for i in range(parts):
        gain = jnp.exp2(tops[i] - top)
        total += gain * parts_ref[i, rows : 2 * rows, :]
        x += gain * parts_ref[i, 2 * rows : 3 * rows, :]
        y += gain * parts_ref[i, 3 * rows : 4 * rows, :]
    pull = jnp.concatenate([x / total, y / total], axis=0) - place_ref[...]
    for i in range(out_ref.shape[0]):
        out_ref[i] = pull


def combine(parts, place, copies):
    return pl.pallas_call(
        combine_kernel,
        out_shape=jax.ShapeDtypeStruct((copies,) + place.shape, jnp.float32),
        in_specs=in_vmem(2),
        out_specs=pl.BlockSpec(memory_space=pltpu.VMEM),
        compiler_params=pltpu.CompilerParams(vmem_limit_bytes=VMEM_BYTES),
        name="combine",
    )(parts, place)


def one_hot(at, length, limits):
    count = at.shape[1]
    parts, done = [], 0
    for low, high in limits:
        spot = lax.broadcasted_iota(jnp.int32, (high - low, count), 0) + low
        if low > done:
            parts.append(jnp.zeros((low - done, count), jnp.bfloat16))
        parts.append(jnp.where(spot == at, 1.0, 0.0).astype(jnp.bfloat16))
        done = high
    if length > done:
        parts.append(jnp.zeros((length - done, count), jnp.bfloat16))
    return jnp.concatenate(parts, axis=0)


def flat(value):
    return jnp.concatenate([value[i : i + 1, :] for i in range(value.shape[0])], axis=1)


def hits(side, halo, tall, wide, row, col):
    up = lambda n: -(-n // 16) * 16
    limits = ((0, up(side + halo)), (wide - up(halo), wide))
    return one_hot(flat(row), tall, ((0, tall),)), one_hot(flat(col), wide, limits)


def ranked(rank, row, values):
    sums = [0.0] * len(values)
    for tile in range(rank.shape[0]):
        here = rank[tile] == row
        sums = [total + jnp.where(here, v[tile], 0.0) for total, v in zip(sums, values)]
    return [jnp.sum(total, axis=0, keepdims=True) for total in sums]


def spots_kernel(
    side,
    halo,
    key_tiles,
    at_ref,
    parts_ref,
    rounds_ref,
    rank_ref,
    spot_ref,
    rows_ref,
    cols_ref,
    count_ref,
    hit_buf,
):
    shares, tile_rows, _, _ = parts_ref.shape
    count = rank_ref.shape[1]
    rows = count // shares
    tall, wide = count_ref.shape

    def folded(at, length):
        return jnp.where(
            (at >= 0) & (at < side + halo), at, jnp.where((at < 0) & (at >= -halo), at + length, -1)
        )

    number = jnp.zeros((1, LANES), jnp.int32)
    point_row = lax.broadcasted_iota(jnp.int32, (count, LANES), 0)
    for i in range(tile_rows):
        for j in range(key_tiles):
            ids = jnp.concatenate(
                [parts_ref[k, i, pl.ds((4 + j) * rows, rows), :] for k in range(shares)], axis=0
            ).astype(jnp.int32)
            tile_of = lax.div(ids, side * side)
            within = lax.rem(ids, side * side)
            row = lax.div(tile_of, key_tiles) * side + lax.div(within, side) - at_ref[0]
            col = lax.rem(tile_of, key_tiles) * side + lax.rem(within, side) - at_ref[1]
            row, col = folded(row, side + 2 * halo), folded(col, wide)
            here = (row >= 0) & (col >= 0)
            hit = here.astype(jnp.int32)
            by = 1
            while by < count:
                hit = hit + jnp.where(point_row >= by, pltpu.roll(hit, by, 0), 0)
                by *= 2
            tile = i * key_tiles + at_ref[6 + tile_rows + j]
            rank_ref[tile] = jnp.where(here, number + hit - 1, -1)
            hit_buf[0, tile] = row.astype(jnp.float32) + 1.0
            hit_buf[1, tile] = col.astype(jnp.float32) + 1.0
            number = number + hit[count - 1 : count, :]
    rounds = lax.div(jnp.max(number) + ROUND - 1, ROUND)
    rounds_ref[0] = rounds
    count_ref[...] = jnp.zeros_like(count_ref)

    @pl.loop(0, rounds)
    def _(k):
        found = [ranked(rank_ref, k * ROUND + r, (hit_buf.at[0], hit_buf.at[1])) for r in range(ROUND)]
        row, col = (jnp.concatenate(v, axis=0).astype(jnp.int32) - 1 for v in zip(*found))
        spot_ref[k, 0] = row
        spot_ref[k, 1] = col
        row_hit, col_hit = hits(side, halo, tall, wide, row, col)
        count_ref[...] += nt_dot(row_hit, col_hit)

        @pl.when(k < READY)
        def _():
            rows_ref[k] = row_hit
            cols_ref[k] = col_hit


def spots(side, halo, key_tiles, wide, at, parts, rows):
    tall = -(-(side + 2 * halo) // 16) * 16
    count = parts.shape[0] * rows
    tiles = parts.shape[1] * key_tiles
    rounds = -(-tiles * count // ROUND)
    return pl.pallas_call(
        functools.partial(spots_kernel, side, halo, key_tiles),
        out_shape=(
            jax.ShapeDtypeStruct((1,), jnp.int32),
            jax.ShapeDtypeStruct((tiles, count, LANES), jnp.int32),
            jax.ShapeDtypeStruct((rounds, 2, ROUND, LANES), jnp.int32),
            jax.ShapeDtypeStruct((READY, tall, ROUND * LANES), jnp.bfloat16),
            jax.ShapeDtypeStruct((READY, wide, ROUND * LANES), jnp.bfloat16),
            jax.ShapeDtypeStruct((tall, wide), jnp.float32),
        ),
        in_specs=[in_smem()] + in_vmem(1),
        out_specs=(in_smem(),) + (pl.BlockSpec(memory_space=pltpu.VMEM),) * 5,
        scratch_shapes=[pltpu.VMEM((2, tiles, count, LANES), jnp.float32)],
        compiler_params=pltpu.CompilerParams(vmem_limit_bytes=VMEM_BYTES),
        cost_estimate=pl.CostEstimate(
            flops=8 * tall * ROUND * LANES * wide,
            bytes_accessed=8 * parts.size,
            transcendentals=0,
        ),
        name="spots",
    )(at, parts)


def vertex_sums(side, halo, rounds_ref, rank_ref, spot_ref, rows_ref, cols_ref, points_ref, sum_ref, point_buf):
    _, tall, wide = sum_ref.shape
    shares, tiles, both_rows, _ = points_ref.shape
    rows = both_rows // 2
    sum_ref[...] = jnp.zeros_like(sum_ref)
    for tile in range(tiles):
        for share in range(shares):
            for c in range(2):
                point_buf[c, tile, pl.ds(share * rows, rows), :] = points_ref[
                    share, tile, pl.ds(c * rows, rows), :
                ]

    def add(k, row_hit, col_hit):
        found = [
            ranked(rank_ref, k * ROUND + r, (point_buf.at[0], point_buf.at[1])) for r in range(ROUND)
        ]
        parts = []
        for value in zip(*found):
            value = jnp.concatenate(value, axis=1)
            high = value.astype(jnp.bfloat16)
            low = (value - high.astype(jnp.float32)).astype(jnp.bfloat16)
            parts += [row_hit * high, row_hit * low]
        summed = nt_dot(jnp.concatenate(parts, axis=0), col_hit)
        sum_ref[0] += summed[0:tall] + summed[tall : 2 * tall]
        sum_ref[1] += summed[2 * tall : 3 * tall] + summed[3 * tall :]

    @pl.loop(0, jnp.minimum(rounds_ref[0], READY))
    def _(k):
        add(k, rows_ref[k], cols_ref[k])

    @pl.loop(READY, jnp.maximum(rounds_ref[0], READY))
    def _(k):
        add(k, *hits(side, halo, tall, wide, spot_ref[k, 0], spot_ref[k, 1]))


def sums_kernel(
    side, halo, rounds_ref, rank_ref, spot_ref, rows_ref, cols_ref, points_ref, out_ref, sum_ref, point_buf
):
    vertex_sums(
        side, halo, rounds_ref, rank_ref, spot_ref, rows_ref, cols_ref, points_ref, sum_ref, point_buf
    )
    out_ref[...] = sum_ref[:, pl.ds(0, out_ref.shape[1]), :]


def neighbours(u):
    return (
        pltpu.roll(u, 1, 0)
        + pltpu.roll(u, u.shape[0] - 1, 0)
        + pltpu.roll(u, 1, 1)
        + pltpu.roll(u, u.shape[1] - 1, 1)
    )


def begin_kernel(side, halo, extent, at_ref, count_ref, mesh_ref, moved_ref, step_ref):
    span, wide = mesh_ref.shape[1:]
    row = lax.broadcasted_iota(jnp.int32, (span, wide), 0)
    col = lax.broadcasted_iota(jnp.int32, (span, wide), 1)
    row = jnp.where(row < side + halo, row, row - span) + at_ref[0]
    col = jnp.where(col < side + halo, col, col - wide) + at_ref[1]
    inside = (row >= 0) & (row < extent[0]) & (col >= 0) & (col < extent[1])
    own_pulled = (at_ref[2] == 0).astype(jnp.float32)
    linked = 1.0
    matched = count_ref[pl.ds(0, span), :]
    for part, pulled in enumerate((own_pulled, 1.0 - own_pulled)):
        gain = mesh_ref[part * 3 + 2]
        diagonal = 4.0 * gain + spring_sec * linked + spring_match * matched * pulled
        step = jnp.where(inside, relax_rate / diagonal, 0.0)
        step_ref[part] = step
        for c in range(2):
            u, other = mesh_ref[part * 3 + c], mesh_ref[(1 - part) * 3 + c]
            force = gain * neighbours(u) + spring_sec * other
            moved_ref[part * 2 + c] = (1.0 - relax_rate) * u + step * force


def begin(side, halo, extent, at, number, mesh_values):
    span, wide = mesh_values.shape[1:]
    return pl.pallas_call(
        functools.partial(begin_kernel, side, halo, extent),
        out_shape=(
            jax.ShapeDtypeStruct((4, span, wide), jnp.float32),
            jax.ShapeDtypeStruct((2, span, wide), jnp.float32),
        ),
        in_specs=[in_smem()] + in_vmem(2),
        out_specs=(pl.BlockSpec(memory_space=pltpu.VMEM),) * 2,
        compiler_params=pltpu.CompilerParams(vmem_limit_bytes=VMEM_BYTES),
        cost_estimate=pl.CostEstimate(
            flops=60 * span * wide, bytes_accessed=4 * 14 * span * wide, transcendentals=0
        ),
        name="begin",
    )(at, number, mesh_values)


def relax_kernel(
    side,
    halo,
    at_ref,
    rounds_ref,
    rank_ref,
    spot_ref,
    rows_ref,
    cols_ref,
    points_ref,
    mesh_ref,
    moved_ref,
    step_ref,
    out_ref,
    sum_ref,
    point_buf,
):
    vertex_sums(
        side, halo, rounds_ref, rank_ref, spot_ref, rows_ref, cols_ref, points_ref, sum_ref, point_buf
    )
    span = moved_ref.shape[1]
    own_pulled = (at_ref[2] == 0).astype(jnp.float32)
    moving, pulls, gains, across = [], [], [], []
    for part, pulled in enumerate((own_pulled, 1.0 - own_pulled)):
        step = step_ref[part]
        gains.append(step * mesh_ref[part * 3 + 2])
        across.append(spring_sec * step)
        pulls.append([step * (sum_ref[c, pl.ds(0, span), :] * pulled) for c in range(2)])
        moving.append([moved_ref[part * 2 + c] + pulls[part][c] for c in range(2)])
    for sweep in range(1, ITERS):
        moving = [
            [
                (1.0 - relax_rate) * moving[part][c]
                + gains[part] * neighbours(moving[part][c])
                + across[part] * moving[1 - part][c]
                + pulls[part][c]
                for c in range(2)
            ]
            for part in range(2 if sweep < ITERS - 1 else 1)
        ]
    for c in range(2):
        out_ref[c] = moving[0][c][0:side, 0:side]


def col_edges(value, halo):
    after = passed_along(value[:, :, :halo].swapaxes(1, 2), "tx", -1)
    before = passed_along(value[:, :, value.shape[2] - halo :].swapaxes(1, 2), "tx", 1)
    return jnp.concatenate([after, before], axis=1)


def sweeps(moving, gains, sums, number, at, side, halo, extent):
    sections = lax.axis_size("sec")
    sec_index = at[2]
    has_next = (sec_index < sections - 1).astype(jnp.float32)
    linked = (sec_index > 0).astype(jnp.float32) + has_next
    pulled, matched = sums * has_next, number * has_next
    span, wide = moving.shape[1:]
    row = jnp.arange(span)[:, None]
    col = jnp.arange(wide)[None, :]
    row = jnp.where(row < side + halo, row, row - span) + at[0]
    col = jnp.where(col < side + halo, col, col - wide) + at[1]
    inside = (row >= 0) & (row < extent[0]) & (col >= 0) & (col < extent[1])
    diagonal = 4.0 * gains + spring_sec * linked + spring_match * matched
    step = jnp.where(inside, relax_rate / jnp.where(inside, diagonal, 1.0), 0.0)
    for sweep in range(ITERS):
        lower_sec = passed_along(moving, "sec", 1)
        upper_sec = passed_along(moving, "sec", -1)
        laplace = (
            jnp.roll(moving, 1, 1)
            + jnp.roll(moving, -1, 1)
            + jnp.roll(moving, 1, 2)
            + jnp.roll(moving, -1, 2)
            - 4.0 * moving
        )
        force = (
            gains * laplace
            + spring_sec * (lower_sec + upper_sec - linked * moving)
            + spring_match * (pulled - matched * moving)
        )
        moving = moving + step * force
    return moving[:, :side, :side]


def pack_kernel(
    shares,
    tile_cols,
    desc_hbm,
    place_hbm,
    ids_hbm,
    list_hbm,
    count_hbm,
    first_ref,
    second_ref,
    place_ref,
    ids_ref,
    list_ref,
    count_ref,
    last_ref,
    sems,
):
    half = second_ref.shape[0]
    copies = [
        pltpu.make_async_copy(source, target, sems.at[i])
        for i, (source, target) in enumerate(
            (
                (place_hbm, place_ref),
                (ids_hbm, ids_ref),
                (list_hbm, list_ref),
                (count_hbm, count_ref),
                (desc_hbm.at[pl.ds(0, half), :], first_ref.at[pl.ds(0, half), :]),
                (desc_hbm.at[pl.ds(half, half), :], second_ref),
            )
        )
    ]
    for copy in copies:
        copy.start()
    for copy in copies[:4]:
        copy.wait()

    def cut(row):
        return [row[:, i : i + LANES] for i in range(0, row.shape[1], LANES)]

    place, ids, blocks = place_ref[...].astype(jnp.float32), ids_ref[...], list_ref[...]
    rows = cut(place[0:1]) + cut(place[1:2])
    for i in range(DIGITS):
        digit = lax.rem(lax.div(ids, BASE**i), BASE)
        rows += cut(digit.astype(jnp.float32))
    per_tile = place.shape[1] // BLK
    part = per_tile // shares
    tile, within = lax.div(blocks, per_tile), lax.rem(blocks, per_tile)
    device = lax.div(tile, tile_cols) * shares + lax.div(within, part)
    spot = lax.rem(tile, tile_cols) * part + lax.rem(within, part)
    live = lax.broadcasted_iota(jnp.int32, blocks.shape, 1) < count_ref[0, 0]
    last_ref[...] = jnp.full_like(last_ref, BASE - 1.0)
    last_ref[0:1, 0 : blocks.shape[1]] = jnp.where(live, device, BASE - 1).astype(jnp.float32)
    last_ref[1:2, 0 : blocks.shape[1]] = spot.astype(jnp.float32)
    count = first_ref.shape[0] - half
    gap = jnp.zeros((count - len(rows) - PLACE_ROWS, LANES), jnp.float32)
    rows += ([gap] if gap.shape[0] else []) + [last_ref[...]]
    first_ref[pl.ds(half, count), :] = jnp.concatenate(rows, axis=0).astype(jnp.bfloat16)
    for copy in copies[4:]:
        copy.wait()


def pack(desc, place, ids, blocks, count, shares, tile_cols):
    points, width = desc.shape
    half = points // 2
    rows = -(-(2 + DIGITS) * (points // LANES) // 16) * 16 + PLACE_ROWS
    return pl.pallas_call(
        functools.partial(pack_kernel, shares, tile_cols),
        out_shape=(
            jax.ShapeDtypeStruct((half + rows, width), jnp.bfloat16),
            jax.ShapeDtypeStruct((half, width), jnp.bfloat16),
        ),
        in_specs=[pl.BlockSpec(memory_space=pltpu.HBM)] * 5,
        out_specs=(pl.BlockSpec(memory_space=pltpu.VMEM),) * 2,
        scratch_shapes=[
            pltpu.VMEM(place.shape, place.dtype),
            pltpu.VMEM(ids.shape, ids.dtype),
            pltpu.VMEM(blocks.shape, blocks.dtype),
            pltpu.SMEM(count.shape, count.dtype),
            pltpu.VMEM((PLACE_ROWS, LANES), jnp.float32),
            pltpu.SemaphoreType.DMA((6,)),
        ],
        name="pack",
    )(desc, place, ids, blocks, count)


def turns(axis):
    devices, here = lax.axis_size(axis), lax.axis_index(axis)
    if devices & (devices - 1):
        pairs = [[(i, (i + j) % devices) for i in range(devices)] for j in range(1, devices)]
        return pairs, jnp.mod(here - jnp.arange(devices), devices)
    pairs = [[(i, i ^ j) for i in range(devices)] for j in range(1, devices)]
    return pairs, here ^ jnp.arange(devices)


def key_kernel(shares, sec_ref, first_ref, second_ref, other_ref, key_ref, place_ref):
    half = second_ref.shape[0]
    per_tile = 2 * half // LANES
    part = per_tile // shares
    own, other = first_ref, first_ref
    if shares == 2:
        other = other_ref
    at_first = sec_ref[0] == 0

    def rest(ref, share):
        rows = ref[pl.ds(half, (2 + DIGITS) * per_tile), :].astype(jnp.float32)
        kept = [
            rows[i * per_tile + share * part : i * per_tile + (share + 1) * part]
            for i in range(2 + DIGITS)
        ]
        return jnp.concatenate(kept[:2], axis=0), kept[2:]

    if shares == 2:
        keys = jnp.where(at_first, other[pl.ds(0, half), :], second_ref[...])
        key_ref[pl.ds(0, half), :] = keys
        (own_0, ids_0), (own_1, _) = rest(own, 0), rest(own, 1)
        (other_0, _), (other_1, ids_1) = rest(other, 0), rest(other, 1)
        key_place = jnp.where(at_first, other_0, own_1)
        place_ref[...] = jnp.where(at_first, own_0, other_1)
        ids = [jnp.where(at_first, a, b) for a, b in zip(ids_0, ids_1)]
    else:
        key_ref[pl.ds(0, half), :] = own[pl.ds(0, half), :]
        key_ref[pl.ds(half, half), :] = second_ref[...]
        key_place, _ = rest(own, 0)
        place_ref[...], ids = rest(other_ref, 0)
    done = part * BLK
    filler = jnp.zeros((-(2 + DIGITS) * part % 16, LANES), jnp.float32)
    rows = [key_place] + ids + ([filler] if filler.shape[0] else [])
    key_ref[pl.ds(done, key_ref.shape[0] - done), :] = jnp.concatenate(rows, axis=0).astype(
        jnp.bfloat16
    )


def key_payload(sec, first_half, second_half, other, shares):
    half, width = second_half.shape
    part = 2 * half // LANES // shares
    rows = part * BLK + -(-(2 + DIGITS) * part // 16) * 16
    return pl.pallas_call(
        functools.partial(key_kernel, shares),
        out_shape=(
            jax.ShapeDtypeStruct((rows, width), jnp.bfloat16),
            jax.ShapeDtypeStruct((2 * part, LANES), jnp.float32),
        ),
        in_specs=[in_smem()] + in_vmem(3),
        out_specs=(pl.BlockSpec(memory_space=pltpu.VMEM),) * 2,
        compiler_params=pltpu.CompilerParams(vmem_limit_bytes=VMEM_BYTES),
        name="key_payload",
    )(sec, first_half, second_half, other)


def query_kernel(shares, sec_ref, first_ref, second_ref, other_ref, came_ref, out_ref):
    half = second_ref.shape[0]
    last = first_ref.shape[0] - PLACE_ROWS

    def chosen(own, other):
        return jnp.where(sec_ref[0] == 0, own, other) if shares == 2 else other

    for target, rows in ((0, pl.ds(0, half)), (2 * half, pl.ds(last, PLACE_ROWS))):
        out_ref[pl.ds(target, rows.size), :] = chosen(first_ref[rows, :], other_ref[rows, :])
    out_ref[pl.ds(half, half), :] = chosen(second_ref[...], came_ref[...])


def query_payload(sec, first_half, second_half, other, came, shares):
    half, width = second_half.shape
    return pl.pallas_call(
        functools.partial(query_kernel, shares),
        out_shape=jax.ShapeDtypeStruct((2 * half + PLACE_ROWS, width), jnp.bfloat16),
        in_specs=[in_smem()] + in_vmem(4),
        out_specs=pl.BlockSpec(memory_space=pltpu.VMEM),
        compiler_params=pltpu.CompilerParams(vmem_limit_bytes=VMEM_BYTES),
        name="query_payload",
    )(sec, first_half, second_half, other, came)


def gathered(values, axes, beside):
    held, steps = [], []
    for value, axis in zip(values, axes):
        devices = lax.axis_size(axis)
        if devices & (devices - 1):
            moved = [lax.ppermute(value, axis, pairs) for pairs in turns(axis)[0]]
            held.append(dict(enumerate([value] + moved)))
            steps.append(0)
        else:
            held.append({0: value})
            steps.append(devices.bit_length() - 1)
    for step in range(1, max(steps) + 1):
        for i, axis in enumerate(axes):
            devices = lax.axis_size(axis)
            for at in range(devices - 1, 0, -1):
                if steps[i] and at.bit_count() == step:
                    by = at & -at
                    pairs = [(j, j ^ by) for j in range(devices)]
                    held[i][at] = lax.ppermute(held[i][at ^ by], axis, pairs)
        if step == 1:
            held, beside = lax.optimization_barrier((held, beside))
    return [[h[i] for i in range(len(h))] for h in held], beside


def per_device(
    descriptors, positions, vertex_ids, candidate_blocks, candidate_count, displacement, stiffness
):
    point_total, width = descriptors.shape[3:]
    per_tile = point_total // BLK
    tile_rows, tile_cols = lax.axis_size("ty"), lax.axis_size("tx")
    sections = lax.axis_size("sec")
    sec_index = lax.axis_index("sec")
    tiles = tile_rows * tile_cols
    side = displacement.shape[3]
    halo = ITERS
    span = side + 2 * halo
    wide = -(-span // LANES) * LANES
    cand = candidate_blocks.shape[3]
    shares = 2 if sections == 2 and per_tile % 2 == 0 else 1
    part = per_tile // shares
    key_rows = part * BLK

    first_half, second_half = pack(
        descriptors[0, 0, 0],
        positions[0, 0, 0],
        vertex_ids[0, 0],
        candidate_blocks[0, 0],
        candidate_count[0, 0][None],
        shares,
        tile_cols,
    )
    half = point_total // 2
    swap = [(i, 1 - i) for i in range(2)]

    sec = jnp.asarray(sec_index, jnp.int32)[None]
    own_mesh = jnp.concatenate([displacement[0], stiffness], axis=0)
    if shares == 2:
        share = sec_index
        other = lax.ppermute(first_half, "sec", swap)
    else:
        share = 0
        other = passed_along(first_half, "sec", 1)
    came = passed_along(second_half, "sec", 1)
    cols = col_edges(own_mesh, halo)
    key, place = key_payload(sec, first_half, second_half, other, shares)
    meshes = [own_mesh]
    if shares == 2:
        tied, key = lax.optimization_barrier((own_mesh, key))
        meshes.append(lax.ppermute(tied, "sec", swap))
    query = query_payload(sec, first_half, second_half, other, came, shares)
    (queries, keys), (cols, meshes) = gathered((query, key), ("ty", "tx"), (cols, meshes))
    at = jnp.concatenate(
        [
            jnp.stack([lax.axis_index("ty") * side, lax.axis_index("tx") * side, sec_index]),
            jnp.stack([lax.axis_index("ty"), jnp.asarray(share), jnp.asarray(shares)]),
            turns("ty")[1],
            turns("tx")[1],
        ]
    ).astype(jnp.int32)
    extent = (side * tile_rows, side * tile_cols)
    sum_shapes = [
        pltpu.VMEM((2, -(-span // 16) * 16, wide), jnp.float32),
        pltpu.VMEM((2, tiles, per_tile, LANES), jnp.float32),
    ]

    top, end = own_mesh[:, :halo], own_mesh[:, side - halo :]
    corners = [
        jnp.pad(v.swapaxes(1, 2), ((0, 0), (0, 0), (0, side - 2 * halo)))
        for v in (cols[:, :, :halo], cols[:, :, side - halo :])
    ]
    edges = [jnp.concatenate(v, axis=0) for v in ((top, corners[0]), (end, corners[1]))]
    edges = jnp.stack([v.reshape(-1, LANES) for v in edges + [cols]])
    parts = match(at, queries, keys, edges, 16.0 / width, shares, part)
    shape = parts.shape
    parts = exchanged(parts.reshape((-1,) + shape[2:]), ("sec", "ty") if shares == 2 else "ty")
    pulls = combine(parts, place, shares * tiles)
    parts, pulls, meshes = lax.optimization_barrier((parts, pulls, meshes))

    def edge_rows(by):
        near = lax.axis_index("ty") + by
        rows = parts.reshape(shape)[:, :, -edges.shape[1] :]
        rows = lax.dynamic_index_in_dim(rows, jnp.clip(near, 0, tile_rows - 1), 1, keepdims=False)
        rows = jnp.where((near >= 0) & (near < tile_rows), rows, 0.0)
        rows = rows.reshape(shares, 2, 3, halo, side)
        if shares == 2:
            rows = jnp.where(sec_index == 0, rows, rows[::-1])
        return [
            jnp.concatenate([rows[i, 0], rows[i, 1, :, :, : 2 * halo]], axis=2)
            for i in range(shares)
        ]

    after, before = edge_rows(1), edge_rows(-1)
    cols = [cols]
    if shares == 2:
        sent = parts.reshape(shape)[:, :, -edges.shape[1] :]
        sent = lax.dynamic_index_in_dim(sent, lax.axis_index("ty"), 1, keepdims=False)
        cols.append(jnp.where(sec_index == 0, sent[1], sent[0]).reshape(cols[0].shape))
    framed = []
    for i, mesh in enumerate(meshes):
        whole = jnp.concatenate([mesh, cols[i].swapaxes(1, 2)], axis=2)
        framed.append(jnp.concatenate([whole, after[i], before[i]], axis=1))
    framed = jnp.concatenate(framed, axis=0)
    gap = jnp.zeros(framed.shape[:2] + (wide - span,), framed.dtype)
    mesh_values = jnp.concatenate(
        [framed[:, :, : side + halo], gap, framed[:, :, side + halo :]], axis=2
    )
    if shares == 2:
        points = exchanged(pulls, ("sec", "ty", "tx"))
        rounds, *found, number = spots(side, halo, tile_cols, wide, at, parts.reshape(shape), part)
        moved, step = begin(side, halo, extent, at, number, mesh_values)
        relaxed = pl.pallas_call(
            functools.partial(relax_kernel, side, halo),
            out_shape=jax.ShapeDtypeStruct((2, side, side), jnp.float32),
            in_specs=[in_smem()] * 2 + in_vmem(8),
            out_specs=pl.BlockSpec(memory_space=pltpu.VMEM),
            scratch_shapes=sum_shapes,
            compiler_params=pltpu.CompilerParams(vmem_limit_bytes=VMEM_BYTES),
            name="relax",
        )(at, rounds, *found, points.reshape(2, tiles, -1, LANES), mesh_values, moved, step)
        return relaxed[None]

    points = passed_along(exchanged(pulls, ("ty", "tx")), "sec", -1)
    parts = passed_along(parts, "sec", -1)
    rounds, *found, number = spots(side, halo, tile_cols, wide, at, parts[None], part)
    sums = pl.pallas_call(
        functools.partial(sums_kernel, side, halo),
        out_shape=jax.ShapeDtypeStruct((2, span, wide), jnp.float32),
        in_specs=[in_smem()] + in_vmem(5),
        out_specs=pl.BlockSpec(memory_space=pltpu.VMEM),
        scratch_shapes=sum_shapes,
        compiler_params=pltpu.CompilerParams(vmem_limit_bytes=VMEM_BYTES),
        name="sums",
    )(rounds, *found, points[None])
    moving, gains = mesh_values[0:2], mesh_values[2]
    return sweeps(moving, gains, sums, number[:span], at, side, halo, extent)[None]


def solution(mesh):
    in_specs = (
        P("sec", "ty", "tx", None, None),
        P("sec", "ty", "tx", None, None),
        P("sec", "ty", "tx", None),
        P("sec", "ty", "tx", None),
        P("sec", "ty", "tx"),
        P("sec", None, "ty", "tx"),
        P("sec", "ty", "tx"),
    )
    out_specs = P("sec", None, "ty", "tx")
    return jax.shard_map(
        per_device, mesh=mesh, in_specs=in_specs, out_specs=out_specs, check_vma=False
    )
```

```python
import functools
import math

import jax
import jax.numpy as jnp
from jax import lax
from jax.experimental import pallas as pl
from jax.experimental.pallas import tpu as pltpu
from jax.sharding import PartitionSpec as P

BLK = 128
ITERS = 4
LANES = 128
PLACE_ROWS = 16
GROUP = 4
ROUND = 8
BASE = 256
DIGITS = 3
VMEM_BYTES = 24 * 1024 * 1024

spring_sec = 0.5
spring_match = 1.0
relax_rate = 0.8


def passed_along(value, axis, by):
    devices = lax.axis_size(axis)
    pairs = [(i, i + by) for i in range(devices) if 0 <= i + by < devices]
    return lax.ppermute(value, axis, pairs)


def exchanged(value, axes):
    return lax.all_to_all(value, axes, split_axis=0, concat_axis=0, tiled=True)


def spread(value, axes):
    copies = jnp.broadcast_to(value[None], (lax.axis_size(axes),) + value.shape)
    return exchanged(copies, axes)


def nt_dot(a, b):
    return lax.dot_general(a, b, (((1,), (1,)), ((), ())), preferred_element_type=jnp.float32)


def in_vmem(count):
    return [pl.BlockSpec(memory_space=pltpu.VMEM)] * count


def in_smem():
    return pl.BlockSpec(memory_space=pltpu.SMEM)


def match_kernel(scale, plan, last, at_ref, *refs):
    tile_rows = max(i for i, _ in plan) + 1
    key_tiles = max(max(among) for _, among in plan if among) + 1
    query_refs, refs = refs[:tile_rows], refs[tile_rows:]
    key_refs, refs = refs[:key_tiles], refs[key_tiles:]
    if last:
        before_ref, edge_ref, out_ref = refs[:3]
        refs = refs[3:]
    else:
        (out_ref,) = refs[:1]
        refs = refs[1:]
    query_buf, key_buf, place_buf, state_buf, list_buf = refs
    point_total = state_buf.shape[2]
    all_tiles, key_rows = key_buf.shape[:2]
    part = key_rows // BLK
    total = all_tiles * part
    own_row, share, shares = at_ref[3], at_ref[4], at_ref[5]
    rows_at, cols_at = 6, 6 + query_buf.shape[0]

    number = 0
    for tile, among in plan:
        met = [at_ref[cols_at + i] for i in among]
        listed = query_refs[tile][pl.ds(point_total, PLACE_ROWS), :]
        listed = listed.astype(jnp.float32).astype(jnp.int32)
        here = listed[0:1] == own_row * shares + share
        for low in range(0, total, 16):
            place = listed[1:2] - low
            bits = jnp.where(here & (place >= 0) & (place < 16), 1 << jnp.clip(place, 0, 15), 0)
            bits = jnp.sum(bits)
            for i in range(low, min(low + 16, total)):
                allowed = functools.reduce(jnp.logical_or, [col == i // part for col in met])
                list_buf[number] = tile * total + i
                number = number + jnp.where(allowed, (bits >> (i - low)) & 1, 0)
        list_buf[number] = -1
        number = number + lax.rem(number, 2)
    for i in range(2 * GROUP):
        list_buf[number + i] = -1
    groups = lax.div(number + 2 * GROUP - 1, 2 * GROUP)

    row_at = lax.broadcasted_iota(jnp.int32, (PLACE_ROWS, LANES), 0)
    ids = []
    for tile, key_ref in enumerate(key_refs):
        col = at_ref[cols_at + tile]
        key_buf[col] = key_ref[pl.ds(0, key_rows), :]
        rest = key_ref[pl.ds(key_rows, key_ref.shape[0] - key_rows), :].astype(jnp.float32)
        for j in range(part):
            x, y = rest[j : j + 1, :], rest[part + j : part + j + 1, :]
            stacked = jnp.where(
                row_at == 0, x, jnp.where(row_at == 1, y, jnp.where(row_at == 2, 1.0, 0.0))
            )
            place_buf[col * part + j] = stacked.astype(jnp.bfloat16)
        digits = [rest[(2 + i) * part : (3 + i) * part] for i in range(DIGITS)]
        ids.append(sum(digit * float(BASE**i) for i, digit in enumerate(digits)))
    for tile, query_ref in enumerate(query_refs):
        query_buf[tile] = query_ref[pl.ds(0, point_total), :]

    state_row = lax.broadcasted_iota(jnp.int32, state_buf.shape[1:], 0)
    for tile in range(tile_rows):
        if last and tile < before_ref.shape[0]:
            state_buf[tile] = before_ref[tile]
        else:
            state_buf[tile] = jnp.where(state_row == 3, -1e30, 0.0)

    def item(at):
        codes = [list_buf[2 * at + i] for i in range(2)]
        tile = lax.div(jnp.maximum(codes[0], 0), total)
        keys, places = [], []
        for i, code in enumerate(codes):
            block = lax.rem(jnp.maximum(jnp.where(code >= 0, code, codes[0]), 0), total)
            block = jnp.where(codes[0] >= 0, block, at_ref[cols_at] * part)
            start = pl.multiple_of(lax.rem(block, part) * BLK, BLK)
            keys.append(key_buf[lax.div(block, part), pl.ds(start, BLK), :])
            kept = jnp.where(code >= 0, 1.0, 0.0).astype(jnp.bfloat16)
            places.append(place_buf[block] * kept)
        return tile, codes[0] >= 0, jnp.concatenate(keys, axis=0), jnp.concatenate(places, axis=1)

    @pl.loop(0, groups)
    def _(group):
        items = [item(group * GROUP + i) for i in range(GROUP)]
        scores = [nt_dot(keys, query_buf[tile]) * scale for tile, _, keys, _ in items]
        tops = [jnp.max(score, axis=0, keepdims=True) for score in scores]
        weights = [jnp.exp2(s - top).astype(jnp.bfloat16) for s, top in zip(scores, tops)]
        sums = [
            jnp.dot(place, weight, preferred_element_type=jnp.float32)[0:8]
            for (_, _, _, place), weight in zip(items, weights)
        ]
        for (tile, live, _, _), top, added in zip(items, tops, sums):
            top = jnp.where(live, top, -1e30)
            state = state_buf[tile]
            before = state[3:4, :]
            both = jnp.maximum(before, top)
            state = state * jnp.exp2(before - both) + added * jnp.exp2(top - both)
            state_buf[tile] = jnp.where(state_row == 3, both, state)

    if not last:
        out_ref[...] = state_buf[pl.ds(0, tile_rows)]
        return
    edge_rows = edge_ref.shape[1]
    for tile in range(tile_rows):
        to = at_ref[rows_at + tile]
        for row in range(point_total // LANES):
            lanes = pl.ds(row * LANES, LANES)
            for place, held in enumerate((3, 2, 0, 1)):
                out_ref[row // part, to, pl.ds(place * part + row % part, 1), :] = state_buf[
                    tile, pl.ds(held, 1), lanes
                ]
        for share in range(out_ref.shape[0]):
            out_ref[share, tile, pl.ds(4 * part, key_tiles * part), :] = jnp.concatenate(ids, axis=0)
            out_ref[share, tile, pl.ds((4 + key_tiles) * part, edge_rows), :] = jnp.where(
                tile > own_row, edge_ref[1], jnp.where(tile < own_row, edge_ref[0], edge_ref[2])
            )


def match(at, queries, keys, edges, score_factor, shares, part):
    tile_rows, key_tiles = len(queries), len(keys)
    point_total, width = queries[0].shape[0] - PLACE_ROWS, queries[0].shape[1]
    total = key_tiles * part

    def call(plan, out_shape, *more):
        many_rows = max(i for i, _ in plan) + 1
        many_keys = max(max(among) for _, among in plan if among) + 1
        scores = sum(len(among) for _, among in plan) * part * point_total * BLK
        return pl.pallas_call(
            functools.partial(
                match_kernel, score_factor * math.log2(math.e), plan, len(more) > 0
            ),
            out_shape=jax.ShapeDtypeStruct(out_shape, jnp.float32),
            in_specs=[in_smem()] + in_vmem(many_rows + many_keys + len(more)),
            out_specs=pl.BlockSpec(memory_space=pltpu.VMEM),
            scratch_shapes=[
                pltpu.VMEM((tile_rows, point_total, width), jnp.bfloat16),
                pltpu.VMEM((key_tiles, part * BLK, width), jnp.bfloat16),
                pltpu.VMEM((total, PLACE_ROWS, LANES), jnp.bfloat16),
                pltpu.VMEM((tile_rows, 8, point_total), jnp.float32),
                pltpu.SMEM((tile_rows * (total + 1) + 2 * GROUP + 1,), jnp.int32),
            ],
            compiler_params=pltpu.CompilerParams(vmem_limit_bytes=VMEM_BYTES),
            cost_estimate=pl.CostEstimate(
                flops=scores * width, bytes_accessed=4 * scores // BLK, transcendentals=scores // 4
            ),
            name="match_rest" if more else "match",
        )(at, *queries[:many_rows], *keys[:many_keys], *more)

    there = [
        [i for i in range(n) if i.bit_count() < 2 or n & (n - 1)] for n in (tile_rows, key_tiles)
    ]
    first = [(i, tuple(there[1])) for i in there[0]]
    rest = [(i, tuple(j for j in range(key_tiles) if j not in there[1])) for i in there[0]]
    rest = [v for v in rest if v[1]]
    rest += [(i, tuple(range(key_tiles))) for i in range(tile_rows) if i not in there[0]]
    if rest:
        state = call(first, (len(first), 8, point_total))
    else:
        rest, row = first, jnp.arange(8)[None, :, None]
        state = jnp.where(row == 3, -1e30, jnp.zeros((tile_rows, 8, point_total), jnp.float32))
    shape = (shares, tile_rows, (4 + key_tiles) * part + edges.shape[1], LANES)
    return call(rest, shape, state, edges)


def combine_kernel(parts_ref, place_ref, out_ref):
    parts = parts_ref.shape[0]
    rows = place_ref.shape[0] // 2
    tops = [parts_ref[i, 0:rows, :] for i in range(parts)]
    top = functools.reduce(jnp.maximum, tops)
    total = x = y = jnp.zeros_like(top)
    for i in range(parts):
        gain = jnp.exp2(tops[i] - top)
        total += gain * parts_ref[i, rows : 2 * rows, :]
        x += gain * parts_ref[i, 2 * rows : 3 * rows, :]
        y += gain * parts_ref[i, 3 * rows : 4 * rows, :]
    pull = jnp.concatenate([x / total, y / total], axis=0) - place_ref[...]
    for i in range(out_ref.shape[0]):
        out_ref[i] = pull


def combine(parts, place, copies):
    return pl.pallas_call(
        combine_kernel,
        out_shape=jax.ShapeDtypeStruct((copies,) + place.shape, jnp.float32),
        in_specs=in_vmem(2),
        out_specs=pl.BlockSpec(memory_space=pltpu.VMEM),
        compiler_params=pltpu.CompilerParams(vmem_limit_bytes=VMEM_BYTES),
        name="combine",
    )(parts, place)


def one_hot(at, length, limits):
    count = at.shape[1]
    parts, done = [], 0
    for low, high in limits:
        spot = lax.broadcasted_iota(jnp.int32, (high - low, count), 0) + low
        if low > done:
            parts.append(jnp.zeros((low - done, count), jnp.bfloat16))
        parts.append(jnp.where(spot == at, 1.0, 0.0).astype(jnp.bfloat16))
        done = high
    if length > done:
        parts.append(jnp.zeros((length - done, count), jnp.bfloat16))
    return jnp.concatenate(parts, axis=0)


def flat(value):
    return jnp.concatenate([value[i : i + 1, :] for i in range(value.shape[0])], axis=1)


def hits(side, halo, tall, wide, row, col):
    up = lambda n: -(-n // 16) * 16
    limits = ((0, up(side + halo)), (wide - up(halo), wide))
    return one_hot(flat(row), tall, ((0, tall),)), one_hot(flat(col), wide, limits)


def ranked(rank, row, values):
    sums = [0.0] * len(values)
    for tile in range(rank.shape[0]):
        here = rank[tile] == row
        sums = [total + jnp.where(here, v[tile], 0.0) for total, v in zip(sums, values)]
    return [jnp.sum(total, axis=0, keepdims=True) for total in sums]


def spots_kernel(
    side, halo, key_tiles, at_ref, parts_ref, rounds_ref, rank_ref, spot_ref, count_ref, hit_buf
):
    shares, tile_rows, _, _ = parts_ref.shape
    count = rank_ref.shape[1]
    rows = count // shares
    tall, wide = count_ref.shape

    def folded(at, length):
        return jnp.where(
            (at >= 0) & (at < side + halo), at, jnp.where((at < 0) & (at >= -halo), at + length, -1)
        )

    number = jnp.zeros((1, LANES), jnp.int32)
    point_row = lax.broadcasted_iota(jnp.int32, (count, LANES), 0)
    for i in range(tile_rows):
        for j in range(key_tiles):
            ids = jnp.concatenate(
                [parts_ref[k, i, pl.ds((4 + j) * rows, rows), :] for k in range(shares)], axis=0
            ).astype(jnp.int32)
            tile_of = lax.div(ids, side * side)
            within = lax.rem(ids, side * side)
            row = lax.div(tile_of, key_tiles) * side + lax.div(within, side) - at_ref[0]
            col = lax.rem(tile_of, key_tiles) * side + lax.rem(within, side) - at_ref[1]
            row, col = folded(row, side + 2 * halo), folded(col, wide)
            here = (row >= 0) & (col >= 0)
            hit = here.astype(jnp.int32)
            by = 1
            while by < count:
                hit = hit + jnp.where(point_row >= by, pltpu.roll(hit, by, 0), 0)
                by *= 2
            tile = i * key_tiles + at_ref[6 + tile_rows + j]
            rank_ref[tile] = jnp.where(here, number + hit - 1, -1)
            hit_buf[0, tile] = row.astype(jnp.float32) + 1.0
            hit_buf[1, tile] = col.astype(jnp.float32) + 1.0
            number = number + hit[count - 1 : count, :]
    rounds = lax.div(jnp.max(number) + ROUND - 1, ROUND)
    rounds_ref[0] = rounds
    count_ref[...] = jnp.zeros_like(count_ref)

    @pl.loop(0, rounds)
    def _(k):
        found = [ranked(rank_ref, k * ROUND + r, (hit_buf.at[0], hit_buf.at[1])) for r in range(ROUND)]
        row, col = (jnp.concatenate(v, axis=0).astype(jnp.int32) - 1 for v in zip(*found))
        spot_ref[k, 0] = row
        spot_ref[k, 1] = col
        row_hit, col_hit = hits(side, halo, tall, wide, row, col)
        count_ref[...] += nt_dot(row_hit, col_hit)


def spots(side, halo, key_tiles, wide, at, parts, rows):
    tall = -(-(side + 2 * halo) // 16) * 16
    count = parts.shape[0] * rows
    tiles = parts.shape[1] * key_tiles
    rounds = -(-tiles * count // ROUND)
    return pl.pallas_call(
        functools.partial(spots_kernel, side, halo, key_tiles),
        out_shape=(
            jax.ShapeDtypeStruct((1,), jnp.int32),
            jax.ShapeDtypeStruct((tiles, count, LANES), jnp.int32),
            jax.ShapeDtypeStruct((rounds, 2, ROUND, LANES), jnp.int32),
            jax.ShapeDtypeStruct((tall, wide), jnp.float32),
        ),
        in_specs=[in_smem()] + in_vmem(1),
        out_specs=(in_smem(),) + (pl.BlockSpec(memory_space=pltpu.VMEM),) * 3,
        scratch_shapes=[pltpu.VMEM((2, tiles, count, LANES), jnp.float32)],
        compiler_params=pltpu.CompilerParams(vmem_limit_bytes=VMEM_BYTES),
        cost_estimate=pl.CostEstimate(
            flops=8 * tall * ROUND * LANES * wide,
            bytes_accessed=8 * parts.size,
            transcendentals=0,
        ),
        name="spots",
    )(at, parts)


def vertex_sums(side, halo, rounds_ref, rank_ref, spot_ref, points_ref, sum_ref, point_buf):
    _, tall, wide = sum_ref.shape
    shares, tiles, both_rows, _ = points_ref.shape
    rows = both_rows // 2
    sum_ref[...] = jnp.zeros_like(sum_ref)
    for tile in range(tiles):
        for share in range(shares):
            for c in range(2):
                point_buf[c, tile, pl.ds(share * rows, rows), :] = points_ref[
                    share, tile, pl.ds(c * rows, rows), :
                ]

    @pl.loop(0, rounds_ref[0])
    def _(k):
        found = [
            ranked(rank_ref, k * ROUND + r, (point_buf.at[0], point_buf.at[1])) for r in range(ROUND)
        ]
        row_hit, col_hit = hits(side, halo, tall, wide, spot_ref[k, 0], spot_ref[k, 1])
        parts = []
        for value in zip(*found):
            value = jnp.concatenate(value, axis=1)
            high = value.astype(jnp.bfloat16)
            low = (value - high.astype(jnp.float32)).astype(jnp.bfloat16)
            parts += [row_hit * high, row_hit * low]
        summed = nt_dot(jnp.concatenate(parts, axis=0), col_hit)
        sum_ref[0] += summed[0:tall] + summed[tall : 2 * tall]
        sum_ref[1] += summed[2 * tall : 3 * tall] + summed[3 * tall :]


def sums_kernel(side, halo, rounds_ref, rank_ref, spot_ref, points_ref, out_ref, sum_ref, point_buf):
    vertex_sums(side, halo, rounds_ref, rank_ref, spot_ref, points_ref, sum_ref, point_buf)
    out_ref[...] = sum_ref[:, pl.ds(0, out_ref.shape[1]), :]


def relax_kernel(
    side,
    halo,
    extent,
    at_ref,
    rounds_ref,
    rank_ref,
    spot_ref,
    count_ref,
    points_ref,
    mesh_ref,
    out_ref,
    sum_ref,
    point_buf,
):
    vertex_sums(side, halo, rounds_ref, rank_ref, spot_ref, points_ref, sum_ref, point_buf)
    span = side + 2 * halo
    wide = sum_ref.shape[2]
    shape = (span, wide)
    row = lax.broadcasted_iota(jnp.int32, shape, 0)
    col = lax.broadcasted_iota(jnp.int32, shape, 1)
    row = jnp.where(row < side + halo, row, row - span) + at_ref[0]
    col = jnp.where(col < side + halo, col, col - wide) + at_ref[1]
    inside = (row >= 0) & (row < extent[0]) & (col >= 0) & (col < extent[1])
    own_pulled = (at_ref[2] == 0).astype(jnp.float32)
    linked = 1.0
    matched = count_ref[pl.ds(0, span), :]
    moving, gains, has, step = [], [], [], []
    for part, pulled in enumerate((own_pulled, 1.0 - own_pulled)):
        gain = mesh_ref[part * 3 + 2]
        diagonal = 4.0 * gain + spring_sec * linked + spring_match * matched * pulled
        gains.append(gain)
        has.append(matched * pulled)
        step.append(jnp.where(inside, relax_rate / diagonal, 0.0))
        moving.append(
            [(mesh_ref[part * 3 + c], sum_ref[c, pl.ds(0, span), :] * pulled) for c in range(2)]
        )
    for sweep in range(ITERS):
        later = []
        for part in range(2):
            row_of = []
            for c in range(2):
                u, pulled = moving[part][c]
                other = moving[1 - part][c][0]
                laplace = (
                    pltpu.roll(u, 1, 0)
                    + pltpu.roll(u, span - 1, 0)
                    + pltpu.roll(u, 1, 1)
                    + pltpu.roll(u, wide - 1, 1)
                    - 4.0 * u
                )
                force = (
                    gains[part] * laplace
                    + spring_sec * (other - linked * u)
                    + spring_match * (pulled - has[part] * u)
                )
                row_of.append((u + step[part] * force, pulled))
            later.append(row_of)
        moving = later
    for c in range(2):
        out_ref[c] = moving[0][c][0][0:side, 0:side]


def col_edges(value, halo):
    after = passed_along(value[:, :, :halo].swapaxes(1, 2), "tx", -1)
    before = passed_along(value[:, :, value.shape[2] - halo :].swapaxes(1, 2), "tx", 1)
    return jnp.concatenate([after, before], axis=1)


def sweeps(moving, gains, sums, number, at, side, halo, extent):
    sections = lax.axis_size("sec")
    sec_index = at[2]
    has_next = (sec_index < sections - 1).astype(jnp.float32)
    linked = (sec_index > 0).astype(jnp.float32) + has_next
    pulled, matched = sums * has_next, number * has_next
    span, wide = moving.shape[1:]
    row = jnp.arange(span)[:, None]
    col = jnp.arange(wide)[None, :]
    row = jnp.where(row < side + halo, row, row - span) + at[0]
    col = jnp.where(col < side + halo, col, col - wide) + at[1]
    inside = (row >= 0) & (row < extent[0]) & (col >= 0) & (col < extent[1])
    diagonal = 4.0 * gains + spring_sec * linked + spring_match * matched
    step = jnp.where(inside, relax_rate / jnp.where(inside, diagonal, 1.0), 0.0)
    for sweep in range(ITERS):
        lower_sec = passed_along(moving, "sec", 1)
        upper_sec = passed_along(moving, "sec", -1)
        laplace = (
            jnp.roll(moving, 1, 1)
            + jnp.roll(moving, -1, 1)
            + jnp.roll(moving, 1, 2)
            + jnp.roll(moving, -1, 2)
            - 4.0 * moving
        )
        force = (
            gains * laplace
            + spring_sec * (lower_sec + upper_sec - linked * moving)
            + spring_match * (pulled - matched * moving)
        )
        moving = moving + step * force
    return moving[:, :side, :side]


def pack_kernel(
    shares,
    tile_cols,
    desc_hbm,
    place_hbm,
    ids_hbm,
    list_hbm,
    count_hbm,
    first_ref,
    second_ref,
    place_ref,
    ids_ref,
    list_ref,
    count_ref,
    last_ref,
    sems,
):
    half = second_ref.shape[0]
    copies = [
        pltpu.make_async_copy(source, target, sems.at[i])
        for i, (source, target) in enumerate(
            (
                (place_hbm, place_ref),
                (ids_hbm, ids_ref),
                (list_hbm, list_ref),
                (count_hbm, count_ref),
                (desc_hbm.at[pl.ds(0, half), :], first_ref.at[pl.ds(0, half), :]),
                (desc_hbm.at[pl.ds(half, half), :], second_ref),
            )
        )
    ]
    for copy in copies:
        copy.start()
    for copy in copies[:4]:
        copy.wait()

    def cut(row):
        return [row[:, i : i + LANES] for i in range(0, row.shape[1], LANES)]

    place, ids, blocks = place_ref[...].astype(jnp.float32), ids_ref[...], list_ref[...]
    rows = cut(place[0:1]) + cut(place[1:2])
    for i in range(DIGITS):
        digit = lax.rem(lax.div(ids, BASE**i), BASE)
        rows += cut(digit.astype(jnp.float32))
    per_tile = place.shape[1] // BLK
    part = per_tile // shares
    tile, within = lax.div(blocks, per_tile), lax.rem(blocks, per_tile)
    device = lax.div(tile, tile_cols) * shares + lax.div(within, part)
    spot = lax.rem(tile, tile_cols) * part + lax.rem(within, part)
    live = lax.broadcasted_iota(jnp.int32, blocks.shape, 1) < count_ref[0, 0]
    last_ref[...] = jnp.full_like(last_ref, BASE - 1.0)
    last_ref[0:1, 0 : blocks.shape[1]] = jnp.where(live, device, BASE - 1).astype(jnp.float32)
    last_ref[1:2, 0 : blocks.shape[1]] = spot.astype(jnp.float32)
    count = first_ref.shape[0] - half
    gap = jnp.zeros((count - len(rows) - PLACE_ROWS, LANES), jnp.float32)
    rows += ([gap] if gap.shape[0] else []) + [last_ref[...]]
    first_ref[pl.ds(half, count), :] = jnp.concatenate(rows, axis=0).astype(jnp.bfloat16)
    for copy in copies[4:]:
        copy.wait()


def pack(desc, place, ids, blocks, count, shares, tile_cols):
    points, width = desc.shape
    half = points // 2
    rows = -(-(2 + DIGITS) * (points // LANES) // 16) * 16 + PLACE_ROWS
    return pl.pallas_call(
        functools.partial(pack_kernel, shares, tile_cols),
        out_shape=(
            jax.ShapeDtypeStruct((half + rows, width), jnp.bfloat16),
            jax.ShapeDtypeStruct((half, width), jnp.bfloat16),
        ),
        in_specs=[pl.BlockSpec(memory_space=pltpu.HBM)] * 5,
        out_specs=(pl.BlockSpec(memory_space=pltpu.VMEM),) * 2,
        scratch_shapes=[
            pltpu.VMEM(place.shape, place.dtype),
            pltpu.VMEM(ids.shape, ids.dtype),
            pltpu.VMEM(blocks.shape, blocks.dtype),
            pltpu.SMEM(count.shape, count.dtype),
            pltpu.VMEM((PLACE_ROWS, LANES), jnp.float32),
            pltpu.SemaphoreType.DMA((6,)),
        ],
        name="pack",
    )(desc, place, ids, blocks, count)


def turns(axis):
    devices, here = lax.axis_size(axis), lax.axis_index(axis)
    if devices & (devices - 1):
        pairs = [[(i, (i + j) % devices) for i in range(devices)] for j in range(1, devices)]
        return pairs, jnp.mod(here - jnp.arange(devices), devices)
    pairs = [[(i, i ^ j) for i in range(devices)] for j in range(1, devices)]
    return pairs, here ^ jnp.arange(devices)


def key_kernel(shares, sec_ref, first_ref, second_ref, other_ref, key_ref, place_ref):
    half = second_ref.shape[0]
    per_tile = 2 * half // LANES
    part = per_tile // shares
    own, other = first_ref, first_ref
    if shares == 2:
        other = other_ref
    at_first = sec_ref[0] == 0

    def rest(ref, share):
        rows = ref[pl.ds(half, (2 + DIGITS) * per_tile), :].astype(jnp.float32)
        kept = [
            rows[i * per_tile + share * part : i * per_tile + (share + 1) * part]
            for i in range(2 + DIGITS)
        ]
        return jnp.concatenate(kept[:2], axis=0), kept[2:]

    if shares == 2:
        keys = jnp.where(at_first, other[pl.ds(0, half), :], second_ref[...])
        key_ref[pl.ds(0, half), :] = keys
        (own_0, ids_0), (own_1, _) = rest(own, 0), rest(own, 1)
        (other_0, _), (other_1, ids_1) = rest(other, 0), rest(other, 1)
        key_place = jnp.where(at_first, other_0, own_1)
        place_ref[...] = jnp.where(at_first, own_0, other_1)
        ids = [jnp.where(at_first, a, b) for a, b in zip(ids_0, ids_1)]
    else:
        key_ref[pl.ds(0, half), :] = own[pl.ds(0, half), :]
        key_ref[pl.ds(half, half), :] = second_ref[...]
        key_place, _ = rest(own, 0)
        place_ref[...], ids = rest(other_ref, 0)
    done = part * BLK
    filler = jnp.zeros((-(2 + DIGITS) * part % 16, LANES), jnp.float32)
    rows = [key_place] + ids + ([filler] if filler.shape[0] else [])
    key_ref[pl.ds(done, key_ref.shape[0] - done), :] = jnp.concatenate(rows, axis=0).astype(
        jnp.bfloat16
    )


def key_payload(sec, first_half, second_half, other, shares):
    half, width = second_half.shape
    part = 2 * half // LANES // shares
    rows = part * BLK + -(-(2 + DIGITS) * part // 16) * 16
    return pl.pallas_call(
        functools.partial(key_kernel, shares),
        out_shape=(
            jax.ShapeDtypeStruct((rows, width), jnp.bfloat16),
            jax.ShapeDtypeStruct((2 * part, LANES), jnp.float32),
        ),
        in_specs=[in_smem()] + in_vmem(3),
        out_specs=(pl.BlockSpec(memory_space=pltpu.VMEM),) * 2,
        compiler_params=pltpu.CompilerParams(vmem_limit_bytes=VMEM_BYTES),
        name="key_payload",
    )(sec, first_half, second_half, other)


def query_kernel(shares, sec_ref, first_ref, second_ref, other_ref, came_ref, out_ref):
    half = second_ref.shape[0]
    last = first_ref.shape[0] - PLACE_ROWS

    def chosen(own, other):
        return jnp.where(sec_ref[0] == 0, own, other) if shares == 2 else other

    for target, rows in ((0, pl.ds(0, half)), (2 * half, pl.ds(last, PLACE_ROWS))):
        out_ref[pl.ds(target, rows.size), :] = chosen(first_ref[rows, :], other_ref[rows, :])
    out_ref[pl.ds(half, half), :] = chosen(second_ref[...], came_ref[...])


def query_payload(sec, first_half, second_half, other, came, shares):
    half, width = second_half.shape
    return pl.pallas_call(
        functools.partial(query_kernel, shares),
        out_shape=jax.ShapeDtypeStruct((2 * half + PLACE_ROWS, width), jnp.bfloat16),
        in_specs=[in_smem()] + in_vmem(4),
        out_specs=pl.BlockSpec(memory_space=pltpu.VMEM),
        compiler_params=pltpu.CompilerParams(vmem_limit_bytes=VMEM_BYTES),
        name="query_payload",
    )(sec, first_half, second_half, other, came)


def gathered(values, axes, beside):
    held, steps = [], []
    for value, axis in zip(values, axes):
        devices = lax.axis_size(axis)
        if devices & (devices - 1):
            moved = [lax.ppermute(value, axis, pairs) for pairs in turns(axis)[0]]
            held.append(dict(enumerate([value] + moved)))
            steps.append(0)
        else:
            held.append({0: value})
            steps.append(devices.bit_length() - 1)
    for step in range(1, max(steps) + 1):
        for i, axis in enumerate(axes):
            devices = lax.axis_size(axis)
            for at in range(devices - 1, 0, -1):
                if steps[i] and at.bit_count() == step:
                    by = at & -at
                    pairs = [(j, j ^ by) for j in range(devices)]
                    held[i][at] = lax.ppermute(held[i][at ^ by], axis, pairs)
        if step == 1:
            held, beside = lax.optimization_barrier((held, beside))
    return [[h[i] for i in range(len(h))] for h in held], beside


def per_device(
    descriptors, positions, vertex_ids, candidate_blocks, candidate_count, displacement, stiffness
):
    point_total, width = descriptors.shape[3:]
    per_tile = point_total // BLK
    tile_rows, tile_cols = lax.axis_size("ty"), lax.axis_size("tx")
    sections = lax.axis_size("sec")
    sec_index = lax.axis_index("sec")
    tiles = tile_rows * tile_cols
    side = displacement.shape[3]
    halo = ITERS
    span = side + 2 * halo
    wide = -(-span // LANES) * LANES
    cand = candidate_blocks.shape[3]
    shares = 2 if sections == 2 and per_tile % 2 == 0 else 1
    part = per_tile // shares
    key_rows = part * BLK

    first_half, second_half = pack(
        descriptors[0, 0, 0],
        positions[0, 0, 0],
        vertex_ids[0, 0],
        candidate_blocks[0, 0],
        candidate_count[0, 0][None],
        shares,
        tile_cols,
    )
    half = point_total // 2
    swap = [(i, 1 - i) for i in range(2)]

    sec = jnp.asarray(sec_index, jnp.int32)[None]
    own_mesh = jnp.concatenate([displacement[0], stiffness], axis=0)
    if shares == 2:
        share = sec_index
        other = lax.ppermute(first_half, "sec", swap)
    else:
        share = 0
        other = passed_along(first_half, "sec", 1)
    came = passed_along(second_half, "sec", 1)
    cols = col_edges(own_mesh, halo)
    key, place = key_payload(sec, first_half, second_half, other, shares)
    meshes = [own_mesh]
    if shares == 2:
        tied, key = lax.optimization_barrier((own_mesh, key))
        meshes.append(lax.ppermute(tied, "sec", swap))
    query = query_payload(sec, first_half, second_half, other, came, shares)
    (queries, keys), (cols, meshes) = gathered((query, key), ("ty", "tx"), (cols, meshes))
    at = jnp.concatenate(
        [
            jnp.stack([lax.axis_index("ty") * side, lax.axis_index("tx") * side, sec_index]),
            jnp.stack([lax.axis_index("ty"), jnp.asarray(share), jnp.asarray(shares)]),
            turns("ty")[1],
            turns("tx")[1],
        ]
    ).astype(jnp.int32)
    extent = (side * tile_rows, side * tile_cols)
    sum_shapes = [
        pltpu.VMEM((2, -(-span // 16) * 16, wide), jnp.float32),
        pltpu.VMEM((2, tiles, per_tile, LANES), jnp.float32),
    ]

    top, end = own_mesh[:, :halo], own_mesh[:, side - halo :]
    corners = [
        jnp.pad(v.swapaxes(1, 2), ((0, 0), (0, 0), (0, side - 2 * halo)))
        for v in (cols[:, :, :halo], cols[:, :, side - halo :])
    ]
    edges = [jnp.concatenate(v, axis=0) for v in ((top, corners[0]), (end, corners[1]))]
    edges = jnp.stack([v.reshape(-1, LANES) for v in edges + [cols]])
    parts = match(at, queries, keys, edges, 16.0 / width, shares, part)
    shape = parts.shape
    parts = exchanged(parts.reshape((-1,) + shape[2:]), ("sec", "ty") if shares == 2 else "ty")
    pulls = combine(parts, place, shares * tiles)
    parts, pulls, meshes = lax.optimization_barrier((parts, pulls, meshes))

    def edge_rows(by):
        near = lax.axis_index("ty") + by
        rows = parts.reshape(shape)[:, :, -edges.shape[1] :]
        rows = lax.dynamic_index_in_dim(rows, jnp.clip(near, 0, tile_rows - 1), 1, keepdims=False)
        rows = jnp.where((near >= 0) & (near < tile_rows), rows, 0.0)
        rows = rows.reshape(shares, 2, 3, halo, side)
        if shares == 2:
            rows = jnp.where(sec_index == 0, rows, rows[::-1])
        return [
            jnp.concatenate([rows[i, 0], rows[i, 1, :, :, : 2 * halo]], axis=2)
            for i in range(shares)
        ]

    after, before = edge_rows(1), edge_rows(-1)
    cols = [cols]
    if shares == 2:
        sent = parts.reshape(shape)[:, :, -edges.shape[1] :]
        sent = lax.dynamic_index_in_dim(sent, lax.axis_index("ty"), 1, keepdims=False)
        cols.append(jnp.where(sec_index == 0, sent[1], sent[0]).reshape(cols[0].shape))
    framed = []
    for i, mesh in enumerate(meshes):
        whole = jnp.concatenate([mesh, cols[i].swapaxes(1, 2)], axis=2)
        framed.append(jnp.concatenate([whole, after[i], before[i]], axis=1))
    framed = jnp.concatenate(framed, axis=0)
    gap = jnp.zeros(framed.shape[:2] + (wide - span,), framed.dtype)
    mesh_values = jnp.concatenate(
        [framed[:, :, : side + halo], gap, framed[:, :, side + halo :]], axis=2
    )
    if shares == 2:
        points = exchanged(pulls, ("sec", "ty", "tx"))
        rounds, rank, spot, number = spots(side, halo, tile_cols, wide, at, parts.reshape(shape), part)
        relaxed = pl.pallas_call(
            functools.partial(relax_kernel, side, halo, extent),
            out_shape=jax.ShapeDtypeStruct((2, side, side), jnp.float32),
            in_specs=[in_smem()] * 2 + in_vmem(5),
            out_specs=pl.BlockSpec(memory_space=pltpu.VMEM),
            scratch_shapes=sum_shapes,
            compiler_params=pltpu.CompilerParams(vmem_limit_bytes=VMEM_BYTES),
            name="relax",
        )(at, rounds, rank, spot, number, points.reshape(2, tiles, -1, LANES), mesh_values)
        return relaxed[None]

    points = passed_along(exchanged(pulls, ("ty", "tx")), "sec", -1)
    parts = passed_along(parts, "sec", -1)
    rounds, rank, spot, number = spots(side, halo, tile_cols, wide, at, parts[None], part)
    sums = pl.pallas_call(
        functools.partial(sums_kernel, side, halo),
        out_shape=jax.ShapeDtypeStruct((2, span, wide), jnp.float32),
        in_specs=[in_smem()] + in_vmem(3),
        out_specs=pl.BlockSpec(memory_space=pltpu.VMEM),
        scratch_shapes=sum_shapes,
        compiler_params=pltpu.CompilerParams(vmem_limit_bytes=VMEM_BYTES),
        name="sums",
    )(rounds, rank, spot, points[None])
    moving, gains = mesh_values[0:2], mesh_values[2]
    return sweeps(moving, gains, sums, number[:span], at, side, halo, extent)[None]


def solution(mesh):
    in_specs = (
        P("sec", "ty", "tx", None, None),
        P("sec", "ty", "tx", None, None),
        P("sec", "ty", "tx", None),
        P("sec", "ty", "tx", None),
        P("sec", "ty", "tx"),
        P("sec", None, "ty", "tx"),
        P("sec", "ty", "tx"),
    )
    out_specs = P("sec", None, "ty", "tx")
    return jax.shard_map(
        per_device, mesh=mesh, in_specs=in_specs, out_specs=out_specs, check_vma=False
    )
```

```python
import functools
import math

import jax
import jax.numpy as jnp
from jax import lax
from jax.experimental import pallas as pl
from jax.experimental.pallas import tpu as pltpu
from jax.sharding import PartitionSpec as P

BLK = 128
ITERS = 4
LANES = 128
PLACE_ROWS = 16
GROUP = 1
ROUND = 8
BASE = 256
DIGITS = 3
VMEM_BYTES = 24 * 1024 * 1024

spring_sec = 0.5
spring_match = 1.0
relax_rate = 0.8


def passed_along(value, axis, by):
    devices = lax.axis_size(axis)
    pairs = [(i, i + by) for i in range(devices) if 0 <= i + by < devices]
    return lax.ppermute(value, axis, pairs)


def exchanged(value, axes):
    return lax.all_to_all(value, axes, split_axis=0, concat_axis=0, tiled=True)


def spread(value, axes):
    copies = jnp.broadcast_to(value[None], (lax.axis_size(axes),) + value.shape)
    return exchanged(copies, axes)


def nt_dot(a, b):
    return lax.dot_general(a, b, (((1,), (1,)), ((), ())), preferred_element_type=jnp.float32)


def in_vmem(count):
    return [pl.BlockSpec(memory_space=pltpu.VMEM)] * count


def in_smem():
    return pl.BlockSpec(memory_space=pltpu.SMEM)


def match_kernel(scale, plan, last, at_ref, *refs):
    tile_rows = max(i for i, _ in plan) + 1
    key_tiles = max(max(among) for _, among in plan if among) + 1
    query_refs, refs = refs[:tile_rows], refs[tile_rows:]
    key_refs, refs = refs[:key_tiles], refs[key_tiles:]
    if last:
        before_ref, edge_ref, out_ref = refs[:3]
        refs = refs[3:]
    else:
        (out_ref,) = refs[:1]
        refs = refs[1:]
    query_buf, key_buf, place_buf, state_buf, list_buf = refs
    point_total = state_buf.shape[2]
    all_tiles, key_rows = key_buf.shape[:2]
    part = key_rows // BLK
    total = all_tiles * part
    own_row, share, shares = at_ref[3], at_ref[4], at_ref[5]
    rows_at, cols_at = 6, 6 + query_buf.shape[0]

    number = 0
    for tile, among in plan:
        met = [at_ref[cols_at + i] for i in among]
        listed = query_refs[tile][pl.ds(point_total, PLACE_ROWS), :]
        listed = listed.astype(jnp.float32).astype(jnp.int32)
        here = listed[0:1] == own_row * shares + share
        for low in range(0, total, 16):
            place = listed[1:2] - low
            bits = jnp.where(here & (place >= 0) & (place < 16), 1 << jnp.clip(place, 0, 15), 0)
            bits = jnp.sum(bits)
            for i in range(low, min(low + 16, total)):
                allowed = functools.reduce(jnp.logical_or, [col == i // part for col in met])
                list_buf[number] = tile * total + i
                number = number + jnp.where(allowed, (bits >> (i - low)) & 1, 0)
        list_buf[number] = -1
        number = number + lax.rem(number, 2)
    for i in range(2 * GROUP):
        list_buf[number + i] = -1
    groups = lax.div(number + 2 * GROUP - 1, 2 * GROUP)

    row_at = lax.broadcasted_iota(jnp.int32, (PLACE_ROWS, LANES), 0)
    ids = []
    for tile, key_ref in enumerate(key_refs):
        col = at_ref[cols_at + tile]
        key_buf[col] = key_ref[pl.ds(0, key_rows), :]
        rest = key_ref[pl.ds(key_rows, key_ref.shape[0] - key_rows), :].astype(jnp.float32)
        for j in range(part):
            x, y = rest[j : j + 1, :], rest[part + j : part + j + 1, :]
            stacked = jnp.where(
                row_at == 0, x, jnp.where(row_at == 1, y, jnp.where(row_at == 2, 1.0, 0.0))
            )
            place_buf[col * part + j] = stacked.astype(jnp.bfloat16)
        digits = [rest[(2 + i) * part : (3 + i) * part] for i in range(DIGITS)]
        ids.append(sum(digit * float(BASE**i) for i, digit in enumerate(digits)))
    for tile, query_ref in enumerate(query_refs):
        query_buf[tile] = query_ref[pl.ds(0, point_total), :]

    state_row = lax.broadcasted_iota(jnp.int32, state_buf.shape[1:], 0)
    for tile in range(tile_rows):
        if last and tile < before_ref.shape[0]:
            state_buf[tile] = before_ref[tile]
        else:
            state_buf[tile] = jnp.where(state_row == 3, -1e30, 0.0)

    def item(at):
        codes = [list_buf[2 * at + i] for i in range(2)]
        tile = lax.div(jnp.maximum(codes[0], 0), total)
        keys, places = [], []
        for i, code in enumerate(codes):
            block = lax.rem(jnp.maximum(jnp.where(code >= 0, code, codes[0]), 0), total)
            block = jnp.where(codes[0] >= 0, block, at_ref[cols_at] * part)
            start = pl.multiple_of(lax.rem(block, part) * BLK, BLK)
            keys.append(key_buf[lax.div(block, part), pl.ds(start, BLK), :])
            kept = jnp.where(code >= 0, 1.0, 0.0).astype(jnp.bfloat16)
            places.append(place_buf[block] * kept)
        return tile, codes[0] >= 0, jnp.concatenate(keys, axis=0), jnp.concatenate(places, axis=1)

    @pl.loop(0, groups)
    def _(group):
        items = [item(group * GROUP + i) for i in range(GROUP)]
        scores = [nt_dot(keys, query_buf[tile]) * scale for tile, _, keys, _ in items]
        tops = [jnp.max(score, axis=0, keepdims=True) for score in scores]
        weights = [jnp.exp2(s - top).astype(jnp.bfloat16) for s, top in zip(scores, tops)]
        sums = [
            jnp.dot(place, weight, preferred_element_type=jnp.float32)[0:8]
            for (_, _, _, place), weight in zip(items, weights)
        ]
        for (tile, live, _, _), top, added in zip(items, tops, sums):
            top = jnp.where(live, top, -1e30)
            state = state_buf[tile]
            before = state[3:4, :]
            both = jnp.maximum(before, top)
            state = state * jnp.exp2(before - both) + added * jnp.exp2(top - both)
            state_buf[tile] = jnp.where(state_row == 3, both, state)

    if not last:
        out_ref[...] = state_buf[pl.ds(0, tile_rows)]
        return
    edge_rows = edge_ref.shape[1]
    for tile in range(tile_rows):
        to = at_ref[rows_at + tile]
        for row in range(point_total // LANES):
            lanes = pl.ds(row * LANES, LANES)
            for place, held in enumerate((3, 2, 0, 1)):
                out_ref[row // part, to, pl.ds(place * part + row % part, 1), :] = state_buf[
                    tile, pl.ds(held, 1), lanes
                ]
        for share in range(out_ref.shape[0]):
            out_ref[share, tile, pl.ds(4 * part, key_tiles * part), :] = jnp.concatenate(ids, axis=0)
            out_ref[share, tile, pl.ds((4 + key_tiles) * part, edge_rows), :] = jnp.where(
                tile > own_row, edge_ref[1], jnp.where(tile < own_row, edge_ref[0], edge_ref[2])
            )


def match(at, queries, keys, edges, score_factor, shares, part):
    tile_rows, key_tiles = len(queries), len(keys)
    point_total, width = queries[0].shape[0] - PLACE_ROWS, queries[0].shape[1]
    total = key_tiles * part

    def call(plan, out_shape, *more):
        many_rows = max(i for i, _ in plan) + 1
        many_keys = max(max(among) for _, among in plan if among) + 1
        scores = sum(len(among) for _, among in plan) * part * point_total * BLK
        return pl.pallas_call(
            functools.partial(
                match_kernel, score_factor * math.log2(math.e), plan, len(more) > 0
            ),
            out_shape=jax.ShapeDtypeStruct(out_shape, jnp.float32),
            in_specs=[in_smem()] + in_vmem(many_rows + many_keys + len(more)),
            out_specs=pl.BlockSpec(memory_space=pltpu.VMEM),
            scratch_shapes=[
                pltpu.VMEM((tile_rows, point_total, width), jnp.bfloat16),
                pltpu.VMEM((key_tiles, part * BLK, width), jnp.bfloat16),
                pltpu.VMEM((total, PLACE_ROWS, LANES), jnp.bfloat16),
                pltpu.VMEM((tile_rows, 8, point_total), jnp.float32),
                pltpu.SMEM((tile_rows * (total + 1) + 2 * GROUP + 1,), jnp.int32),
            ],
            compiler_params=pltpu.CompilerParams(vmem_limit_bytes=VMEM_BYTES),
            cost_estimate=pl.CostEstimate(
                flops=scores * width, bytes_accessed=4 * scores // BLK, transcendentals=scores // 4
            ),
            name="match_rest" if more else "match",
        )(at, *queries[:many_rows], *keys[:many_keys], *more)

    there = [
        [i for i in range(n) if i.bit_count() < 2 or n & (n - 1)] for n in (tile_rows, key_tiles)
    ]
    first = [(i, tuple(there[1])) for i in there[0]]
    rest = [(i, tuple(j for j in range(key_tiles) if j not in there[1])) for i in there[0]]
    rest = [v for v in rest if v[1]]
    rest += [(i, tuple(range(key_tiles))) for i in range(tile_rows) if i not in there[0]]
    if rest:
        state = call(first, (len(first), 8, point_total))
    else:
        rest, row = first, jnp.arange(8)[None, :, None]
        state = jnp.where(row == 3, -1e30, jnp.zeros((tile_rows, 8, point_total), jnp.float32))
    shape = (shares, tile_rows, (4 + key_tiles) * part + edges.shape[1], LANES)
    return call(rest, shape, state, edges)


def combine_kernel(parts_ref, place_ref, out_ref):
    parts = parts_ref.shape[0]
    rows = place_ref.shape[0] // 2
    tops = [parts_ref[i, 0:rows, :] for i in range(parts)]
    top = functools.reduce(jnp.maximum, tops)
    total = x = y = jnp.zeros_like(top)
    for i in range(parts):
        gain = jnp.exp2(tops[i] - top)
        total += gain * parts_ref[i, rows : 2 * rows, :]
        x += gain * parts_ref[i, 2 * rows : 3 * rows, :]
        y += gain * parts_ref[i, 3 * rows : 4 * rows, :]
    pull = jnp.concatenate([x / total, y / total], axis=0) - place_ref[...]
    for i in range(out_ref.shape[0]):
        out_ref[i] = pull


def combine(parts, place, copies):
    return pl.pallas_call(
        combine_kernel,
        out_shape=jax.ShapeDtypeStruct((copies,) + place.shape, jnp.float32),
        in_specs=in_vmem(2),
        out_specs=pl.BlockSpec(memory_space=pltpu.VMEM),
        compiler_params=pltpu.CompilerParams(vmem_limit_bytes=VMEM_BYTES),
        name="combine",
    )(parts, place)


def one_hot(at, length, limits):
    count = at.shape[1]
    parts, done = [], 0
    for low, high in limits:
        spot = lax.broadcasted_iota(jnp.int32, (high - low, count), 0) + low
        if low > done:
            parts.append(jnp.zeros((low - done, count), jnp.bfloat16))
        parts.append(jnp.where(spot == at, 1.0, 0.0).astype(jnp.bfloat16))
        done = high
    if length > done:
        parts.append(jnp.zeros((length - done, count), jnp.bfloat16))
    return jnp.concatenate(parts, axis=0)


def flat(value):
    return jnp.concatenate([value[i : i + 1, :] for i in range(value.shape[0])], axis=1)


def hits(side, halo, tall, wide, row, col):
    up = lambda n: -(-n // 16) * 16
    limits = ((0, up(side + halo)), (wide - up(halo), wide))
    return one_hot(flat(row), tall, ((0, tall),)), one_hot(flat(col), wide, limits)


def ranked(rank_ref, values_ref, first, row_buf):
    @pl.loop(0, ROUND)
    def _(r):
        here = rank_ref[...] == first + r
        for i in range(2):
            row_buf[i, pl.ds(r, 1), :] = jnp.sum(
                jnp.where(here, values_ref[i], 0.0), axis=(0, 1)
            )[None]

    return row_buf[0], row_buf[1]


def spots_kernel(
    side, halo, key_tiles, at_ref, parts_ref, rounds_ref, rank_ref, spot_ref, count_ref, hit_buf, row_buf
):
    shares, tile_rows, _, _ = parts_ref.shape
    count = rank_ref.shape[1]
    rows = count // shares
    tall, wide = count_ref.shape

    def folded(at, length):
        return jnp.where(
            (at >= 0) & (at < side + halo), at, jnp.where((at < 0) & (at >= -halo), at + length, -1)
        )

    number = jnp.zeros((1, LANES), jnp.int32)
    point_row = lax.broadcasted_iota(jnp.int32, (count, LANES), 0)
    for i in range(tile_rows):
        for j in range(key_tiles):
            ids = jnp.concatenate(
                [parts_ref[k, i, pl.ds((4 + j) * rows, rows), :] for k in range(shares)], axis=0
            ).astype(jnp.int32)
            tile_of = lax.div(ids, side * side)
            within = lax.rem(ids, side * side)
            row = lax.div(tile_of, key_tiles) * side + lax.div(within, side) - at_ref[0]
            col = lax.rem(tile_of, key_tiles) * side + lax.rem(within, side) - at_ref[1]
            row, col = folded(row, side + 2 * halo), folded(col, wide)
            here = (row >= 0) & (col >= 0)
            hit = here.astype(jnp.int32)
            by = 1
            while by < count:
                hit = hit + jnp.where(point_row >= by, pltpu.roll(hit, by, 0), 0)
                by *= 2
            tile = i * key_tiles + at_ref[6 + tile_rows + j]
            rank_ref[tile] = jnp.where(here, number + hit - 1, -1)
            hit_buf[0, tile] = row.astype(jnp.float32) + 1.0
            hit_buf[1, tile] = col.astype(jnp.float32) + 1.0
            number = number + hit[count - 1 : count, :]
    rounds = lax.div(jnp.max(number) + ROUND - 1, ROUND)
    rounds_ref[0] = rounds
    count_ref[...] = jnp.zeros_like(count_ref)

    @pl.loop(0, rounds)
    def _(k):
        row, col = (v.astype(jnp.int32) - 1 for v in ranked(rank_ref, hit_buf, k * ROUND, row_buf))
        spot_ref[k, 0] = row
        spot_ref[k, 1] = col
        row_hit, col_hit = hits(side, halo, tall, wide, row, col)
        count_ref[...] += nt_dot(row_hit, col_hit)


def spots(side, halo, key_tiles, wide, at, parts, rows):
    tall = -(-(side + 2 * halo) // 16) * 16
    count = parts.shape[0] * rows
    tiles = parts.shape[1] * key_tiles
    rounds = -(-tiles * count // ROUND)
    return pl.pallas_call(
        functools.partial(spots_kernel, side, halo, key_tiles),
        out_shape=(
            jax.ShapeDtypeStruct((1,), jnp.int32),
            jax.ShapeDtypeStruct((tiles, count, LANES), jnp.int32),
            jax.ShapeDtypeStruct((rounds, 2, ROUND, LANES), jnp.int32),
            jax.ShapeDtypeStruct((tall, wide), jnp.float32),
        ),
        in_specs=[in_smem()] + in_vmem(1),
        out_specs=(in_smem(),) + (pl.BlockSpec(memory_space=pltpu.VMEM),) * 3,
        scratch_shapes=[
            pltpu.VMEM((2, tiles, count, LANES), jnp.float32),
            pltpu.VMEM((2, ROUND, LANES), jnp.float32),
        ],
        compiler_params=pltpu.CompilerParams(vmem_limit_bytes=VMEM_BYTES),
        cost_estimate=pl.CostEstimate(
            flops=8 * tall * ROUND * LANES * wide,
            bytes_accessed=8 * parts.size,
            transcendentals=0,
        ),
        name="spots",
    )(at, parts)


def vertex_sums(side, halo, rounds_ref, rank_ref, spot_ref, points_ref, sum_ref, point_buf, row_buf):
    _, tall, wide = sum_ref.shape
    shares, tiles, both_rows, _ = points_ref.shape
    rows = both_rows // 2
    sum_ref[...] = jnp.zeros_like(sum_ref)

    @pl.loop(0, tiles)
    def _(tile):
        for share in range(shares):
            for c in range(2):
                point_buf[c, tile, pl.ds(share * rows, rows), :] = points_ref[
                    share, tile, pl.ds(c * rows, rows), :
                ]

    @pl.loop(0, rounds_ref[0])
    def _(k):
        found = ranked(rank_ref, point_buf, k * ROUND, row_buf)
        row_hit, col_hit = hits(side, halo, tall, wide, spot_ref[k, 0], spot_ref[k, 1])
        parts = []
        for value in map(flat, found):
            high = value.astype(jnp.bfloat16)
            low = (value - high.astype(jnp.float32)).astype(jnp.bfloat16)
            parts += [row_hit * high, row_hit * low]
        summed = nt_dot(jnp.concatenate(parts, axis=0), col_hit)
        sum_ref[0] += summed[0:tall] + summed[tall : 2 * tall]
        sum_ref[1] += summed[2 * tall : 3 * tall] + summed[3 * tall :]


def sums_kernel(
    side, halo, rounds_ref, rank_ref, spot_ref, points_ref, out_ref, sum_ref, point_buf, row_buf
):
    vertex_sums(side, halo, rounds_ref, rank_ref, spot_ref, points_ref, sum_ref, point_buf, row_buf)
    out_ref[...] = sum_ref[:, pl.ds(0, out_ref.shape[1]), :]


def relax_kernel(
    side,
    halo,
    extent,
    at_ref,
    rounds_ref,
    rank_ref,
    spot_ref,
    count_ref,
    points_ref,
    mesh_ref,
    out_ref,
    sum_ref,
    point_buf,
    row_buf,
    moving_buf,
    factor_buf,
    pull_buf,
):
    vertex_sums(side, halo, rounds_ref, rank_ref, spot_ref, points_ref, sum_ref, point_buf, row_buf)
    span, wide = mesh_ref.shape[1:]
    row = lax.broadcasted_iota(jnp.int32, (span, wide), 0)
    col = lax.broadcasted_iota(jnp.int32, (span, wide), 1)
    row = jnp.where(row < side + halo, row, row - span) + at_ref[0]
    col = jnp.where(col < side + halo, col, col - wide) + at_ref[1]
    inside = (row >= 0) & (row < extent[0]) & (col >= 0) & (col < extent[1])
    linked = 1.0

    @pl.loop(0, 2)
    def _(part):
        pulled = jnp.where(part == at_ref[2], 1.0, 0.0).astype(jnp.float32)
        gain = mesh_ref[part * 3 + 2]
        matched = count_ref[pl.ds(0, span), :] * pulled
        diagonal = 4.0 * gain + spring_sec * linked + spring_match * matched
        step = jnp.where(inside, relax_rate / diagonal, 0.0)
        factor_buf[part, 0] = step * gain
        factor_buf[part, 1] = step * spring_sec
        for c in range(2):
            moving_buf[0, part, c] = mesh_ref[part * 3 + c]
            pull_buf[part, c] = step * (sum_ref[c, pl.ds(0, span), :] * pulled)

    @pl.loop(0, ITERS)
    def _(sweep):
        now = lax.rem(sweep, 2)

        @pl.loop(0, jnp.where(sweep < ITERS - 1, 4, 2))
        def _(plane):
            part, c = lax.div(plane, 2), lax.rem(plane, 2)
            u = moving_buf[now, part, c]
            near = (
                pltpu.roll(u, 1, 0)
                + pltpu.roll(u, span - 1, 0)
                + pltpu.roll(u, 1, 1)
                + pltpu.roll(u, wide - 1, 1)
            )
            moving_buf[1 - now, part, c] = (
                (1.0 - relax_rate) * u
                + factor_buf[part, 0] * near
                + factor_buf[part, 1] * moving_buf[now, 1 - part, c]
                + pull_buf[part, c]
            )

    for c in range(2):
        out_ref[c] = moving_buf[ITERS % 2, 0, c, pl.ds(0, side), pl.ds(0, side)]


def col_edges(value, halo):
    after = passed_along(value[:, :, :halo].swapaxes(1, 2), "tx", -1)
    before = passed_along(value[:, :, value.shape[2] - halo :].swapaxes(1, 2), "tx", 1)
    return jnp.concatenate([after, before], axis=1)


def sweeps(moving, gains, sums, number, at, side, halo, extent):
    sections = lax.axis_size("sec")
    sec_index = at[2]
    has_next = (sec_index < sections - 1).astype(jnp.float32)
    linked = (sec_index > 0).astype(jnp.float32) + has_next
    pulled, matched = sums * has_next, number * has_next
    span, wide = moving.shape[1:]
    row = jnp.arange(span)[:, None]
    col = jnp.arange(wide)[None, :]
    row = jnp.where(row < side + halo, row, row - span) + at[0]
    col = jnp.where(col < side + halo, col, col - wide) + at[1]
    inside = (row >= 0) & (row < extent[0]) & (col >= 0) & (col < extent[1])
    diagonal = 4.0 * gains + spring_sec * linked + spring_match * matched
    step = jnp.where(inside, relax_rate / jnp.where(inside, diagonal, 1.0), 0.0)
    for sweep in range(ITERS):
        lower_sec = passed_along(moving, "sec", 1)
        upper_sec = passed_along(moving, "sec", -1)
        laplace = (
            jnp.roll(moving, 1, 1)
            + jnp.roll(moving, -1, 1)
            + jnp.roll(moving, 1, 2)
            + jnp.roll(moving, -1, 2)
            - 4.0 * moving
        )
        force = (
            gains * laplace
            + spring_sec * (lower_sec + upper_sec - linked * moving)
            + spring_match * (pulled - matched * moving)
        )
        moving = moving + step * force
    return moving[:, :side, :side]


def pack_kernel(
    shares,
    tile_cols,
    desc_hbm,
    place_hbm,
    ids_hbm,
    list_hbm,
    count_hbm,
    first_ref,
    second_ref,
    place_ref,
    ids_ref,
    list_ref,
    count_ref,
    last_ref,
    sems,
):
    half = second_ref.shape[0]
    copies = [
        pltpu.make_async_copy(source, target, sems.at[i])
        for i, (source, target) in enumerate(
            (
                (place_hbm, place_ref),
                (ids_hbm, ids_ref),
                (list_hbm, list_ref),
                (count_hbm, count_ref),
                (desc_hbm.at[pl.ds(0, half), :], first_ref.at[pl.ds(0, half), :]),
                (desc_hbm.at[pl.ds(half, half), :], second_ref),
            )
        )
    ]
    for copy in copies:
        copy.start()
    for copy in copies[:4]:
        copy.wait()

    def cut(row):
        return [row[:, i : i + LANES] for i in range(0, row.shape[1], LANES)]

    place, ids, blocks = place_ref[...].astype(jnp.float32), ids_ref[...], list_ref[...]
    rows = cut(place[0:1]) + cut(place[1:2])
    for i in range(DIGITS):
        digit = lax.rem(lax.div(ids, BASE**i), BASE)
        rows += cut(digit.astype(jnp.float32))
    per_tile = place.shape[1] // BLK
    part = per_tile // shares
    tile, within = lax.div(blocks, per_tile), lax.rem(blocks, per_tile)
    device = lax.div(tile, tile_cols) * shares + lax.div(within, part)
    spot = lax.rem(tile, tile_cols) * part + lax.rem(within, part)
    live = lax.broadcasted_iota(jnp.int32, blocks.shape, 1) < count_ref[0, 0]
    last_ref[...] = jnp.full_like(last_ref, BASE - 1.0)
    last_ref[0:1, 0 : blocks.shape[1]] = jnp.where(live, device, BASE - 1).astype(jnp.float32)
    last_ref[1:2, 0 : blocks.shape[1]] = spot.astype(jnp.float32)
    count = first_ref.shape[0] - half
    gap = jnp.zeros((count - len(rows) - PLACE_ROWS, LANES), jnp.float32)
    rows += ([gap] if gap.shape[0] else []) + [last_ref[...]]
    first_ref[pl.ds(half, count), :] = jnp.concatenate(rows, axis=0).astype(jnp.bfloat16)
    for copy in copies[4:]:
        copy.wait()


def pack(desc, place, ids, blocks, count, shares, tile_cols):
    points, width = desc.shape
    half = points // 2
    rows = -(-(2 + DIGITS) * (points // LANES) // 16) * 16 + PLACE_ROWS
    return pl.pallas_call(
        functools.partial(pack_kernel, shares, tile_cols),
        out_shape=(
            jax.ShapeDtypeStruct((half + rows, width), jnp.bfloat16),
            jax.ShapeDtypeStruct((half, width), jnp.bfloat16),
        ),
        in_specs=[pl.BlockSpec(memory_space=pltpu.HBM)] * 5,
        out_specs=(pl.BlockSpec(memory_space=pltpu.VMEM),) * 2,
        scratch_shapes=[
            pltpu.VMEM(place.shape, place.dtype),
            pltpu.VMEM(ids.shape, ids.dtype),
            pltpu.VMEM(blocks.shape, blocks.dtype),
            pltpu.SMEM(count.shape, count.dtype),
            pltpu.VMEM((PLACE_ROWS, LANES), jnp.float32),
            pltpu.SemaphoreType.DMA((6,)),
        ],
        name="pack",
    )(desc, place, ids, blocks, count)


def turns(axis):
    devices, here = lax.axis_size(axis), lax.axis_index(axis)
    if devices & (devices - 1):
        pairs = [[(i, (i + j) % devices) for i in range(devices)] for j in range(1, devices)]
        return pairs, jnp.mod(here - jnp.arange(devices), devices)
    pairs = [[(i, i ^ j) for i in range(devices)] for j in range(1, devices)]
    return pairs, here ^ jnp.arange(devices)


def key_kernel(shares, sec_ref, first_ref, second_ref, other_ref, key_ref, place_ref):
    half = second_ref.shape[0]
    per_tile = 2 * half // LANES
    part = per_tile // shares
    own, other = first_ref, first_ref
    if shares == 2:
        other = other_ref
    at_first = sec_ref[0] == 0

    def rest(ref, share):
        rows = ref[pl.ds(half, (2 + DIGITS) * per_tile), :].astype(jnp.float32)
        kept = [
            rows[i * per_tile + share * part : i * per_tile + (share + 1) * part]
            for i in range(2 + DIGITS)
        ]
        return jnp.concatenate(kept[:2], axis=0), kept[2:]

    if shares == 2:
        keys = jnp.where(at_first, other[pl.ds(0, half), :], second_ref[...])
        key_ref[pl.ds(0, half), :] = keys
        (own_0, ids_0), (own_1, _) = rest(own, 0), rest(own, 1)
        (other_0, _), (other_1, ids_1) = rest(other, 0), rest(other, 1)
        key_place = jnp.where(at_first, other_0, own_1)
        place_ref[...] = jnp.where(at_first, own_0, other_1)
        ids = [jnp.where(at_first, a, b) for a, b in zip(ids_0, ids_1)]
    else:
        key_ref[pl.ds(0, half), :] = own[pl.ds(0, half), :]
        key_ref[pl.ds(half, half), :] = second_ref[...]
        key_place, _ = rest(own, 0)
        place_ref[...], ids = rest(other_ref, 0)
    done = part * BLK
    filler = jnp.zeros((-(2 + DIGITS) * part % 16, LANES), jnp.float32)
    rows = [key_place] + ids + ([filler] if filler.shape[0] else [])
    key_ref[pl.ds(done, key_ref.shape[0] - done), :] = jnp.concatenate(rows, axis=0).astype(
        jnp.bfloat16
    )


def key_payload(sec, first_half, second_half, other, shares):
    half, width = second_half.shape
    part = 2 * half // LANES // shares
    rows = part * BLK + -(-(2 + DIGITS) * part // 16) * 16
    return pl.pallas_call(
        functools.partial(key_kernel, shares),
        out_shape=(
            jax.ShapeDtypeStruct((rows, width), jnp.bfloat16),
            jax.ShapeDtypeStruct((2 * part, LANES), jnp.float32),
        ),
        in_specs=[in_smem()] + in_vmem(3),
        out_specs=(pl.BlockSpec(memory_space=pltpu.VMEM),) * 2,
        compiler_params=pltpu.CompilerParams(vmem_limit_bytes=VMEM_BYTES),
        name="key_payload",
    )(sec, first_half, second_half, other)


def query_kernel(shares, sec_ref, first_ref, second_ref, other_ref, came_ref, out_ref):
    half = second_ref.shape[0]
    last = first_ref.shape[0] - PLACE_ROWS

    def chosen(own, other):
        return jnp.where(sec_ref[0] == 0, own, other) if shares == 2 else other

    for target, rows in ((0, pl.ds(0, half)), (2 * half, pl.ds(last, PLACE_ROWS))):
        out_ref[pl.ds(target, rows.size), :] = chosen(first_ref[rows, :], other_ref[rows, :])
    out_ref[pl.ds(half, half), :] = chosen(second_ref[...], came_ref[...])


def query_payload(sec, first_half, second_half, other, came, shares):
    half, width = second_half.shape
    return pl.pallas_call(
        functools.partial(query_kernel, shares),
        out_shape=jax.ShapeDtypeStruct((2 * half + PLACE_ROWS, width), jnp.bfloat16),
        in_specs=[in_smem()] + in_vmem(4),
        out_specs=pl.BlockSpec(memory_space=pltpu.VMEM),
        compiler_params=pltpu.CompilerParams(vmem_limit_bytes=VMEM_BYTES),
        name="query_payload",
    )(sec, first_half, second_half, other, came)


def gathered(values, axes, beside):
    held, steps = [], []
    for value, axis in zip(values, axes):
        devices = lax.axis_size(axis)
        if devices & (devices - 1):
            moved = [lax.ppermute(value, axis, pairs) for pairs in turns(axis)[0]]
            held.append(dict(enumerate([value] + moved)))
            steps.append(0)
        else:
            held.append({0: value})
            steps.append(devices.bit_length() - 1)
    for step in range(1, max(steps) + 1):
        for i, axis in enumerate(axes):
            devices = lax.axis_size(axis)
            for at in range(devices - 1, 0, -1):
                if steps[i] and at.bit_count() == step:
                    by = at & -at
                    pairs = [(j, j ^ by) for j in range(devices)]
                    held[i][at] = lax.ppermute(held[i][at ^ by], axis, pairs)
        if step == 1:
            held, beside = lax.optimization_barrier((held, beside))
    return [[h[i] for i in range(len(h))] for h in held], beside


def per_device(
    descriptors, positions, vertex_ids, candidate_blocks, candidate_count, displacement, stiffness
):
    point_total, width = descriptors.shape[3:]
    per_tile = point_total // BLK
    tile_rows, tile_cols = lax.axis_size("ty"), lax.axis_size("tx")
    sections = lax.axis_size("sec")
    sec_index = lax.axis_index("sec")
    tiles = tile_rows * tile_cols
    side = displacement.shape[3]
    halo = ITERS
    span = side + 2 * halo
    wide = -(-span // LANES) * LANES
    cand = candidate_blocks.shape[3]
    shares = 2 if sections == 2 and per_tile % 2 == 0 else 1
    part = per_tile // shares
    key_rows = part * BLK

    first_half, second_half = pack(
        descriptors[0, 0, 0],
        positions[0, 0, 0],
        vertex_ids[0, 0],
        candidate_blocks[0, 0],
        candidate_count[0, 0][None],
        shares,
        tile_cols,
    )
    half = point_total // 2
    swap = [(i, 1 - i) for i in range(2)]

    sec = jnp.asarray(sec_index, jnp.int32)[None]
    own_mesh = jnp.concatenate([displacement[0], stiffness], axis=0)
    if shares == 2:
        share = sec_index
        other = lax.ppermute(first_half, "sec", swap)
    else:
        share = 0
        other = passed_along(first_half, "sec", 1)
    came = passed_along(second_half, "sec", 1)
    cols = col_edges(own_mesh, halo)
    key, place = key_payload(sec, first_half, second_half, other, shares)
    meshes = [own_mesh]
    if shares == 2:
        tied, key = lax.optimization_barrier((own_mesh, key))
        meshes.append(lax.ppermute(tied, "sec", swap))
    query = query_payload(sec, first_half, second_half, other, came, shares)
    (queries, keys), (cols, meshes) = gathered((query, key), ("ty", "tx"), (cols, meshes))
    at = jnp.concatenate(
        [
            jnp.stack([lax.axis_index("ty") * side, lax.axis_index("tx") * side, sec_index]),
            jnp.stack([lax.axis_index("ty"), jnp.asarray(share), jnp.asarray(shares)]),
            turns("ty")[1],
            turns("tx")[1],
        ]
    ).astype(jnp.int32)
    extent = (side * tile_rows, side * tile_cols)
    sum_shapes = [
        pltpu.VMEM((2, -(-span // 16) * 16, wide), jnp.float32),
        pltpu.VMEM((2, tiles, per_tile, LANES), jnp.float32),
        pltpu.VMEM((2, ROUND, LANES), jnp.float32),
    ]

    top, end = own_mesh[:, :halo], own_mesh[:, side - halo :]
    corners = [
        jnp.pad(v.swapaxes(1, 2), ((0, 0), (0, 0), (0, side - 2 * halo)))
        for v in (cols[:, :, :halo], cols[:, :, side - halo :])
    ]
    edges = [jnp.concatenate(v, axis=0) for v in ((top, corners[0]), (end, corners[1]))]
    edges = jnp.stack([v.reshape(-1, LANES) for v in edges + [cols]])
    parts = match(at, queries, keys, edges, 16.0 / width, shares, part)
    shape = parts.shape
    parts = exchanged(parts.reshape((-1,) + shape[2:]), ("sec", "ty") if shares == 2 else "ty")
    pulls = combine(parts, place, shares * tiles)
    parts, pulls, meshes = lax.optimization_barrier((parts, pulls, meshes))

    def edge_rows(by):
        near = lax.axis_index("ty") + by
        rows = parts.reshape(shape)[:, :, -edges.shape[1] :]
        rows = lax.dynamic_index_in_dim(rows, jnp.clip(near, 0, tile_rows - 1), 1, keepdims=False)
        rows = jnp.where((near >= 0) & (near < tile_rows), rows, 0.0)
        rows = rows.reshape(shares, 2, 3, halo, side)
        if shares == 2:
            rows = jnp.where(sec_index == 0, rows, rows[::-1])
        return [
            jnp.concatenate([rows[i, 0], rows[i, 1, :, :, : 2 * halo]], axis=2)
            for i in range(shares)
        ]

    after, before = edge_rows(1), edge_rows(-1)
    cols = [cols]
    if shares == 2:
        sent = parts.reshape(shape)[:, :, -edges.shape[1] :]
        sent = lax.dynamic_index_in_dim(sent, lax.axis_index("ty"), 1, keepdims=False)
        cols.append(jnp.where(sec_index == 0, sent[1], sent[0]).reshape(cols[0].shape))
    framed = []
    for i, mesh in enumerate(meshes):
        whole = jnp.concatenate([mesh, cols[i].swapaxes(1, 2)], axis=2)
        framed.append(jnp.concatenate([whole, after[i], before[i]], axis=1))
    framed = jnp.concatenate(framed, axis=0)
    gap = jnp.zeros(framed.shape[:2] + (wide - span,), framed.dtype)
    mesh_values = jnp.concatenate(
        [framed[:, :, : side + halo], gap, framed[:, :, side + halo :]], axis=2
    )
    if shares == 2:
        points = exchanged(pulls, ("sec", "ty", "tx"))
        rounds, rank, spot, number = spots(side, halo, tile_cols, wide, at, parts.reshape(shape), part)
        relaxed = pl.pallas_call(
            functools.partial(relax_kernel, side, halo, extent),
            out_shape=jax.ShapeDtypeStruct((2, side, side), jnp.float32),
            in_specs=[in_smem()] * 2 + in_vmem(5),
            out_specs=pl.BlockSpec(memory_space=pltpu.VMEM),
            scratch_shapes=sum_shapes
            + [
                pltpu.VMEM((2, 2, 2, span, wide), jnp.float32),
                pltpu.VMEM((2, 2, span, wide), jnp.float32),
                pltpu.VMEM((2, 2, span, wide), jnp.float32),
            ],
            compiler_params=pltpu.CompilerParams(vmem_limit_bytes=VMEM_BYTES),
            name="relax",
        )(at, rounds, rank, spot, number, points.reshape(2, tiles, -1, LANES), mesh_values)
        return relaxed[None]

    points = passed_along(exchanged(pulls, ("ty", "tx")), "sec", -1)
    parts = passed_along(parts, "sec", -1)
    rounds, rank, spot, number = spots(side, halo, tile_cols, wide, at, parts[None], part)
    sums = pl.pallas_call(
        functools.partial(sums_kernel, side, halo),
        out_shape=jax.ShapeDtypeStruct((2, span, wide), jnp.float32),
        in_specs=[in_smem()] + in_vmem(3),
        out_specs=pl.BlockSpec(memory_space=pltpu.VMEM),
        scratch_shapes=sum_shapes,
        compiler_params=pltpu.CompilerParams(vmem_limit_bytes=VMEM_BYTES),
        name="sums",
    )(rounds, rank, spot, points[None])
    moving, gains = mesh_values[0:2], mesh_values[2]
    return sweeps(moving, gains, sums, number[:span], at, side, halo, extent)[None]


def solution(mesh):
    in_specs = (
        P("sec", "ty", "tx", None, None),
        P("sec", "ty", "tx", None, None),
        P("sec", "ty", "tx", None),
        P("sec", "ty", "tx", None),
        P("sec", "ty", "tx"),
        P("sec", None, "ty", "tx"),
        P("sec", "ty", "tx"),
    )
    out_specs = P("sec", None, "ty", "tx")
    return jax.shard_map(
        per_device, mesh=mesh, in_specs=in_specs, out_specs=out_specs, check_vma=False
    )
```

```python
import functools
import math

import jax
import jax.numpy as jnp
from jax import lax
from jax.experimental import pallas as pl
from jax.experimental.pallas import tpu as pltpu
from jax.sharding import PartitionSpec as P

BLK = 128
ITERS = 4
LANES = 128
PLACE_ROWS = 16
GROUP = 2
ROUND = 8
BASE = 256
DIGITS = 3
VMEM_BYTES = 24 * 1024 * 1024

spring_sec = 0.5
spring_match = 1.0
relax_rate = 0.8


def passed_along(value, axis, by):
    devices = lax.axis_size(axis)
    pairs = [(i, i + by) for i in range(devices) if 0 <= i + by < devices]
    return lax.ppermute(value, axis, pairs)


def exchanged(value, axes):
    return lax.all_to_all(value, axes, split_axis=0, concat_axis=0, tiled=True)


def spread(value, axes):
    copies = jnp.broadcast_to(value[None], (lax.axis_size(axes),) + value.shape)
    return exchanged(copies, axes)


def nt_dot(a, b):
    return lax.dot_general(a, b, (((1,), (1,)), ((), ())), preferred_element_type=jnp.float32)


def in_vmem(count):
    return [pl.BlockSpec(memory_space=pltpu.VMEM)] * count


def in_smem():
    return pl.BlockSpec(memory_space=pltpu.SMEM)


def match_kernel(scale, plan, last, at_ref, *refs):
    tile_rows = max(i for i, _ in plan) + 1
    key_tiles = max(max(among) for _, among in plan if among) + 1
    query_refs, refs = refs[:tile_rows], refs[tile_rows:]
    key_refs, refs = refs[:key_tiles], refs[key_tiles:]
    if last:
        before_ref, edge_ref, out_ref = refs[:3]
        refs = refs[3:]
    else:
        (out_ref,) = refs[:1]
        refs = refs[1:]
    query_buf, key_buf, place_buf, state_buf, list_buf = refs
    point_total = state_buf.shape[2]
    all_tiles, key_rows = key_buf.shape[:2]
    part = key_rows // BLK
    total = all_tiles * part
    own_row, share, shares = at_ref[3], at_ref[4], at_ref[5]
    rows_at, cols_at = 6, 6 + query_buf.shape[0]

    number = 0
    for tile, among in plan:
        met = [at_ref[cols_at + i] for i in among]
        listed = query_refs[tile][pl.ds(point_total, PLACE_ROWS), :]
        listed = listed.astype(jnp.float32).astype(jnp.int32)
        here = listed[0:1] == own_row * shares + share
        for low in range(0, total, 16):
            place = listed[1:2] - low
            bits = jnp.where(here & (place >= 0) & (place < 16), 1 << jnp.clip(place, 0, 15), 0)
            bits = jnp.sum(bits)
            for i in range(low, min(low + 16, total)):
                allowed = functools.reduce(jnp.logical_or, [col == i // part for col in met])
                list_buf[number] = tile * total + i
                number = number + jnp.where(allowed, (bits >> (i - low)) & 1, 0)
        list_buf[number] = -1
        number = number + lax.rem(number, 2)
    for i in range(2 * GROUP):
        list_buf[number + i] = -1
    groups = lax.div(number + 2 * GROUP - 1, 2 * GROUP)

    row_at = lax.broadcasted_iota(jnp.int32, (PLACE_ROWS, LANES), 0)
    ids = []
    for tile, key_ref in enumerate(key_refs):
        col = at_ref[cols_at + tile]
        key_buf[col] = key_ref[pl.ds(0, key_rows), :]
        rest = key_ref[pl.ds(key_rows, key_ref.shape[0] - key_rows), :].astype(jnp.float32)
        for j in range(part):
            x, y = rest[j : j + 1, :], rest[part + j : part + j + 1, :]
            stacked = jnp.where(
                row_at == 0, x, jnp.where(row_at == 1, y, jnp.where(row_at == 2, 1.0, 0.0))
            )
            place_buf[col * part + j] = stacked.astype(jnp.bfloat16)
        digits = [rest[(2 + i) * part : (3 + i) * part] for i in range(DIGITS)]
        ids.append(sum(digit * float(BASE**i) for i, digit in enumerate(digits)))
    for tile, query_ref in enumerate(query_refs):
        query_buf[tile] = query_ref[pl.ds(0, point_total), :]

    state_row = lax.broadcasted_iota(jnp.int32, state_buf.shape[1:], 0)
    for tile in range(tile_rows):
        if last and tile < before_ref.shape[0]:
            state_buf[tile] = before_ref[tile]
        else:
            state_buf[tile] = jnp.where(state_row == 3, -1e30, 0.0)

    def item(at):
        codes = [list_buf[2 * at + i] for i in range(2)]
        tile = lax.div(jnp.maximum(codes[0], 0), total)
        keys, places = [], []
        for i, code in enumerate(codes):
            block = lax.rem(jnp.maximum(jnp.where(code >= 0, code, codes[0]), 0), total)
            block = jnp.where(codes[0] >= 0, block, at_ref[cols_at] * part)
            start = pl.multiple_of(lax.rem(block, part) * BLK, BLK)
            keys.append(key_buf[lax.div(block, part), pl.ds(start, BLK), :])
            kept = jnp.where(code >= 0, 1.0, 0.0).astype(jnp.bfloat16)
            places.append(place_buf[block] * kept)
        return tile, codes[0] >= 0, jnp.concatenate(keys, axis=0), jnp.concatenate(places, axis=1)

    @pl.loop(0, groups)
    def _(group):
        items = [item(group * GROUP + i) for i in range(GROUP)]
        scores = [nt_dot(keys, query_buf[tile]) * scale for tile, _, keys, _ in items]
        tops = [jnp.max(score, axis=0, keepdims=True) for score in scores]
        weights = [jnp.exp2(s - top).astype(jnp.bfloat16) for s, top in zip(scores, tops)]
        sums = [
            jnp.dot(place, weight, preferred_element_type=jnp.float32)[0:8]
            for (_, _, _, place), weight in zip(items, weights)
        ]
        for (tile, live, _, _), top, added in zip(items, tops, sums):
            top = jnp.where(live, top, -1e30)
            state = state_buf[tile]
            before = state[3:4, :]
            both = jnp.maximum(before, top)
            state = state * jnp.exp2(before - both) + added * jnp.exp2(top - both)
            state_buf[tile] = jnp.where(state_row == 3, both, state)

    if not last:
        out_ref[...] = state_buf[pl.ds(0, tile_rows)]
        return
    edge_rows = edge_ref.shape[1]
    for tile in range(tile_rows):
        to = at_ref[rows_at + tile]
        for row in range(point_total // LANES):
            lanes = pl.ds(row * LANES, LANES)
            for place, held in enumerate((3, 2, 0, 1)):
                out_ref[row // part, to, pl.ds(place * part + row % part, 1), :] = state_buf[
                    tile, pl.ds(held, 1), lanes
                ]
        for share in range(out_ref.shape[0]):
            out_ref[share, tile, pl.ds(4 * part, key_tiles * part), :] = jnp.concatenate(ids, axis=0)
            out_ref[share, tile, pl.ds((4 + key_tiles) * part, edge_rows), :] = jnp.where(
                tile > own_row, edge_ref[1], edge_ref[0]
            )


def match(at, queries, keys, edges, score_factor, shares, part):
    tile_rows, key_tiles = len(queries), len(keys)
    point_total, width = queries[0].shape[0] - PLACE_ROWS, queries[0].shape[1]
    total = key_tiles * part

    def call(plan, out_shape, *more):
        many_rows = max(i for i, _ in plan) + 1
        many_keys = max(max(among) for _, among in plan if among) + 1
        scores = sum(len(among) for _, among in plan) * part * point_total * BLK
        return pl.pallas_call(
            functools.partial(
                match_kernel, score_factor * math.log2(math.e), plan, len(more) > 0
            ),
            out_shape=jax.ShapeDtypeStruct(out_shape, jnp.float32),
            in_specs=[in_smem()] + in_vmem(many_rows + many_keys + len(more)),
            out_specs=pl.BlockSpec(memory_space=pltpu.VMEM),
            scratch_shapes=[
                pltpu.VMEM((tile_rows, point_total, width), jnp.bfloat16),
                pltpu.VMEM((key_tiles, part * BLK, width), jnp.bfloat16),
                pltpu.VMEM((total, PLACE_ROWS, LANES), jnp.bfloat16),
                pltpu.VMEM((tile_rows, 8, point_total), jnp.float32),
                pltpu.SMEM((tile_rows * (total + 1) + 2 * GROUP + 1,), jnp.int32),
            ],
            compiler_params=pltpu.CompilerParams(vmem_limit_bytes=VMEM_BYTES),
            cost_estimate=pl.CostEstimate(
                flops=scores * width, bytes_accessed=4 * scores // BLK, transcendentals=scores // 4
            ),
            name="match_rest" if more else "match",
        )(at, *queries[:many_rows], *keys[:many_keys], *more)

    there = [
        [i for i in range(n) if i.bit_count() < 2 or n & (n - 1)] for n in (tile_rows, key_tiles)
    ]
    first = [(i, tuple(there[1])) for i in there[0]]
    rest = [(i, tuple(j for j in range(key_tiles) if j not in there[1])) for i in there[0]]
    rest = [v for v in rest if v[1]]
    rest += [(i, tuple(range(key_tiles))) for i in range(tile_rows) if i not in there[0]]
    if rest:
        state = call(first, (len(first), 8, point_total))
    else:
        rest, row = first, jnp.arange(8)[None, :, None]
        state = jnp.where(row == 3, -1e30, jnp.zeros((tile_rows, 8, point_total), jnp.float32))
    shape = (shares, tile_rows, (4 + key_tiles) * part + edges.shape[1], LANES)
    return call(rest, shape, state, edges)


def combine_kernel(parts_ref, place_ref, out_ref):
    parts = parts_ref.shape[0]
    rows = place_ref.shape[0] // 2
    tops = [parts_ref[i, 0:rows, :] for i in range(parts)]
    top = functools.reduce(jnp.maximum, tops)
    total = x = y = jnp.zeros_like(top)
    for i in range(parts):
        gain = jnp.exp2(tops[i] - top)
        total += gain * parts_ref[i, rows : 2 * rows, :]
        x += gain * parts_ref[i, 2 * rows : 3 * rows, :]
        y += gain * parts_ref[i, 3 * rows : 4 * rows, :]
    pull = jnp.concatenate([x / total, y / total], axis=0) - place_ref[...]
    for i in range(out_ref.shape[0]):
        out_ref[i] = pull


def combine(parts, place, copies):
    return pl.pallas_call(
        combine_kernel,
        out_shape=jax.ShapeDtypeStruct((copies,) + place.shape, jnp.float32),
        in_specs=in_vmem(2),
        out_specs=pl.BlockSpec(memory_space=pltpu.VMEM),
        compiler_params=pltpu.CompilerParams(vmem_limit_bytes=VMEM_BYTES),
        name="combine",
    )(parts, place)


def one_hot(at, length, limits):
    count = at.shape[1]
    parts, done = [], 0
    for low, high in limits:
        spot = lax.broadcasted_iota(jnp.int32, (high - low, count), 0) + low
        if low > done:
            parts.append(jnp.zeros((low - done, count), jnp.bfloat16))
        parts.append(jnp.where(spot == at, 1.0, 0.0).astype(jnp.bfloat16))
        done = high
    if length > done:
        parts.append(jnp.zeros((length - done, count), jnp.bfloat16))
    return jnp.concatenate(parts, axis=0)


def flat(value):
    return jnp.concatenate([value[i : i + 1, :] for i in range(value.shape[0])], axis=1)


def hits(side, halo, tall, wide, row, col):
    up = lambda n: -(-n // 16) * 16
    limits = ((0, up(side + halo)), (wide - up(halo), wide))
    return one_hot(flat(row), tall, ((0, tall),)), one_hot(flat(col), wide, limits)


def ranked(rank, row, values):
    sums = [0.0] * len(values)
    for tile in range(rank.shape[0]):
        here = rank[tile] == row
        sums = [total + jnp.where(here, v[tile], 0.0) for total, v in zip(sums, values)]
    return [jnp.sum(total, axis=0, keepdims=True) for total in sums]


def spots_kernel(
    side, halo, key_tiles, at_ref, parts_ref, rounds_ref, rank_ref, spot_ref, count_ref, hit_buf
):
    shares, tile_rows, _, _ = parts_ref.shape
    count = rank_ref.shape[1]
    rows = count // shares
    tall, wide = count_ref.shape

    def folded(at, length):
        return jnp.where(
            (at >= 0) & (at < side + halo), at, jnp.where((at < 0) & (at >= -halo), at + length, -1)
        )

    number = jnp.zeros((1, LANES), jnp.int32)
    point_row = lax.broadcasted_iota(jnp.int32, (count, LANES), 0)
    for i in range(tile_rows):
        for j in range(key_tiles):
            ids = jnp.concatenate(
                [parts_ref[k, i, pl.ds((4 + j) * rows, rows), :] for k in range(shares)], axis=0
            ).astype(jnp.int32)
            tile_of = lax.div(ids, side * side)
            within = lax.rem(ids, side * side)
            row = lax.div(tile_of, key_tiles) * side + lax.div(within, side) - at_ref[0]
            col = lax.rem(tile_of, key_tiles) * side + lax.rem(within, side) - at_ref[1]
            row, col = folded(row, side + 2 * halo), folded(col, wide)
            here = (row >= 0) & (col >= 0)
            hit = here.astype(jnp.int32)
            by = 1
            while by < count:
                hit = hit + jnp.where(point_row >= by, pltpu.roll(hit, by, 0), 0)
                by *= 2
            tile = i * key_tiles + at_ref[6 + tile_rows + j]
            rank_ref[tile] = jnp.where(here, number + hit - 1, -1)
            hit_buf[0, tile] = row.astype(jnp.float32) + 1.0
            hit_buf[1, tile] = col.astype(jnp.float32) + 1.0
            number = number + hit[count - 1 : count, :]
    rounds = lax.div(jnp.max(number) + ROUND - 1, ROUND)
    rounds_ref[0] = rounds
    count_ref[...] = jnp.zeros_like(count_ref)

    @pl.loop(0, rounds)
    def _(k):
        found = [ranked(rank_ref, k * ROUND + r, (hit_buf.at[0], hit_buf.at[1])) for r in range(ROUND)]
        row, col = (jnp.concatenate(v, axis=0).astype(jnp.int32) - 1 for v in zip(*found))
        spot_ref[k, 0] = row
        spot_ref[k, 1] = col
        row_hit, col_hit = hits(side, halo, tall, wide, row, col)
        count_ref[...] += nt_dot(row_hit, col_hit)


def spots(side, halo, key_tiles, wide, at, parts, rows):
    tall = -(-(side + 2 * halo) // 16) * 16
    count = parts.shape[0] * rows
    tiles = parts.shape[1] * key_tiles
    rounds = -(-tiles * count // ROUND)
    return pl.pallas_call(
        functools.partial(spots_kernel, side, halo, key_tiles),
        out_shape=(
            jax.ShapeDtypeStruct((1,), jnp.int32),
            jax.ShapeDtypeStruct((tiles, count, LANES), jnp.int32),
            jax.ShapeDtypeStruct((rounds, 2, ROUND, LANES), jnp.int32),
            jax.ShapeDtypeStruct((tall, wide), jnp.float32),
        ),
        in_specs=[in_smem()] + in_vmem(1),
        out_specs=(in_smem(),) + (pl.BlockSpec(memory_space=pltpu.VMEM),) * 3,
        scratch_shapes=[pltpu.VMEM((2, tiles, count, LANES), jnp.float32)],
        compiler_params=pltpu.CompilerParams(vmem_limit_bytes=VMEM_BYTES),
        cost_estimate=pl.CostEstimate(
            flops=8 * tall * ROUND * LANES * wide,
            bytes_accessed=8 * parts.size,
            transcendentals=0,
        ),
        name="spots",
    )(at, parts)


def vertex_sums(side, halo, rounds_ref, rank_ref, spot_ref, points_ref, sum_ref, point_buf):
    _, tall, wide = sum_ref.shape
    shares, tiles, both_rows, _ = points_ref.shape
    rows = both_rows // 2
    sum_ref[...] = jnp.zeros_like(sum_ref)
    for tile in range(tiles):
        for share in range(shares):
            for c in range(2):
                point_buf[c, tile, pl.ds(share * rows, rows), :] = points_ref[
                    share, tile, pl.ds(c * rows, rows), :
                ]

    @pl.loop(0, rounds_ref[0])
    def _(k):
        found = [
            ranked(rank_ref, k * ROUND + r, (point_buf.at[0], point_buf.at[1])) for r in range(ROUND)
        ]
        row_hit, col_hit = hits(side, halo, tall, wide, spot_ref[k, 0], spot_ref[k, 1])
        parts = []
        for value in zip(*found):
            value = jnp.concatenate(value, axis=1)
            high = value.astype(jnp.bfloat16)
            low = (value - high.astype(jnp.float32)).astype(jnp.bfloat16)
            parts += [row_hit * high, row_hit * low]
        summed = nt_dot(jnp.concatenate(parts, axis=0), col_hit)
        sum_ref[0] += summed[0:tall] + summed[tall : 2 * tall]
        sum_ref[1] += summed[2 * tall : 3 * tall] + summed[3 * tall :]


def sums_kernel(side, halo, rounds_ref, rank_ref, spot_ref, points_ref, out_ref, sum_ref, point_buf):
    vertex_sums(side, halo, rounds_ref, rank_ref, spot_ref, points_ref, sum_ref, point_buf)
    out_ref[...] = sum_ref[:, pl.ds(0, out_ref.shape[1]), :]


def relax_kernel(
    side,
    halo,
    extent,
    at_ref,
    rounds_ref,
    rank_ref,
    spot_ref,
    count_ref,
    points_ref,
    mesh_ref,
    out_ref,
    sum_ref,
    point_buf,
):
    vertex_sums(side, halo, rounds_ref, rank_ref, spot_ref, points_ref, sum_ref, point_buf)
    span = side + 2 * halo
    wide = sum_ref.shape[2]
    shape = (span, wide)
    row = lax.broadcasted_iota(jnp.int32, shape, 0)
    col = lax.broadcasted_iota(jnp.int32, shape, 1)
    row = jnp.where(row < side + halo, row, row - span) + at_ref[0]
    col = jnp.where(col < side + halo, col, col - wide) + at_ref[1]
    inside = (row >= 0) & (row < extent[0]) & (col >= 0) & (col < extent[1])
    own_pulled = (at_ref[2] == 0).astype(jnp.float32)
    linked = 1.0
    matched = count_ref[pl.ds(0, span), :]
    moving, gains, across, pulls = [], [], [], []
    for part, pulled in enumerate((own_pulled, 1.0 - own_pulled)):
        gain = mesh_ref[part * 3 + 2]
        diagonal = 4.0 * gain + spring_sec * linked + spring_match * matched * pulled
        step = jnp.where(inside, relax_rate / diagonal, 0.0)
        gains.append(step * gain)
        across.append(step * spring_sec)
        pulls.append([step * (sum_ref[c, pl.ds(0, span), :] * pulled) for c in range(2)])
        moving.append([mesh_ref[part * 3 + c] for c in range(2)])
    for sweep in range(ITERS):
        later = []
        for part in range(2 if sweep < ITERS - 1 else 1):
            row_of = []
            for c in range(2):
                u = moving[part][c]
                near = (
                    pltpu.roll(u, 1, 0)
                    + pltpu.roll(u, span - 1, 0)
                    + pltpu.roll(u, 1, 1)
                    + pltpu.roll(u, wide - 1, 1)
                )
                row_of.append(
                    (1.0 - relax_rate) * u
                    + gains[part] * near
                    + across[part] * moving[1 - part][c]
                    + pulls[part][c]
                )
            later.append(row_of)
        moving = later
    for c in range(2):
        out_ref[c] = moving[0][c][0:side, 0:side]


def col_edges(value, halo):
    after = passed_along(value[:, :, :halo].swapaxes(1, 2), "tx", -1)
    before = passed_along(value[:, :, value.shape[2] - halo :].swapaxes(1, 2), "tx", 1)
    return jnp.concatenate([after, before], axis=1)


def sweeps(moving, gains, sums, number, at, side, halo, extent):
    sections = lax.axis_size("sec")
    sec_index = at[2]
    has_next = (sec_index < sections - 1).astype(jnp.float32)
    linked = (sec_index > 0).astype(jnp.float32) + has_next
    pulled, matched = sums * has_next, number * has_next
    span, wide = moving.shape[1:]
    row = jnp.arange(span)[:, None]
    col = jnp.arange(wide)[None, :]
    row = jnp.where(row < side + halo, row, row - span) + at[0]
    col = jnp.where(col < side + halo, col, col - wide) + at[1]
    inside = (row >= 0) & (row < extent[0]) & (col >= 0) & (col < extent[1])
    diagonal = 4.0 * gains + spring_sec * linked + spring_match * matched
    step = jnp.where(inside, relax_rate / jnp.where(inside, diagonal, 1.0), 0.0)
    for sweep in range(ITERS):
        lower_sec = passed_along(moving, "sec", 1)
        upper_sec = passed_along(moving, "sec", -1)
        laplace = (
            jnp.roll(moving, 1, 1)
            + jnp.roll(moving, -1, 1)
            + jnp.roll(moving, 1, 2)
            + jnp.roll(moving, -1, 2)
            - 4.0 * moving
        )
        force = (
            gains * laplace
            + spring_sec * (lower_sec + upper_sec - linked * moving)
            + spring_match * (pulled - matched * moving)
        )
        moving = moving + step * force
    return moving[:, :side, :side]


def pack_kernel(
    shares,
    tile_cols,
    desc_hbm,
    place_hbm,
    ids_hbm,
    list_hbm,
    count_hbm,
    first_ref,
    second_ref,
    place_ref,
    ids_ref,
    list_ref,
    count_ref,
    last_ref,
    sems,
):
    half = second_ref.shape[0]
    copies = [
        pltpu.make_async_copy(source, target, sems.at[i])
        for i, (source, target) in enumerate(
            (
                (place_hbm, place_ref),
                (ids_hbm, ids_ref),
                (list_hbm, list_ref),
                (count_hbm, count_ref),
                (desc_hbm.at[pl.ds(0, half), :], first_ref.at[pl.ds(0, half), :]),
                (desc_hbm.at[pl.ds(half, half), :], second_ref),
            )
        )
    ]
    for copy in copies:
        copy.start()
    for copy in copies[:4]:
        copy.wait()

    def cut(row):
        return [row[:, i : i + LANES] for i in range(0, row.shape[1], LANES)]

    place, ids, blocks = place_ref[...].astype(jnp.float32), ids_ref[...], list_ref[...]
    rows = cut(place[0:1]) + cut(place[1:2])
    for i in range(DIGITS):
        digit = lax.rem(lax.div(ids, BASE**i), BASE)
        rows += cut(digit.astype(jnp.float32))
    per_tile = place.shape[1] // BLK
    part = per_tile // shares
    tile, within = lax.div(blocks, per_tile), lax.rem(blocks, per_tile)
    device = lax.div(tile, tile_cols) * shares + lax.div(within, part)
    spot = lax.rem(tile, tile_cols) * part + lax.rem(within, part)
    live = lax.broadcasted_iota(jnp.int32, blocks.shape, 1) < count_ref[0, 0]
    last_ref[...] = jnp.full_like(last_ref, BASE - 1.0)
    last_ref[0:1, 0 : blocks.shape[1]] = jnp.where(live, device, BASE - 1).astype(jnp.float32)
    last_ref[1:2, 0 : blocks.shape[1]] = spot.astype(jnp.float32)
    count = first_ref.shape[0] - half
    gap = jnp.zeros((count - len(rows) - PLACE_ROWS, LANES), jnp.float32)
    rows += ([gap] if gap.shape[0] else []) + [last_ref[...]]
    first_ref[pl.ds(half, count), :] = jnp.concatenate(rows, axis=0).astype(jnp.bfloat16)
    for copy in copies[4:]:
        copy.wait()


def pack(desc, place, ids, blocks, count, shares, tile_cols):
    points, width = desc.shape
    half = points // 2
    rows = -(-(2 + DIGITS) * (points // LANES) // 16) * 16 + PLACE_ROWS
    return pl.pallas_call(
        functools.partial(pack_kernel, shares, tile_cols),
        out_shape=(
            jax.ShapeDtypeStruct((half + rows, width), jnp.bfloat16),
            jax.ShapeDtypeStruct((half, width), jnp.bfloat16),
        ),
        in_specs=[pl.BlockSpec(memory_space=pltpu.HBM)] * 5,
        out_specs=(pl.BlockSpec(memory_space=pltpu.VMEM),) * 2,
        scratch_shapes=[
            pltpu.VMEM(place.shape, place.dtype),
            pltpu.VMEM(ids.shape, ids.dtype),
            pltpu.VMEM(blocks.shape, blocks.dtype),
            pltpu.SMEM(count.shape, count.dtype),
            pltpu.VMEM((PLACE_ROWS, LANES), jnp.float32),
            pltpu.SemaphoreType.DMA((6,)),
        ],
        name="pack",
    )(desc, place, ids, blocks, count)


def turns(axis):
    devices, here = lax.axis_size(axis), lax.axis_index(axis)
    if devices & (devices - 1):
        pairs = [[(i, (i + j) % devices) for i in range(devices)] for j in range(1, devices)]
        return pairs, jnp.mod(here - jnp.arange(devices), devices)
    pairs = [[(i, i ^ j) for i in range(devices)] for j in range(1, devices)]
    return pairs, here ^ jnp.arange(devices)


def key_kernel(shares, sec_ref, first_ref, second_ref, other_ref, key_ref, place_ref):
    half = second_ref.shape[0]
    per_tile = 2 * half // LANES
    part = per_tile // shares
    own, other = first_ref, first_ref
    if shares == 2:
        other = other_ref
    at_first = sec_ref[0] == 0

    def rest(ref, share):
        rows = ref[pl.ds(half, (2 + DIGITS) * per_tile), :].astype(jnp.float32)
        kept = [
            rows[i * per_tile + share * part : i * per_tile + (share + 1) * part]
            for i in range(2 + DIGITS)
        ]
        return jnp.concatenate(kept[:2], axis=0), kept[2:]

    if shares == 2:
        keys = jnp.where(at_first, other[pl.ds(0, half), :], second_ref[...])
        key_ref[pl.ds(0, half), :] = keys
        (own_0, ids_0), (own_1, _) = rest(own, 0), rest(own, 1)
        (other_0, _), (other_1, ids_1) = rest(other, 0), rest(other, 1)
        key_place = jnp.where(at_first, other_0, own_1)
        place_ref[...] = jnp.where(at_first, own_0, other_1)
        ids = [jnp.where(at_first, a, b) for a, b in zip(ids_0, ids_1)]
    else:
        key_ref[pl.ds(0, half), :] = own[pl.ds(0, half), :]
        key_ref[pl.ds(half, half), :] = second_ref[...]
        key_place, _ = rest(own, 0)
        place_ref[...], ids = rest(other_ref, 0)
    done = part * BLK
    filler = jnp.zeros((-(2 + DIGITS) * part % 16, LANES), jnp.float32)
    rows = [key_place] + ids + ([filler] if filler.shape[0] else [])
    key_ref[pl.ds(done, key_ref.shape[0] - done), :] = jnp.concatenate(rows, axis=0).astype(
        jnp.bfloat16
    )


def key_payload(sec, first_half, second_half, other, shares):
    half, width = second_half.shape
    part = 2 * half // LANES // shares
    rows = part * BLK + -(-(2 + DIGITS) * part // 16) * 16
    return pl.pallas_call(
        functools.partial(key_kernel, shares),
        out_shape=(
            jax.ShapeDtypeStruct((rows, width), jnp.bfloat16),
            jax.ShapeDtypeStruct((2 * part, LANES), jnp.float32),
        ),
        in_specs=[in_smem()] + in_vmem(3),
        out_specs=(pl.BlockSpec(memory_space=pltpu.VMEM),) * 2,
        compiler_params=pltpu.CompilerParams(vmem_limit_bytes=VMEM_BYTES),
        name="key_payload",
    )(sec, first_half, second_half, other)


def query_kernel(shares, sec_ref, first_ref, second_ref, other_ref, came_ref, out_ref):
    half = second_ref.shape[0]
    last = first_ref.shape[0] - PLACE_ROWS

    def chosen(own, other):
        return jnp.where(sec_ref[0] == 0, own, other) if shares == 2 else other

    for target, rows in ((0, pl.ds(0, half)), (2 * half, pl.ds(last, PLACE_ROWS))):
        out_ref[pl.ds(target, rows.size), :] = chosen(first_ref[rows, :], other_ref[rows, :])
    out_ref[pl.ds(half, half), :] = chosen(second_ref[...], came_ref[...])


def query_payload(sec, first_half, second_half, other, came, shares):
    half, width = second_half.shape
    return pl.pallas_call(
        functools.partial(query_kernel, shares),
        out_shape=jax.ShapeDtypeStruct((2 * half + PLACE_ROWS, width), jnp.bfloat16),
        in_specs=[in_smem()] + in_vmem(4),
        out_specs=pl.BlockSpec(memory_space=pltpu.VMEM),
        compiler_params=pltpu.CompilerParams(vmem_limit_bytes=VMEM_BYTES),
        name="query_payload",
    )(sec, first_half, second_half, other, came)


def gathered(values, axes, beside):
    held, steps = [], []
    for value, axis in zip(values, axes):
        devices = lax.axis_size(axis)
        if devices & (devices - 1):
            moved = [lax.ppermute(value, axis, pairs) for pairs in turns(axis)[0]]
            held.append(dict(enumerate([value] + moved)))
            steps.append(0)
        else:
            held.append({0: value})
            steps.append(devices.bit_length() - 1)
    for step in range(1, max(steps) + 1):
        for i, axis in enumerate(axes):
            devices = lax.axis_size(axis)
            for at in range(devices - 1, 0, -1):
                if steps[i] and at.bit_count() == step:
                    by = at & -at
                    pairs = [(j, j ^ by) for j in range(devices)]
                    held[i][at] = lax.ppermute(held[i][at ^ by], axis, pairs)
        if step == 1:
            held, beside = lax.optimization_barrier((held, beside))
    return [[h[i] for i in range(len(h))] for h in held], beside


def per_device(
    descriptors, positions, vertex_ids, candidate_blocks, candidate_count, displacement, stiffness
):
    point_total, width = descriptors.shape[3:]
    per_tile = point_total // BLK
    tile_rows, tile_cols = lax.axis_size("ty"), lax.axis_size("tx")
    sections = lax.axis_size("sec")
    sec_index = lax.axis_index("sec")
    tiles = tile_rows * tile_cols
    side = displacement.shape[3]
    halo = ITERS
    span = side + 2 * halo
    wide = -(-span // LANES) * LANES
    cand = candidate_blocks.shape[3]
    shares = 2 if sections == 2 and per_tile % 2 == 0 else 1
    part = per_tile // shares
    key_rows = part * BLK

    first_half, second_half = pack(
        descriptors[0, 0, 0],
        positions[0, 0, 0],
        vertex_ids[0, 0],
        candidate_blocks[0, 0],
        candidate_count[0, 0][None],
        shares,
        tile_cols,
    )
    half = point_total // 2
    swap = [(i, 1 - i) for i in range(2)]

    sec = jnp.asarray(sec_index, jnp.int32)[None]
    own_mesh = jnp.concatenate([displacement[0], stiffness], axis=0)
    if shares == 2:
        share = sec_index
        other = lax.ppermute(first_half, "sec", swap)
    else:
        share = 0
        other = passed_along(first_half, "sec", 1)
    came = passed_along(second_half, "sec", 1)
    cols = col_edges(own_mesh, halo)
    key, place = key_payload(sec, first_half, second_half, other, shares)
    meshes = [own_mesh]
    if shares == 2:
        tied, key = lax.optimization_barrier((jnp.concatenate([own_mesh, cols], axis=1), key))
        meshes.append(lax.ppermute(tied, "sec", swap))
    query = query_payload(sec, first_half, second_half, other, came, shares)
    (queries, keys), (cols, meshes) = gathered((query, key), ("ty", "tx"), (cols, meshes))
    at = jnp.concatenate(
        [
            jnp.stack([lax.axis_index("ty") * side, lax.axis_index("tx") * side, sec_index]),
            jnp.stack([lax.axis_index("ty"), jnp.asarray(share), jnp.asarray(shares)]),
            turns("ty")[1],
            turns("tx")[1],
        ]
    ).astype(jnp.int32)
    extent = (side * tile_rows, side * tile_cols)
    sum_shapes = [
        pltpu.VMEM((2, -(-span // 16) * 16, wide), jnp.float32),
        pltpu.VMEM((2, tiles, per_tile, LANES), jnp.float32),
    ]

    def packed(strip, corner):
        corner = corner.reshape(-1)
        corner = jnp.pad(corner, (0, -corner.shape[0] % (halo * LANES))).reshape(-1, LANES)
        return jnp.concatenate([strip.reshape(-1, LANES), corner], axis=0)

    edges = jnp.stack(
        [
            packed(own_mesh[:, :halo], cols[:, :, :halo]),
            packed(own_mesh[:, side - halo :], cols[:, :, side - halo :]),
        ]
    )
    parts = match(at, queries, keys, edges, 16.0 / width, shares, part)
    shape = parts.shape
    parts = exchanged(parts.reshape((-1,) + shape[2:]), ("sec", "ty") if shares == 2 else "ty")
    pulls = combine(parts, place, shares * tiles)
    parts, pulls, meshes = lax.optimization_barrier((parts, pulls, meshes))

    def edge_rows(by):
        near = lax.axis_index("ty") + by
        rows = parts.reshape(shape)[:, :, -edges.shape[1] :]
        rows = lax.dynamic_index_in_dim(rows, jnp.clip(near, 0, tile_rows - 1), 1, keepdims=False)
        rows = jnp.where((near >= 0) & (near < tile_rows), rows, 0.0)
        if shares == 2:
            rows = jnp.where(sec_index == 0, rows, rows[::-1])
        strip = rows[:, : 3 * halo].reshape(shares, 3, halo, side)
        corner = rows[:, 3 * halo :].reshape(shares, -1)[:, : 6 * halo * halo]
        corner = corner.reshape(shares, 3, 2 * halo, halo).swapaxes(2, 3)
        return jnp.concatenate([strip, corner], axis=3)

    after, before = edge_rows(1), edge_rows(-1)
    cols = [cols] + [mesh[:, side:] for mesh in meshes[1:]]
    meshes = [mesh[:, :side] for mesh in meshes]
    framed = []
    for i, mesh in enumerate(meshes):
        whole = jnp.concatenate([mesh, cols[i].swapaxes(1, 2)], axis=2)
        framed.append(jnp.concatenate([whole, after[i], before[i]], axis=1))
    framed = jnp.concatenate(framed, axis=0)
    gap = jnp.zeros(framed.shape[:2] + (wide - span,), framed.dtype)
    mesh_values = jnp.concatenate(
        [framed[:, :, : side + halo], gap, framed[:, :, side + halo :]], axis=2
    )
    if shares == 2:
        points = exchanged(pulls, ("sec", "ty", "tx"))
        rounds, rank, spot, number = spots(side, halo, tile_cols, wide, at, parts.reshape(shape), part)
        relaxed = pl.pallas_call(
            functools.partial(relax_kernel, side, halo, extent),
            out_shape=jax.ShapeDtypeStruct((2, side, side), jnp.float32),
            in_specs=[in_smem()] * 2 + in_vmem(5),
            out_specs=pl.BlockSpec(memory_space=pltpu.VMEM),
            scratch_shapes=sum_shapes,
            compiler_params=pltpu.CompilerParams(vmem_limit_bytes=VMEM_BYTES),
            name="relax",
        )(at, rounds, rank, spot, number, points.reshape(2, tiles, -1, LANES), mesh_values)
        return relaxed[None]

    points = passed_along(exchanged(pulls, ("ty", "tx")), "sec", -1)
    parts = passed_along(parts, "sec", -1)
    rounds, rank, spot, number = spots(side, halo, tile_cols, wide, at, parts[None], part)
    sums = pl.pallas_call(
        functools.partial(sums_kernel, side, halo),
        out_shape=jax.ShapeDtypeStruct((2, span, wide), jnp.float32),
        in_specs=[in_smem()] + in_vmem(3),
        out_specs=pl.BlockSpec(memory_space=pltpu.VMEM),
        scratch_shapes=sum_shapes,
        compiler_params=pltpu.CompilerParams(vmem_limit_bytes=VMEM_BYTES),
        name="sums",
    )(rounds, rank, spot, points[None])
    moving, gains = mesh_values[0:2], mesh_values[2]
    return sweeps(moving, gains, sums, number[:span], at, side, halo, extent)[None]


def solution(mesh):
    in_specs = (
        P("sec", "ty", "tx", None, None),
        P("sec", "ty", "tx", None, None),
        P("sec", "ty", "tx", None),
        P("sec", "ty", "tx", None),
        P("sec", "ty", "tx"),
        P("sec", None, "ty", "tx"),
        P("sec", "ty", "tx"),
    )
    out_specs = P("sec", None, "ty", "tx")
    return jax.shard_map(
        per_device, mesh=mesh, in_specs=in_specs, out_specs=out_specs, check_vma=False
    )
```

```python
import functools
import math

import jax
import jax.numpy as jnp
from jax import lax
from jax.experimental import pallas as pl
from jax.experimental.pallas import tpu as pltpu
from jax.sharding import PartitionSpec as P

BLK = 128
ITERS = 4
LANES = 128
PLACE_ROWS = 16
GROUP = 2
ROUND = 8
BASE = 256
DIGITS = 3
VMEM_BYTES = 24 * 1024 * 1024

spring_sec = 0.5
spring_match = 1.0
relax_rate = 0.8


def passed_along(value, axis, by):
    devices = lax.axis_size(axis)
    pairs = [(i, i + by) for i in range(devices) if 0 <= i + by < devices]
    return lax.ppermute(value, axis, pairs)


def exchanged(value, axes):
    return lax.all_to_all(value, axes, split_axis=0, concat_axis=0, tiled=True)


def spread(value, axes):
    copies = jnp.broadcast_to(value[None], (lax.axis_size(axes),) + value.shape)
    return exchanged(copies, axes)


def nt_dot(a, b):
    return lax.dot_general(a, b, (((1,), (1,)), ((), ())), preferred_element_type=jnp.float32)


def in_vmem(count):
    return [pl.BlockSpec(memory_space=pltpu.VMEM)] * count


def in_smem():
    return pl.BlockSpec(memory_space=pltpu.SMEM)


def match_kernel(scale, plan, last, at_ref, *refs):
    tile_rows = max(i for i, _ in plan) + 1
    key_tiles = max(max(among) for _, among in plan if among) + 1
    query_refs, refs = refs[:tile_rows], refs[tile_rows:]
    key_refs, refs = refs[:key_tiles], refs[key_tiles:]
    if last:
        before_ref, edge_ref, out_ref = refs[:3]
        refs = refs[3:]
    else:
        (out_ref,) = refs[:1]
        refs = refs[1:]
    query_buf, key_buf, place_buf, state_buf, list_buf = refs
    point_total = state_buf.shape[2]
    all_tiles, key_rows = key_buf.shape[:2]
    part = key_rows // BLK
    total = all_tiles * part
    own_row, share, shares = at_ref[3], at_ref[4], at_ref[5]
    rows_at, cols_at = 6, 6 + query_buf.shape[0]

    number = 0
    for tile, among in plan:
        met = [at_ref[cols_at + i] for i in among]
        listed = query_refs[tile][pl.ds(point_total, PLACE_ROWS), :]
        listed = listed.astype(jnp.float32).astype(jnp.int32)
        here = listed[0:1] == own_row * shares + share
        for low in range(0, total, 16):
            place = listed[1:2] - low
            bits = jnp.where(here & (place >= 0) & (place < 16), 1 << jnp.clip(place, 0, 15), 0)
            bits = jnp.sum(bits)
            for i in range(low, min(low + 16, total)):
                allowed = functools.reduce(jnp.logical_or, [col == i // part for col in met])
                list_buf[number] = tile * total + i
                number = number + jnp.where(allowed, (bits >> (i - low)) & 1, 0)
        list_buf[number] = -1
        number = number + lax.rem(number, 2)
    for i in range(2 * GROUP):
        list_buf[number + i] = -1
    groups = lax.div(number + 2 * GROUP - 1, 2 * GROUP)

    row_at = lax.broadcasted_iota(jnp.int32, (PLACE_ROWS, LANES), 0)
    ids = []
    for tile, key_ref in enumerate(key_refs):
        col = at_ref[cols_at + tile]
        key_buf[col] = key_ref[pl.ds(0, key_rows), :]
        rest = key_ref[pl.ds(key_rows, key_ref.shape[0] - key_rows), :].astype(jnp.float32)
        for j in range(part):
            x, y = rest[j : j + 1, :], rest[part + j : part + j + 1, :]
            stacked = jnp.where(
                row_at == 0, x, jnp.where(row_at == 1, y, jnp.where(row_at == 2, 1.0, 0.0))
            )
            place_buf[col * part + j] = stacked.astype(jnp.bfloat16)
        digits = [rest[(2 + i) * part : (3 + i) * part] for i in range(DIGITS)]
        ids.append(sum(digit * float(BASE**i) for i, digit in enumerate(digits)))
    for tile, query_ref in enumerate(query_refs):
        query_buf[tile] = query_ref[pl.ds(0, point_total), :]

    state_row = lax.broadcasted_iota(jnp.int32, state_buf.shape[1:], 0)
    for tile in range(tile_rows):
        if last and tile < before_ref.shape[0]:
            state_buf[tile] = before_ref[tile]
        else:
            state_buf[tile] = jnp.where(state_row == 3, -1e30, 0.0)

    def item(at):
        codes = [list_buf[2 * at + i] for i in range(2)]
        tile = lax.div(jnp.maximum(codes[0], 0), total)
        keys, places = [], []
        for i, code in enumerate(codes):
            block = lax.rem(jnp.maximum(jnp.where(code >= 0, code, codes[0]), 0), total)
            block = jnp.where(codes[0] >= 0, block, at_ref[cols_at] * part)
            start = pl.multiple_of(lax.rem(block, part) * BLK, BLK)
            keys.append(key_buf[lax.div(block, part), pl.ds(start, BLK), :])
            kept = jnp.where(code >= 0, 1.0, 0.0).astype(jnp.bfloat16)
            places.append(place_buf[block] * kept)
        return tile, codes[0] >= 0, jnp.concatenate(keys, axis=0), jnp.concatenate(places, axis=1)

    @pl.loop(0, groups)
    def _(group):
        items = [item(group * GROUP + i) for i in range(GROUP)]
        scores = [nt_dot(keys, query_buf[tile]) * scale for tile, _, keys, _ in items]
        tops = [jnp.max(score, axis=0, keepdims=True) for score in scores]
        weights = [jnp.exp2(s - top).astype(jnp.bfloat16) for s, top in zip(scores, tops)]
        sums = [
            jnp.dot(place, weight, preferred_element_type=jnp.float32)[0:8]
            for (_, _, _, place), weight in zip(items, weights)
        ]
        for (tile, live, _, _), top, added in zip(items, tops, sums):
            top = jnp.where(live, top, -1e30)
            state = state_buf[tile]
            before = state[3:4, :]
            both = jnp.maximum(before, top)
            state = state * jnp.exp2(before - both) + added * jnp.exp2(top - both)
            state_buf[tile] = jnp.where(state_row == 3, both, state)

    if not last:
        out_ref[...] = state_buf[pl.ds(0, tile_rows)]
        return
    edge_rows = edge_ref.shape[1]
    for tile in range(tile_rows):
        to = at_ref[rows_at + tile]
        for row in range(point_total // LANES):
            lanes = pl.ds(row * LANES, LANES)
            for place, held in enumerate((3, 2, 0, 1)):
                out_ref[row // part, to, pl.ds(place * part + row % part, 1), :] = state_buf[
                    tile, pl.ds(held, 1), lanes
                ]
        for share in range(out_ref.shape[0]):
            out_ref[share, tile, pl.ds(4 * part, key_tiles * part), :] = jnp.concatenate(ids, axis=0)
            out_ref[share, tile, pl.ds((4 + key_tiles) * part, edge_rows), :] = jnp.where(
                tile > own_row, edge_ref[1], jnp.where(tile < own_row, edge_ref[0], edge_ref[2])
            )


def match(at, queries, keys, edges, score_factor, shares, part):
    tile_rows, key_tiles = len(queries), len(keys)
    point_total, width = queries[0].shape[0] - PLACE_ROWS, queries[0].shape[1]
    total = key_tiles * part

    def call(plan, out_shape, *more):
        many_rows = max(i for i, _ in plan) + 1
        many_keys = max(max(among) for _, among in plan if among) + 1
        scores = sum(len(among) for _, among in plan) * part * point_total * BLK
        return pl.pallas_call(
            functools.partial(
                match_kernel, score_factor * math.log2(math.e), plan, len(more) > 0
            ),
            out_shape=jax.ShapeDtypeStruct(out_shape, jnp.float32),
            in_specs=[in_smem()] + in_vmem(many_rows + many_keys + len(more)),
            out_specs=pl.BlockSpec(memory_space=pltpu.VMEM),
            scratch_shapes=[
                pltpu.VMEM((tile_rows, point_total, width), jnp.bfloat16),
                pltpu.VMEM((key_tiles, part * BLK, width), jnp.bfloat16),
                pltpu.VMEM((total, PLACE_ROWS, LANES), jnp.bfloat16),
                pltpu.VMEM((tile_rows, 8, point_total), jnp.float32),
                pltpu.SMEM((tile_rows * (total + 1) + 2 * GROUP + 1,), jnp.int32),
            ],
            compiler_params=pltpu.CompilerParams(vmem_limit_bytes=VMEM_BYTES),
            cost_estimate=pl.CostEstimate(
                flops=scores * width, bytes_accessed=4 * scores // BLK, transcendentals=scores // 4
            ),
            name="match_rest" if more else "match",
        )(at, *queries[:many_rows], *keys[:many_keys], *more)

    there = [
        [i for i in range(n) if i.bit_count() < 2 or n & (n - 1)] for n in (tile_rows, key_tiles)
    ]
    first = [(i, tuple(there[1])) for i in there[0]]
    rest = [(i, tuple(j for j in range(key_tiles) if j not in there[1])) for i in there[0]]
    rest = [v for v in rest if v[1]]
    rest += [(i, tuple(range(key_tiles))) for i in range(tile_rows) if i not in there[0]]
    if rest:
        state = call(first, (len(first), 8, point_total))
    else:
        rest, row = first, jnp.arange(8)[None, :, None]
        state = jnp.where(row == 3, -1e30, jnp.zeros((tile_rows, 8, point_total), jnp.float32))
    shape = (shares, tile_rows, (4 + key_tiles) * part + edges.shape[1], LANES)
    return call(rest, shape, state, edges)


def combine_kernel(parts_ref, place_ref, out_ref):
    parts = parts_ref.shape[0]
    rows = place_ref.shape[0] // 2
    tops = [parts_ref[i, 0:rows, :] for i in range(parts)]
    top = functools.reduce(jnp.maximum, tops)
    total = x = y = jnp.zeros_like(top)
    for i in range(parts):
        gain = jnp.exp2(tops[i] - top)
        total += gain * parts_ref[i, rows : 2 * rows, :]
        x += gain * parts_ref[i, 2 * rows : 3 * rows, :]
        y += gain * parts_ref[i, 3 * rows : 4 * rows, :]
    pull = jnp.concatenate([x / total, y / total], axis=0) - place_ref[...]
    for i in range(out_ref.shape[0]):
        out_ref[i] = pull


def combine(parts, place, copies):
    return pl.pallas_call(
        combine_kernel,
        out_shape=jax.ShapeDtypeStruct((copies,) + place.shape, jnp.float32),
        in_specs=in_vmem(2),
        out_specs=pl.BlockSpec(memory_space=pltpu.VMEM),
        compiler_params=pltpu.CompilerParams(vmem_limit_bytes=VMEM_BYTES),
        name="combine",
    )(parts, place)


def one_hot(at, length, limits):
    count = at.shape[1]
    parts, done = [], 0
    for low, high in limits:
        spot = lax.broadcasted_iota(jnp.int32, (high - low, count), 0) + low
        if low > done:
            parts.append(jnp.zeros((low - done, count), jnp.bfloat16))
        parts.append(jnp.where(spot == at, 1.0, 0.0).astype(jnp.bfloat16))
        done = high
    if length > done:
        parts.append(jnp.zeros((length - done, count), jnp.bfloat16))
    return jnp.concatenate(parts, axis=0)


def flat(value):
    return jnp.concatenate([value[i : i + 1, :] for i in range(value.shape[0])], axis=1)


def hits(side, halo, tall, wide, row, col):
    up = lambda n: -(-n // 16) * 16
    limits = ((0, up(side + halo)), (wide - up(halo), wide))
    return one_hot(flat(row), tall, ((0, tall),)), one_hot(flat(col), wide, limits)


def ranked(rank, row, values):
    sums = [0.0] * len(values)
    for tile in range(rank.shape[0]):
        here = rank[tile] == row
        sums = [total + jnp.where(here, v[tile], 0.0) for total, v in zip(sums, values)]
    return [jnp.sum(total, axis=0, keepdims=True) for total in sums]


def spots_kernel(
    side, halo, key_tiles, at_ref, parts_ref, rounds_ref, rank_ref, spot_ref, count_ref, hit_buf
):
    shares, tile_rows, _, _ = parts_ref.shape
    count = rank_ref.shape[1]
    rows = count // shares
    tall, wide = count_ref.shape

    def folded(at, length):
        return jnp.where(
            (at >= 0) & (at < side + halo), at, jnp.where((at < 0) & (at >= -halo), at + length, -1)
        )

    number = jnp.zeros((1, LANES), jnp.int32)
    point_row = lax.broadcasted_iota(jnp.int32, (count, LANES), 0)
    for i in range(tile_rows):
        for j in range(key_tiles):
            ids = jnp.concatenate(
                [parts_ref[k, i, pl.ds((4 + j) * rows, rows), :] for k in range(shares)], axis=0
            ).astype(jnp.int32)
            tile_of = lax.div(ids, side * side)
            within = lax.rem(ids, side * side)
            row = lax.div(tile_of, key_tiles) * side + lax.div(within, side) - at_ref[0]
            col = lax.rem(tile_of, key_tiles) * side + lax.rem(within, side) - at_ref[1]
            row, col = folded(row, side + 2 * halo), folded(col, wide)
            here = (row >= 0) & (col >= 0)
            hit = here.astype(jnp.int32)
            by = 1
            while by < count:
                hit = hit + jnp.where(point_row >= by, pltpu.roll(hit, by, 0), 0)
                by *= 2
            tile = i * key_tiles + at_ref[6 + tile_rows + j]
            rank_ref[tile] = jnp.where(here, number + hit - 1, -1)
            hit_buf[0, tile] = row.astype(jnp.float32) + 1.0
            hit_buf[1, tile] = col.astype(jnp.float32) + 1.0
            number = number + hit[count - 1 : count, :]
    rounds = lax.div(jnp.max(number) + ROUND - 1, ROUND)
    rounds_ref[0] = rounds
    count_ref[...] = jnp.zeros_like(count_ref)

    @pl.loop(0, rounds)
    def _(k):
        found = [ranked(rank_ref, k * ROUND + r, (hit_buf.at[0], hit_buf.at[1])) for r in range(ROUND)]
        row, col = (jnp.concatenate(v, axis=0).astype(jnp.int32) - 1 for v in zip(*found))
        spot_ref[k, 0] = row
        spot_ref[k, 1] = col
        row_hit, col_hit = hits(side, halo, tall, wide, row, col)
        count_ref[...] += nt_dot(row_hit, col_hit)


def spots(side, halo, key_tiles, wide, at, parts, rows):
    tall = -(-(side + 2 * halo) // 16) * 16
    count = parts.shape[0] * rows
    tiles = parts.shape[1] * key_tiles
    rounds = -(-tiles * count // ROUND)
    return pl.pallas_call(
        functools.partial(spots_kernel, side, halo, key_tiles),
        out_shape=(
            jax.ShapeDtypeStruct((1,), jnp.int32),
            jax.ShapeDtypeStruct((tiles, count, LANES), jnp.int32),
            jax.ShapeDtypeStruct((rounds, 2, ROUND, LANES), jnp.int32),
            jax.ShapeDtypeStruct((tall, wide), jnp.float32),
        ),
        in_specs=[in_smem()] + in_vmem(1),
        out_specs=(in_smem(),) + (pl.BlockSpec(memory_space=pltpu.VMEM),) * 3,
        scratch_shapes=[pltpu.VMEM((2, tiles, count, LANES), jnp.float32)],
        compiler_params=pltpu.CompilerParams(vmem_limit_bytes=VMEM_BYTES),
        cost_estimate=pl.CostEstimate(
            flops=8 * tall * ROUND * LANES * wide,
            bytes_accessed=8 * parts.size,
            transcendentals=0,
        ),
        name="spots",
    )(at, parts)


def vertex_sums(side, halo, rounds_ref, rank_ref, spot_ref, points_ref, sum_ref, point_buf):
    _, tall, wide = sum_ref.shape
    shares, tiles, both_rows, _ = points_ref.shape
    rows = both_rows // 2
    sum_ref[...] = jnp.zeros_like(sum_ref)
    for tile in range(tiles):
        for share in range(shares):
            for c in range(2):
                point_buf[c, tile, pl.ds(share * rows, rows), :] = points_ref[
                    share, tile, pl.ds(c * rows, rows), :
                ]

    @pl.loop(0, rounds_ref[0])
    def _(k):
        found = [
            ranked(rank_ref, k * ROUND + r, (point_buf.at[0], point_buf.at[1])) for r in range(ROUND)
        ]
        _, col_hit = hits(side, halo, tall, wide, spot_ref[k, 0], spot_ref[k, 1])
        row = flat(spot_ref[k, 0])
        row_hit = lax.broadcasted_iota(jnp.int32, (tall, row.shape[1]), 0) == row
        parts = []
        for value in zip(*found):
            value = jnp.concatenate(value, axis=1)
            high = value.astype(jnp.bfloat16).astype(jnp.float32)
            for part in (high, value - high):
                parts.append(jnp.where(row_hit, part, 0.0).astype(jnp.bfloat16))
        summed = nt_dot(jnp.concatenate(parts, axis=0), col_hit)
        sum_ref[0] += summed[0:tall] + summed[tall : 2 * tall]
        sum_ref[1] += summed[2 * tall : 3 * tall] + summed[3 * tall :]


def sums_kernel(side, halo, rounds_ref, rank_ref, spot_ref, points_ref, out_ref, sum_ref, point_buf):
    vertex_sums(side, halo, rounds_ref, rank_ref, spot_ref, points_ref, sum_ref, point_buf)
    out_ref[...] = sum_ref[:, pl.ds(0, out_ref.shape[1]), :]


def relax_kernel(
    side,
    halo,
    extent,
    at_ref,
    rounds_ref,
    rank_ref,
    spot_ref,
    count_ref,
    points_ref,
    mesh_ref,
    out_ref,
    sum_ref,
    point_buf,
):
    vertex_sums(side, halo, rounds_ref, rank_ref, spot_ref, points_ref, sum_ref, point_buf)
    span = side + 2 * halo
    wide = sum_ref.shape[2]
    shape = (span, wide)
    row = lax.broadcasted_iota(jnp.int32, shape, 0)
    col = lax.broadcasted_iota(jnp.int32, shape, 1)
    row = jnp.where(row < side + halo, row, row - span) + at_ref[0]
    col = jnp.where(col < side + halo, col, col - wide) + at_ref[1]
    inside = (row >= 0) & (row < extent[0]) & (col >= 0) & (col < extent[1])
    own_pulled = (at_ref[2] == 0).astype(jnp.float32)
    linked = 1.0
    matched = count_ref[pl.ds(0, span), :]
    moving, gains, has, step = [], [], [], []
    for part, pulled in enumerate((own_pulled, 1.0 - own_pulled)):
        gain = mesh_ref[part * 3 + 2]
        diagonal = 4.0 * gain + spring_sec * linked + spring_match * matched * pulled
        gains.append(gain)
        has.append(matched * pulled)
        step.append(jnp.where(inside, relax_rate / diagonal, 0.0))
        moving.append(
            [(mesh_ref[part * 3 + c], sum_ref[c, pl.ds(0, span), :] * pulled) for c in range(2)]
        )
    for sweep in range(ITERS):
        later = []
        for part in range(2):
            row_of = []
            for c in range(2):
                u, pulled = moving[part][c]
                other = moving[1 - part][c][0]
                laplace = (
                    pltpu.roll(u, 1, 0)
                    + pltpu.roll(u, span - 1, 0)
                    + pltpu.roll(u, 1, 1)
                    + pltpu.roll(u, wide - 1, 1)
                    - 4.0 * u
                )
                force = (
                    gains[part] * laplace
                    + spring_sec * (other - linked * u)
                    + spring_match * (pulled - has[part] * u)
                )
                row_of.append((u + step[part] * force, pulled))
            later.append(row_of)
        moving = later
    for c in range(2):
        out_ref[c] = moving[0][c][0][0:side, 0:side]


def col_edges(value, halo):
    after = passed_along(value[:, :, :halo].swapaxes(1, 2), "tx", -1)
    before = passed_along(value[:, :, value.shape[2] - halo :].swapaxes(1, 2), "tx", 1)
    return jnp.concatenate([after, before], axis=1)


def sweeps(moving, gains, sums, number, at, side, halo, extent):
    sections = lax.axis_size("sec")
    sec_index = at[2]
    has_next = (sec_index < sections - 1).astype(jnp.float32)
    linked = (sec_index > 0).astype(jnp.float32) + has_next
    pulled, matched = sums * has_next, number * has_next
    span, wide = moving.shape[1:]
    row = jnp.arange(span)[:, None]
    col = jnp.arange(wide)[None, :]
    row = jnp.where(row < side + halo, row, row - span) + at[0]
    col = jnp.where(col < side + halo, col, col - wide) + at[1]
    inside = (row >= 0) & (row < extent[0]) & (col >= 0) & (col < extent[1])
    diagonal = 4.0 * gains + spring_sec * linked + spring_match * matched
    step = jnp.where(inside, relax_rate / jnp.where(inside, diagonal, 1.0), 0.0)
    for sweep in range(ITERS):
        lower_sec = passed_along(moving, "sec", 1)
        upper_sec = passed_along(moving, "sec", -1)
        laplace = (
            jnp.roll(moving, 1, 1)
            + jnp.roll(moving, -1, 1)
            + jnp.roll(moving, 1, 2)
            + jnp.roll(moving, -1, 2)
            - 4.0 * moving
        )
        force = (
            gains * laplace
            + spring_sec * (lower_sec + upper_sec - linked * moving)
            + spring_match * (pulled - matched * moving)
        )
        moving = moving + step * force
    return moving[:, :side, :side]


def pack_kernel(
    shares,
    tile_cols,
    desc_hbm,
    place_hbm,
    ids_hbm,
    list_hbm,
    count_hbm,
    first_ref,
    second_ref,
    place_ref,
    ids_ref,
    list_ref,
    count_ref,
    last_ref,
    sems,
):
    half = second_ref.shape[0]
    copies = [
        pltpu.make_async_copy(source, target, sems.at[i])
        for i, (source, target) in enumerate(
            (
                (place_hbm, place_ref),
                (ids_hbm, ids_ref),
                (list_hbm, list_ref),
                (count_hbm, count_ref),
                (desc_hbm.at[pl.ds(0, half), :], first_ref.at[pl.ds(0, half), :]),
                (desc_hbm.at[pl.ds(half, half), :], second_ref),
            )
        )
    ]
    for copy in copies:
        copy.start()
    for copy in copies[:4]:
        copy.wait()

    def cut(row):
        return [row[:, i : i + LANES] for i in range(0, row.shape[1], LANES)]

    place, ids, blocks = place_ref[...].astype(jnp.float32), ids_ref[...], list_ref[...]
    rows = cut(place[0:1]) + cut(place[1:2])
    for i in range(DIGITS):
        digit = lax.rem(lax.div(ids, BASE**i), BASE)
        rows += cut(digit.astype(jnp.float32))
    per_tile = place.shape[1] // BLK
    part = per_tile // shares
    tile, within = lax.div(blocks, per_tile), lax.rem(blocks, per_tile)
    device = lax.div(tile, tile_cols) * shares + lax.div(within, part)
    spot = lax.rem(tile, tile_cols) * part + lax.rem(within, part)
    live = lax.broadcasted_iota(jnp.int32, blocks.shape, 1) < count_ref[0, 0]
    last_ref[...] = jnp.full_like(last_ref, BASE - 1.0)
    last_ref[0:1, 0 : blocks.shape[1]] = jnp.where(live, device, BASE - 1).astype(jnp.float32)
    last_ref[1:2, 0 : blocks.shape[1]] = spot.astype(jnp.float32)
    count = first_ref.shape[0] - half
    gap = jnp.zeros((count - len(rows) - PLACE_ROWS, LANES), jnp.float32)
    rows += ([gap] if gap.shape[0] else []) + [last_ref[...]]
    first_ref[pl.ds(half, count), :] = jnp.concatenate(rows, axis=0).astype(jnp.bfloat16)
    for copy in copies[4:]:
        copy.wait()


def pack(desc, place, ids, blocks, count, shares, tile_cols):
    points, width = desc.shape
    half = points // 2
    rows = -(-(2 + DIGITS) * (points // LANES) // 16) * 16 + PLACE_ROWS
    return pl.pallas_call(
        functools.partial(pack_kernel, shares, tile_cols),
        out_shape=(
            jax.ShapeDtypeStruct((half + rows, width), jnp.bfloat16),
            jax.ShapeDtypeStruct((half, width), jnp.bfloat16),
        ),
        in_specs=[pl.BlockSpec(memory_space=pltpu.HBM)] * 5,
        out_specs=(pl.BlockSpec(memory_space=pltpu.VMEM),) * 2,
        scratch_shapes=[
            pltpu.VMEM(place.shape, place.dtype),
            pltpu.VMEM(ids.shape, ids.dtype),
            pltpu.VMEM(blocks.shape, blocks.dtype),
            pltpu.SMEM(count.shape, count.dtype),
            pltpu.VMEM((PLACE_ROWS, LANES), jnp.float32),
            pltpu.SemaphoreType.DMA((6,)),
        ],
        name="pack",
    )(desc, place, ids, blocks, count)


def turns(axis):
    devices, here = lax.axis_size(axis), lax.axis_index(axis)
    if devices & (devices - 1):
        pairs = [[(i, (i + j) % devices) for i in range(devices)] for j in range(1, devices)]
        return pairs, jnp.mod(here - jnp.arange(devices), devices)
    pairs = [[(i, i ^ j) for i in range(devices)] for j in range(1, devices)]
    return pairs, here ^ jnp.arange(devices)


def key_kernel(shares, sec_ref, first_ref, second_ref, other_ref, key_ref, place_ref):
    half = second_ref.shape[0]
    per_tile = 2 * half // LANES
    part = per_tile // shares
    own, other = first_ref, first_ref
    if shares == 2:
        other = other_ref
    at_first = sec_ref[0] == 0

    def rest(ref, share):
        rows = ref[pl.ds(half, (2 + DIGITS) * per_tile), :].astype(jnp.float32)
        kept = [
            rows[i * per_tile + share * part : i * per_tile + (share + 1) * part]
            for i in range(2 + DIGITS)
        ]
        return jnp.concatenate(kept[:2], axis=0), kept[2:]

    if shares == 2:
        keys = jnp.where(at_first, other[pl.ds(0, half), :], second_ref[...])
        key_ref[pl.ds(0, half), :] = keys
        (own_0, ids_0), (own_1, _) = rest(own, 0), rest(own, 1)
        (other_0, _), (other_1, ids_1) = rest(other, 0), rest(other, 1)
        key_place = jnp.where(at_first, other_0, own_1)
        place_ref[...] = jnp.where(at_first, own_0, other_1)
        ids = [jnp.where(at_first, a, b) for a, b in zip(ids_0, ids_1)]
    else:
        key_ref[pl.ds(0, half), :] = own[pl.ds(0, half), :]
        key_ref[pl.ds(half, half), :] = second_ref[...]
        key_place, _ = rest(own, 0)
        place_ref[...], ids = rest(other_ref, 0)
    done = part * BLK
    filler = jnp.zeros((-(2 + DIGITS) * part % 16, LANES), jnp.float32)
    rows = [key_place] + ids + ([filler] if filler.shape[0] else [])
    key_ref[pl.ds(done, key_ref.shape[0] - done), :] = jnp.concatenate(rows, axis=0).astype(
        jnp.bfloat16
    )


def key_payload(sec, first_half, second_half, other, shares):
    half, width = second_half.shape
    part = 2 * half // LANES // shares
    rows = part * BLK + -(-(2 + DIGITS) * part // 16) * 16
    return pl.pallas_call(
        functools.partial(key_kernel, shares),
        out_shape=(
            jax.ShapeDtypeStruct((rows, width), jnp.bfloat16),
            jax.ShapeDtypeStruct((2 * part, LANES), jnp.float32),
        ),
        in_specs=[in_smem()] + in_vmem(3),
        out_specs=(pl.BlockSpec(memory_space=pltpu.VMEM),) * 2,
        compiler_params=pltpu.CompilerParams(vmem_limit_bytes=VMEM_BYTES),
        name="key_payload",
    )(sec, first_half, second_half, other)


def query_kernel(shares, sec_ref, first_ref, second_ref, other_ref, came_ref, out_ref):
    half = second_ref.shape[0]
    last = first_ref.shape[0] - PLACE_ROWS

    def chosen(own, other):
        return jnp.where(sec_ref[0] == 0, own, other) if shares == 2 else other

    for target, rows in ((0, pl.ds(0, half)), (2 * half, pl.ds(last, PLACE_ROWS))):
        out_ref[pl.ds(target, rows.size), :] = chosen(first_ref[rows, :], other_ref[rows, :])
    out_ref[pl.ds(half, half), :] = chosen(second_ref[...], came_ref[...])


def query_payload(sec, first_half, second_half, other, came, shares):
    half, width = second_half.shape
    return pl.pallas_call(
        functools.partial(query_kernel, shares),
        out_shape=jax.ShapeDtypeStruct((2 * half + PLACE_ROWS, width), jnp.bfloat16),
        in_specs=[in_smem()] + in_vmem(4),
        out_specs=pl.BlockSpec(memory_space=pltpu.VMEM),
        compiler_params=pltpu.CompilerParams(vmem_limit_bytes=VMEM_BYTES),
        name="query_payload",
    )(sec, first_half, second_half, other, came)


def gathered(values, axes, beside):
    held, steps = [], []
    for value, axis in zip(values, axes):
        devices = lax.axis_size(axis)
        if devices & (devices - 1):
            moved = [lax.ppermute(value, axis, pairs) for pairs in turns(axis)[0]]
            held.append(dict(enumerate([value] + moved)))
            steps.append(0)
        else:
            held.append({0: value})
            steps.append(devices.bit_length() - 1)
    for step in range(1, max(steps) + 1):
        for i, axis in enumerate(axes):
            devices = lax.axis_size(axis)
            for at in range(devices - 1, 0, -1):
                if steps[i] and at.bit_count() == step:
                    by = at & -at
                    pairs = [(j, j ^ by) for j in range(devices)]
                    held[i][at] = lax.ppermute(held[i][at ^ by], axis, pairs)
        if step == 1:
            held, beside = lax.optimization_barrier((held, beside))
    return [[h[i] for i in range(len(h))] for h in held], beside


def per_device(
    descriptors, positions, vertex_ids, candidate_blocks, candidate_count, displacement, stiffness
):
    point_total, width = descriptors.shape[3:]
    per_tile = point_total // BLK
    tile_rows, tile_cols = lax.axis_size("ty"), lax.axis_size("tx")
    sections = lax.axis_size("sec")
    sec_index = lax.axis_index("sec")
    tiles = tile_rows * tile_cols
    side = displacement.shape[3]
    halo = ITERS
    span = side + 2 * halo
    wide = -(-span // LANES) * LANES
    cand = candidate_blocks.shape[3]
    shares = 2 if sections == 2 and per_tile % 2 == 0 else 1
    part = per_tile // shares
    key_rows = part * BLK

    first_half, second_half = pack(
        descriptors[0, 0, 0],
        positions[0, 0, 0],
        vertex_ids[0, 0],
        candidate_blocks[0, 0],
        candidate_count[0, 0][None],
        shares,
        tile_cols,
    )
    half = point_total // 2
    swap = [(i, 1 - i) for i in range(2)]

    sec = jnp.asarray(sec_index, jnp.int32)[None]
    own_mesh = jnp.concatenate([displacement[0], stiffness], axis=0)
    if shares == 2:
        share = sec_index
        other = lax.ppermute(first_half, "sec", swap)
    else:
        share = 0
        other = passed_along(first_half, "sec", 1)
    came = passed_along(second_half, "sec", 1)
    cols = col_edges(own_mesh, halo)
    key, place = key_payload(sec, first_half, second_half, other, shares)
    meshes = [own_mesh]
    if shares == 2:
        tied, key = lax.optimization_barrier((own_mesh, key))
        meshes.append(lax.ppermute(tied, "sec", swap))
    query = query_payload(sec, first_half, second_half, other, came, shares)
    (queries, keys), (cols, meshes) = gathered((query, key), ("ty", "tx"), (cols, meshes))
    at = jnp.concatenate(
        [
            jnp.stack([lax.axis_index("ty") * side, lax.axis_index("tx") * side, sec_index]),
            jnp.stack([lax.axis_index("ty"), jnp.asarray(share), jnp.asarray(shares)]),
            turns("ty")[1],
            turns("tx")[1],
        ]
    ).astype(jnp.int32)
    extent = (side * tile_rows, side * tile_cols)
    sum_shapes = [
        pltpu.VMEM((2, -(-span // 16) * 16, wide), jnp.float32),
        pltpu.VMEM((2, tiles, per_tile, LANES), jnp.float32),
    ]

    top, end = own_mesh[:, :halo], own_mesh[:, side - halo :]
    corners = [
        jnp.pad(v.swapaxes(1, 2), ((0, 0), (0, 0), (0, side - 2 * halo)))
        for v in (cols[:, :, :halo], cols[:, :, side - halo :])
    ]
    edges = [jnp.concatenate(v, axis=0) for v in ((top, corners[0]), (end, corners[1]))]
    edges = jnp.stack([v.reshape(-1, LANES) for v in edges + [cols]])
    parts = match(at, queries, keys, edges, 16.0 / width, shares, part)
    shape = parts.shape
    parts = exchanged(parts.reshape((-1,) + shape[2:]), ("sec", "ty") if shares == 2 else "ty")
    pulls = combine(parts, place, shares * tiles)
    parts, pulls, meshes = lax.optimization_barrier((parts, pulls, meshes))

    def edge_rows(by):
        near = lax.axis_index("ty") + by
        rows = parts.reshape(shape)[:, :, -edges.shape[1] :]
        rows = lax.dynamic_index_in_dim(rows, jnp.clip(near, 0, tile_rows - 1), 1, keepdims=False)
        rows = jnp.where((near >= 0) & (near < tile_rows), rows, 0.0)
        rows = rows.reshape(shares, 2, 3, halo, side)
        if shares == 2:
            rows = jnp.where(sec_index == 0, rows, rows[::-1])
        return [
            jnp.concatenate([rows[i, 0], rows[i, 1, :, :, : 2 * halo]], axis=2)
            for i in range(shares)
        ]

    after, before = edge_rows(1), edge_rows(-1)
    cols = [cols]
    if shares == 2:
        sent = parts.reshape(shape)[:, :, -edges.shape[1] :]
        sent = lax.dynamic_index_in_dim(sent, lax.axis_index("ty"), 1, keepdims=False)
        cols.append(jnp.where(sec_index == 0, sent[1], sent[0]).reshape(cols[0].shape))
    framed = []
    for i, mesh in enumerate(meshes):
        whole = jnp.concatenate([mesh, cols[i].swapaxes(1, 2)], axis=2)
        framed.append(jnp.concatenate([whole, after[i], before[i]], axis=1))
    framed = jnp.concatenate(framed, axis=0)
    gap = jnp.zeros(framed.shape[:2] + (wide - span,), framed.dtype)
    mesh_values = jnp.concatenate(
        [framed[:, :, : side + halo], gap, framed[:, :, side + halo :]], axis=2
    )
    if shares == 2:
        points = exchanged(pulls, ("sec", "ty", "tx"))
        rounds, rank, spot, number = spots(side, halo, tile_cols, wide, at, parts.reshape(shape), part)
        relaxed = pl.pallas_call(
            functools.partial(relax_kernel, side, halo, extent),
            out_shape=jax.ShapeDtypeStruct((2, side, side), jnp.float32),
            in_specs=[in_smem()] * 2 + in_vmem(5),
            out_specs=pl.BlockSpec(memory_space=pltpu.VMEM),
            scratch_shapes=sum_shapes,
            compiler_params=pltpu.CompilerParams(vmem_limit_bytes=VMEM_BYTES),
            name="relax",
        )(at, rounds, rank, spot, number, points.reshape(2, tiles, -1, LANES), mesh_values)
        return relaxed[None]

    points = passed_along(exchanged(pulls, ("ty", "tx")), "sec", -1)
    parts = passed_along(parts, "sec", -1)
    rounds, rank, spot, number = spots(side, halo, tile_cols, wide, at, parts[None], part)
    sums = pl.pallas_call(
        functools.partial(sums_kernel, side, halo),
        out_shape=jax.ShapeDtypeStruct((2, span, wide), jnp.float32),
        in_specs=[in_smem()] + in_vmem(3),
        out_specs=pl.BlockSpec(memory_space=pltpu.VMEM),
        scratch_shapes=sum_shapes,
        compiler_params=pltpu.CompilerParams(vmem_limit_bytes=VMEM_BYTES),
        name="sums",
    )(rounds, rank, spot, points[None])
    moving, gains = mesh_values[0:2], mesh_values[2]
    return sweeps(moving, gains, sums, number[:span], at, side, halo, extent)[None]


def solution(mesh):
    in_specs = (
        P("sec", "ty", "tx", None, None),
        P("sec", "ty", "tx", None, None),
        P("sec", "ty", "tx", None),
        P("sec", "ty", "tx", None),
        P("sec", "ty", "tx"),
        P("sec", None, "ty", "tx"),
        P("sec", "ty", "tx"),
    )
    out_specs = P("sec", None, "ty", "tx")
    return jax.shard_map(
        per_device, mesh=mesh, in_specs=in_specs, out_specs=out_specs, check_vma=False
    )
```

```python
import functools
import math

import jax
import jax.numpy as jnp
from jax import lax
from jax.experimental import pallas as pl
from jax.experimental.pallas import tpu as pltpu
from jax.sharding import PartitionSpec as P

BLK = 128
ITERS = 4
LANES = 128
PLACE_ROWS = 16
GROUP = 2
ROUND = 4
BASE = 256
DIGITS = 3
VMEM_BYTES = 24 * 1024 * 1024

spring_sec = 0.5
spring_match = 1.0
relax_rate = 0.8


def passed_along(value, axis, by):
    devices = lax.axis_size(axis)
    pairs = [(i, i + by) for i in range(devices) if 0 <= i + by < devices]
    return lax.ppermute(value, axis, pairs)


def exchanged(value, axes):
    return lax.all_to_all(value, axes, split_axis=0, concat_axis=0, tiled=True)


def spread(value, axes):
    copies = jnp.broadcast_to(value[None], (lax.axis_size(axes),) + value.shape)
    return exchanged(copies, axes)


def nt_dot(a, b):
    return lax.dot_general(a, b, (((1,), (1,)), ((), ())), preferred_element_type=jnp.float32)


def in_vmem(count):
    return [pl.BlockSpec(memory_space=pltpu.VMEM)] * count


def in_smem():
    return pl.BlockSpec(memory_space=pltpu.SMEM)


def match_kernel(scale, plan, last, at_ref, *refs):
    tile_rows = max(i for i, _ in plan) + 1
    key_tiles = max(max(among) for _, among in plan if among) + 1
    query_refs, refs = refs[:tile_rows], refs[tile_rows:]
    key_refs, refs = refs[:key_tiles], refs[key_tiles:]
    if last:
        before_ref, edge_ref, out_ref = refs[:3]
        refs = refs[3:]
    else:
        (out_ref,) = refs[:1]
        refs = refs[1:]
    query_buf, key_buf, place_buf, state_buf, list_buf = refs
    point_total = state_buf.shape[2]
    all_tiles, key_rows = key_buf.shape[:2]
    part = key_rows // BLK
    total = all_tiles * part
    own_row, share, shares = at_ref[3], at_ref[4], at_ref[5]
    rows_at, cols_at = 6, 6 + query_buf.shape[0]

    number = 0
    for tile, among in plan:
        met = [at_ref[cols_at + i] for i in among]
        listed = query_refs[tile][pl.ds(point_total, PLACE_ROWS), :]
        listed = listed.astype(jnp.float32).astype(jnp.int32)
        here = listed[0:1] == own_row * shares + share
        for low in range(0, total, 16):
            place = listed[1:2] - low
            bits = jnp.where(here & (place >= 0) & (place < 16), 1 << jnp.clip(place, 0, 15), 0)
            bits = jnp.sum(bits)
            for i in range(low, min(low + 16, total)):
                allowed = functools.reduce(jnp.logical_or, [col == i // part for col in met])
                list_buf[number] = tile * total + i
                number = number + jnp.where(allowed, (bits >> (i - low)) & 1, 0)
        list_buf[number] = -1
        number = number + lax.rem(number, 2)
    for i in range(2 * GROUP):
        list_buf[number + i] = -1
    groups = lax.div(number + 2 * GROUP - 1, 2 * GROUP)

    row_at = lax.broadcasted_iota(jnp.int32, (PLACE_ROWS, LANES), 0)
    ids = []
    for tile, key_ref in enumerate(key_refs):
        col = at_ref[cols_at + tile]
        key_buf[col] = key_ref[pl.ds(0, key_rows), :]
        rest = key_ref[pl.ds(key_rows, key_ref.shape[0] - key_rows), :].astype(jnp.float32)
        for j in range(part):
            x, y = rest[j : j + 1, :], rest[part + j : part + j + 1, :]
            stacked = jnp.where(
                row_at == 0, x, jnp.where(row_at == 1, y, jnp.where(row_at == 2, 1.0, 0.0))
            )
            place_buf[col * part + j] = stacked.astype(jnp.bfloat16)
        digits = [rest[(2 + i) * part : (3 + i) * part] for i in range(DIGITS)]
        ids.append(sum(digit * float(BASE**i) for i, digit in enumerate(digits)))
    for tile, query_ref in enumerate(query_refs):
        query_buf[tile] = query_ref[pl.ds(0, point_total), :]

    state_row = lax.broadcasted_iota(jnp.int32, state_buf.shape[1:], 0)
    for tile in range(tile_rows):
        if last and tile < before_ref.shape[0]:
            state_buf[tile] = before_ref[tile]
        else:
            state_buf[tile] = jnp.where(state_row == 3, -1e30, 0.0)

    def item(at):
        codes = [list_buf[2 * at + i] for i in range(2)]
        tile = lax.div(jnp.maximum(codes[0], 0), total)
        keys, places = [], []
        for i, code in enumerate(codes):
            block = lax.rem(jnp.maximum(jnp.where(code >= 0, code, codes[0]), 0), total)
            block = jnp.where(codes[0] >= 0, block, at_ref[cols_at] * part)
            start = pl.multiple_of(lax.rem(block, part) * BLK, BLK)
            keys.append(key_buf[lax.div(block, part), pl.ds(start, BLK), :])
            kept = jnp.where(code >= 0, 1.0, 0.0).astype(jnp.bfloat16)
            places.append(place_buf[block] * kept)
        return tile, codes[0] >= 0, jnp.concatenate(keys, axis=0), jnp.concatenate(places, axis=1)

    @pl.loop(0, groups)
    def _(group):
        items = [item(group * GROUP + i) for i in range(GROUP)]
        scores = [nt_dot(keys, query_buf[tile]) * scale for tile, _, keys, _ in items]
        tops = [jnp.max(score, axis=0, keepdims=True) for score in scores]
        weights = [jnp.exp2(s - top).astype(jnp.bfloat16) for s, top in zip(scores, tops)]
        sums = [
            jnp.dot(place, weight, preferred_element_type=jnp.float32)[0:8]
            for (_, _, _, place), weight in zip(items, weights)
        ]
        for (tile, live, _, _), top, added in zip(items, tops, sums):
            top = jnp.where(live, top, -1e30)
            state = state_buf[tile]
            before = state[3:4, :]
            both = jnp.maximum(before, top)
            state = state * jnp.exp2(before - both) + added * jnp.exp2(top - both)
            state_buf[tile] = jnp.where(state_row == 3, both, state)

    if not last:
        out_ref[...] = state_buf[pl.ds(0, tile_rows)]
        return
    edge_rows = edge_ref.shape[1]
    for tile in range(tile_rows):
        to = at_ref[rows_at + tile]
        for row in range(point_total // LANES):
            lanes = pl.ds(row * LANES, LANES)
            for place, held in enumerate((3, 2, 0, 1)):
                out_ref[row // part, to, pl.ds(place * part + row % part, 1), :] = state_buf[
                    tile, pl.ds(held, 1), lanes
                ]
        for share in range(out_ref.shape[0]):
            out_ref[share, tile, pl.ds(4 * part, key_tiles * part), :] = jnp.concatenate(ids, axis=0)
            out_ref[share, tile, pl.ds((4 + key_tiles) * part, edge_rows), :] = jnp.where(
                tile > own_row, edge_ref[1], jnp.where(tile < own_row, edge_ref[0], edge_ref[2])
            )


def match(at, queries, keys, edges, score_factor, shares, part):
    tile_rows, key_tiles = len(queries), len(keys)
    point_total, width = queries[0].shape[0] - PLACE_ROWS, queries[0].shape[1]
    total = key_tiles * part

    def call(plan, out_shape, *more):
        many_rows = max(i for i, _ in plan) + 1
        many_keys = max(max(among) for _, among in plan if among) + 1
        scores = sum(len(among) for _, among in plan) * part * point_total * BLK
        return pl.pallas_call(
            functools.partial(
                match_kernel, score_factor * math.log2(math.e), plan, len(more) > 0
            ),
            out_shape=jax.ShapeDtypeStruct(out_shape, jnp.float32),
            in_specs=[in_smem()] + in_vmem(many_rows + many_keys + len(more)),
            out_specs=pl.BlockSpec(memory_space=pltpu.VMEM),
            scratch_shapes=[
                pltpu.VMEM((tile_rows, point_total, width), jnp.bfloat16),
                pltpu.VMEM((key_tiles, part * BLK, width), jnp.bfloat16),
                pltpu.VMEM((total, PLACE_ROWS, LANES), jnp.bfloat16),
                pltpu.VMEM((tile_rows, 8, point_total), jnp.float32),
                pltpu.SMEM((tile_rows * (total + 1) + 2 * GROUP + 1,), jnp.int32),
            ],
            compiler_params=pltpu.CompilerParams(vmem_limit_bytes=VMEM_BYTES),
            cost_estimate=pl.CostEstimate(
                flops=scores * width, bytes_accessed=4 * scores // BLK, transcendentals=scores // 4
            ),
            name="match_rest" if more else "match",
        )(at, *queries[:many_rows], *keys[:many_keys], *more)

    there = [
        [i for i in range(n) if i.bit_count() < 2 or n & (n - 1)] for n in (tile_rows, key_tiles)
    ]
    first = [(i, tuple(there[1])) for i in there[0]]
    rest = [(i, tuple(j for j in range(key_tiles) if j not in there[1])) for i in there[0]]
    rest = [v for v in rest if v[1]]
    rest += [(i, tuple(range(key_tiles))) for i in range(tile_rows) if i not in there[0]]
    if rest:
        state = call(first, (len(first), 8, point_total))
    else:
        rest, row = first, jnp.arange(8)[None, :, None]
        state = jnp.where(row == 3, -1e30, jnp.zeros((tile_rows, 8, point_total), jnp.float32))
    shape = (shares, tile_rows, (4 + key_tiles) * part + edges.shape[1], LANES)
    return call(rest, shape, state, edges)


def combine_kernel(parts_ref, place_ref, out_ref):
    parts = parts_ref.shape[0]
    rows = place_ref.shape[0] // 2
    tops = [parts_ref[i, 0:rows, :] for i in range(parts)]
    top = functools.reduce(jnp.maximum, tops)
    total = x = y = jnp.zeros_like(top)
    for i in range(parts):
        gain = jnp.exp2(tops[i] - top)
        total += gain * parts_ref[i, rows : 2 * rows, :]
        x += gain * parts_ref[i, 2 * rows : 3 * rows, :]
        y += gain * parts_ref[i, 3 * rows : 4 * rows, :]
    pull = jnp.concatenate([x / total, y / total], axis=0) - place_ref[...]
    for i in range(out_ref.shape[0]):
        out_ref[i] = pull


def combine(parts, place, copies):
    return pl.pallas_call(
        combine_kernel,
        out_shape=jax.ShapeDtypeStruct((copies,) + place.shape, jnp.float32),
        in_specs=in_vmem(2),
        out_specs=pl.BlockSpec(memory_space=pltpu.VMEM),
        compiler_params=pltpu.CompilerParams(vmem_limit_bytes=VMEM_BYTES),
        name="combine",
    )(parts, place)


def one_hot(at, length, limits):
    count = at.shape[1]
    parts, done = [], 0
    for low, high in limits:
        spot = lax.broadcasted_iota(jnp.int32, (high - low, count), 0) + low
        if low > done:
            parts.append(jnp.zeros((low - done, count), jnp.bfloat16))
        parts.append(jnp.where(spot == at, 1.0, 0.0).astype(jnp.bfloat16))
        done = high
    if length > done:
        parts.append(jnp.zeros((length - done, count), jnp.bfloat16))
    return jnp.concatenate(parts, axis=0)


def flat(value):
    return jnp.concatenate([value[i : i + 1, :] for i in range(value.shape[0])], axis=1)


def hits(side, halo, tall, wide, row, col):
    up = lambda n: -(-n // 16) * 16
    limits = ((0, up(side + halo)), (wide - up(halo), wide))
    return one_hot(flat(row), tall, ((0, tall),)), one_hot(flat(col), wide, limits)


def ranked(rank, row, values):
    sums = [0.0] * len(values)
    for tile in range(rank.shape[0]):
        here = rank[tile] == row
        sums = [total + jnp.where(here, v[tile], 0.0) for total, v in zip(sums, values)]
    return [jnp.sum(total, axis=0, keepdims=True) for total in sums]


def spots_kernel(
    side, halo, key_tiles, at_ref, parts_ref, rounds_ref, rank_ref, spot_ref, count_ref, hit_buf
):
    shares, tile_rows, _, _ = parts_ref.shape
    count = rank_ref.shape[1]
    rows = count // shares
    tall, wide = count_ref.shape

    def folded(at, length):
        return jnp.where(
            (at >= 0) & (at < side + halo), at, jnp.where((at < 0) & (at >= -halo), at + length, -1)
        )

    number = jnp.zeros((1, LANES), jnp.int32)
    point_row = lax.broadcasted_iota(jnp.int32, (count, LANES), 0)
    for i in range(tile_rows):
        for j in range(key_tiles):
            ids = jnp.concatenate(
                [parts_ref[k, i, pl.ds((4 + j) * rows, rows), :] for k in range(shares)], axis=0
            ).astype(jnp.int32)
            tile_of = lax.div(ids, side * side)
            within = lax.rem(ids, side * side)
            row = lax.div(tile_of, key_tiles) * side + lax.div(within, side) - at_ref[0]
            col = lax.rem(tile_of, key_tiles) * side + lax.rem(within, side) - at_ref[1]
            row, col = folded(row, side + 2 * halo), folded(col, wide)
            here = (row >= 0) & (col >= 0)
            hit = here.astype(jnp.int32)
            by = 1
            while by < count:
                hit = hit + jnp.where(point_row >= by, pltpu.roll(hit, by, 0), 0)
                by *= 2
            tile = i * key_tiles + at_ref[6 + tile_rows + j]
            rank_ref[tile] = jnp.where(here, number + hit - 1, -1)
            hit_buf[0, tile] = row.astype(jnp.float32) + 1.0
            hit_buf[1, tile] = col.astype(jnp.float32) + 1.0
            number = number + hit[count - 1 : count, :]
    rounds = lax.div(jnp.max(number) + ROUND - 1, ROUND)
    rounds_ref[0] = rounds
    count_ref[...] = jnp.zeros_like(count_ref)

    @pl.loop(0, rounds)
    def _(k):
        found = [ranked(rank_ref, k * ROUND + r, (hit_buf.at[0], hit_buf.at[1])) for r in range(ROUND)]
        row, col = (jnp.concatenate(v, axis=0).astype(jnp.int32) - 1 for v in zip(*found))
        spot_ref[k, 0] = row
        spot_ref[k, 1] = col
        row_hit, col_hit = hits(side, halo, tall, wide, row, col)
        count_ref[...] += nt_dot(row_hit, col_hit)


def spots(side, halo, key_tiles, wide, at, parts, rows):
    tall = -(-(side + 2 * halo) // 16) * 16
    count = parts.shape[0] * rows
    tiles = parts.shape[1] * key_tiles
    rounds = -(-tiles * count // ROUND)
    return pl.pallas_call(
        functools.partial(spots_kernel, side, halo, key_tiles),
        out_shape=(
            jax.ShapeDtypeStruct((1,), jnp.int32),
            jax.ShapeDtypeStruct((tiles, count, LANES), jnp.int32),
            jax.ShapeDtypeStruct((rounds, 2, ROUND, LANES), jnp.int32),
            jax.ShapeDtypeStruct((tall, wide), jnp.float32),
        ),
        in_specs=[in_smem()] + in_vmem(1),
        out_specs=(in_smem(),) + (pl.BlockSpec(memory_space=pltpu.VMEM),) * 3,
        scratch_shapes=[pltpu.VMEM((2, tiles, count, LANES), jnp.float32)],
        compiler_params=pltpu.CompilerParams(vmem_limit_bytes=VMEM_BYTES),
        cost_estimate=pl.CostEstimate(
            flops=8 * tall * ROUND * LANES * wide,
            bytes_accessed=8 * parts.size,
            transcendentals=0,
        ),
        name="spots",
    )(at, parts)


def vertex_sums(side, halo, rounds_ref, rank_ref, spot_ref, points_ref, sum_ref, point_buf):
    _, tall, wide = sum_ref.shape
    shares, tiles, both_rows, _ = points_ref.shape
    rows = both_rows // 2
    sum_ref[...] = jnp.zeros_like(sum_ref)
    for tile in range(tiles):
        for share in range(shares):
            for c in range(2):
                point_buf[c, tile, pl.ds(share * rows, rows), :] = points_ref[
                    share, tile, pl.ds(c * rows, rows), :
                ]

    @pl.loop(0, rounds_ref[0])
    def _(k):
        found = [
            ranked(rank_ref, k * ROUND + r, (point_buf.at[0], point_buf.at[1])) for r in range(ROUND)
        ]
        _, col_hit = hits(side, halo, tall, wide, spot_ref[k, 0], spot_ref[k, 1])
        row = flat(spot_ref[k, 0])
        row_hit = lax.broadcasted_iota(jnp.int32, (tall, row.shape[1]), 0) == row
        parts = []
        for value in zip(*found):
            value = jnp.concatenate(value, axis=1)
            high = value.astype(jnp.bfloat16).astype(jnp.float32)
            for part in (high, value - high):
                parts.append(jnp.where(row_hit, part, 0.0).astype(jnp.bfloat16))
        summed = nt_dot(jnp.concatenate(parts, axis=0), col_hit)
        sum_ref[0] += summed[0:tall] + summed[tall : 2 * tall]
        sum_ref[1] += summed[2 * tall : 3 * tall] + summed[3 * tall :]


def sums_kernel(side, halo, rounds_ref, rank_ref, spot_ref, points_ref, out_ref, sum_ref, point_buf):
    vertex_sums(side, halo, rounds_ref, rank_ref, spot_ref, points_ref, sum_ref, point_buf)
    out_ref[...] = sum_ref[:, pl.ds(0, out_ref.shape[1]), :]


def relax_kernel(
    side,
    halo,
    extent,
    at_ref,
    rounds_ref,
    rank_ref,
    spot_ref,
    count_ref,
    points_ref,
    mesh_ref,
    out_ref,
    sum_ref,
    point_buf,
):
    vertex_sums(side, halo, rounds_ref, rank_ref, spot_ref, points_ref, sum_ref, point_buf)
    span = side + 2 * halo
    wide = sum_ref.shape[2]
    shape = (span, wide)
    row = lax.broadcasted_iota(jnp.int32, shape, 0)
    col = lax.broadcasted_iota(jnp.int32, shape, 1)
    row = jnp.where(row < side + halo, row, row - span) + at_ref[0]
    col = jnp.where(col < side + halo, col, col - wide) + at_ref[1]
    inside = (row >= 0) & (row < extent[0]) & (col >= 0) & (col < extent[1])
    own_pulled = (at_ref[2] == 0).astype(jnp.float32)
    linked = 1.0
    matched = count_ref[pl.ds(0, span), :]
    moving, gains, has, step = [], [], [], []
    for part, pulled in enumerate((own_pulled, 1.0 - own_pulled)):
        gain = mesh_ref[part * 3 + 2]
        diagonal = 4.0 * gain + spring_sec * linked + spring_match * matched * pulled
        gains.append(gain)
        has.append(matched * pulled)
        step.append(jnp.where(inside, relax_rate / diagonal, 0.0))
        moving.append(
            [(mesh_ref[part * 3 + c], sum_ref[c, pl.ds(0, span), :] * pulled) for c in range(2)]
        )
    for sweep in range(ITERS):
        later = []
        for part in range(2):
            row_of = []
            for c in range(2):
                u, pulled = moving[part][c]
                other = moving[1 - part][c][0]
                laplace = (
                    pltpu.roll(u, 1, 0)
                    + pltpu.roll(u, span - 1, 0)
                    + pltpu.roll(u, 1, 1)
                    + pltpu.roll(u, wide - 1, 1)
                    - 4.0 * u
                )
                force = (
                    gains[part] * laplace
                    + spring_sec * (other - linked * u)
                    + spring_match * (pulled - has[part] * u)
                )
                row_of.append((u + step[part] * force, pulled))
            later.append(row_of)
        moving = later
    for c in range(2):
        out_ref[c] = moving[0][c][0][0:side, 0:side]


def col_edges(value, halo):
    after = passed_along(value[:, :, :halo].swapaxes(1, 2), "tx", -1)
    before = passed_along(value[:, :, value.shape[2] - halo :].swapaxes(1, 2), "tx", 1)
    return jnp.concatenate([after, before], axis=1)


def sweeps(moving, gains, sums, number, at, side, halo, extent):
    sections = lax.axis_size("sec")
    sec_index = at[2]
    has_next = (sec_index < sections - 1).astype(jnp.float32)
    linked = (sec_index > 0).astype(jnp.float32) + has_next
    pulled, matched = sums * has_next, number * has_next
    span, wide = moving.shape[1:]
    row = jnp.arange(span)[:, None]
    col = jnp.arange(wide)[None, :]
    row = jnp.where(row < side + halo, row, row - span) + at[0]
    col = jnp.where(col < side + halo, col, col - wide) + at[1]
    inside = (row >= 0) & (row < extent[0]) & (col >= 0) & (col < extent[1])
    diagonal = 4.0 * gains + spring_sec * linked + spring_match * matched
    step = jnp.where(inside, relax_rate / jnp.where(inside, diagonal, 1.0), 0.0)
    for sweep in range(ITERS):
        lower_sec = passed_along(moving, "sec", 1)
        upper_sec = passed_along(moving, "sec", -1)
        laplace = (
            jnp.roll(moving, 1, 1)
            + jnp.roll(moving, -1, 1)
            + jnp.roll(moving, 1, 2)
            + jnp.roll(moving, -1, 2)
            - 4.0 * moving
        )
        force = (
            gains * laplace
            + spring_sec * (lower_sec + upper_sec - linked * moving)
            + spring_match * (pulled - matched * moving)
        )
        moving = moving + step * force
    return moving[:, :side, :side]


def pack_kernel(
    shares,
    tile_cols,
    desc_hbm,
    place_hbm,
    ids_hbm,
    list_hbm,
    count_hbm,
    first_ref,
    second_ref,
    place_ref,
    ids_ref,
    list_ref,
    count_ref,
    last_ref,
    sems,
):
    half = second_ref.shape[0]
    copies = [
        pltpu.make_async_copy(source, target, sems.at[i])
        for i, (source, target) in enumerate(
            (
                (place_hbm, place_ref),
                (ids_hbm, ids_ref),
                (list_hbm, list_ref),
                (count_hbm, count_ref),
                (desc_hbm.at[pl.ds(0, half), :], first_ref.at[pl.ds(0, half), :]),
                (desc_hbm.at[pl.ds(half, half), :], second_ref),
            )
        )
    ]
    for copy in copies:
        copy.start()
    for copy in copies[:4]:
        copy.wait()

    def cut(row):
        return [row[:, i : i + LANES] for i in range(0, row.shape[1], LANES)]

    place, ids, blocks = place_ref[...].astype(jnp.float32), ids_ref[...], list_ref[...]
    rows = cut(place[0:1]) + cut(place[1:2])
    for i in range(DIGITS):
        digit = lax.rem(lax.div(ids, BASE**i), BASE)
        rows += cut(digit.astype(jnp.float32))
    per_tile = place.shape[1] // BLK
    part = per_tile // shares
    tile, within = lax.div(blocks, per_tile), lax.rem(blocks, per_tile)
    device = lax.div(tile, tile_cols) * shares + lax.div(within, part)
    spot = lax.rem(tile, tile_cols) * part + lax.rem(within, part)
    live = lax.broadcasted_iota(jnp.int32, blocks.shape, 1) < count_ref[0, 0]
    last_ref[...] = jnp.full_like(last_ref, BASE - 1.0)
    last_ref[0:1, 0 : blocks.shape[1]] = jnp.where(live, device, BASE - 1).astype(jnp.float32)
    last_ref[1:2, 0 : blocks.shape[1]] = spot.astype(jnp.float32)
    count = first_ref.shape[0] - half
    gap = jnp.zeros((count - len(rows) - PLACE_ROWS, LANES), jnp.float32)
    rows += ([gap] if gap.shape[0] else []) + [last_ref[...]]
    first_ref[pl.ds(half, count), :] = jnp.concatenate(rows, axis=0).astype(jnp.bfloat16)
    for copy in copies[4:]:
        copy.wait()


def pack(desc, place, ids, blocks, count, shares, tile_cols):
    points, width = desc.shape
    half = points // 2
    rows = -(-(2 + DIGITS) * (points // LANES) // 16) * 16 + PLACE_ROWS
    return pl.pallas_call(
        functools.partial(pack_kernel, shares, tile_cols),
        out_shape=(
            jax.ShapeDtypeStruct((half + rows, width), jnp.bfloat16),
            jax.ShapeDtypeStruct((half, width), jnp.bfloat16),
        ),
        in_specs=[pl.BlockSpec(memory_space=pltpu.HBM)] * 5,
        out_specs=(pl.BlockSpec(memory_space=pltpu.VMEM),) * 2,
        scratch_shapes=[
            pltpu.VMEM(place.shape, place.dtype),
            pltpu.VMEM(ids.shape, ids.dtype),
            pltpu.VMEM(blocks.shape, blocks.dtype),
            pltpu.SMEM(count.shape, count.dtype),
            pltpu.VMEM((PLACE_ROWS, LANES), jnp.float32),
            pltpu.SemaphoreType.DMA((6,)),
        ],
        name="pack",
    )(desc, place, ids, blocks, count)


def turns(axis):
    devices, here = lax.axis_size(axis), lax.axis_index(axis)
    if devices & (devices - 1):
        pairs = [[(i, (i + j) % devices) for i in range(devices)] for j in range(1, devices)]
        return pairs, jnp.mod(here - jnp.arange(devices), devices)
    pairs = [[(i, i ^ j) for i in range(devices)] for j in range(1, devices)]
    return pairs, here ^ jnp.arange(devices)


def key_kernel(shares, sec_ref, first_ref, second_ref, other_ref, key_ref, place_ref):
    half = second_ref.shape[0]
    per_tile = 2 * half // LANES
    part = per_tile // shares
    own, other = first_ref, first_ref
    if shares == 2:
        other = other_ref
    at_first = sec_ref[0] == 0

    def rest(ref, share):
        rows = ref[pl.ds(half, (2 + DIGITS) * per_tile), :].astype(jnp.float32)
        kept = [
            rows[i * per_tile + share * part : i * per_tile + (share + 1) * part]
            for i in range(2 + DIGITS)
        ]
        return jnp.concatenate(kept[:2], axis=0), kept[2:]

    if shares == 2:
        keys = jnp.where(at_first, other[pl.ds(0, half), :], second_ref[...])
        key_ref[pl.ds(0, half), :] = keys
        (own_0, ids_0), (own_1, _) = rest(own, 0), rest(own, 1)
        (other_0, _), (other_1, ids_1) = rest(other, 0), rest(other, 1)
        key_place = jnp.where(at_first, other_0, own_1)
        place_ref[...] = jnp.where(at_first, own_0, other_1)
        ids = [jnp.where(at_first, a, b) for a, b in zip(ids_0, ids_1)]
    else:
        key_ref[pl.ds(0, half), :] = own[pl.ds(0, half), :]
        key_ref[pl.ds(half, half), :] = second_ref[...]
        key_place, _ = rest(own, 0)
        place_ref[...], ids = rest(other_ref, 0)
    done = part * BLK
    filler = jnp.zeros((-(2 + DIGITS) * part % 16, LANES), jnp.float32)
    rows = [key_place] + ids + ([filler] if filler.shape[0] else [])
    key_ref[pl.ds(done, key_ref.shape[0] - done), :] = jnp.concatenate(rows, axis=0).astype(
        jnp.bfloat16
    )


def key_payload(sec, first_half, second_half, other, shares):
    half, width = second_half.shape
    part = 2 * half // LANES // shares
    rows = part * BLK + -(-(2 + DIGITS) * part // 16) * 16
    return pl.pallas_call(
        functools.partial(key_kernel, shares),
        out_shape=(
            jax.ShapeDtypeStruct((rows, width), jnp.bfloat16),
            jax.ShapeDtypeStruct((2 * part, LANES), jnp.float32),
        ),
        in_specs=[in_smem()] + in_vmem(3),
        out_specs=(pl.BlockSpec(memory_space=pltpu.VMEM),) * 2,
        compiler_params=pltpu.CompilerParams(vmem_limit_bytes=VMEM_BYTES),
        name="key_payload",
    )(sec, first_half, second_half, other)


def query_kernel(shares, sec_ref, first_ref, second_ref, other_ref, came_ref, out_ref):
    half = second_ref.shape[0]
    last = first_ref.shape[0] - PLACE_ROWS

    def chosen(own, other):
        return jnp.where(sec_ref[0] == 0, own, other) if shares == 2 else other

    for target, rows in ((0, pl.ds(0, half)), (2 * half, pl.ds(last, PLACE_ROWS))):
        out_ref[pl.ds(target, rows.size), :] = chosen(first_ref[rows, :], other_ref[rows, :])
    out_ref[pl.ds(half, half), :] = chosen(second_ref[...], came_ref[...])


def query_payload(sec, first_half, second_half, other, came, shares):
    half, width = second_half.shape
    return pl.pallas_call(
        functools.partial(query_kernel, shares),
        out_shape=jax.ShapeDtypeStruct((2 * half + PLACE_ROWS, width), jnp.bfloat16),
        in_specs=[in_smem()] + in_vmem(4),
        out_specs=pl.BlockSpec(memory_space=pltpu.VMEM),
        compiler_params=pltpu.CompilerParams(vmem_limit_bytes=VMEM_BYTES),
        name="query_payload",
    )(sec, first_half, second_half, other, came)


def gathered(values, axes, beside):
    held, steps = [], []
    for value, axis in zip(values, axes):
        devices = lax.axis_size(axis)
        if devices & (devices - 1):
            moved = [lax.ppermute(value, axis, pairs) for pairs in turns(axis)[0]]
            held.append(dict(enumerate([value] + moved)))
            steps.append(0)
        else:
            held.append({0: value})
            steps.append(devices.bit_length() - 1)
    for step in range(1, max(steps) + 1):
        for i, axis in enumerate(axes):
            devices = lax.axis_size(axis)
            for at in range(devices - 1, 0, -1):
                if steps[i] and at.bit_count() == step:
                    by = at & -at
                    pairs = [(j, j ^ by) for j in range(devices)]
                    held[i][at] = lax.ppermute(held[i][at ^ by], axis, pairs)
        if step == 1:
            held, beside = lax.optimization_barrier((held, beside))
    return [[h[i] for i in range(len(h))] for h in held], beside


def per_device(
    descriptors, positions, vertex_ids, candidate_blocks, candidate_count, displacement, stiffness
):
    point_total, width = descriptors.shape[3:]
    per_tile = point_total // BLK
    tile_rows, tile_cols = lax.axis_size("ty"), lax.axis_size("tx")
    sections = lax.axis_size("sec")
    sec_index = lax.axis_index("sec")
    tiles = tile_rows * tile_cols
    side = displacement.shape[3]
    halo = ITERS
    span = side + 2 * halo
    wide = -(-span // LANES) * LANES
    cand = candidate_blocks.shape[3]
    shares = 2 if sections == 2 and per_tile % 2 == 0 else 1
    part = per_tile // shares
    key_rows = part * BLK

    first_half, second_half = pack(
        descriptors[0, 0, 0],
        positions[0, 0, 0],
        vertex_ids[0, 0],
        candidate_blocks[0, 0],
        candidate_count[0, 0][None],
        shares,
        tile_cols,
    )
    half = point_total // 2
    swap = [(i, 1 - i) for i in range(2)]

    sec = jnp.asarray(sec_index, jnp.int32)[None]
    own_mesh = jnp.concatenate([displacement[0], stiffness], axis=0)
    if shares == 2:
        share = sec_index
        other = lax.ppermute(first_half, "sec", swap)
    else:
        share = 0
        other = passed_along(first_half, "sec", 1)
    came = passed_along(second_half, "sec", 1)
    cols = col_edges(own_mesh, halo)
    key, place = key_payload(sec, first_half, second_half, other, shares)
    meshes = [own_mesh]
    if shares == 2:
        tied, key = lax.optimization_barrier((own_mesh, key))
        meshes.append(lax.ppermute(tied, "sec", swap))
    query = query_payload(sec, first_half, second_half, other, came, shares)
    (queries, keys), (cols, meshes) = gathered((query, key), ("ty", "tx"), (cols, meshes))
    at = jnp.concatenate(
        [
            jnp.stack([lax.axis_index("ty") * side, lax.axis_index("tx") * side, sec_index]),
            jnp.stack([lax.axis_index("ty"), jnp.asarray(share), jnp.asarray(shares)]),
            turns("ty")[1],
            turns("tx")[1],
        ]
    ).astype(jnp.int32)
    extent = (side * tile_rows, side * tile_cols)
    sum_shapes = [
        pltpu.VMEM((2, -(-span // 16) * 16, wide), jnp.float32),
        pltpu.VMEM((2, tiles, per_tile, LANES), jnp.float32),
    ]

    top, end = own_mesh[:, :halo], own_mesh[:, side - halo :]
    corners = [
        jnp.pad(v.swapaxes(1, 2), ((0, 0), (0, 0), (0, side - 2 * halo)))
        for v in (cols[:, :, :halo], cols[:, :, side - halo :])
    ]
    edges = [jnp.concatenate(v, axis=0) for v in ((top, corners[0]), (end, corners[1]))]
    edges = jnp.stack([v.reshape(-1, LANES) for v in edges + [cols]])
    parts = match(at, queries, keys, edges, 16.0 / width, shares, part)
    shape = parts.shape
    parts = exchanged(parts.reshape((-1,) + shape[2:]), ("sec", "ty") if shares == 2 else "ty")
    pulls = combine(parts, place, shares * tiles)
    parts, pulls, meshes = lax.optimization_barrier((parts, pulls, meshes))

    def edge_rows(by):
        near = lax.axis_index("ty") + by
        rows = parts.reshape(shape)[:, :, -edges.shape[1] :]
        rows = lax.dynamic_index_in_dim(rows, jnp.clip(near, 0, tile_rows - 1), 1, keepdims=False)
        rows = jnp.where((near >= 0) & (near < tile_rows), rows, 0.0)
        rows = rows.reshape(shares, 2, 3, halo, side)
        if shares == 2:
            rows = jnp.where(sec_index == 0, rows, rows[::-1])
        return [
            jnp.concatenate([rows[i, 0], rows[i, 1, :, :, : 2 * halo]], axis=2)
            for i in range(shares)
        ]

    after, before = edge_rows(1), edge_rows(-1)
    cols = [cols]
    if shares == 2:
        sent = parts.reshape(shape)[:, :, -edges.shape[1] :]
        sent = lax.dynamic_index_in_dim(sent, lax.axis_index("ty"), 1, keepdims=False)
        cols.append(jnp.where(sec_index == 0, sent[1], sent[0]).reshape(cols[0].shape))
    framed = []
    for i, mesh in enumerate(meshes):
        whole = jnp.concatenate([mesh, cols[i].swapaxes(1, 2)], axis=2)
        framed.append(jnp.concatenate([whole, after[i], before[i]], axis=1))
    framed = jnp.concatenate(framed, axis=0)
    gap = jnp.zeros(framed.shape[:2] + (wide - span,), framed.dtype)
    mesh_values = jnp.concatenate(
        [framed[:, :, : side + halo], gap, framed[:, :, side + halo :]], axis=2
    )
    if shares == 2:
        points = exchanged(pulls, ("sec", "ty", "tx"))
        rounds, rank, spot, number = spots(side, halo, tile_cols, wide, at, parts.reshape(shape), part)
        relaxed = pl.pallas_call(
            functools.partial(relax_kernel, side, halo, extent),
            out_shape=jax.ShapeDtypeStruct((2, side, side), jnp.float32),
            in_specs=[in_smem()] * 2 + in_vmem(5),
            out_specs=pl.BlockSpec(memory_space=pltpu.VMEM),
            scratch_shapes=sum_shapes,
            compiler_params=pltpu.CompilerParams(vmem_limit_bytes=VMEM_BYTES),
            name="relax",
        )(at, rounds, rank, spot, number, points.reshape(2, tiles, -1, LANES), mesh_values)
        return relaxed[None]

    points = passed_along(exchanged(pulls, ("ty", "tx")), "sec", -1)
    parts = passed_along(parts, "sec", -1)
    rounds, rank, spot, number = spots(side, halo, tile_cols, wide, at, parts[None], part)
    sums = pl.pallas_call(
        functools.partial(sums_kernel, side, halo),
        out_shape=jax.ShapeDtypeStruct((2, span, wide), jnp.float32),
        in_specs=[in_smem()] + in_vmem(3),
        out_specs=pl.BlockSpec(memory_space=pltpu.VMEM),
        scratch_shapes=sum_shapes,
        compiler_params=pltpu.CompilerParams(vmem_limit_bytes=VMEM_BYTES),
        name="sums",
    )(rounds, rank, spot, points[None])
    moving, gains = mesh_values[0:2], mesh_values[2]
    return sweeps(moving, gains, sums, number[:span], at, side, halo, extent)[None]


def solution(mesh):
    in_specs = (
        P("sec", "ty", "tx", None, None),
        P("sec", "ty", "tx", None, None),
        P("sec", "ty", "tx", None),
        P("sec", "ty", "tx", None),
        P("sec", "ty", "tx"),
        P("sec", None, "ty", "tx"),
        P("sec", "ty", "tx"),
    )
    out_specs = P("sec", None, "ty", "tx")
    return jax.shard_map(
        per_device, mesh=mesh, in_specs=in_specs, out_specs=out_specs, check_vma=False
    )
```

```python
import functools
import math

import jax
import jax.numpy as jnp
from jax import lax
from jax.experimental import pallas as pl
from jax.experimental.pallas import tpu as pltpu
from jax.sharding import PartitionSpec as P

BLK = 128
ITERS = 4
LANES = 128
PLACE_ROWS = 16
GROUP = 2
ROUND = 24
BASE = 256
DIGITS = 3
VMEM_BYTES = 24 * 1024 * 1024

spring_sec = 0.5
spring_match = 1.0
relax_rate = 0.8


def passed_along(value, axis, by):
    devices = lax.axis_size(axis)
    pairs = [(i, i + by) for i in range(devices) if 0 <= i + by < devices]
    return lax.ppermute(value, axis, pairs)


def exchanged(value, axes):
    return lax.all_to_all(value, axes, split_axis=0, concat_axis=0, tiled=True)


def spread(value, axes):
    copies = jnp.broadcast_to(value[None], (lax.axis_size(axes),) + value.shape)
    return exchanged(copies, axes)


def nt_dot(a, b):
    return lax.dot_general(a, b, (((1,), (1,)), ((), ())), preferred_element_type=jnp.float32)


def in_vmem(count):
    return [pl.BlockSpec(memory_space=pltpu.VMEM)] * count


def in_smem():
    return pl.BlockSpec(memory_space=pltpu.SMEM)


def match_kernel(scale, plan, last, at_ref, *refs):
    tile_rows = max(i for i, _ in plan) + 1
    key_tiles = max(max(among) for _, among in plan if among) + 1
    query_refs, refs = refs[:tile_rows], refs[tile_rows:]
    key_refs, refs = refs[:key_tiles], refs[key_tiles:]
    if last:
        before_ref, edge_ref, out_ref = refs[:3]
        refs = refs[3:]
    else:
        (out_ref,) = refs[:1]
        refs = refs[1:]
    query_buf, key_buf, place_buf, state_buf, list_buf = refs
    point_total = state_buf.shape[2]
    all_tiles, key_rows = key_buf.shape[:2]
    part = key_rows // BLK
    total = all_tiles * part
    own_row, share, shares = at_ref[3], at_ref[4], at_ref[5]
    rows_at, cols_at = 6, 6 + query_buf.shape[0]

    number = 0
    for tile, among in plan:
        met = [at_ref[cols_at + i] for i in among]
        listed = query_refs[tile][pl.ds(point_total, PLACE_ROWS), :]
        listed = listed.astype(jnp.float32).astype(jnp.int32)
        here = listed[0:1] == own_row * shares + share
        for low in range(0, total, 16):
            place = listed[1:2] - low
            bits = jnp.where(here & (place >= 0) & (place < 16), 1 << jnp.clip(place, 0, 15), 0)
            bits = jnp.sum(bits)
            for i in range(low, min(low + 16, total)):
                allowed = functools.reduce(jnp.logical_or, [col == i // part for col in met])
                list_buf[number] = tile * total + i
                number = number + jnp.where(allowed, (bits >> (i - low)) & 1, 0)
        list_buf[number] = -1
        number = number + lax.rem(number, 2)
    for i in range(2 * GROUP):
        list_buf[number + i] = -1
    groups = lax.div(number + 2 * GROUP - 1, 2 * GROUP)

    row_at = lax.broadcasted_iota(jnp.int32, (PLACE_ROWS, LANES), 0)
    ids = []
    for tile, key_ref in enumerate(key_refs):
        col = at_ref[cols_at + tile]
        key_buf[col] = key_ref[pl.ds(0, key_rows), :]
        rest = key_ref[pl.ds(key_rows, key_ref.shape[0] - key_rows), :].astype(jnp.float32)
        for j in range(part):
            x, y = rest[j : j + 1, :], rest[part + j : part + j + 1, :]
            stacked = jnp.where(
                row_at == 0, x, jnp.where(row_at == 1, y, jnp.where(row_at == 2, 1.0, 0.0))
            )
            place_buf[col * part + j] = stacked.astype(jnp.bfloat16)
        digits = [rest[(2 + i) * part : (3 + i) * part] for i in range(DIGITS)]
        ids.append(sum(digit * float(BASE**i) for i, digit in enumerate(digits)))
    for tile, query_ref in enumerate(query_refs):
        query_buf[tile] = query_ref[pl.ds(0, point_total), :]

    state_row = lax.broadcasted_iota(jnp.int32, state_buf.shape[1:], 0)
    for tile in range(tile_rows):
        if last and tile < before_ref.shape[0]:
            state_buf[tile] = before_ref[tile]
        else:
            state_buf[tile] = jnp.where(state_row == 3, -1e30, 0.0)

    def item(at):
        codes = [list_buf[2 * at + i] for i in range(2)]
        tile = lax.div(jnp.maximum(codes[0], 0), total)
        keys, places = [], []
        for i, code in enumerate(codes):
            block = lax.rem(jnp.maximum(jnp.where(code >= 0, code, codes[0]), 0), total)
            block = jnp.where(codes[0] >= 0, block, at_ref[cols_at] * part)
            start = pl.multiple_of(lax.rem(block, part) * BLK, BLK)
            keys.append(key_buf[lax.div(block, part), pl.ds(start, BLK), :])
            kept = jnp.where(code >= 0, 1.0, 0.0).astype(jnp.bfloat16)
            places.append(place_buf[block] * kept)
        return tile, codes[0] >= 0, jnp.concatenate(keys, axis=0), jnp.concatenate(places, axis=1)

    @pl.loop(0, groups)
    def _(group):
        items = [item(group * GROUP + i) for i in range(GROUP)]
        scores = [nt_dot(keys, query_buf[tile]) * scale for tile, _, keys, _ in items]
        tops = [jnp.max(score, axis=0, keepdims=True) for score in scores]
        weights = [jnp.exp2(s - top).astype(jnp.bfloat16) for s, top in zip(scores, tops)]
        sums = [
            jnp.dot(place, weight, preferred_element_type=jnp.float32)[0:8]
            for (_, _, _, place), weight in zip(items, weights)
        ]
        for (tile, live, _, _), top, added in zip(items, tops, sums):
            top = jnp.where(live, top, -1e30)
            state = state_buf[tile]
            before = state[3:4, :]
            both = jnp.maximum(before, top)
            state = state * jnp.exp2(before - both) + added * jnp.exp2(top - both)
            state_buf[tile] = jnp.where(state_row == 3, both, state)

    if not last:
        out_ref[...] = state_buf[pl.ds(0, tile_rows)]
        return
    edge_rows = edge_ref.shape[1]
    for tile in range(tile_rows):
        to = at_ref[rows_at + tile]
        for row in range(point_total // LANES):
            lanes = pl.ds(row * LANES, LANES)
            for place, held in enumerate((3, 2, 0, 1)):
                out_ref[row // part, to, pl.ds(place * part + row % part, 1), :] = state_buf[
                    tile, pl.ds(held, 1), lanes
                ]
        for share in range(out_ref.shape[0]):
            out_ref[share, tile, pl.ds(4 * part, key_tiles * part), :] = jnp.concatenate(ids, axis=0)
            out_ref[share, tile, pl.ds((4 + key_tiles) * part, edge_rows), :] = jnp.where(
                tile > own_row, edge_ref[1], jnp.where(tile < own_row, edge_ref[0], edge_ref[2])
            )


def match(at, queries, keys, edges, score_factor, shares, part):
    tile_rows, key_tiles = len(queries), len(keys)
    point_total, width = queries[0].shape[0] - PLACE_ROWS, queries[0].shape[1]
    total = key_tiles * part

    def call(plan, out_shape, *more):
        many_rows = max(i for i, _ in plan) + 1
        many_keys = max(max(among) for _, among in plan if among) + 1
        scores = sum(len(among) for _, among in plan) * part * point_total * BLK
        return pl.pallas_call(
            functools.partial(
                match_kernel, score_factor * math.log2(math.e), plan, len(more) > 0
            ),
            out_shape=jax.ShapeDtypeStruct(out_shape, jnp.float32),
            in_specs=[in_smem()] + in_vmem(many_rows + many_keys + len(more)),
            out_specs=pl.BlockSpec(memory_space=pltpu.VMEM),
            scratch_shapes=[
                pltpu.VMEM((tile_rows, point_total, width), jnp.bfloat16),
                pltpu.VMEM((key_tiles, part * BLK, width), jnp.bfloat16),
                pltpu.VMEM((total, PLACE_ROWS, LANES), jnp.bfloat16),
                pltpu.VMEM((tile_rows, 8, point_total), jnp.float32),
                pltpu.SMEM((tile_rows * (total + 1) + 2 * GROUP + 1,), jnp.int32),
            ],
            compiler_params=pltpu.CompilerParams(vmem_limit_bytes=VMEM_BYTES),
            cost_estimate=pl.CostEstimate(
                flops=scores * width, bytes_accessed=4 * scores // BLK, transcendentals=scores // 4
            ),
            name="match_rest" if more else "match",
        )(at, *queries[:many_rows], *keys[:many_keys], *more)

    there = [
        [i for i in range(n) if i.bit_count() < 2 or n & (n - 1)] for n in (tile_rows, key_tiles)
    ]
    first = [(i, tuple(there[1])) for i in there[0]]
    rest = [(i, tuple(j for j in range(key_tiles) if j not in there[1])) for i in there[0]]
    rest = [v for v in rest if v[1]]
    rest += [(i, tuple(range(key_tiles))) for i in range(tile_rows) if i not in there[0]]
    if rest:
        state = call(first, (len(first), 8, point_total))
    else:
        rest, row = first, jnp.arange(8)[None, :, None]
        state = jnp.where(row == 3, -1e30, jnp.zeros((tile_rows, 8, point_total), jnp.float32))
    shape = (shares, tile_rows, (4 + key_tiles) * part + edges.shape[1], LANES)
    return call(rest, shape, state, edges)


def combine_kernel(parts_ref, place_ref, out_ref):
    parts = parts_ref.shape[0]
    rows = place_ref.shape[0] // 2
    tops = [parts_ref[i, 0:rows, :] for i in range(parts)]
    top = functools.reduce(jnp.maximum, tops)
    total = x = y = jnp.zeros_like(top)
    for i in range(parts):
        gain = jnp.exp2(tops[i] - top)
        total += gain * parts_ref[i, rows : 2 * rows, :]
        x += gain * parts_ref[i, 2 * rows : 3 * rows, :]
        y += gain * parts_ref[i, 3 * rows : 4 * rows, :]
    pull = jnp.concatenate([x / total, y / total], axis=0) - place_ref[...]
    for i in range(out_ref.shape[0]):
        out_ref[i] = pull


def combine(parts, place, copies):
    return pl.pallas_call(
        combine_kernel,
        out_shape=jax.ShapeDtypeStruct((copies,) + place.shape, jnp.float32),
        in_specs=in_vmem(2),
        out_specs=pl.BlockSpec(memory_space=pltpu.VMEM),
        compiler_params=pltpu.CompilerParams(vmem_limit_bytes=VMEM_BYTES),
        name="combine",
    )(parts, place)


def one_hot(at, length, limits):
    count = at.shape[1]
    parts, done = [], 0
    for low, high in limits:
        spot = lax.broadcasted_iota(jnp.int32, (high - low, count), 0) + low
        if low > done:
            parts.append(jnp.zeros((low - done, count), jnp.bfloat16))
        parts.append(jnp.where(spot == at, 1.0, 0.0).astype(jnp.bfloat16))
        done = high
    if length > done:
        parts.append(jnp.zeros((length - done, count), jnp.bfloat16))
    return jnp.concatenate(parts, axis=0)


def flat(value):
    return jnp.concatenate([value[i : i + 1, :] for i in range(value.shape[0])], axis=1)


def hits(side, halo, tall, wide, row, col):
    up = lambda n: -(-n // 16) * 16
    limits = ((0, up(side + halo)), (wide - up(halo), wide))
    return one_hot(flat(row), tall, ((0, tall),)), one_hot(flat(col), wide, limits)


def ranked(rank, row, values):
    sums = [0.0] * len(values)
    for tile in range(rank.shape[0]):
        here = rank[tile] == row
        sums = [total + jnp.where(here, v[tile], 0.0) for total, v in zip(sums, values)]
    return [jnp.sum(total, axis=0, keepdims=True) for total in sums]


def spots_kernel(
    side, halo, key_tiles, at_ref, parts_ref, rounds_ref, rank_ref, spot_ref, count_ref, hit_buf
):
    shares, tile_rows, _, _ = parts_ref.shape
    count = rank_ref.shape[1]
    rows = count // shares
    tall, wide = count_ref.shape

    def folded(at, length):
        return jnp.where(
            (at >= 0) & (at < side + halo), at, jnp.where((at < 0) & (at >= -halo), at + length, -1)
        )

    number = jnp.zeros((1, LANES), jnp.int32)
    point_row = lax.broadcasted_iota(jnp.int32, (count, LANES), 0)
    for i in range(tile_rows):
        for j in range(key_tiles):
            ids = jnp.concatenate(
                [parts_ref[k, i, pl.ds((4 + j) * rows, rows), :] for k in range(shares)], axis=0
            ).astype(jnp.int32)
            tile_of = lax.div(ids, side * side)
            within = lax.rem(ids, side * side)
            row = lax.div(tile_of, key_tiles) * side + lax.div(within, side) - at_ref[0]
            col = lax.rem(tile_of, key_tiles) * side + lax.rem(within, side) - at_ref[1]
            row, col = folded(row, side + 2 * halo), folded(col, wide)
            here = (row >= 0) & (col >= 0)
            hit = here.astype(jnp.int32)
            by = 1
            while by < count:
                hit = hit + jnp.where(point_row >= by, pltpu.roll(hit, by, 0), 0)
                by *= 2
            tile = i * key_tiles + at_ref[6 + tile_rows + j]
            rank_ref[tile] = jnp.where(here, number + hit - 1, -1)
            hit_buf[0, tile] = row.astype(jnp.float32) + 1.0
            hit_buf[1, tile] = col.astype(jnp.float32) + 1.0
            number = number + hit[count - 1 : count, :]
    rounds = lax.div(jnp.max(number) + ROUND - 1, ROUND)
    rounds_ref[0] = rounds
    count_ref[...] = jnp.zeros_like(count_ref)

    @pl.loop(0, rounds)
    def _(k):
        found = [ranked(rank_ref, k * ROUND + r, (hit_buf.at[0], hit_buf.at[1])) for r in range(ROUND)]
        row, col = (jnp.concatenate(v, axis=0).astype(jnp.int32) - 1 for v in zip(*found))
        spot_ref[k, 0] = row
        spot_ref[k, 1] = col
        row_hit, col_hit = hits(side, halo, tall, wide, row, col)
        count_ref[...] += nt_dot(row_hit, col_hit)


def spots(side, halo, key_tiles, wide, at, parts, rows):
    tall = -(-(side + 2 * halo) // 16) * 16
    count = parts.shape[0] * rows
    tiles = parts.shape[1] * key_tiles
    rounds = -(-tiles * count // ROUND)
    return pl.pallas_call(
        functools.partial(spots_kernel, side, halo, key_tiles),
        out_shape=(
            jax.ShapeDtypeStruct((1,), jnp.int32),
            jax.ShapeDtypeStruct((tiles, count, LANES), jnp.int32),
            jax.ShapeDtypeStruct((rounds, 2, ROUND, LANES), jnp.int32),
            jax.ShapeDtypeStruct((tall, wide), jnp.float32),
        ),
        in_specs=[in_smem()] + in_vmem(1),
        out_specs=(in_smem(),) + (pl.BlockSpec(memory_space=pltpu.VMEM),) * 3,
        scratch_shapes=[pltpu.VMEM((2, tiles, count, LANES), jnp.float32)],
        compiler_params=pltpu.CompilerParams(vmem_limit_bytes=VMEM_BYTES),
        cost_estimate=pl.CostEstimate(
            flops=8 * tall * ROUND * LANES * wide,
            bytes_accessed=8 * parts.size,
            transcendentals=0,
        ),
        name="spots",
    )(at, parts)


def vertex_sums(side, halo, rounds_ref, rank_ref, spot_ref, points_ref, sum_ref, point_buf):
    _, tall, wide = sum_ref.shape
    shares, tiles, both_rows, _ = points_ref.shape
    rows = both_rows // 2
    sum_ref[...] = jnp.zeros_like(sum_ref)
    for tile in range(tiles):
        for share in range(shares):
            for c in range(2):
                point_buf[c, tile, pl.ds(share * rows, rows), :] = points_ref[
                    share, tile, pl.ds(c * rows, rows), :
                ]

    @pl.loop(0, rounds_ref[0])
    def _(k):
        found = [
            ranked(rank_ref, k * ROUND + r, (point_buf.at[0], point_buf.at[1])) for r in range(ROUND)
        ]
        _, col_hit = hits(side, halo, tall, wide, spot_ref[k, 0], spot_ref[k, 1])
        row = flat(spot_ref[k, 0])
        row_hit = lax.broadcasted_iota(jnp.int32, (tall, row.shape[1]), 0) == row
        parts = []
        for value in zip(*found):
            value = jnp.concatenate(value, axis=1)
            high = value.astype(jnp.bfloat16).astype(jnp.float32)
            for part in (high, value - high):
                parts.append(jnp.where(row_hit, part, 0.0).astype(jnp.bfloat16))
        summed = nt_dot(jnp.concatenate(parts, axis=0), col_hit)
        sum_ref[0] += summed[0:tall] + summed[tall : 2 * tall]
        sum_ref[1] += summed[2 * tall : 3 * tall] + summed[3 * tall :]


def sums_kernel(side, halo, rounds_ref, rank_ref, spot_ref, points_ref, out_ref, sum_ref, point_buf):
    vertex_sums(side, halo, rounds_ref, rank_ref, spot_ref, points_ref, sum_ref, point_buf)
    out_ref[...] = sum_ref[:, pl.ds(0, out_ref.shape[1]), :]


def relax_kernel(
    side,
    halo,
    extent,
    at_ref,
    rounds_ref,
    rank_ref,
    spot_ref,
    count_ref,
    points_ref,
    mesh_ref,
    out_ref,
    sum_ref,
    point_buf,
):
    vertex_sums(side, halo, rounds_ref, rank_ref, spot_ref, points_ref, sum_ref, point_buf)
    span = side + 2 * halo
    wide = sum_ref.shape[2]
    shape = (span, wide)
    row = lax.broadcasted_iota(jnp.int32, shape, 0)
    col = lax.broadcasted_iota(jnp.int32, shape, 1)
    row = jnp.where(row < side + halo, row, row - span) + at_ref[0]
    col = jnp.where(col < side + halo, col, col - wide) + at_ref[1]
    inside = (row >= 0) & (row < extent[0]) & (col >= 0) & (col < extent[1])
    own_pulled = (at_ref[2] == 0).astype(jnp.float32)
    linked = 1.0
    matched = count_ref[pl.ds(0, span), :]
    moving, gains, has, step = [], [], [], []
    for part, pulled in enumerate((own_pulled, 1.0 - own_pulled)):
        gain = mesh_ref[part * 3 + 2]
        diagonal = 4.0 * gain + spring_sec * linked + spring_match * matched * pulled
        gains.append(gain)
        has.append(matched * pulled)
        step.append(jnp.where(inside, relax_rate / diagonal, 0.0))
        moving.append(
            [(mesh_ref[part * 3 + c], sum_ref[c, pl.ds(0, span), :] * pulled) for c in range(2)]
        )
    for sweep in range(ITERS):
        later = []
        for part in range(2):
            row_of = []
            for c in range(2):
                u, pulled = moving[part][c]
                other = moving[1 - part][c][0]
                laplace = (
                    pltpu.roll(u, 1, 0)
                    + pltpu.roll(u, span - 1, 0)
                    + pltpu.roll(u, 1, 1)
                    + pltpu.roll(u, wide - 1, 1)
                    - 4.0 * u
                )
                force = (
                    gains[part] * laplace
                    + spring_sec * (other - linked * u)
                    + spring_match * (pulled - has[part] * u)
                )
                row_of.append((u + step[part] * force, pulled))
            later.append(row_of)
        moving = later
    for c in range(2):
        out_ref[c] = moving[0][c][0][0:side, 0:side]


def col_edges(value, halo):
    after = passed_along(value[:, :, :halo].swapaxes(1, 2), "tx", -1)
    before = passed_along(value[:, :, value.shape[2] - halo :].swapaxes(1, 2), "tx", 1)
    return jnp.concatenate([after, before], axis=1)


def sweeps(moving, gains, sums, number, at, side, halo, extent):
    sections = lax.axis_size("sec")
    sec_index = at[2]
    has_next = (sec_index < sections - 1).astype(jnp.float32)
    linked = (sec_index > 0).astype(jnp.float32) + has_next
    pulled, matched = sums * has_next, number * has_next
    span, wide = moving.shape[1:]
    row = jnp.arange(span)[:, None]
    col = jnp.arange(wide)[None, :]
    row = jnp.where(row < side + halo, row, row - span) + at[0]
    col = jnp.where(col < side + halo, col, col - wide) + at[1]
    inside = (row >= 0) & (row < extent[0]) & (col >= 0) & (col < extent[1])
    diagonal = 4.0 * gains + spring_sec * linked + spring_match * matched
    step = jnp.where(inside, relax_rate / jnp.where(inside, diagonal, 1.0), 0.0)
    for sweep in range(ITERS):
        lower_sec = passed_along(moving, "sec", 1)
        upper_sec = passed_along(moving, "sec", -1)
        laplace = (
            jnp.roll(moving, 1, 1)
            + jnp.roll(moving, -1, 1)
            + jnp.roll(moving, 1, 2)
            + jnp.roll(moving, -1, 2)
            - 4.0 * moving
        )
        force = (
            gains * laplace
            + spring_sec * (lower_sec + upper_sec - linked * moving)
            + spring_match * (pulled - matched * moving)
        )
        moving = moving + step * force
    return moving[:, :side, :side]


def pack_kernel(
    shares,
    tile_cols,
    desc_hbm,
    place_hbm,
    ids_hbm,
    list_hbm,
    count_hbm,
    first_ref,
    second_ref,
    place_ref,
    ids_ref,
    list_ref,
    count_ref,
    last_ref,
    sems,
):
    half = second_ref.shape[0]
    copies = [
        pltpu.make_async_copy(source, target, sems.at[i])
        for i, (source, target) in enumerate(
            (
                (place_hbm, place_ref),
                (ids_hbm, ids_ref),
                (list_hbm, list_ref),
                (count_hbm, count_ref),
                (desc_hbm.at[pl.ds(0, half), :], first_ref.at[pl.ds(0, half), :]),
                (desc_hbm.at[pl.ds(half, half), :], second_ref),
            )
        )
    ]
    for copy in copies:
        copy.start()
    for copy in copies[:4]:
        copy.wait()

    def cut(row):
        return [row[:, i : i + LANES] for i in range(0, row.shape[1], LANES)]

    place, ids, blocks = place_ref[...].astype(jnp.float32), ids_ref[...], list_ref[...]
    rows = cut(place[0:1]) + cut(place[1:2])
    for i in range(DIGITS):
        digit = lax.rem(lax.div(ids, BASE**i), BASE)
        rows += cut(digit.astype(jnp.float32))
    per_tile = place.shape[1] // BLK
    part = per_tile // shares
    tile, within = lax.div(blocks, per_tile), lax.rem(blocks, per_tile)
    device = lax.div(tile, tile_cols) * shares + lax.div(within, part)
    spot = lax.rem(tile, tile_cols) * part + lax.rem(within, part)
    live = lax.broadcasted_iota(jnp.int32, blocks.shape, 1) < count_ref[0, 0]
    last_ref[...] = jnp.full_like(last_ref, BASE - 1.0)
    last_ref[0:1, 0 : blocks.shape[1]] = jnp.where(live, device, BASE - 1).astype(jnp.float32)
    last_ref[1:2, 0 : blocks.shape[1]] = spot.astype(jnp.float32)
    count = first_ref.shape[0] - half
    gap = jnp.zeros((count - len(rows) - PLACE_ROWS, LANES), jnp.float32)
    rows += ([gap] if gap.shape[0] else []) + [last_ref[...]]
    first_ref[pl.ds(half, count), :] = jnp.concatenate(rows, axis=0).astype(jnp.bfloat16)
    for copy in copies[4:]:
        copy.wait()


def pack(desc, place, ids, blocks, count, shares, tile_cols):
    points, width = desc.shape
    half = points // 2
    rows = -(-(2 + DIGITS) * (points // LANES) // 16) * 16 + PLACE_ROWS
    return pl.pallas_call(
        functools.partial(pack_kernel, shares, tile_cols),
        out_shape=(
            jax.ShapeDtypeStruct((half + rows, width), jnp.bfloat16),
            jax.ShapeDtypeStruct((half, width), jnp.bfloat16),
        ),
        in_specs=[pl.BlockSpec(memory_space=pltpu.HBM)] * 5,
        out_specs=(pl.BlockSpec(memory_space=pltpu.VMEM),) * 2,
        scratch_shapes=[
            pltpu.VMEM(place.shape, place.dtype),
            pltpu.VMEM(ids.shape, ids.dtype),
            pltpu.VMEM(blocks.shape, blocks.dtype),
            pltpu.SMEM(count.shape, count.dtype),
            pltpu.VMEM((PLACE_ROWS, LANES), jnp.float32),
            pltpu.SemaphoreType.DMA((6,)),
        ],
        name="pack",
    )(desc, place, ids, blocks, count)


def turns(axis):
    devices, here = lax.axis_size(axis), lax.axis_index(axis)
    if devices & (devices - 1):
        pairs = [[(i, (i + j) % devices) for i in range(devices)] for j in range(1, devices)]
        return pairs, jnp.mod(here - jnp.arange(devices), devices)
    pairs = [[(i, i ^ j) for i in range(devices)] for j in range(1, devices)]
    return pairs, here ^ jnp.arange(devices)


def key_kernel(shares, sec_ref, first_ref, second_ref, other_ref, key_ref, place_ref):
    half = second_ref.shape[0]
    per_tile = 2 * half // LANES
    part = per_tile // shares
    own, other = first_ref, first_ref
    if shares == 2:
        other = other_ref
    at_first = sec_ref[0] == 0

    def rest(ref, share):
        rows = ref[pl.ds(half, (2 + DIGITS) * per_tile), :].astype(jnp.float32)
        kept = [
            rows[i * per_tile + share * part : i * per_tile + (share + 1) * part]
            for i in range(2 + DIGITS)
        ]
        return jnp.concatenate(kept[:2], axis=0), kept[2:]

    if shares == 2:
        keys = jnp.where(at_first, other[pl.ds(0, half), :], second_ref[...])
        key_ref[pl.ds(0, half), :] = keys
        (own_0, ids_0), (own_1, _) = rest(own, 0), rest(own, 1)
        (other_0, _), (other_1, ids_1) = rest(other, 0), rest(other, 1)
        key_place = jnp.where(at_first, other_0, own_1)
        place_ref[...] = jnp.where(at_first, own_0, other_1)
        ids = [jnp.where(at_first, a, b) for a, b in zip(ids_0, ids_1)]
    else:
        key_ref[pl.ds(0, half), :] = own[pl.ds(0, half), :]
        key_ref[pl.ds(half, half), :] = second_ref[...]
        key_place, _ = rest(own, 0)
        place_ref[...], ids = rest(other_ref, 0)
    done = part * BLK
    filler = jnp.zeros((-(2 + DIGITS) * part % 16, LANES), jnp.float32)
    rows = [key_place] + ids + ([filler] if filler.shape[0] else [])
    key_ref[pl.ds(done, key_ref.shape[0] - done), :] = jnp.concatenate(rows, axis=0).astype(
        jnp.bfloat16
    )


def key_payload(sec, first_half, second_half, other, shares):
    half, width = second_half.shape
    part = 2 * half // LANES // shares
    rows = part * BLK + -(-(2 + DIGITS) * part // 16) * 16
    return pl.pallas_call(
        functools.partial(key_kernel, shares),
        out_shape=(
            jax.ShapeDtypeStruct((rows, width), jnp.bfloat16),
            jax.ShapeDtypeStruct((2 * part, LANES), jnp.float32),
        ),
        in_specs=[in_smem()] + in_vmem(3),
        out_specs=(pl.BlockSpec(memory_space=pltpu.VMEM),) * 2,
        compiler_params=pltpu.CompilerParams(vmem_limit_bytes=VMEM_BYTES),
        name="key_payload",
    )(sec, first_half, second_half, other)


def query_kernel(shares, sec_ref, first_ref, second_ref, other_ref, came_ref, out_ref):
    half = second_ref.shape[0]
    last = first_ref.shape[0] - PLACE_ROWS

    def chosen(own, other):
        return jnp.where(sec_ref[0] == 0, own, other) if shares == 2 else other

    for target, rows in ((0, pl.ds(0, half)), (2 * half, pl.ds(last, PLACE_ROWS))):
        out_ref[pl.ds(target, rows.size), :] = chosen(first_ref[rows, :], other_ref[rows, :])
    out_ref[pl.ds(half, half), :] = chosen(second_ref[...], came_ref[...])


def query_payload(sec, first_half, second_half, other, came, shares):
    half, width = second_half.shape
    return pl.pallas_call(
        functools.partial(query_kernel, shares),
        out_shape=jax.ShapeDtypeStruct((2 * half + PLACE_ROWS, width), jnp.bfloat16),
        in_specs=[in_smem()] + in_vmem(4),
        out_specs=pl.BlockSpec(memory_space=pltpu.VMEM),
        compiler_params=pltpu.CompilerParams(vmem_limit_bytes=VMEM_BYTES),
        name="query_payload",
    )(sec, first_half, second_half, other, came)


def gathered(values, axes, beside):
    held, steps = [], []
    for value, axis in zip(values, axes):
        devices = lax.axis_size(axis)
        if devices & (devices - 1):
            moved = [lax.ppermute(value, axis, pairs) for pairs in turns(axis)[0]]
            held.append(dict(enumerate([value] + moved)))
            steps.append(0)
        else:
            held.append({0: value})
            steps.append(devices.bit_length() - 1)
    for step in range(1, max(steps) + 1):
        for i, axis in enumerate(axes):
            devices = lax.axis_size(axis)
            for at in range(devices - 1, 0, -1):
                if steps[i] and at.bit_count() == step:
                    by = at & -at
                    pairs = [(j, j ^ by) for j in range(devices)]
                    held[i][at] = lax.ppermute(held[i][at ^ by], axis, pairs)
        if step == 1:
            held, beside = lax.optimization_barrier((held, beside))
    return [[h[i] for i in range(len(h))] for h in held], beside


def per_device(
    descriptors, positions, vertex_ids, candidate_blocks, candidate_count, displacement, stiffness
):
    point_total, width = descriptors.shape[3:]
    per_tile = point_total // BLK
    tile_rows, tile_cols = lax.axis_size("ty"), lax.axis_size("tx")
    sections = lax.axis_size("sec")
    sec_index = lax.axis_index("sec")
    tiles = tile_rows * tile_cols
    side = displacement.shape[3]
    halo = ITERS
    span = side + 2 * halo
    wide = -(-span // LANES) * LANES
    cand = candidate_blocks.shape[3]
    shares = 2 if sections == 2 and per_tile % 2 == 0 else 1
    part = per_tile // shares
    key_rows = part * BLK

    first_half, second_half = pack(
        descriptors[0, 0, 0],
        positions[0, 0, 0],
        vertex_ids[0, 0],
        candidate_blocks[0, 0],
        candidate_count[0, 0][None],
        shares,
        tile_cols,
    )
    half = point_total // 2
    swap = [(i, 1 - i) for i in range(2)]

    sec = jnp.asarray(sec_index, jnp.int32)[None]
    own_mesh = jnp.concatenate([displacement[0], stiffness], axis=0)
    if shares == 2:
        share = sec_index
        other = lax.ppermute(first_half, "sec", swap)
    else:
        share = 0
        other = passed_along(first_half, "sec", 1)
    came = passed_along(second_half, "sec", 1)
    cols = col_edges(own_mesh, halo)
    key, place = key_payload(sec, first_half, second_half, other, shares)
    meshes = [own_mesh]
    if shares == 2:
        tied, key = lax.optimization_barrier((own_mesh, key))
        meshes.append(lax.ppermute(tied, "sec", swap))
    query = query_payload(sec, first_half, second_half, other, came, shares)
    (queries, keys), (cols, meshes) = gathered((query, key), ("ty", "tx"), (cols, meshes))
    at = jnp.concatenate(
        [
            jnp.stack([lax.axis_index("ty") * side, lax.axis_index("tx") * side, sec_index]),
            jnp.stack([lax.axis_index("ty"), jnp.asarray(share), jnp.asarray(shares)]),
            turns("ty")[1],
            turns("tx")[1],
        ]
    ).astype(jnp.int32)
    extent = (side * tile_rows, side * tile_cols)
    sum_shapes = [
        pltpu.VMEM((2, -(-span // 16) * 16, wide), jnp.float32),
        pltpu.VMEM((2, tiles, per_tile, LANES), jnp.float32),
    ]

    top, end = own_mesh[:, :halo], own_mesh[:, side - halo :]
    corners = [
        jnp.pad(v.swapaxes(1, 2), ((0, 0), (0, 0), (0, side - 2 * halo)))
        for v in (cols[:, :, :halo], cols[:, :, side - halo :])
    ]
    edges = [jnp.concatenate(v, axis=0) for v in ((top, corners[0]), (end, corners[1]))]
    edges = jnp.stack([v.reshape(-1, LANES) for v in edges + [cols]])
    parts = match(at, queries, keys, edges, 16.0 / width, shares, part)
    shape = parts.shape
    parts = exchanged(parts.reshape((-1,) + shape[2:]), ("sec", "ty") if shares == 2 else "ty")
    pulls = combine(parts, place, shares * tiles)
    parts, pulls, meshes = lax.optimization_barrier((parts, pulls, meshes))

    def edge_rows(by):
        near = lax.axis_index("ty") + by
        rows = parts.reshape(shape)[:, :, -edges.shape[1] :]
        rows = lax.dynamic_index_in_dim(rows, jnp.clip(near, 0, tile_rows - 1), 1, keepdims=False)
        rows = jnp.where((near >= 0) & (near < tile_rows), rows, 0.0)
        rows = rows.reshape(shares, 2, 3, halo, side)
        if shares == 2:
            rows = jnp.where(sec_index == 0, rows, rows[::-1])
        return [
            jnp.concatenate([rows[i, 0], rows[i, 1, :, :, : 2 * halo]], axis=2)
            for i in range(shares)
        ]

    after, before = edge_rows(1), edge_rows(-1)
    cols = [cols]
    if shares == 2:
        sent = parts.reshape(shape)[:, :, -edges.shape[1] :]
        sent = lax.dynamic_index_in_dim(sent, lax.axis_index("ty"), 1, keepdims=False)
        cols.append(jnp.where(sec_index == 0, sent[1], sent[0]).reshape(cols[0].shape))
    framed = []
    for i, mesh in enumerate(meshes):
        whole = jnp.concatenate([mesh, cols[i].swapaxes(1, 2)], axis=2)
        framed.append(jnp.concatenate([whole, after[i], before[i]], axis=1))
    framed = jnp.concatenate(framed, axis=0)
    gap = jnp.zeros(framed.shape[:2] + (wide - span,), framed.dtype)
    mesh_values = jnp.concatenate(
        [framed[:, :, : side + halo], gap, framed[:, :, side + halo :]], axis=2
    )
    if shares == 2:
        points = exchanged(pulls, ("sec", "ty", "tx"))
        rounds, rank, spot, number = spots(side, halo, tile_cols, wide, at, parts.reshape(shape), part)
        relaxed = pl.pallas_call(
            functools.partial(relax_kernel, side, halo, extent),
            out_shape=jax.ShapeDtypeStruct((2, side, side), jnp.float32),
            in_specs=[in_smem()] * 2 + in_vmem(5),
            out_specs=pl.BlockSpec(memory_space=pltpu.VMEM),
            scratch_shapes=sum_shapes,
            compiler_params=pltpu.CompilerParams(vmem_limit_bytes=VMEM_BYTES),
            name="relax",
        )(at, rounds, rank, spot, number, points.reshape(2, tiles, -1, LANES), mesh_values)
        return relaxed[None]

    points = passed_along(exchanged(pulls, ("ty", "tx")), "sec", -1)
    parts = passed_along(parts, "sec", -1)
    rounds, rank, spot, number = spots(side, halo, tile_cols, wide, at, parts[None], part)
    sums = pl.pallas_call(
        functools.partial(sums_kernel, side, halo),
        out_shape=jax.ShapeDtypeStruct((2, span, wide), jnp.float32),
        in_specs=[in_smem()] + in_vmem(3),
        out_specs=pl.BlockSpec(memory_space=pltpu.VMEM),
        scratch_shapes=sum_shapes,
        compiler_params=pltpu.CompilerParams(vmem_limit_bytes=VMEM_BYTES),
        name="sums",
    )(rounds, rank, spot, points[None])
    moving, gains = mesh_values[0:2], mesh_values[2]
    return sweeps(moving, gains, sums, number[:span], at, side, halo, extent)[None]


def solution(mesh):
    in_specs = (
        P("sec", "ty", "tx", None, None),
        P("sec", "ty", "tx", None, None),
        P("sec", "ty", "tx", None),
        P("sec", "ty", "tx", None),
        P("sec", "ty", "tx"),
        P("sec", None, "ty", "tx"),
        P("sec", "ty", "tx"),
    )
    out_specs = P("sec", None, "ty", "tx")
    return jax.shard_map(
        per_device, mesh=mesh, in_specs=in_specs, out_specs=out_specs, check_vma=False
    )
```
